32 devices in a mesh: rep: 4 (over x, core), shard: 8 (over z, y).
Axes of the slice: x: 2, y: 2, z: 4, core: 2. Of those that a mesh axis runs over, the one named last changes fastest.
Arguments:
- tokens: bfloat16 [4096, 2304], P(('rep', 'shard')), may hold values from -6 to 6
- cotangent: bfloat16 [4096, 2304], P(('rep', 'shard')), may hold values from -6 to 6
- piece_starts: int32 [4, 2], replicated, may hold values from 0 to 768, as said below
- inproj: float32 [2304, 4096], P(('rep', 'shard'))
- outproj: float32 [2048, 2304], P(('rep', 'shard'))
- ffn_gate: float32 [2304, 9216], P(('rep', 'shard'))
- ffn_up: float32 [2304, 9216], P(('rep', 'shard'))
- ffn_down: float32 [9216, 2304], P(('rep', 'shard'))
- norm_gains: float32 [2304, 4], P(('rep', 'shard'))
- mean_inproj: float32 [2304, 4096], P(('rep', 'shard'))
- mean_outproj: float32 [2048, 2304], P(('rep', 'shard'))
- mean_gate: float32 [2304, 9216], P(('rep', 'shard'))
- mean_up: float32 [2304, 9216], P(('rep', 'shard'))
- mean_down: float32 [9216, 2304], P(('rep', 'shard'))
- mean_gains: float32 [2304, 4], P(('rep', 'shard'))
- square_inproj: float32 [2304, 4096], P(('rep', 'shard')), may hold values from 409.6 to 1638.4
- square_outproj: float32 [2048, 2304], P(('rep', 'shard')), may hold values from 409.6 to 1638.4
- square_gate: float32 [2304, 9216], P(('rep', 'shard')), may hold values from 409.6 to 1638.4
- square_up: float32 [2304, 9216], P(('rep', 'shard')), may hold values from 409.6 to 1638.4
- square_down: float32 [9216, 2304], P(('rep', 'shard')), may hold values from 409.6 to 1638.4
- square_gains: float32 [2304, 4], P(('rep', 'shard')), may hold values from 409.6 to 1638.4
Outputs:
- layer_out: bfloat16 [4096, 2304], P(('rep', 'shard'))
- input_grad: float32 [4096, 2304], P(('rep', 'shard'))
- grad_inproj: float32 [2304, 4096], P(('rep', 'shard'))
- grad_outproj: float32 [2048, 2304], P(('rep', 'shard'))
- grad_gate: float32 [2304, 9216], P(('rep', 'shard'))
- grad_up: float32 [2304, 9216], P(('rep', 'shard'))
- grad_down: float32 [9216, 2304], P(('rep', 'shard'))
- grad_gains: float32 [2304, 4], P(('rep', 'shard'))
- newmean_inproj: float32 [2304, 4096], P(('rep', 'shard'))
- newmean_outproj: float32 [2048, 2304], P(('rep', 'shard'))
- newmean_gate: float32 [2304, 9216], P(('rep', 'shard'))
- newmean_up: float32 [2304, 9216], P(('rep', 'shard'))
- newmean_down: float32 [9216, 2304], P(('rep', 'shard'))
- newmean_gains: float32 [2304, 4], P(('rep', 'shard'))
- newsquare_inproj: float32 [2304, 4096], P(('rep', 'shard'))
- newsquare_outproj: float32 [2048, 2304], P(('rep', 'shard'))
- newsquare_gate: float32 [2304, 9216], P(('rep', 'shard'))
- newsquare_up: float32 [2304, 9216], P(('rep', 'shard'))
- newsquare_down: float32 [9216, 2304], P(('rep', 'shard'))
- newsquare_gains: float32 [2304, 4], P(('rep', 'shard'))
- new_inproj: float32 [2304, 4096], P(('rep', 'shard'))
- new_outproj: float32 [2048, 2304], P(('rep', 'shard'))
- new_gate: float32 [2304, 9216], P(('rep', 'shard'))
- new_up: float32 [2304, 9216], P(('rep', 'shard'))
- new_down: float32 [9216, 2304], P(('rep', 'shard'))
- new_gains: float32 [2304, 4], P(('rep', 'shard'))
- norm_table: float32 [2, 6], replicated
The draws below stay inside these ranges and needn't reach their ends.
Inputs may be any that keep to these rules, and one draw needn't show every extreme that they name: `piece_starts`: each sequence's 2 picture pieces of 256 positions start in increasing order, lie inside the sequence and do not intersect.
All inputs are finite; a program needn't handle non-finite values.
Results may differ from the reference program's by a relative error of at most 0.019.
Values may be sent and summed in bfloat16 or wider, within the bound.
A program may use at most 512 MiB of HBM per device.

```python
import math
import jax
import jax.numpy as jnp
from jax import lax

D = 2304
FF = 9216
HEADS = 8
KV_HEADS = 4
HEAD_DIM = 256
PIC = 256
PICS = 2
SEQ_LEN = 1024
TOKENS = 4096
NSEQ = 4


def rising(key, rows, cols, scale):
    ramp = jnp.arange(rows, dtype=jnp.float32) / max(rows - 1, 1)
    factor = 0.5 + ramp
    base = jnp.clip(jax.random.normal(key, (rows, cols), jnp.float32), -6.0, 6.0)
    return base * scale * factor[:, None]


def draw_inproj(key, part):
    return rising(jax.random.fold_in(key, 1), D, (HEADS + 2 * KV_HEADS) * HEAD_DIM, D ** (-0.5))


def draw_outproj(key, part):
    return rising(jax.random.fold_in(key, 2), HEADS * HEAD_DIM, D, (HEADS * HEAD_DIM) ** (-0.5))


def draw_ffn_gate(key, part):
    return rising(jax.random.fold_in(key, 3), D, FF, D ** (-0.5))


def draw_ffn_up(key, part):
    return rising(jax.random.fold_in(key, 4), D, FF, D ** (-0.5))


def draw_ffn_down(key, part):
    return rising(jax.random.fold_in(key, 5), FF, D, FF ** (-0.5))


def draw_norm_gains(key, part):
    return rising(jax.random.fold_in(key, 6), D, 4, 0.3)


def draw_mean_inproj(key, part):
    return rising(jax.random.fold_in(key, 11), D, (HEADS + 2 * KV_HEADS) * HEAD_DIM, 0.5 * TOKENS ** 0.5)


def draw_mean_outproj(key, part):
    return rising(jax.random.fold_in(key, 12), HEADS * HEAD_DIM, D, 0.5 * TOKENS ** 0.5)


def draw_mean_gate(key, part):
    return rising(jax.random.fold_in(key, 13), D, FF, 0.5 * TOKENS ** 0.5)


def draw_mean_up(key, part):
    return rising(jax.random.fold_in(key, 14), D, FF, 0.5 * TOKENS ** 0.5)


def draw_mean_down(key, part):
    return rising(jax.random.fold_in(key, 15), FF, D, 0.5 * TOKENS ** 0.5)


def draw_mean_gains(key, part):
    return rising(jax.random.fold_in(key, 16), D, 4, 0.5 * TOKENS ** 0.5)


def draw_piece_starts(key, part):
    spare = SEQ_LEN - PICS * PIC
    offsets = jax.random.randint(jax.random.fold_in(key, 20), (NSEQ, PICS), 0, spare + 1, dtype=jnp.int32)
    offsets = jnp.sort(offsets, axis=1)
    offsets = offsets.at[0, PICS - 1].set(spare)
    offsets = offsets.at[NSEQ - 1, 0].set(0)
    return offsets + jnp.arange(PICS, dtype=jnp.int32)[None, :] * PIC


def levels(stream_key, shape, cuts, low, largest):
    loudness, own = 1.0, jax.random.fold_in(stream_key, 6)
    for axis_at, parts in cuts:
        steps = jnp.exp(jax.random.uniform(jax.random.fold_in(own, axis_at), (parts,), jnp.float32, low / len(cuts), largest / len(cuts)))
        loudness = loudness * jnp.repeat(steps, shape[axis_at] // parts).reshape([-1 if axis == axis_at else 1 for axis in range(len(shape))])
    return loudness


def noise(stream_key, shape, scale, reach, split=(), kind=jnp.bfloat16):
    array = jax.random.normal(stream_key, shape, jnp.float32) * scale
    if len(split) > 0:
        array = levels(stream_key, shape, split, -0.22, 0.18) * array
    return jnp.clip(array, min=-reach, max=reach).astype(kind)


def setup_inputs(seed: int = 0) -> dict:
    arg_keys = jax.random.split(jax.random.key(seed), 22)
    tokens = noise(arg_keys[0], (TOKENS, D), 1.0, 6.0, ((0, 32),))
    cotangent = noise(arg_keys[1], (TOKENS, D), 1.0, 6.0, ((0, 32),))
    piece_starts = draw_piece_starts(jax.random.fold_in(arg_keys[21], 71), 0)
    inproj = draw_inproj(jax.random.fold_in(arg_keys[21], 71), 0)
    outproj = draw_outproj(jax.random.fold_in(arg_keys[21], 71), 0)
    ffn_gate = draw_ffn_gate(jax.random.fold_in(arg_keys[21], 71), 0)
    ffn_up = draw_ffn_up(jax.random.fold_in(arg_keys[21], 71), 0)
    ffn_down = draw_ffn_down(jax.random.fold_in(arg_keys[21], 71), 0)
    norm_gains = draw_norm_gains(jax.random.fold_in(arg_keys[21], 71), 0)
    mean_inproj = draw_mean_inproj(jax.random.fold_in(arg_keys[21], 71), 0)
    mean_outproj = draw_mean_outproj(jax.random.fold_in(arg_keys[21], 71), 0)
    mean_gate = draw_mean_gate(jax.random.fold_in(arg_keys[21], 71), 0)
    mean_up = draw_mean_up(jax.random.fold_in(arg_keys[21], 71), 0)
    mean_down = draw_mean_down(jax.random.fold_in(arg_keys[21], 71), 0)
    mean_gains = draw_mean_gains(jax.random.fold_in(arg_keys[21], 71), 0)
    square_inproj = jnp.clip(jnp.exp(math.log(1638.4) - 1.3862944 * jax.random.uniform(arg_keys[15], (D, (HEADS + 2 * KV_HEADS) * HEAD_DIM), jnp.float32) ** levels(arg_keys[15], (D, (HEADS + 2 * KV_HEADS) * HEAD_DIM), ((0, 32),), -0.2, 0.2)), 409.6, 1638.4)
    square_outproj = jnp.clip(jnp.exp(math.log(1638.4) - 1.3862944 * jax.random.uniform(arg_keys[16], (HEADS * HEAD_DIM, D), jnp.float32) ** levels(arg_keys[16], (HEADS * HEAD_DIM, D), ((0, 32),), -0.2, 0.2)), 409.6, 1638.4)
    square_gate = jnp.clip(jnp.exp(math.log(1638.4) - 1.3862944 * jax.random.uniform(arg_keys[17], (D, FF), jnp.float32) ** levels(arg_keys[17], (D, FF), ((0, 32),), -0.2, 0.2)), 409.6, 1638.4)
    square_up = jnp.clip(jnp.exp(math.log(1638.4) - 1.3862944 * jax.random.uniform(arg_keys[18], (D, FF), jnp.float32) ** levels(arg_keys[18], (D, FF), ((0, 32),), -0.2, 0.2)), 409.6, 1638.4)
    square_down = jnp.clip(jnp.exp(math.log(1638.4) - 1.3862944 * jax.random.uniform(arg_keys[19], (FF, D), jnp.float32) ** levels(arg_keys[19], (FF, D), ((0, 32),), -0.2, 0.2)), 409.6, 1638.4)
    square_gains = jnp.clip(jnp.exp(math.log(1638.4) - 1.3862944 * jax.random.uniform(arg_keys[20], (D, 4), jnp.float32) ** levels(arg_keys[20], (D, 4), ((0, 32),), -0.2, 0.2)), 409.6, 1638.4)
    return {"tokens": tokens, "cotangent": cotangent, "piece_starts": piece_starts, "inproj": inproj, "outproj": outproj, "ffn_gate": ffn_gate, "ffn_up": ffn_up, "ffn_down": ffn_down, "norm_gains": norm_gains, "mean_inproj": mean_inproj, "mean_outproj": mean_outproj, "mean_gate": mean_gate, "mean_up": mean_up, "mean_down": mean_down, "mean_gains": mean_gains, "square_inproj": square_inproj, "square_outproj": square_outproj, "square_gate": square_gate, "square_up": square_up, "square_down": square_down, "square_gains": square_gains}


@jax.custom_vjp
def low(v):
    return lax.optimization_barrier(v.astype(jnp.bfloat16)).astype(jnp.float32)

@jax.custom_vjp
def low_back(v):
    return v

def low_keep(v):
    return (low(v), None)

def low_pass(kept, grad):
    return (grad,)

def back_keep(v):
    return (v, None)

def back_low(kept, grad):
    return (low(grad),)
low.defvjp(low_keep, low_pass)
low_back.defvjp(back_keep, back_low)

def rms_norm(values_in, gain_col):
    return values_in * lax.rsqrt(lax.optimization_barrier(jnp.mean(values_in * values_in, axis=-1, keepdims=True)) + 1e-06) * (1.0 + gain_col)

def rotate(vectors, position):
    width = vectors.shape[-1]
    half = width // 2
    freq = 10000.0 ** (-(jnp.arange(half, dtype=jnp.float32) * 2.0 / width))
    angle = position.astype(jnp.float32)[:, None] * freq[None, :]
    cosine = jnp.cos(angle)[:, None, :]
    sine = jnp.sin(angle)[:, None, :]
    first = vectors[..., :half]
    second = vectors[..., half:]
    return jnp.concatenate([first * cosine - second * sine, second * cosine + first * sine], axis=-1)

def layer_block(block_rows, starts, weights):
    w_in, w_out, w_gate, w_up, w_down, gains = weights
    highest = lax.Precision.HIGHEST
    seq_count = starts.shape[0]
    row_count = seq_count * SEQ_LEN
    q_width = HEADS * HEAD_DIM
    k_width = KV_HEADS * HEAD_DIM
    normed_in = low(rms_norm(block_rows, gains[:, 0]))
    projected = low_back(jnp.dot(normed_in, w_in, precision=highest))
    position = jnp.arange(SEQ_LEN, dtype=jnp.int32)
    query_raw = projected[:, :q_width].reshape(seq_count, SEQ_LEN, HEADS, HEAD_DIM)
    key_raw = projected[:, q_width:q_width + k_width].reshape(seq_count, SEQ_LEN, KV_HEADS, HEAD_DIM)
    value_raw = projected[:, q_width + k_width:].reshape(seq_count, SEQ_LEN, KV_HEADS, HEAD_DIM)
    queries = low(rotate(query_raw, position) * HEAD_DIM ** (-0.5))
    keys = low(rotate(key_raw, position))
    values = low(value_raw)
    query_heads = queries.reshape(seq_count, SEQ_LEN, KV_HEADS, HEADS // KV_HEADS, HEAD_DIM)
    raw_scores = low_back(jnp.einsum('nqgrd,nkgd->ngrqk', query_heads, keys, precision=highest))
    capped = 50.0 * jnp.tanh(raw_scores / 50.0)
    inside = (position[None, :, None] >= starts[:, None, :]) & (position[None, :, None] < starts[:, None, :] + PIC)
    shared = jnp.any(inside[:, :, None, :] & inside[:, None, :, :], axis=-1)
    visible = (position[None, None, :] <= position[None, :, None]) | shared
    masked = jnp.where(visible[:, None, None], capped, -1e+30)
    top_score = lax.optimization_barrier(jnp.max(masked, axis=-1, keepdims=True))
    expo = jnp.exp(masked - top_score)
    attn_probs = low(expo / lax.optimization_barrier(jnp.sum(expo, axis=-1, keepdims=True)))
    attended = jnp.einsum('ngrqk,nkgd->nqgrd', attn_probs, values, precision=highest).reshape(row_count, q_width)
    attended = low(low_back(attended))
    attn_proj = low_back(jnp.dot(attended, w_out, precision=highest))
    middle = block_rows + rms_norm(attn_proj, gains[:, 1])
    normed_mid = low(rms_norm(middle, gains[:, 2]))
    gate_lin = low_back(jnp.dot(normed_mid, w_gate, precision=highest))
    up_lin = low_back(jnp.dot(normed_mid, w_up, precision=highest))
    hidden = low(jax.nn.gelu(gate_lin, approximate=True) * up_lin)
    ffn_proj = low_back(jnp.dot(hidden, w_down, precision=highest))
    return middle + rms_norm(ffn_proj, gains[:, 3])

def lamb_step(master, gradient, first, second):
    newmean = 0.5 * first + 0.5 * gradient
    newsquare = 0.5 * second + 0.5 * gradient * gradient
    step_dir = newmean / (jnp.sqrt(newsquare) + 1e-06) + 0.01 * master
    weight_rms = jnp.sqrt(jnp.mean(master * master) + 1e-06)
    step_rms = jnp.sqrt(jnp.mean(step_dir * step_dir) + 1e-06)
    fresh = master - 0.3 * weight_rms / step_rms * step_dir
    return (newmean, newsquare, fresh, weight_rms, step_rms)

def reference(tokens, cotangent, piece_starts, inproj, outproj, ffn_gate, ffn_up, ffn_down, norm_gains, mean_inproj, mean_outproj, mean_gate, mean_up, mean_down, mean_gains, square_inproj, square_outproj, square_gate, square_up, square_down, square_gains):
    residual = tokens.astype(jnp.float32)
    group_size = 2 if NSEQ % 2 == 0 and 2 * SEQ_LEN <= 4096 else 1
    block_count = NSEQ // group_size

    def forward(rows_in, w_in, w_out, w_gate, w_up, w_down, gains):
        weights = (low(w_in), low(w_out), low(w_gate), low(w_up), low(w_down), low(gains))

        def advance(carry, item):
            return (carry, jax.checkpoint(layer_block)(item[0], item[1], weights))
        _, outputs = lax.scan(advance, jnp.zeros((), jnp.float32), (rows_in.reshape(block_count, group_size * SEQ_LEN, D), piece_starts.reshape(block_count, group_size, PICS)))
        return outputs.reshape(TOKENS, D)
    layer_f32, backward = jax.vjp(forward, residual, inproj, outproj, ffn_gate, ffn_up, ffn_down, norm_gains)
    grads = backward(cotangent.astype(jnp.float32))
    r_in = lamb_step(inproj, grads[1], mean_inproj, square_inproj)
    r_out = lamb_step(outproj, grads[2], mean_outproj, square_outproj)
    r_gate = lamb_step(ffn_gate, grads[3], mean_gate, square_gate)
    r_up = lamb_step(ffn_up, grads[4], mean_up, square_up)
    r_down = lamb_step(ffn_down, grads[5], mean_down, square_down)
    r_gains = lamb_step(norm_gains, grads[6], mean_gains, square_gains)
    results = (r_in, r_out, r_gate, r_up, r_down, r_gains)
    norm_table = jnp.stack([jnp.stack([item[3] for item in results]), jnp.stack([item[4] for item in results])])
    return (layer_f32.astype(jnp.bfloat16), grads[0], grads[1], grads[2], grads[3], grads[4], grads[5], grads[6], r_in[0], r_out[0], r_gate[0], r_up[0], r_down[0], r_gains[0], r_in[1], r_out[1], r_gate[1], r_up[1], r_down[1], r_gains[1], r_in[2], r_out[2], r_gate[2], r_up[2], r_down[2], r_gains[2], norm_table)
```

```python
import functools

import jax
import jax.numpy as jnp
from jax import lax
from jax.experimental import pallas as pl
from jax.experimental.pallas import tpu as pltpu
from jax.sharding import PartitionSpec as P

HEADS = 8
KV_HEADS = 4
HEAD_DIM = 256
PIC = 256


def rms_norm(values_in, gain_col):
    return (
        values_in
        * lax.rsqrt(jnp.mean(values_in * values_in, axis=-1, keepdims=True) + 1e-06)
        * (1.0 + gain_col)
    )


def geglu(gate_lin, up_lin):
    return jax.nn.gelu(gate_lin, approximate=True) * up_lin


def rotate(flat, position, head_count, sign):
    row_count = flat.shape[0]
    width = flat.shape[1] // head_count
    half = width // 2
    vectors = flat.reshape(row_count, head_count, width)
    freq = 10000.0 ** (-(jnp.arange(half, dtype=jnp.float32) * 2.0 / width))
    angle = position.astype(jnp.float32)[:, None] * freq[None, :]
    cosine = jnp.cos(angle)[:, None, :]
    sine = sign * jnp.sin(angle)[:, None, :]
    first = vectors[..., :half]
    second = vectors[..., half:]
    turned = jnp.concatenate(
        [first * cosine - second * sine, second * cosine + first * sine], axis=-1
    )
    return turned.reshape(row_count, head_count * width)


def owned_rows(activation, gradient, rep_index, width):
    piece = lax.dynamic_slice_in_dim(activation, rep_index * width, width, 1)
    return lax.dot_general(
        piece, gradient, (((0,), (0,)), ((), ())), preferred_element_type=jnp.float32
    )


def back_dot(gradient, weight):
    return lax.dot_general(
        gradient, weight, (((1,), (1,)), ((), ())), preferred_element_type=jnp.float32
    )


def describe(rows, piece_starts, seq_offset, seq_len):
    local_seq = rows // seq_len
    position = rows % seq_len
    global_seq = local_seq + seq_offset
    seq_total = piece_starts.shape[0]
    piece_count = piece_starts.shape[1]
    select = (global_seq[:, None] == jnp.arange(seq_total, dtype=jnp.int32)[None, :]).astype(
        jnp.int32
    )
    starts = jnp.sum(select[:, :, None] * piece_starts[None, :, :], axis=1)
    inside = ((position[:, None] >= starts) & (position[:, None] < starts + PIC)).astype(jnp.int32)
    labels = (
        global_seq[:, None] * piece_count + jnp.arange(piece_count, dtype=jnp.int32)[None, :] + 1
    )
    return (local_seq, position, jnp.sum(inside * labels, axis=1))


def visibility(piece_starts, query_rows, key_rows, seq_offset, seq_len):
    seq_q, pos_q, tag_q = describe(query_rows, piece_starts, seq_offset, seq_len)
    seq_k, pos_k, tag_k = describe(key_rows, piece_starts, seq_offset, seq_len)
    causal = pos_k[None, :] <= pos_q[:, None]
    same_piece = (tag_q[:, None] == tag_k[None, :]) & (tag_q[:, None] > 0)
    return (seq_q[:, None] == seq_k[None, :]) & (causal | same_piece)


def lamb_local(master, gradient, first, second):
    newmean = 0.5 * first + 0.5 * gradient
    newsquare = 0.5 * second + 0.5 * gradient * gradient
    step_dir = newmean / (jnp.sqrt(newsquare) + 1e-06) + 0.01 * master
    return (newmean, newsquare, step_dir)


def per_device(
    tokens,
    cotangent,
    piece_starts,
    inproj,
    outproj,
    ffn_gate,
    ffn_up,
    ffn_down,
    norm_gains,
    mean_inproj,
    mean_outproj,
    mean_gate,
    mean_up,
    mean_down,
    mean_gains,
    square_inproj,
    square_outproj,
    square_gate,
    square_up,
    square_down,
    square_gains,
):
    bf16 = jnp.bfloat16
    f32 = jnp.float32
    rep_count = lax.axis_size("rep")
    shard_count = lax.axis_size("shard")
    rep_index = lax.axis_index("rep")
    w_in, w_out, w_gate, w_up, w_down, gain_copy = (
        lax.all_gather(inproj.astype(bf16), ("rep", "shard"), axis=0, tiled=True),
        lax.all_gather(outproj.astype(bf16), ("rep", "shard"), axis=0, tiled=True),
        lax.all_gather(ffn_gate.astype(bf16), ("rep", "shard"), axis=0, tiled=True),
        lax.all_gather(ffn_up.astype(bf16), ("rep", "shard"), axis=0, tiled=True),
        lax.all_gather(ffn_down.astype(bf16), ("rep", "shard"), axis=0, tiled=True),
        lax.all_gather(norm_gains.astype(bf16), ("rep", "shard"), axis=0, tiled=True),
    )
    gains_used = gain_copy.astype(f32)
    residual = tokens.astype(f32)
    row_count = residual.shape[0]
    seq_len = row_count * shard_count
    q_width = HEADS * HEAD_DIM
    k_width = KV_HEADS * HEAD_DIM
    group_size = HEADS // KV_HEADS
    query_scale = HEAD_DIM ** (-0.5)
    local_rows = lax.axis_index("shard") * row_count + jnp.arange(row_count, dtype=jnp.int32)
    position = local_rows % seq_len
    normed_in = rms_norm(residual, gains_used[:, 0]).astype(bf16)
    projected = jnp.dot(normed_in, w_in, preferred_element_type=f32)
    queries = (rotate(projected[:, :q_width], position, HEADS, 1.0) * query_scale).astype(bf16)
    keys = rotate(projected[:, q_width : q_width + k_width], position, KV_HEADS, 1.0).astype(bf16)
    values = projected[:, q_width + k_width :].astype(bf16)
    all_keys, all_values = (
        lax.all_gather(keys, "shard", axis=0, tiled=True),
        lax.all_gather(values, "shard", axis=0, tiled=True),
    )
    key_rows = all_keys.shape[0]
    visible = visibility(
        piece_starts,
        local_rows,
        jnp.arange(key_rows, dtype=jnp.int32),
        rep_index * (key_rows // seq_len),
        seq_len,
    )
    query_heads = queries.reshape(row_count, KV_HEADS, group_size, HEAD_DIM)
    key_heads = all_keys.reshape(key_rows, KV_HEADS, HEAD_DIM)
    value_heads = all_values.reshape(key_rows, KV_HEADS, HEAD_DIM)

    def capped_scores():
        raw_scores = jnp.einsum(
            "tgrd,kgd->grtk", query_heads, key_heads, preferred_element_type=f32
        )
        bent_scores = jnp.tanh(raw_scores / 50.0)
        return (bent_scores, jnp.where(visible, 50.0 * bent_scores, -1e30))

    bent_scores, masked = capped_scores()
    top_score = jnp.max(masked, axis=-1, keepdims=True)
    log_total = top_score + jnp.log(jnp.sum(jnp.exp(masked - top_score), axis=-1, keepdims=True))
    probs_low = jnp.exp(masked - log_total).astype(bf16)
    attended = (
        jnp.einsum("grtk,kgd->tgrd", probs_low, value_heads, preferred_element_type=f32)
        .reshape(row_count, q_width)
        .astype(bf16)
    )
    attn_proj = jnp.dot(attended, w_out, preferred_element_type=f32)
    middle = residual + rms_norm(attn_proj, gains_used[:, 1])
    normed_mid = rms_norm(middle, gains_used[:, 2]).astype(bf16)
    gate_lin = jnp.dot(normed_mid, w_gate, preferred_element_type=f32)
    up_lin = jnp.dot(normed_mid, w_up, preferred_element_type=f32)
    hidden = geglu(gate_lin, up_lin).astype(bf16)
    ffn_proj = jnp.dot(hidden, w_down, preferred_element_type=f32)
    layer_out = (middle + rms_norm(ffn_proj, gains_used[:, 3])).astype(bf16)
    d_out = cotangent.astype(f32)
    _, post_back = jax.vjp(rms_norm, ffn_proj, gains_used[:, 3])
    d_ffn, d_gain3 = post_back(d_out)
    d_ffn_low = d_ffn.astype(bf16)
    hidden_all, d_ffn_all = (
        lax.all_gather(hidden, "rep", axis=0, tiled=True),
        lax.all_gather(d_ffn_low, "rep", axis=0, tiled=True),
    )
    part_down = owned_rows(hidden_all, d_ffn_all, rep_index, hidden.shape[1] // rep_count)
    d_hidden = back_dot(d_ffn_low, w_down)
    _, glu_back = jax.vjp(geglu, gate_lin, up_lin)
    d_gate, d_up = glu_back(d_hidden)
    d_gate_low = d_gate.astype(bf16)
    d_up_low = d_up.astype(bf16)
    gate_up_grad = jnp.concatenate([d_gate_low, d_up_low], axis=1)
    mid_all, gate_up_all = (
        lax.all_gather(normed_mid, "rep", axis=0, tiled=True),
        lax.all_gather(gate_up_grad, "rep", axis=0, tiled=True),
    )
    part_gate_up = owned_rows(mid_all, gate_up_all, rep_index, normed_mid.shape[1] // rep_count)
    d_mid_in = back_dot(d_gate_low, w_gate) + back_dot(d_up_low, w_up)
    _, pre_back = jax.vjp(rms_norm, middle, gains_used[:, 2])
    d_mid_part, d_gain2 = pre_back(d_mid_in)
    d_middle = d_out + d_mid_part
    _, attn_back = jax.vjp(rms_norm, attn_proj, gains_used[:, 1])
    d_attn, d_gain1 = attn_back(d_middle)
    d_attn_low = d_attn.astype(bf16)
    d_attended = back_dot(d_attn_low, w_out).astype(bf16)
    d_heads = d_attended.reshape(row_count, KV_HEADS, group_size, HEAD_DIM)
    bent_again, masked_again = capped_scores()
    attn_probs = jnp.exp(masked_again - log_total)
    probs_again = attn_probs.astype(bf16)
    d_probs = jnp.einsum("tgrd,kgd->grtk", d_heads, value_heads, preferred_element_type=f32)
    d_scores = (
        attn_probs
        * (d_probs - jnp.sum(attn_probs * d_probs, axis=-1, keepdims=True))
        * (1.0 - bent_again * bent_again)
    ).astype(bf16)
    d_queries = jnp.einsum(
        "grtk,kgd->tgrd", d_scores, key_heads, preferred_element_type=f32
    ).reshape(row_count, q_width)
    d_key = jnp.einsum("grtk,tgrd->kgd", d_scores, query_heads, preferred_element_type=f32).reshape(
        row_count * lax.axis_size("shard"), k_width
    )
    d_value = jnp.einsum(
        "grtk,tgrd->kgd", probs_again, d_heads, preferred_element_type=f32
    ).reshape(row_count * lax.axis_size("shard"), k_width)
    d_key_value = lax.psum_scatter(
        jnp.concatenate([d_key, d_value], axis=1), "shard", scatter_dimension=0, tiled=True
    )
    d_projected = jnp.concatenate(
        [
            rotate(d_queries, position, HEADS, -1.0) * query_scale,
            rotate(d_key_value[:, :k_width], position, KV_HEADS, -1.0),
            d_key_value[:, k_width:],
        ],
        axis=1,
    ).astype(bf16)
    d_normed_in = back_dot(d_projected, w_in)
    _, first_back = jax.vjp(rms_norm, residual, gains_used[:, 0])
    d_input_part, d_gain0 = first_back(d_normed_in)
    input_grad = d_middle + d_input_part
    gain_grad = jnp.stack([d_gain0, d_gain1, d_gain2, d_gain3], axis=1)
    attended_all, d_attn_all, normed_all, d_proj_all = (
        lax.all_gather(attended, "rep", axis=0, tiled=True),
        lax.all_gather(d_attn_low, "rep", axis=0, tiled=True),
        lax.all_gather(normed_in, "rep", axis=0, tiled=True),
        lax.all_gather(d_projected, "rep", axis=0, tiled=True),
    )
    part_out = owned_rows(attended_all, d_attn_all, rep_index, attended.shape[1] // rep_count)
    part_in = owned_rows(normed_all, d_proj_all, rep_index, normed_in.shape[1] // rep_count)
    part_gain = lax.psum_scatter(gain_grad, "rep", scatter_dimension=0, tiled=True)
    owned = (
        lax.psum_scatter(part_in, "shard", scatter_dimension=0, tiled=True),
        lax.psum_scatter(part_gain, "shard", scatter_dimension=0, tiled=True),
        lax.psum_scatter(part_out, "shard", scatter_dimension=0, tiled=True),
        lax.psum_scatter(part_gate_up, "shard", scatter_dimension=0, tiled=True),
        lax.psum_scatter(part_down, "shard", scatter_dimension=0, tiled=True),
    )
    grad_inproj, grad_gains, grad_outproj, grad_gate_up, grad_down = owned
    split_at = grad_gate_up.shape[1] // 2
    grad_gate = grad_gate_up[:, :split_at]
    grad_up = grad_gate_up[:, split_at:]
    masters = (inproj, outproj, ffn_gate, ffn_up, ffn_down, norm_gains)
    gradients = (grad_inproj, grad_outproj, grad_gate, grad_up, grad_down, grad_gains)
    firsts = (mean_inproj, mean_outproj, mean_gate, mean_up, mean_down, mean_gains)
    seconds = (square_inproj, square_outproj, square_gate, square_up, square_down, square_gains)
    results = [
        lamb_local(masters[index], gradients[index], firsts[index], seconds[index])
        for index in range(6)
    ]
    weight_sums = jnp.stack([jnp.sum(master * master) for master in masters])
    step_sums = jnp.stack([jnp.sum(item[2] * item[2]) for item in results])
    totals = lax.psum(jnp.stack([weight_sums, step_sums]), ("rep", "shard"))
    counts = jnp.array([float(master.size * rep_count * shard_count) for master in masters], f32)
    norm_table = jnp.sqrt(totals / counts[None, :] + 1e-06)
    fresh = [
        masters[index] - 0.3 * norm_table[0, index] / norm_table[1, index] * results[index][2]
        for index in range(6)
    ]
    return (
        layer_out,
        input_grad,
        grad_inproj,
        grad_outproj,
        grad_gate,
        grad_up,
        grad_down,
        grad_gains,
        results[0][0],
        results[1][0],
        results[2][0],
        results[3][0],
        results[4][0],
        results[5][0],
        results[0][1],
        results[1][1],
        results[2][1],
        results[3][1],
        results[4][1],
        results[5][1],
        fresh[0],
        fresh[1],
        fresh[2],
        fresh[3],
        fresh[4],
        fresh[5],
        norm_table,
    )


MESH = pl.DeviceIdType.MESH
VM = pltpu.VMEM
HB = pl.ANY
UNITS = 4
VMEM_LIMIT = 60 << 20


def ring_places(count):
    inner = 2 if count == 8 else 4
    outer = count // inner

    def place(shard):
        major = shard // inner
        minor = shard % inner
        return minor * outer + major + (minor % 2) * (outer - 1 - 2 * major)

    def shard_at(spot):
        minor = spot // outer
        major = spot % outer
        return (major + (minor % 2) * (outer - 1 - 2 * major)) * inner + minor

    return place, shard_at


def meet(devices):
    barrier = pltpu.get_barrier_semaphore()
    for device in devices:
        pl.semaphore_signal(barrier, inc=1, device_id=device, device_id_type=MESH)
    pl.semaphore_wait(barrier, len(devices))


def remote(src, dst, send_sem, recv_sem, device):
    return pltpu.make_async_remote_copy(
        src_ref=src,
        dst_ref=dst,
        send_sem=send_sem,
        recv_sem=recv_sem,
        device_id=device,
        device_id_type=MESH,
    )


class Ring:
    def __init__(self, count):
        place, shard_at = ring_places(count)
        self.count = count
        self.half = count // 2
        self.rep = lax.axis_index("rep")
        self.me = lax.axis_index("shard")
        self.spot = place(self.me)
        self.shard_at = shard_at
        self.next = [(self.rep, self.at(1)), (self.rep, self.at(count - 1))]

    def at(self, ahead):
        return self.shard_at((self.spot + ahead) % self.count)

    def away(self, way, hops):
        return self.at(hops if way == 0 else self.count - hops)

    def units(self, way, hop):
        order = list(range(UNITS)) if way == 0 else list(range(UNITS))[::-1]
        return order if hop < self.half else order[: UNITS // 2]


def ring_gather_kernel(count, x_ref, out_ref, send, recv, local):
    ring = Ring(count)
    rows = x_ref.shape[0] // UNITS

    def part(unit):
        return pl.ds(unit * rows, rows)

    def hop_copy(way, hop, unit):
        origin = ring.away(1 - way, hop - 1) if hop > 1 else ring.me
        src = x_ref.at[part(unit)] if hop == 1 else out_ref.at[origin, part(unit)]
        return remote(
            src,
            out_ref.at[origin, part(unit)],
            send.at[way, hop - 1, unit],
            recv.at[way, hop - 1, unit],
            ring.next[way],
        )

    meet(ring.next)
    own = pltpu.make_async_copy(x_ref, out_ref.at[ring.me], local)
    own.start()
    started = []
    for index in range(UNITS):
        for way in (0, 1):
            copy = hop_copy(way, 1, ring.units(way, 1)[index])
            copy.start()
            started.append(copy)
    for hop in range(1, ring.half + 1):
        for index in range(len(ring.units(0, hop))):
            for way in (0, 1):
                unit = ring.units(way, hop)[index]
                hop_copy(way, hop, unit).wait_recv()
                if hop < ring.half and unit in ring.units(way, hop + 1):
                    copy = hop_copy(way, hop + 1, unit)
                    copy.start()
                    started.append(copy)
    for copy in started:
        copy.wait_send()
    own.wait()


def ring_gather(block, count, collective_id):
    rows, columns = block.shape
    hops = count // 2
    gathered = pl.pallas_call(
        functools.partial(ring_gather_kernel, count),
        out_shape=jax.ShapeDtypeStruct((count, rows, columns), block.dtype),
        in_specs=[pl.BlockSpec(memory_space=VM)],
        out_specs=pl.BlockSpec(memory_space=VM),
        scratch_shapes=[
            pltpu.SemaphoreType.DMA((2, hops, UNITS)),
            pltpu.SemaphoreType.DMA((2, hops, UNITS)),
            pltpu.SemaphoreType.DMA,
        ],
        compiler_params=pltpu.CompilerParams(
            collective_id=collective_id, has_side_effects=True, vmem_limit_bytes=VMEM_LIMIT
        ),
        name=f"ring_gather_{collective_id}",
    )(block)
    return gathered.reshape(count * rows, columns)


def ring_reduce_kernel(count, x_ref, out_ref, held, landed, send, recv):
    ring = Ring(count)
    rows = out_ref.shape[0] // UNITS
    hops = ring.half

    def part(unit):
        return pl.ds(unit * rows, rows)

    def step_copy(way, step, unit):
        return remote(
            held.at[way, step, part(unit)],
            landed.at[way, step, part(unit)],
            send.at[way, step, unit],
            recv.at[way, step, unit],
            ring.next[way],
        )

    meet(ring.next)
    started = []
    for step in range(hops):
        order = ring.units(0, hops - step), ring.units(1, hops - step)
        before = [ring.units(way, hops - step + 1) if step else [] for way in (0, 1)]
        for index in range(len(order[0])):
            for way in (0, 1):
                unit = order[way][index]
                block = x_ref[ring.away(way, hops - step), part(unit), :].astype(jnp.float32)
                if unit in before[way]:
                    step_copy(way, step - 1, unit).wait_recv()
                    block += landed[way, step - 1, part(unit), :].astype(jnp.float32)
                held[way, step, part(unit), :] = block.astype(held.dtype)
                copy = step_copy(way, step, unit)
                copy.start()
                started.append(copy)
    for index in range(UNITS):
        unit = index
        total = x_ref[ring.me, part(unit), :].astype(jnp.float32)
        for way in (0, 1):
            step_copy(way, hops - 1, unit).wait_recv()
            total += landed[way, hops - 1, part(unit), :].astype(jnp.float32)
        out_ref[part(unit), :] = total
    for copy in started:
        copy.wait_send()


def ring_reduce(partial, count, collective_id):
    rows, columns = partial.shape[0] // count, partial.shape[1]
    hops = count // 2
    return pl.pallas_call(
        functools.partial(ring_reduce_kernel, count),
        out_shape=jax.ShapeDtypeStruct((rows, columns), jnp.float32),
        in_specs=[pl.BlockSpec(memory_space=VM)],
        out_specs=pl.BlockSpec(memory_space=VM),
        scratch_shapes=[
            pltpu.VMEM((2, hops, rows, columns), jnp.bfloat16),
            pltpu.VMEM((2, hops, rows, columns), jnp.bfloat16),
            pltpu.SemaphoreType.DMA((2, hops, UNITS)),
            pltpu.SemaphoreType.DMA((2, hops, UNITS)),
        ],
        compiler_params=pltpu.CompilerParams(
            collective_id=collective_id, has_side_effects=True, vmem_limit_bytes=VMEM_LIMIT
        ),
        name=f"ring_reduce_{collective_id}",
    )(partial.reshape(count, rows, columns))


def rep_partners(rep):
    return (rep + 2) % 4, rep + 1 - 2 * (rep % 2)


def everyone(rep, me, reps, count):
    here = rep * count + me
    total = reps * count
    return [
        (((here + k) % total) // count, ((here + k) % total) % count) for k in range(1, total)
    ]


def weights_kernel(
    reps, count, in_ref, gu_ref, dn_ref, ou_ref, w_in, w_gu, w_dn, w_ou, a_send, a_recv, x_send, x_recv,
    c_send, c_recv, d_send, d_recv, o_send, o_recv, n_send, n_recv, loc
):
    rep = lax.axis_index("rep")
    me = lax.axis_index("shard")
    across, beside = rep_partners(rep)
    meet(everyone(rep, me, reps, count))
    started = []

    def go(copy):
        copy.start()
        started.append(copy)

    per_head = count * reps // HEADS
    mine = rep * count + me
    target = mine // per_head
    slot = mine % per_head
    locals_ = []

    def ou_copy(j):
        return remote(ou_ref.at[j], w_ou.at[j, slot], o_send.at[j], o_recv.at[slot], (j, target))

    def is_self(j):
        return (rep == j) & (me == target)

    for j in range(reps):
        @pl.when(jnp.logical_not(is_self(j)))
        def _():
            ou_copy(j).start()

        @pl.when(is_self(j))
        def _():
            pltpu.make_async_copy(ou_ref.at[j], w_ou.at[j, slot], o_recv.at[slot]).start()

    pairs = ((in_ref, w_in), (gu_ref, w_gu))

    def spread(which, k):
        to = (me + k) % count
        src, dst = pairs[which]
        return remote(
            src.at[to], dst.at[rep, me], a_send.at[which, k], a_recv.at[which, k], (rep, to)
        )

    def arrived(which, k):
        frm = (me + count - k) % count
        src, dst = pairs[which]
        return remote(
            src.at[frm], dst.at[rep, frm], a_send.at[which, k], a_recv.at[which, k], (rep, frm)
        )

    def forward(which, k, hop):
        frm = (me + count - k) % count
        src, dst = pairs[which]
        block = src.at[me] if k == 0 else dst.at[rep, frm]
        if hop == 0:
            return remote(
                block, dst.at[rep, frm], x_send.at[which, k], x_recv.at[which, k], (across, me)
            )
        if hop == 1:
            return remote(
                block, dst.at[rep, frm], c_send.at[which, k], c_recv.at[which, k], (beside, me)
            )
        return remote(
            dst.at[across, frm], dst.at[across, frm], d_send.at[which, k], d_recv.at[which, k],
            (beside, me),
        )

    for k in range(1, count):
        go(spread(0, k))
    go(forward(0, 0, 0))
    go(forward(0, 0, 1))
    dn_x = remote(dn_ref, w_dn.at[rep], n_send.at[0], n_recv.at[0], (across, me))
    dn_c = remote(dn_ref, w_dn.at[rep], n_send.at[1], n_recv.at[1], (beside, me))
    dn_d = remote(w_dn.at[across], w_dn.at[across], n_send.at[2], n_recv.at[2], (beside, me))
    go(dn_x)
    go(dn_c)
    for k in range(1, count):
        go(spread(1, k))
    go(forward(1, 0, 0))
    go(forward(1, 0, 1))
    for index, (src, dst) in enumerate(
        ((in_ref.at[me], w_in.at[rep, me]), (gu_ref.at[me], w_gu.at[rep, me]), (dn_ref, w_dn.at[rep]))
    ):
        copy = pltpu.make_async_copy(src, dst, loc.at[index])
        copy.start()
        locals_.append(copy)
    for k in range(1, count):
        arrived(0, k).wait_recv()
        go(forward(0, k, 0))
        go(forward(0, k, 1))
    for k in range(count):
        forward(0, k, 0).wait_recv()
        go(forward(0, k, 2))
    for i in range(per_head):
        remote(
            ou_ref.at[0], w_ou.at[rep, i], o_send.at[0], o_recv.at[i], (across, me)
        ).wait_recv()
    ou_x = remote(w_ou.at[rep], w_ou.at[rep], n_send.at[3], n_recv.at[3], (across, me))
    ou_c = remote(w_ou.at[rep], w_ou.at[rep], n_send.at[4], n_recv.at[4], (beside, me))
    ou_d = remote(w_ou.at[across], w_ou.at[across], n_send.at[5], n_recv.at[5], (beside, me))
    go(ou_x)
    go(ou_c)
    for k in range(1, count):
        arrived(1, k).wait_recv()
        go(forward(1, k, 0))
        go(forward(1, k, 1))
    dn_x.wait_recv()
    go(dn_d)
    ou_x.wait_recv()
    go(ou_d)
    for k in range(count):
        forward(1, k, 0).wait_recv()
        go(forward(1, k, 2))
    for which in (0, 1):
        for k in range(count):
            forward(which, k, 1).wait_recv()
            forward(which, k, 2).wait_recv()
    for copy in (dn_c, dn_d, ou_c, ou_d):
        copy.wait_recv()
    for copy in started:
        copy.wait_send()
    for j in range(reps):
        @pl.when(jnp.logical_not(is_self(j)))
        def _():
            ou_copy(j).wait_send()
    for copy in locals_:
        copy.wait()


def spread_weights(reps, count, w_in, w_gu, w_dn, w_ou, collective_id):
    dma = pltpu.SemaphoreType.DMA
    per_head = count * reps // HEADS
    low = jnp.bfloat16
    return pl.pallas_call(
        functools.partial(weights_kernel, reps, count),
        out_shape=[
            jax.ShapeDtypeStruct((reps,) + w_in.shape, low),
            jax.ShapeDtypeStruct((reps,) + w_gu.shape, low),
            jax.ShapeDtypeStruct((reps,) + w_dn.shape, low),
            jax.ShapeDtypeStruct((reps, per_head) + w_ou.shape[1:], low),
        ],
        in_specs=[pl.BlockSpec(memory_space=HB)] * 4,
        out_specs=[pl.BlockSpec(memory_space=HB)] * 4,
        scratch_shapes=[dma((2, count))] * 8 + [dma((reps,)), dma((per_head,)), dma((6,)), dma((6,)), dma((3,))],
        compiler_params=pltpu.CompilerParams(
            collective_id=collective_id, has_side_effects=True, vmem_limit_bytes=VMEM_LIMIT
        ),
        name="spread_weights",
    )(w_in, w_gu, w_dn, w_ou)


def rep_sum(part, from_core, to_across, from_across, sums, sems, rep, me, pieces, emit):
    across, beside = rep_partners(rep)
    core = rep % 2
    chip = rep // 2
    far = 1 - chip
    c_send, c_recv, x_send, x_recv = sems
    f32 = jnp.float32

    def core_copy(side, piece):
        owner_chip = far if side == 0 else chip
        return remote(
            part.at[owner_chip * 2 + 1 - core, piece],
            from_core.at[side, piece],
            c_send.at[side, piece],
            c_recv.at[side, piece],
            (beside, me),
        )

    def cross_copy(piece):
        return remote(
            to_across.at[piece], from_across.at[piece], x_send.at[piece], x_recv.at[piece], (across, me)
        )

    for side in (0, 1):
        for piece in pieces:
            core_copy(side, piece).start()
    for piece in pieces:
        core_copy(0, piece).wait_recv()
        to_across[piece] = (
            part[far * 2 + core, piece].astype(f32) + from_core[0, piece].astype(f32)
        ).astype(to_across.dtype)
        cross_copy(piece).start()
    for piece in pieces:
        core_copy(1, piece).wait_recv()
        cross_copy(piece).wait_recv()
        emit(
            piece,
            part[rep, piece].astype(f32)
            + from_core[1, piece].astype(f32)
            + from_across[piece].astype(f32),
        )
    for piece in pieces:
        core_copy(0, piece).wait_send()
        core_copy(1, piece).wait_send()
        cross_copy(piece).wait_send()


def grads_kernel(
    reps, count, full, a_part, b_part, a_out, b_out, a_core, a_to, a_from, a_sum, b_core, b_to, b_from, b_sum,
    ac_s, ac_r, ax_s, ax_r, bc_s, bc_r, bx_s, bx_r, s_send, s_recv, o_send, o_recv
):
    rep = lax.axis_index("rep")
    me = lax.axis_index("shard")
    meet(everyone(rep, me, reps, count))

    a_pieces = [(me + k) % count for k in range(1, count)] + [me]

    def a_send(k):
        to = (me + k) % count
        return remote(a_sum.at[to], a_out.at[me], s_send.at[k], s_recv.at[k], (rep, to))

    def a_arrived(k):
        frm = (me + count - k) % count
        return remote(a_sum.at[frm], a_out.at[frm], s_send.at[k], s_recv.at[k], (rep, frm))

    order = {id(piece): k for k, piece in zip(list(range(1, count)) + [0], a_pieces)}

    def a_emit(piece, total):
        k = order[id(piece)]
        if k == 0:
            a_out[me] = total.astype(a_out.dtype)
        else:
            a_sum[piece] = total.astype(a_sum.dtype)
            a_send(k).start()

    rep_sum(a_part, a_core, a_to, a_from, a_sum, (ac_s, ac_r, ax_s, ax_r), rep, me, a_pieces, a_emit)

    b_pieces = list(range(b_part.shape[1]))
    if full is None:
        def b_emit(piece, total):
            b_out[piece] = total
    else:
        def b_send(piece):
            block = me * full + piece
            owner = (block // count, block % count)
            return remote(b_sum.at[piece], b_out.at[rep], o_send.at[piece], o_recv.at[rep], owner)

        def b_self(piece):
            return me * full + piece == rep * count + me

        def b_emit(piece, total):
            b_sum[piece] = total.astype(b_sum.dtype)

            @pl.when(jnp.logical_not(b_self(piece)))
            def _():
                b_send(piece).start()

            @pl.when(b_self(piece))
            def _():
                pltpu.make_async_copy(b_sum.at[piece], b_out.at[rep], o_recv.at[rep]).start()

    rep_sum(b_part, b_core, b_to, b_from, b_sum, (bc_s, bc_r, bx_s, bx_r), rep, me, b_pieces, b_emit)

    for k in range(1, count):
        a_arrived(k).wait_recv()
    for k in range(1, count):
        a_send(k).wait_send()
    if full is not None:
        for j in range(reps):
            remote(
                b_sum.at[0], b_out.at[j], o_send.at[0], o_recv.at[j], (rep, (me + 1) % count)
            ).wait_recv()
        for piece in b_pieces:
            @pl.when(jnp.logical_not(b_self(piece)))
            def _():
                b_send(piece).wait_send()


def return_grads(reps, count, full, a_part, b_part, collective_id):
    dma = pltpu.SemaphoreType.DMA
    low = jnp.bfloat16
    a_block = a_part.shape[1:]
    b_block = b_part.shape[1:]
    b_count = b_block[0]
    b_shape = (
        jax.ShapeDtypeStruct(b_block, jnp.float32)
        if full is None
        else jax.ShapeDtypeStruct((reps,) + b_block[1:], low)
    )
    b_sum = b_block if full is not None else (1, 16, 128)
    scratch = [
        pltpu.VMEM((2,) + a_block, low),
        pltpu.VMEM(a_block, low),
        pltpu.VMEM(a_block, low),
        pltpu.VMEM(a_block, low),
        pltpu.VMEM((2,) + b_block, low),
        pltpu.VMEM(b_block, low),
        pltpu.VMEM(b_block, low),
        pltpu.VMEM(b_sum, low),
        dma((2, count)),
        dma((2, count)),
        dma((count,)),
        dma((count,)),
        dma((2, b_count)),
        dma((2, b_count)),
        dma((b_count,)),
        dma((b_count,)),
        dma((count,)),
        dma((count,)),
        dma((b_count,)),
        dma((reps,)),
    ]
    return pl.pallas_call(
        functools.partial(grads_kernel, reps, count, full),
        out_shape=[jax.ShapeDtypeStruct(a_block, low), b_shape],
        in_specs=[pl.BlockSpec(memory_space=VM)] * 2,
        out_specs=[pl.BlockSpec(memory_space=VM)] * 2,
        scratch_shapes=scratch,
        compiler_params=pltpu.CompilerParams(
            collective_id=collective_id, has_side_effects=True, vmem_limit_bytes=VMEM_LIMIT
        ),
        name=f"return_grads_{collective_id}",
    )(a_part, b_part)


def small_kernel(reps, count, spread, x_ref, out_ref, send, recv):
    rep = lax.axis_index("rep")
    me = lax.axis_index("shard")
    here = rep * count + me
    total = reps * count
    others = everyone(rep, me, reps, count)
    meet(others)
    copies = []
    for k, device in enumerate(others):
        to = (here + k + 1) % total
        src = x_ref.at[to] if spread else x_ref
        copy = remote(src, out_ref.at[here], send.at[k], recv.at[k], device)
        copy.start()
        copies.append(copy)
    out_ref[here] = x_ref[here] if spread else x_ref[...]
    for k in range(total - 1):
        frm = (here + total - k - 1) % total
        remote(out_ref.at[frm], out_ref.at[frm], send.at[k], recv.at[k], others[k]).wait_recv()
    for copy in copies:
        copy.wait_send()


def small_exchange(tiles, reps, count, spread, collective_id):
    total = reps * count
    return pl.pallas_call(
        functools.partial(small_kernel, reps, count, spread),
        out_shape=jax.ShapeDtypeStruct((total,) + tiles.shape[-2:], tiles.dtype),
        in_specs=[pl.BlockSpec(memory_space=VM)],
        out_specs=pl.BlockSpec(memory_space=VM),
        scratch_shapes=[pltpu.SemaphoreType.DMA((total - 1,)), pltpu.SemaphoreType.DMA((total - 1,))],
        compiler_params=pltpu.CompilerParams(
            collective_id=collective_id, has_side_effects=True, vmem_limit_bytes=VMEM_LIMIT
        ),
        name=f"small_exchange_{collective_id}",
    )(tiles)


def as_tile(flat):
    width = flat.shape[-1]
    filled = -(-width // 1024) * 1024
    padded = jnp.pad(flat, [(0, 0)] * (flat.ndim - 1) + [(0, filled - width)])
    return padded.reshape(flat.shape[:-1] + (filled // 128, 128))


def turn(flat, cosine, sine):
    half = flat.shape[1] // 2
    first, second = flat[:, :half], flat[:, half:]
    return jnp.concatenate([first * cosine - second * sine, second * cosine + first * sine], axis=1)


def norm_back(value, gain_col, grad):
    scale = lax.rsqrt(jnp.mean(value * value, axis=-1, keepdims=True) + 1e-06)
    normed = value * scale
    weighted = grad * (1.0 + gain_col)
    inner = jnp.mean(weighted * normed, axis=-1, keepdims=True)
    return scale * (weighted - normed * inner), jnp.sum(grad * normed, axis=0)


def dot_tn(left, right):
    return lax.dot_general(left, right, (((0,), (0,)), ((), ())), preferred_element_type=jnp.float32)


def split_device(
    tokens, cotangent, piece_starts, inproj, outproj, ffn_gate, ffn_up, ffn_down, norm_gains,
    mean_inproj, mean_outproj, mean_gate, mean_up, mean_down, mean_gains,
    square_inproj, square_outproj, square_gate, square_up, square_down, square_gains,
):
    bf16, f32 = jnp.bfloat16, jnp.float32
    reps, count = lax.axis_size("rep"), lax.axis_size("shard")
    rep = lax.axis_index("rep")
    me = lax.axis_index("shard")
    total = reps * count
    rows, width = tokens.shape
    seq_len = rows * count
    group = HEADS // KV_HEADS
    q_width, k_width = HEADS * HEAD_DIM, KV_HEADS * HEAD_DIM
    d_rows = inproj.shape[0]
    ff = ffn_gate.shape[1]
    ff_block = ff // total
    ff_part = ff // count
    o_rows = outproj.shape[0]
    per_head = HEAD_DIM // o_rows
    piece = o_rows // reps

    low_in = inproj.astype(bf16)
    q_cols = low_in[:, :q_width].reshape(d_rows, HEADS, HEAD_DIM)
    k_cols = jnp.repeat(low_in[:, q_width : q_width + k_width].reshape(d_rows, KV_HEADS, HEAD_DIM), group, axis=1)
    v_cols = jnp.repeat(low_in[:, q_width + k_width :].reshape(d_rows, KV_HEADS, HEAD_DIM), group, axis=1)
    cut_in = jnp.concatenate([q_cols, k_cols, v_cols], axis=2).transpose(1, 0, 2)

    def cut_ff(weight):
        return weight.astype(bf16).reshape(d_rows, reps, count, ff_block).transpose(2, 0, 1, 3).reshape(
            count, d_rows, ff_part
        )

    cut_gu = jnp.concatenate([cut_ff(ffn_gate), cut_ff(ffn_up)], axis=1)
    cut_out = outproj.astype(bf16).reshape(reps, piece, width)
    got_in, got_gu, got_down, got_out = spread_weights(
        reps, count, cut_in, cut_gu, ffn_down.astype(bf16), cut_out, 1
    )
    w_in = got_in.reshape(width, -1)
    got_gu = got_gu.reshape(total, 2, d_rows, ff_part)
    w_gate = got_gu[:, 0].reshape(width, ff_part)
    w_up = got_gu[:, 1].reshape(width, ff_part)
    w_down = got_down.reshape(ff_part, width)
    w_out = got_out.transpose(1, 0, 2, 3).reshape(HEAD_DIM, width)
    gain_tiles = small_exchange(as_tile(norm_gains.astype(bf16).astype(f32).reshape(-1)), reps, count, False, 2)
    gains = gain_tiles.reshape(total, -1)[:, : d_rows * 4].reshape(width, 4)

    all_tokens = ring_gather(tokens, count, 3)
    normed_in = rms_norm(all_tokens.astype(f32), gains[:, 0]).astype(bf16)
    projected = jnp.dot(normed_in, w_in, preferred_element_type=f32)
    half = HEAD_DIM // 2
    position = jnp.arange(seq_len, dtype=jnp.int32)
    freq = 10000.0 ** (-(jnp.arange(half, dtype=f32) * 2.0 / HEAD_DIM))
    angle = position.astype(f32)[:, None] * freq[None, :]
    cosine, sine = jnp.cos(angle), jnp.sin(angle)
    query_scale = HEAD_DIM ** (-0.5)
    queries = (turn(projected[:, :HEAD_DIM], cosine, sine) * query_scale).astype(bf16)
    keys = turn(projected[:, HEAD_DIM : 2 * HEAD_DIM], cosine, sine).astype(bf16)
    values = projected[:, 2 * HEAD_DIM :].astype(bf16)
    starts = lax.dynamic_slice_in_dim(piece_starts, rep, 1, 0)[0]
    inside = (position[:, None] >= starts[None, :]) & (position[:, None] < starts[None, :] + PIC)
    tag = jnp.sum(inside.astype(jnp.int32) * (jnp.arange(starts.shape[0], dtype=jnp.int32)[None, :] + 1), axis=1)
    visible = (position[None, :] <= position[:, None]) | ((tag[:, None] == tag[None, :]) & (tag[:, None] > 0))
    raw = lax.dot_general(queries, keys, (((1,), (1,)), ((), ())), preferred_element_type=f32)
    bent = jnp.tanh(raw / 50.0)
    masked = jnp.where(visible, 50.0 * bent, -1e30)
    top_score = jnp.max(masked, axis=-1, keepdims=True)
    expo = jnp.exp(masked - top_score)
    probs = expo / jnp.sum(expo, axis=-1, keepdims=True)
    probs_low = probs.astype(bf16)
    attended = jnp.dot(probs_low, values, preferred_element_type=f32).astype(bf16)
    attn_proj = ring_reduce(jnp.dot(attended, w_out, preferred_element_type=f32).astype(bf16), count, 4)

    residual = tokens.astype(f32)
    d_out = cotangent.astype(f32)
    middle = residual + rms_norm(attn_proj, gains[:, 1])
    normed_mid = ring_gather(rms_norm(middle, gains[:, 2]).astype(bf16), count, 5)
    gate_lin = jnp.dot(normed_mid, w_gate, preferred_element_type=f32)
    up_lin = jnp.dot(normed_mid, w_up, preferred_element_type=f32)
    hidden = geglu(gate_lin, up_lin).astype(bf16)
    ffn_proj = ring_reduce(jnp.dot(hidden, w_down, preferred_element_type=f32).astype(bf16), count, 6)
    layer_out = (middle + rms_norm(ffn_proj, gains[:, 3])).astype(bf16)
    d_ffn, d_gain3 = norm_back(ffn_proj, gains[:, 3], d_out)
    d_ffn = ring_gather(d_ffn.astype(bf16), count, 7)
    d_hidden = back_dot(d_ffn, w_down)
    _, glu_back = jax.vjp(geglu, gate_lin, up_lin)
    d_gate, d_up = glu_back(d_hidden)
    d_gate, d_up = d_gate.astype(bf16), d_up.astype(bf16)
    d_mid_in = ring_reduce((back_dot(d_gate, w_gate) + back_dot(d_up, w_up)).astype(bf16), count, 8)
    part_down = dot_tn(hidden, d_ffn).astype(bf16).reshape(reps, 3, ff_block // 3, width)
    part_gate = dot_tn(normed_mid, d_gate).astype(bf16).reshape(reps, count, d_rows, ff_part)
    part_up = dot_tn(normed_mid, d_up).astype(bf16).reshape(reps, count, d_rows, ff_part)
    sum_gu, grad_down = return_grads(
        reps, count, None, jnp.concatenate([part_gate, part_up], axis=2), part_down, 9
    )
    grad_down = grad_down.reshape(ff_block, width)

    def join_ff(parts):
        return parts.reshape(count, d_rows, reps, ff_block).transpose(1, 2, 0, 3).reshape(d_rows, ff).astype(f32)

    grad_gate, grad_up = join_ff(sum_gu[:, :d_rows]), join_ff(sum_gu[:, d_rows:])
    d_mid_part, d_gain2 = norm_back(middle, gains[:, 2], d_mid_in)
    d_middle = d_out + d_mid_part
    d_attn, d_gain1 = norm_back(attn_proj, gains[:, 1], d_middle)
    d_attn = ring_gather(d_attn.astype(bf16), count, 10)
    d_attended = back_dot(d_attn, w_out).astype(bf16)
    d_probs = back_dot(d_attended, values)
    d_values = dot_tn(probs_low, d_attended)
    d_scores = (
        probs * (d_probs - jnp.sum(probs * d_probs, axis=-1, keepdims=True)) * (1.0 - bent * bent)
    ).astype(bf16)
    d_queries = jnp.dot(d_scores, keys, preferred_element_type=f32)
    d_keys = dot_tn(d_scores, queries)
    d_projected = jnp.concatenate(
        [turn(d_queries, cosine, -sine) * query_scale, turn(d_keys, cosine, -sine), d_values], axis=1
    ).astype(bf16)
    d_normed_in = ring_reduce(back_dot(d_projected, w_in).astype(bf16), count, 11)
    d_input_part, d_gain0 = norm_back(residual, gains[:, 0], d_normed_in)
    input_grad = d_middle + d_input_part
    part_in = dot_tn(normed_in, d_projected).astype(bf16).reshape(reps, count, d_rows, 3 * HEAD_DIM)
    part_out = (
        dot_tn(attended, d_attn).astype(bf16).reshape(per_head, reps, piece, width).transpose(1, 0, 2, 3)
    )
    sum_in, sum_out = return_grads(reps, count, per_head, part_in, part_out, 12)
    sum_in = sum_in.astype(f32)
    grad_q = sum_in[:, :, :HEAD_DIM].transpose(1, 0, 2).reshape(d_rows, q_width)

    def join_kv(parts):
        return parts.reshape(KV_HEADS, group, d_rows, HEAD_DIM).sum(axis=1).transpose(1, 0, 2).reshape(d_rows, k_width)

    grad_inproj = jnp.concatenate(
        [grad_q, join_kv(sum_in[:, :, HEAD_DIM : 2 * HEAD_DIM]), join_kv(sum_in[:, :, 2 * HEAD_DIM :])], axis=1
    )
    grad_outproj = sum_out.reshape(o_rows, width).astype(f32)
    gain_grad = jnp.stack([d_gain0, d_gain1, d_gain2, d_gain3], axis=1).reshape(total, d_rows * 4)
    gain_sum = jnp.sum(small_exchange(as_tile(gain_grad), reps, count, True, 13), axis=0)
    grad_gains = gain_sum.reshape(-1)[: d_rows * 4].reshape(d_rows, 4)

    masters = (inproj, outproj, ffn_gate, ffn_up, ffn_down, norm_gains)
    gradients = (grad_inproj, grad_outproj, grad_gate, grad_up, grad_down, grad_gains)
    firsts = (mean_inproj, mean_outproj, mean_gate, mean_up, mean_down, mean_gains)
    seconds = (square_inproj, square_outproj, square_gate, square_up, square_down, square_gains)
    results = [lamb_local(*item) for item in zip(masters, gradients, firsts, seconds)]
    sums = jnp.stack(
        [jnp.sum(master * master) for master in masters] + [jnp.sum(item[2] * item[2]) for item in results]
    )
    totals = jnp.sum(small_exchange(as_tile(sums), reps, count, False, 14), axis=0)
    totals = totals.reshape(-1)[:12].reshape(2, 6)
    counts = jnp.array([float(master.size * total) for master in masters], f32)
    norm_table = jnp.sqrt(totals / counts[None, :] + 1e-06)
    fresh = [
        masters[index] - 0.3 * norm_table[0, index] / norm_table[1, index] * results[index][2]
        for index in range(6)
    ]
    return (
        layer_out,
        input_grad,
        *gradients,
        *[item[0] for item in results],
        *[item[1] for item in results],
        *fresh,
        norm_table,
    )


def fits(mesh, shapes):
    reps, count = mesh.shape["rep"], mesh.shape["shard"]
    total = reps * count
    tokens, piece_starts, outproj, ffn_gate = shapes
    o_rows = outproj[0] // total
    return (
        reps == 4
        and count == HEADS
        and piece_starts[0] == reps
        and tokens[0] % (total * UNITS * 16) == 0
        and HEAD_DIM % o_rows == 0
        and o_rows % (16 * reps) == 0
        and HEAD_DIM // o_rows == total // HEADS
        and ffn_gate[1] % (total * 96) == 0
    )


def solution(mesh):
    split = P(("rep", "shard"), None)

    def step(*args):
        shapes = args[0].shape, args[2].shape, args[4].shape, args[5].shape
        body = split_device if fits(mesh, shapes) else per_device
        return jax.shard_map(
            body,
            mesh=mesh,
            in_specs=(split, split, P()) + (split,) * 18,
            out_specs=(split,) * 26 + (P(),),
            check_vma=False,
        )(*args)

    return step
```

```python
import functools

import jax
import jax.numpy as jnp
from jax import lax
from jax.experimental import pallas as pl
from jax.experimental.pallas import tpu as pltpu
from jax.sharding import PartitionSpec as P

HEADS = 8
KV_HEADS = 4
HEAD_DIM = 256
PIC = 256


def rms_norm(values_in, gain_col):
    return (
        values_in
        * lax.rsqrt(jnp.mean(values_in * values_in, axis=-1, keepdims=True) + 1e-06)
        * (1.0 + gain_col)
    )


def geglu(gate_lin, up_lin):
    return jax.nn.gelu(gate_lin, approximate=True) * up_lin


def rotate(flat, position, head_count, sign):
    row_count = flat.shape[0]
    width = flat.shape[1] // head_count
    half = width // 2
    vectors = flat.reshape(row_count, head_count, width)
    freq = 10000.0 ** (-(jnp.arange(half, dtype=jnp.float32) * 2.0 / width))
    angle = position.astype(jnp.float32)[:, None] * freq[None, :]
    cosine = jnp.cos(angle)[:, None, :]
    sine = sign * jnp.sin(angle)[:, None, :]
    first = vectors[..., :half]
    second = vectors[..., half:]
    turned = jnp.concatenate(
        [first * cosine - second * sine, second * cosine + first * sine], axis=-1
    )
    return turned.reshape(row_count, head_count * width)


def owned_rows(activation, gradient, rep_index, width):
    piece = lax.dynamic_slice_in_dim(activation, rep_index * width, width, 1)
    return lax.dot_general(
        piece, gradient, (((0,), (0,)), ((), ())), preferred_element_type=jnp.float32
    )


def back_dot(gradient, weight):
    return lax.dot_general(
        gradient, weight, (((1,), (1,)), ((), ())), preferred_element_type=jnp.float32
    )


def describe(rows, piece_starts, seq_offset, seq_len):
    local_seq = rows // seq_len
    position = rows % seq_len
    global_seq = local_seq + seq_offset
    seq_total = piece_starts.shape[0]
    piece_count = piece_starts.shape[1]
    select = (global_seq[:, None] == jnp.arange(seq_total, dtype=jnp.int32)[None, :]).astype(
        jnp.int32
    )
    starts = jnp.sum(select[:, :, None] * piece_starts[None, :, :], axis=1)
    inside = ((position[:, None] >= starts) & (position[:, None] < starts + PIC)).astype(jnp.int32)
    labels = (
        global_seq[:, None] * piece_count + jnp.arange(piece_count, dtype=jnp.int32)[None, :] + 1
    )
    return (local_seq, position, jnp.sum(inside * labels, axis=1))


def visibility(piece_starts, query_rows, key_rows, seq_offset, seq_len):
    seq_q, pos_q, tag_q = describe(query_rows, piece_starts, seq_offset, seq_len)
    seq_k, pos_k, tag_k = describe(key_rows, piece_starts, seq_offset, seq_len)
    causal = pos_k[None, :] <= pos_q[:, None]
    same_piece = (tag_q[:, None] == tag_k[None, :]) & (tag_q[:, None] > 0)
    return (seq_q[:, None] == seq_k[None, :]) & (causal | same_piece)


def lamb_local(master, gradient, first, second):
    newmean = 0.5 * first + 0.5 * gradient
    newsquare = 0.5 * second + 0.5 * gradient * gradient
    step_dir = newmean / (jnp.sqrt(newsquare) + 1e-06) + 0.01 * master
    return (newmean, newsquare, step_dir)


def per_device(
    tokens,
    cotangent,
    piece_starts,
    inproj,
    outproj,
    ffn_gate,
    ffn_up,
    ffn_down,
    norm_gains,
    mean_inproj,
    mean_outproj,
    mean_gate,
    mean_up,
    mean_down,
    mean_gains,
    square_inproj,
    square_outproj,
    square_gate,
    square_up,
    square_down,
    square_gains,
):
    bf16 = jnp.bfloat16
    f32 = jnp.float32
    rep_count = lax.axis_size("rep")
    shard_count = lax.axis_size("shard")
    rep_index = lax.axis_index("rep")
    w_in, w_out, w_gate, w_up, w_down, gain_copy = (
        lax.all_gather(inproj.astype(bf16), ("rep", "shard"), axis=0, tiled=True),
        lax.all_gather(outproj.astype(bf16), ("rep", "shard"), axis=0, tiled=True),
        lax.all_gather(ffn_gate.astype(bf16), ("rep", "shard"), axis=0, tiled=True),
        lax.all_gather(ffn_up.astype(bf16), ("rep", "shard"), axis=0, tiled=True),
        lax.all_gather(ffn_down.astype(bf16), ("rep", "shard"), axis=0, tiled=True),
        lax.all_gather(norm_gains.astype(bf16), ("rep", "shard"), axis=0, tiled=True),
    )
    gains_used = gain_copy.astype(f32)
    residual = tokens.astype(f32)
    row_count = residual.shape[0]
    seq_len = row_count * shard_count
    q_width = HEADS * HEAD_DIM
    k_width = KV_HEADS * HEAD_DIM
    group_size = HEADS // KV_HEADS
    query_scale = HEAD_DIM ** (-0.5)
    local_rows = lax.axis_index("shard") * row_count + jnp.arange(row_count, dtype=jnp.int32)
    position = local_rows % seq_len
    normed_in = rms_norm(residual, gains_used[:, 0]).astype(bf16)
    projected = jnp.dot(normed_in, w_in, preferred_element_type=f32)
    queries = (rotate(projected[:, :q_width], position, HEADS, 1.0) * query_scale).astype(bf16)
    keys = rotate(projected[:, q_width : q_width + k_width], position, KV_HEADS, 1.0).astype(bf16)
    values = projected[:, q_width + k_width :].astype(bf16)
    all_keys, all_values = (
        lax.all_gather(keys, "shard", axis=0, tiled=True),
        lax.all_gather(values, "shard", axis=0, tiled=True),
    )
    key_rows = all_keys.shape[0]
    visible = visibility(
        piece_starts,
        local_rows,
        jnp.arange(key_rows, dtype=jnp.int32),
        rep_index * (key_rows // seq_len),
        seq_len,
    )
    query_heads = queries.reshape(row_count, KV_HEADS, group_size, HEAD_DIM)
    key_heads = all_keys.reshape(key_rows, KV_HEADS, HEAD_DIM)
    value_heads = all_values.reshape(key_rows, KV_HEADS, HEAD_DIM)

    def capped_scores():
        raw_scores = jnp.einsum(
            "tgrd,kgd->grtk", query_heads, key_heads, preferred_element_type=f32
        )
        bent_scores = jnp.tanh(raw_scores / 50.0)
        return (bent_scores, jnp.where(visible, 50.0 * bent_scores, -1e30))

    bent_scores, masked = capped_scores()
    top_score = jnp.max(masked, axis=-1, keepdims=True)
    log_total = top_score + jnp.log(jnp.sum(jnp.exp(masked - top_score), axis=-1, keepdims=True))
    probs_low = jnp.exp(masked - log_total).astype(bf16)
    attended = (
        jnp.einsum("grtk,kgd->tgrd", probs_low, value_heads, preferred_element_type=f32)
        .reshape(row_count, q_width)
        .astype(bf16)
    )
    attn_proj = jnp.dot(attended, w_out, preferred_element_type=f32)
    middle = residual + rms_norm(attn_proj, gains_used[:, 1])
    normed_mid = rms_norm(middle, gains_used[:, 2]).astype(bf16)
    gate_lin = jnp.dot(normed_mid, w_gate, preferred_element_type=f32)
    up_lin = jnp.dot(normed_mid, w_up, preferred_element_type=f32)
    hidden = geglu(gate_lin, up_lin).astype(bf16)
    ffn_proj = jnp.dot(hidden, w_down, preferred_element_type=f32)
    layer_out = (middle + rms_norm(ffn_proj, gains_used[:, 3])).astype(bf16)
    d_out = cotangent.astype(f32)
    _, post_back = jax.vjp(rms_norm, ffn_proj, gains_used[:, 3])
    d_ffn, d_gain3 = post_back(d_out)
    d_ffn_low = d_ffn.astype(bf16)
    hidden_all, d_ffn_all = (
        lax.all_gather(hidden, "rep", axis=0, tiled=True),
        lax.all_gather(d_ffn_low, "rep", axis=0, tiled=True),
    )
    part_down = owned_rows(hidden_all, d_ffn_all, rep_index, hidden.shape[1] // rep_count)
    d_hidden = back_dot(d_ffn_low, w_down)
    _, glu_back = jax.vjp(geglu, gate_lin, up_lin)
    d_gate, d_up = glu_back(d_hidden)
    d_gate_low = d_gate.astype(bf16)
    d_up_low = d_up.astype(bf16)
    gate_up_grad = jnp.concatenate([d_gate_low, d_up_low], axis=1)
    mid_all, gate_up_all = (
        lax.all_gather(normed_mid, "rep", axis=0, tiled=True),
        lax.all_gather(gate_up_grad, "rep", axis=0, tiled=True),
    )
    part_gate_up = owned_rows(mid_all, gate_up_all, rep_index, normed_mid.shape[1] // rep_count)
    d_mid_in = back_dot(d_gate_low, w_gate) + back_dot(d_up_low, w_up)
    _, pre_back = jax.vjp(rms_norm, middle, gains_used[:, 2])
    d_mid_part, d_gain2 = pre_back(d_mid_in)
    d_middle = d_out + d_mid_part
    _, attn_back = jax.vjp(rms_norm, attn_proj, gains_used[:, 1])
    d_attn, d_gain1 = attn_back(d_middle)
    d_attn_low = d_attn.astype(bf16)
    d_attended = back_dot(d_attn_low, w_out).astype(bf16)
    d_heads = d_attended.reshape(row_count, KV_HEADS, group_size, HEAD_DIM)
    bent_again, masked_again = capped_scores()
    attn_probs = jnp.exp(masked_again - log_total)
    probs_again = attn_probs.astype(bf16)
    d_probs = jnp.einsum("tgrd,kgd->grtk", d_heads, value_heads, preferred_element_type=f32)
    d_scores = (
        attn_probs
        * (d_probs - jnp.sum(attn_probs * d_probs, axis=-1, keepdims=True))
        * (1.0 - bent_again * bent_again)
    ).astype(bf16)
    d_queries = jnp.einsum(
        "grtk,kgd->tgrd", d_scores, key_heads, preferred_element_type=f32
    ).reshape(row_count, q_width)
    d_key = jnp.einsum("grtk,tgrd->kgd", d_scores, query_heads, preferred_element_type=f32).reshape(
        row_count * lax.axis_size("shard"), k_width
    )
    d_value = jnp.einsum(
        "grtk,tgrd->kgd", probs_again, d_heads, preferred_element_type=f32
    ).reshape(row_count * lax.axis_size("shard"), k_width)
    d_key_value = lax.psum_scatter(
        jnp.concatenate([d_key, d_value], axis=1), "shard", scatter_dimension=0, tiled=True
    )
    d_projected = jnp.concatenate(
        [
            rotate(d_queries, position, HEADS, -1.0) * query_scale,
            rotate(d_key_value[:, :k_width], position, KV_HEADS, -1.0),
            d_key_value[:, k_width:],
        ],
        axis=1,
    ).astype(bf16)
    d_normed_in = back_dot(d_projected, w_in)
    _, first_back = jax.vjp(rms_norm, residual, gains_used[:, 0])
    d_input_part, d_gain0 = first_back(d_normed_in)
    input_grad = d_middle + d_input_part
    gain_grad = jnp.stack([d_gain0, d_gain1, d_gain2, d_gain3], axis=1)
    attended_all, d_attn_all, normed_all, d_proj_all = (
        lax.all_gather(attended, "rep", axis=0, tiled=True),
        lax.all_gather(d_attn_low, "rep", axis=0, tiled=True),
        lax.all_gather(normed_in, "rep", axis=0, tiled=True),
        lax.all_gather(d_projected, "rep", axis=0, tiled=True),
    )
    part_out = owned_rows(attended_all, d_attn_all, rep_index, attended.shape[1] // rep_count)
    part_in = owned_rows(normed_all, d_proj_all, rep_index, normed_in.shape[1] // rep_count)
    part_gain = lax.psum_scatter(gain_grad, "rep", scatter_dimension=0, tiled=True)
    owned = (
        lax.psum_scatter(part_in, "shard", scatter_dimension=0, tiled=True),
        lax.psum_scatter(part_gain, "shard", scatter_dimension=0, tiled=True),
        lax.psum_scatter(part_out, "shard", scatter_dimension=0, tiled=True),
        lax.psum_scatter(part_gate_up, "shard", scatter_dimension=0, tiled=True),
        lax.psum_scatter(part_down, "shard", scatter_dimension=0, tiled=True),
    )
    grad_inproj, grad_gains, grad_outproj, grad_gate_up, grad_down = owned
    split_at = grad_gate_up.shape[1] // 2
    grad_gate = grad_gate_up[:, :split_at]
    grad_up = grad_gate_up[:, split_at:]
    masters = (inproj, outproj, ffn_gate, ffn_up, ffn_down, norm_gains)
    gradients = (grad_inproj, grad_outproj, grad_gate, grad_up, grad_down, grad_gains)
    firsts = (mean_inproj, mean_outproj, mean_gate, mean_up, mean_down, mean_gains)
    seconds = (square_inproj, square_outproj, square_gate, square_up, square_down, square_gains)
    results = [
        lamb_local(masters[index], gradients[index], firsts[index], seconds[index])
        for index in range(6)
    ]
    weight_sums = jnp.stack([jnp.sum(master * master) for master in masters])
    step_sums = jnp.stack([jnp.sum(item[2] * item[2]) for item in results])
    totals = lax.psum(jnp.stack([weight_sums, step_sums]), ("rep", "shard"))
    counts = jnp.array([float(master.size * rep_count * shard_count) for master in masters], f32)
    norm_table = jnp.sqrt(totals / counts[None, :] + 1e-06)
    fresh = [
        masters[index] - 0.3 * norm_table[0, index] / norm_table[1, index] * results[index][2]
        for index in range(6)
    ]
    return (
        layer_out,
        input_grad,
        grad_inproj,
        grad_outproj,
        grad_gate,
        grad_up,
        grad_down,
        grad_gains,
        results[0][0],
        results[1][0],
        results[2][0],
        results[3][0],
        results[4][0],
        results[5][0],
        results[0][1],
        results[1][1],
        results[2][1],
        results[3][1],
        results[4][1],
        results[5][1],
        fresh[0],
        fresh[1],
        fresh[2],
        fresh[3],
        fresh[4],
        fresh[5],
        norm_table,
    )


MESH = pl.DeviceIdType.MESH
VM = pltpu.VMEM
HB = pl.ANY
UNITS = 4
VMEM_LIMIT = 60 << 20


def ring_places(count):
    inner = 2 if count == 8 else 4
    outer = count // inner

    def place(shard):
        major = shard // inner
        minor = shard % inner
        return minor * outer + major + (minor % 2) * (outer - 1 - 2 * major)

    def shard_at(spot):
        minor = spot // outer
        major = spot % outer
        return (major + (minor % 2) * (outer - 1 - 2 * major)) * inner + minor

    return place, shard_at


def meet(devices):
    barrier = pltpu.get_barrier_semaphore()
    for device in devices:
        pl.semaphore_signal(barrier, inc=1, device_id=device, device_id_type=MESH)
    pl.semaphore_wait(barrier, len(devices))


def remote(src, dst, send_sem, recv_sem, device):
    return pltpu.make_async_remote_copy(
        src_ref=src,
        dst_ref=dst,
        send_sem=send_sem,
        recv_sem=recv_sem,
        device_id=device,
        device_id_type=MESH,
    )


class Ring:
    def __init__(self, count):
        place, shard_at = ring_places(count)
        self.count = count
        self.half = count // 2
        self.rep = lax.axis_index("rep")
        self.me = lax.axis_index("shard")
        self.spot = place(self.me)
        self.shard_at = shard_at
        self.next = [(self.rep, self.at(1)), (self.rep, self.at(count - 1))]

    def at(self, ahead):
        return self.shard_at((self.spot + ahead) % self.count)

    def away(self, way, hops):
        return self.at(hops if way == 0 else self.count - hops)

    def units(self, way, hop):
        order = list(range(UNITS)) if way == 0 else list(range(UNITS))[::-1]
        return order if hop < self.half else order[: UNITS // 2]


def ring_gather_kernel(count, x_ref, out_ref, send, recv, local):
    ring = Ring(count)
    rows = x_ref.shape[0] // UNITS

    def part(unit):
        return pl.ds(unit * rows, rows)

    def hop_copy(way, hop, unit):
        origin = ring.away(1 - way, hop - 1) if hop > 1 else ring.me
        src = x_ref.at[part(unit)] if hop == 1 else out_ref.at[origin, part(unit)]
        return remote(
            src,
            out_ref.at[origin, part(unit)],
            send.at[way, hop - 1, unit],
            recv.at[way, hop - 1, unit],
            ring.next[way],
        )

    meet(ring.next)
    own = pltpu.make_async_copy(x_ref, out_ref.at[ring.me], local)
    own.start()
    started = []
    for index in range(UNITS):
        for way in (0, 1):
            copy = hop_copy(way, 1, ring.units(way, 1)[index])
            copy.start()
            started.append(copy)
    for hop in range(1, ring.half + 1):
        for index in range(len(ring.units(0, hop))):
            for way in (0, 1):
                unit = ring.units(way, hop)[index]
                hop_copy(way, hop, unit).wait_recv()
                if hop < ring.half and unit in ring.units(way, hop + 1):
                    copy = hop_copy(way, hop + 1, unit)
                    copy.start()
                    started.append(copy)
    for copy in started:
        copy.wait_send()
    own.wait()


def ring_gather(block, count, collective_id):
    rows, columns = block.shape
    hops = count // 2
    gathered = pl.pallas_call(
        functools.partial(ring_gather_kernel, count),
        out_shape=jax.ShapeDtypeStruct((count, rows, columns), block.dtype),
        in_specs=[pl.BlockSpec(memory_space=VM)],
        out_specs=pl.BlockSpec(memory_space=VM),
        scratch_shapes=[
            pltpu.SemaphoreType.DMA((2, hops, UNITS)),
            pltpu.SemaphoreType.DMA((2, hops, UNITS)),
            pltpu.SemaphoreType.DMA,
        ],
        compiler_params=pltpu.CompilerParams(
            collective_id=collective_id, has_side_effects=True, vmem_limit_bytes=VMEM_LIMIT
        ),
        name=f"ring_gather_{collective_id}",
    )(block)
    return gathered.reshape(count * rows, columns)


def ring_reduce_kernel(count, x_ref, out_ref, held, landed, send, recv):
    ring = Ring(count)
    rows = out_ref.shape[0] // UNITS
    hops = ring.half

    def part(unit):
        return pl.ds(unit * rows, rows)

    def step_copy(way, step, unit):
        return remote(
            held.at[way, step, part(unit)],
            landed.at[way, step, part(unit)],
            send.at[way, step, unit],
            recv.at[way, step, unit],
            ring.next[way],
        )

    meet(ring.next)
    started = []
    for step in range(hops):
        order = ring.units(0, hops - step), ring.units(1, hops - step)
        before = [ring.units(way, hops - step + 1) if step else [] for way in (0, 1)]
        for index in range(len(order[0])):
            for way in (0, 1):
                unit = order[way][index]
                block = x_ref[ring.away(way, hops - step), part(unit), :].astype(jnp.float32)
                if unit in before[way]:
                    step_copy(way, step - 1, unit).wait_recv()
                    block += landed[way, step - 1, part(unit), :].astype(jnp.float32)
                held[way, step, part(unit), :] = block.astype(held.dtype)
                copy = step_copy(way, step, unit)
                copy.start()
                started.append(copy)
    for index in range(UNITS):
        unit = index
        total = x_ref[ring.me, part(unit), :].astype(jnp.float32)
        for way in (0, 1):
            step_copy(way, hops - 1, unit).wait_recv()
            total += landed[way, hops - 1, part(unit), :].astype(jnp.float32)
        out_ref[part(unit), :] = total
    for copy in started:
        copy.wait_send()


def ring_reduce(partial, count, collective_id):
    rows, columns = partial.shape[0] // count, partial.shape[1]
    hops = count // 2
    return pl.pallas_call(
        functools.partial(ring_reduce_kernel, count),
        out_shape=jax.ShapeDtypeStruct((rows, columns), jnp.float32),
        in_specs=[pl.BlockSpec(memory_space=VM)],
        out_specs=pl.BlockSpec(memory_space=VM),
        scratch_shapes=[
            pltpu.VMEM((2, hops, rows, columns), jnp.bfloat16),
            pltpu.VMEM((2, hops, rows, columns), jnp.bfloat16),
            pltpu.SemaphoreType.DMA((2, hops, UNITS)),
            pltpu.SemaphoreType.DMA((2, hops, UNITS)),
        ],
        compiler_params=pltpu.CompilerParams(
            collective_id=collective_id, has_side_effects=True, vmem_limit_bytes=VMEM_LIMIT
        ),
        name=f"ring_reduce_{collective_id}",
    )(partial.reshape(count, rows, columns))


class Flow:
    def __init__(self, ring, rows, send, recv):
        self.ring, self.rows, self.send, self.recv = ring, rows, send, recv
        self.unit_rows = rows // UNITS
        self.started = []

    def span(self, slot, unit):
        return pl.ds(slot * self.rows + unit * self.unit_rows, self.unit_rows)

    def slot(self, way, hops):
        if hops == 0:
            return 0
        return self.ring.count - 1 if hops == self.ring.half else 2 * hops - 1 + way

    def go(self, copy):
        copy.start()
        self.started.append(copy)

    def finish(self):
        for copy in self.started:
            copy.wait_send()

    def gather_copy(self, buffer, way, hop, unit):
        return remote(
            buffer.at[self.span(self.slot(way, hop - 1), unit)],
            buffer.at[self.span(self.slot(way, hop), unit)],
            self.send.at[way, hop - 1, unit],
            self.recv.at[way, hop - 1, unit],
            self.ring.next[way],
        )

    def gather(self, buffer, group_work):
        ring = self.ring
        for index in range(UNITS):
            for way in (0, 1):
                self.go(self.gather_copy(buffer, way, 1, ring.units(way, 1)[index]))
        queue = list(group_work(0, 1))
        for hop in range(1, ring.half + 1):
            length = len(ring.units(0, hop))
            for index in range(length):
                for way in (0, 1):
                    unit = ring.units(way, hop)[index]
                    self.gather_copy(buffer, way, hop, unit).wait_recv()
                    if hop < ring.half and unit in ring.units(way, hop + 1):
                        self.go(self.gather_copy(buffer, way, hop + 1, unit))
                if queue:
                    queue.pop(0)()
            for piece in queue:
                piece()
            queue = list(group_work(2 * hop - 1, 2) if hop < ring.half else group_work(ring.count - 1, 1))
        for piece in queue:
            piece()
        self.finish()

    def reduce_copy(self, first, landed, way, step, unit):
        span = pl.ds(unit * self.unit_rows, self.unit_rows)
        src = first.at[span] if step == 0 else landed.at[way, step - 1, span]
        return remote(
            src,
            landed.at[way, step, span],
            self.send.at[way, step, unit],
            self.recv.at[way, step, unit],
            self.ring.next[way],
        )

    def reduce(self, first, landed, partial, group_work, finish):
        ring = self.ring
        hops = ring.half
        f32 = jnp.float32
        for piece in group_work(ring.count - 1, 1, 0):
            piece()
        queue = list(group_work(2 * (hops - 1) - 1, 2, 1))
        for step in range(hops):
            order = ring.units(0, hops - step), ring.units(1, hops - step)
            before = [ring.units(way, hops - step + 1) if step else [] for way in (0, 1)]
            for index in range(len(order[0])):
                for way in (0, 1):
                    unit = order[way][index]
                    span = pl.ds(unit * self.unit_rows, self.unit_rows)
                    if step == 0:
                        first[span, :] = partial[0, pl.ds(unit * self.unit_rows, self.unit_rows), :].astype(first.dtype)
                    else:
                        side = 1 - way
                        block = partial[
                            step % 2, pl.ds(side * self.rows + unit * self.unit_rows, self.unit_rows), :
                        ]
                        if unit in before[way]:
                            self.reduce_copy(first, landed, way, step - 1, unit).wait_recv()
                            block = block + landed[way, step - 1, span, :].astype(f32)
                        landed[way, step - 1, span, :] = block.astype(landed.dtype)
                    self.go(self.reduce_copy(first, landed, way, step, unit))
                if queue:
                    queue.pop(0)()
            for piece in queue:
                piece()
            ahead = hops - step - 2
            queue = []
            if step < hops - 1:
                queue = list(group_work(2 * ahead - 1, 2, step % 2) if ahead > 0 else group_work(0, 1, step % 2))
        for unit in range(UNITS):
            span = pl.ds(unit * self.unit_rows, self.unit_rows)
            total = partial[hops % 2, span, :]
            for way in (0, 1):
                self.reduce_copy(first, landed, way, hops - 1, unit).wait_recv()
                total = total + landed[way, hops - 1, span, :].astype(f32)
            finish(unit, total)
        self.finish()


def looped(piece, count):
    def all_of_it():
        def body(j, carry):
            piece(j)
            return carry

        lax.fori_loop(0, count, body, 0)

    return [all_of_it]


def gelu_pair(gate):
    inner = 0.7978845608028654 * (gate + 0.044715 * gate * gate * gate)
    bend = jnp.tanh(inner)
    value = 0.5 * gate * (1.0 + bend)
    slope = 0.5 * (1.0 + bend) + 0.5 * gate * (1.0 - bend * bend) * 0.7978845608028654 * (
        1.0 + 0.134145 * gate * gate
    )
    return value, slope


def ffn_kernel(
    count, attn_ref, tokens_ref, cot_ref, gains_ref, gu_ref, dn_ref,
    layer_ref, dmid_ref, dattn_ref, gg_ref, h3_ref, hid_ref, dffn_ref, dgu_ref,
    lin, partial, first, landed, middle, total_ref, s1, r1, s2, r2, s3, r3, s4, r4,
):
    f32, bf16 = jnp.float32, jnp.bfloat16
    ring = Ring(count)
    rows, width = attn_ref.shape
    part = hid_ref.shape[1]
    tile = part // 3
    wide = width // 3
    meet(ring.next)

    def gain(index):
        return 1.0 + gains_ref[index : index + 1, :]

    def scale_of(value):
        return lax.rsqrt(jnp.mean(value * value, axis=-1, keepdims=True) + 1e-06)

    half = rows // 2
    halves = [pl.ds(0, half), pl.ds(half, half)]
    for span in halves:
        proj = attn_ref[span, :]
        mid = tokens_ref[span, :].astype(f32) + proj * scale_of(proj) * gain(1)
        middle[span, :] = mid
        h3_ref[span, :] = (mid * scale_of(mid) * gain(2)).astype(bf16)

    def lin_work(slot, blocks):
        at = pl.ds(slot * rows, blocks * rows)

        def piece(j):
            lo = pl.ds(pl.multiple_of(j * tile, 128), tile)
            hi = pl.ds(pl.multiple_of(part + j * tile, 128), tile)
            gate = jnp.dot(h3_ref[at, :], gu_ref[:, lo], preferred_element_type=f32)
            up = jnp.dot(h3_ref[at, :], gu_ref[:, hi], preferred_element_type=f32)
            value, slope = gelu_pair(gate)
            hid_ref[at, lo] = (value * up).astype(bf16)
            lin[at, lo] = (up * slope).astype(bf16)
            lin[at, hi] = value.astype(bf16)

        return looped(piece, 3)

    def down_work(slot, blocks, side):
        at = pl.ds(slot * rows, blocks * rows)

        def piece(j):
            cols = pl.ds(pl.multiple_of(j * wide, 128), wide)
            partial[side, pl.ds(0, blocks * rows), cols] = jnp.dot(
                hid_ref[at, :], dn_ref[:, cols], preferred_element_type=f32
            )

        return looped(piece, 3)

    def nt(left, right):
        return lax.dot_general(left, right, (((1,), (1,)), ((), ())), preferred_element_type=f32)

    def back_work(slot, blocks):
        at = pl.ds(slot * rows, blocks * rows)

        def piece(j):
            lo = pl.ds(pl.multiple_of(j * tile, 128), tile)
            hi = pl.ds(pl.multiple_of(part + j * tile, 128), tile)
            d_hidden = nt(dffn_ref[at, :], dn_ref[lo, :])
            dgu_ref[at, lo] = (d_hidden * lin[at, lo].astype(f32)).astype(bf16)
            dgu_ref[at, hi] = (d_hidden * lin[at, hi].astype(f32)).astype(bf16)

        return looped(piece, 3)

    def input_work(slot, blocks, side):
        at = pl.ds(slot * rows, blocks * rows)

        def piece(j):
            cols = pl.ds(pl.multiple_of(j * wide, 128), wide)
            partial[side, pl.ds(0, blocks * rows), cols] = nt(dgu_ref[at, :], gu_ref[cols, :])

        return looped(piece, 3)

    def keep(unit, total):
        total_ref[pl.ds(unit * (rows // UNITS), rows // UNITS), :] = total

    Flow(ring, rows, s1, r1).gather(h3_ref, lin_work)
    Flow(ring, rows, s2, r2).reduce(first, landed, partial, down_work, keep)

    def back_norm(value, index, grad):
        scale = scale_of(value)
        normed = value * scale
        weighted = grad * gain(index)
        inner = jnp.mean(weighted * normed, axis=-1, keepdims=True)
        return scale * (weighted - normed * inner), jnp.sum(grad * normed, axis=0, keepdims=True)

    gg = jnp.zeros((1, width), f32)
    for span in halves:
        proj = total_ref[span, :]
        scale = scale_of(proj)
        layer_ref[span, :] = (middle[span, :] + proj * scale * gain(3)).astype(bf16)
        d_ffn, term = back_norm(proj, 3, cot_ref[span, :].astype(f32))
        gg += term
        dffn_ref[span, :] = d_ffn.astype(bf16)
    gg_ref[3:4, :] = gg

    Flow(ring, rows, s3, r3).gather(dffn_ref, back_work)
    Flow(ring, rows, s4, r4).reduce(first, landed, partial, input_work, keep)

    gg1 = jnp.zeros((1, width), f32)
    gg2 = jnp.zeros((1, width), f32)
    for span in halves:
        d_mid, term = back_norm(middle[span, :], 2, total_ref[span, :])
        gg2 += term
        d_mid = d_mid + cot_ref[span, :].astype(f32)
        dmid_ref[span, :] = d_mid
        d_attn, term = back_norm(attn_ref[span, :], 1, d_mid)
        gg1 += term
        dattn_ref[span, :] = d_attn.astype(bf16)
    gg_ref[1:2, :] = gg1
    gg_ref[2:3, :] = gg2
    gg_ref[0:1, :] = jnp.zeros((1, width), f32)
    gg_ref[4:8, :] = jnp.zeros((4, width), f32)


def feed_forward(attn_proj, tokens, cotangent, gain_rows, w_gu, w_down, count, collective_id):
    f32, bf16 = jnp.float32, jnp.bfloat16
    rows, width = attn_proj.shape
    part = w_down.shape[0]
    every = rows * count
    dma = pltpu.SemaphoreType.DMA
    shape = jax.ShapeDtypeStruct
    return pl.pallas_call(
        functools.partial(ffn_kernel, count),
        out_shape=[
            shape((rows, width), bf16),
            shape((rows, width), f32),
            shape((rows, width), bf16),
            shape((8, width), f32),
            shape((every, width), bf16),
            shape((every, part), bf16),
            shape((every, width), bf16),
            shape((every, 2 * part), bf16),
        ],
        in_specs=[pl.BlockSpec(memory_space=VM)] * 6,
        out_specs=[pl.BlockSpec(memory_space=VM)] * 8,
        scratch_shapes=[
            pltpu.VMEM((every, 2 * part), bf16),
            pltpu.VMEM((2, 2 * rows, width), f32),
            pltpu.VMEM((rows, width), bf16),
            pltpu.VMEM((2, count // 2, rows, width), bf16),
            pltpu.VMEM((rows, width), f32),
            pltpu.VMEM((rows, width), f32),
        ]
        + [dma((2, count // 2, UNITS))] * 8,
        compiler_params=pltpu.CompilerParams(
            collective_id=collective_id, has_side_effects=True, vmem_limit_bytes=VMEM_LIMIT
        ),
        name="feed_forward",
    )(attn_proj, tokens, cotangent, gain_rows, w_gu, w_down)


def rep_partners(rep):
    return (rep + 2) % 4, rep + 1 - 2 * (rep % 2)


def everyone(rep, me, reps, count):
    here = rep * count + me
    total = reps * count
    return [
        (((here + k) % total) // count, ((here + k) % total) % count) for k in range(1, total)
    ]


def opening_kernel(
    reps, count, tok_ref, gain_ref, in_ref, gu_ref, dn_ref, ou_ref, tok_out, gain_out, w_in, w_gu, w_dn, w_ou,
    t_send, t_recv, g_send, g_recv, a_send, a_recv, x_send, x_recv, c_send, c_recv, d_send, d_recv,
    o_send, o_recv, n_send, n_recv, loc
):
    ring = Ring(count)
    rep, me = ring.rep, ring.me
    across, beside = rep_partners(rep)
    others = everyone(rep, me, reps, count)
    meet(others)
    started = []

    def go(copy):
        copy.start()
        started.append(copy)

    rows = tok_ref.shape[0] // UNITS

    def hop_copy(way, hop, unit):
        origin = ring.away(1 - way, hop - 1) if hop > 1 else me
        span = pl.ds(unit * rows, rows)
        return remote(
            tok_ref.at[span] if hop == 1 else tok_out.at[origin, span],
            tok_out.at[origin, span],
            t_send.at[way, hop - 1, unit],
            t_recv.at[way, hop - 1, unit],
            ring.next[way],
        )

    def take_hop(hop):
        for index in range(len(ring.units(0, hop))):
            for way in (0, 1):
                unit = ring.units(way, hop)[index]
                hop_copy(way, hop, unit).wait_recv()
                if hop < ring.half and unit in ring.units(way, hop + 1):
                    go(hop_copy(way, hop + 1, unit))

    per_head = count * reps // HEADS
    mine = rep * count + me
    target = mine // per_head
    slot = mine % per_head

    def ou_copy(j):
        return remote(ou_ref.at[j], w_ou.at[j, slot], o_send.at[j], o_recv.at[slot], (j, target))

    def is_self(j):
        return (rep == j) & (me == target)

    pairs = ((in_ref, w_in), (gu_ref, w_gu))

    def spread(which, k):
        to = (me + k) % count
        src, dst = pairs[which]
        return remote(
            src.at[to], dst.at[rep, me], a_send.at[which, k], a_recv.at[which, k], (rep, to)
        )

    def arrived(which, k):
        frm = (me + count - k) % count
        src, dst = pairs[which]
        return remote(
            src.at[frm], dst.at[rep, frm], a_send.at[which, k], a_recv.at[which, k], (rep, frm)
        )

    def forward(which, k, hop):
        frm = (me + count - k) % count
        src, dst = pairs[which]
        block = src.at[me] if k == 0 else dst.at[rep, frm]
        if hop == 0:
            return remote(
                block, dst.at[rep, frm], x_send.at[which, k], x_recv.at[which, k], (across, me)
            )
        if hop == 1:
            return remote(
                block, dst.at[rep, frm], c_send.at[which, k], c_recv.at[which, k], (beside, me)
            )
        return remote(
            dst.at[across, frm], dst.at[across, frm], d_send.at[which, k], d_recv.at[which, k],
            (beside, me),
        )

    def pass_on(which, k):
        if k:
            arrived(which, k).wait_recv()
        go(forward(which, k, 0))
        go(forward(which, k, 1))

    def pass_beside(which, k):
        forward(which, k, 0).wait_recv()
        go(forward(which, k, 2))

    for k in range(1, count):
        go(spread(0, k))
    pass_on(0, 0)
    for index in range(UNITS):
        for way in (0, 1):
            go(hop_copy(way, 1, ring.units(way, 1)[index]))
    for k, device in enumerate(others):
        go(remote(gain_ref, gain_out.at[mine], g_send.at[k], g_recv.at[k], device))
    for j in range(reps):
        @pl.when(jnp.logical_not(is_self(j)))
        def _():
            ou_copy(j).start()

        @pl.when(is_self(j))
        def _():
            pltpu.make_async_copy(ou_ref.at[j], w_ou.at[j, slot], o_recv.at[slot]).start()

    dn_x = remote(dn_ref, w_dn.at[rep], n_send.at[0], n_recv.at[0], (across, me))
    dn_c = remote(dn_ref, w_dn.at[rep], n_send.at[1], n_recv.at[1], (beside, me))
    dn_d = remote(w_dn.at[across], w_dn.at[across], n_send.at[2], n_recv.at[2], (beside, me))
    go(dn_x)
    go(dn_c)
    for k in range(1, count):
        go(spread(1, k))
    pass_on(1, 0)
    locals_ = []
    for index, (src, dst) in enumerate(
        (
            (in_ref.at[me], w_in.at[rep, me]),
            (gu_ref.at[me], w_gu.at[rep, me]),
            (dn_ref, w_dn.at[rep]),
            (tok_ref, tok_out.at[me]),
            (gain_ref, gain_out.at[mine]),
        )
    ):
        copy = pltpu.make_async_copy(src, dst, loc.at[index])
        copy.start()
        locals_.append(copy)

    for k in range(1, count):
        pass_on(0, k)
    take_hop(1)
    for k in range(count):
        pass_beside(0, k)
    take_hop(2)
    for i in range(per_head):
        remote(
            ou_ref.at[0], w_ou.at[rep, i], o_send.at[0], o_recv.at[i], (across, me)
        ).wait_recv()
    ou_x = remote(w_ou.at[rep], w_ou.at[rep], n_send.at[3], n_recv.at[3], (across, me))
    ou_c = remote(w_ou.at[rep], w_ou.at[rep], n_send.at[4], n_recv.at[4], (beside, me))
    ou_d = remote(w_ou.at[across], w_ou.at[across], n_send.at[5], n_recv.at[5], (beside, me))
    go(ou_x)
    go(ou_c)
    for k in range(1, count // 2):
        pass_on(1, k)
    dn_x.wait_recv()
    go(dn_d)
    take_hop(3)
    for k in range(count // 2, count):
        pass_on(1, k)
    for hop in range(4, ring.half + 1):
        take_hop(hop)
    ou_x.wait_recv()
    go(ou_d)
    for k in range(count):
        pass_beside(1, k)
    for which in (0, 1):
        for k in range(count):
            forward(which, k, 1).wait_recv()
            forward(which, k, 2).wait_recv()
    for copy in (dn_c, dn_d, ou_c, ou_d):
        copy.wait_recv()
    for k in range(len(others)):
        frm = (mine + len(others) - k) % (reps * count)
        remote(gain_ref, gain_out.at[frm], g_send.at[k], g_recv.at[k], others[k]).wait_recv()
    for copy in started:
        copy.wait_send()
    for j in range(reps):
        @pl.when(jnp.logical_not(is_self(j)))
        def _():
            ou_copy(j).wait_send()
    for copy in locals_:
        copy.wait()


def opening(reps, count, tokens, gain_tile, w_in, w_gu, w_dn, w_ou, collective_id):
    dma = pltpu.SemaphoreType.DMA
    per_head = count * reps // HEADS
    total = reps * count
    low = jnp.bfloat16
    shape = jax.ShapeDtypeStruct
    hops = dma((2, count // 2, UNITS))
    return pl.pallas_call(
        functools.partial(opening_kernel, reps, count),
        out_shape=[
            shape((count,) + tokens.shape, low),
            shape((total,) + gain_tile.shape, gain_tile.dtype),
            shape((reps,) + w_in.shape, low),
            shape((reps,) + w_gu.shape, low),
            shape((reps,) + w_dn.shape, low),
            shape((reps, per_head) + w_ou.shape[1:], low),
        ],
        in_specs=[pl.BlockSpec(memory_space=HB)] * 6,
        out_specs=[pl.BlockSpec(memory_space=HB)] * 6,
        scratch_shapes=[hops, hops, dma((total - 1,)), dma((total - 1,))]
        + [dma((2, count))] * 8
        + [dma((reps,)), dma((per_head,)), dma((6,)), dma((6,)), dma((5,))],
        compiler_params=pltpu.CompilerParams(
            collective_id=collective_id, has_side_effects=True, vmem_limit_bytes=VMEM_LIMIT
        ),
        name="opening",
    )(tokens, gain_tile, w_in, w_gu, w_dn, w_ou)


def cut_kernel(reps, count, in_ref, gate_ref, up_ref, cut_in, cut_gu):
    low = jnp.bfloat16
    group = HEADS // KV_HEADS
    block = gate_ref.shape[1] // (reps * count)
    part = block * reps
    for shard in range(count):
        for index, ref in enumerate((gate_ref, up_ref)):
            pieces = [ref[:, (r * count + shard) * block : (r * count + shard + 1) * block] for r in range(reps)]
            cut_gu[shard, :, index * part : (index + 1) * part] = jnp.concatenate(pieces, axis=1).astype(low)
        heads = shard, HEADS + shard // group, HEADS + KV_HEADS + shard // group
        for index, head in enumerate(heads):
            cut_in[shard, :, index * HEAD_DIM : (index + 1) * HEAD_DIM] = in_ref[
                :, head * HEAD_DIM : (head + 1) * HEAD_DIM
            ].astype(low)


def cut_weights(reps, count, inproj, ffn_gate, ffn_up):
    rows = inproj.shape[0]
    shape = jax.ShapeDtypeStruct
    return pl.pallas_call(
        functools.partial(cut_kernel, reps, count),
        out_shape=[
            shape((count, rows, 3 * HEAD_DIM), jnp.bfloat16),
            shape((count, rows, 2 * ffn_gate.shape[1] // count), jnp.bfloat16),
        ],
        in_specs=[pl.BlockSpec(memory_space=VM)] * 3,
        out_specs=[pl.BlockSpec(memory_space=VM)] * 2,
        compiler_params=pltpu.CompilerParams(vmem_limit_bytes=VMEM_LIMIT),
        name="cut_weights",
    )(inproj, ffn_gate, ffn_up)


def join_kernel(reps, count, sum_ref, gate_ref, up_ref):
    block = gate_ref.shape[1] // (reps * count)
    part = block * reps
    per = 4
    for index, ref in enumerate((gate_ref, up_ref)):
        for first in range(0, reps * count, per):
            pieces = []
            for b in range(first, first + per):
                r, shard = b // count, b % count
                start = index * part + r * block
                pieces.append(sum_ref[shard, :, start : start + block].astype(jnp.float32))
            ref[:, first * block : (first + per) * block] = jnp.concatenate(pieces, axis=1)


def join_grads(reps, count, sums):
    rows = sums.shape[1]
    shape = jax.ShapeDtypeStruct((rows, sums.shape[2] * count // 2), jnp.float32)
    return pl.pallas_call(
        functools.partial(join_kernel, reps, count),
        out_shape=[shape, shape],
        in_specs=[pl.BlockSpec(memory_space=VM)],
        out_specs=[pl.BlockSpec(memory_space=VM)] * 2,
        compiler_params=pltpu.CompilerParams(vmem_limit_bytes=VMEM_LIMIT),
        name="join_grads",
    )(sums)


class RepSum:
    def __init__(self, part, from_core, to_across, from_across, sems, rep, me):
        self.part, self.from_core = part, from_core
        self.to_across, self.from_across = to_across, from_across
        self.c_send, self.c_recv, self.x_send, self.x_recv = sems
        self.across, self.beside = rep_partners(rep)
        self.rep, self.me = rep, me
        self.core = rep % 2
        self.chip = rep // 2

    def core_copy(self, side, piece):
        chip = 1 - self.chip if side == 0 else self.chip
        return remote(
            self.part(chip * 2 + 1 - self.core, piece),
            self.from_core.at[side, piece],
            self.c_send.at[side, piece],
            self.c_recv.at[side, piece],
            (self.beside, self.me),
        )

    def cross_copy(self, piece):
        return remote(
            self.to_across.at[piece],
            self.from_across.at[piece],
            self.x_send.at[piece],
            self.x_recv.at[piece],
            (self.across, self.me),
        )

    def begin(self, pieces):
        for side in (0, 1):
            for piece in pieces:
                self.core_copy(side, piece).start()

    def cross(self, piece):
        f32 = jnp.float32
        self.core_copy(0, piece).wait_recv()
        mine = self.part((1 - self.chip) * 2 + self.core, piece)[...].astype(f32)
        self.to_across[piece] = (mine + self.from_core[0, piece].astype(f32)).astype(jnp.bfloat16)
        self.cross_copy(piece).start()

    def total(self, piece):
        f32 = jnp.float32
        self.core_copy(1, piece).wait_recv()
        mine = self.part(self.rep, piece)[...].astype(f32) + self.from_core[1, piece].astype(f32)
        self.cross_copy(piece).wait_recv()
        return mine + self.from_across[piece].astype(f32)

    def finish(self, pieces):
        for piece in pieces:
            self.core_copy(0, piece).wait_send()
            self.core_copy(1, piece).wait_send()
            self.cross_copy(piece).wait_send()


class Spread:
    def __init__(self, blocks, out, send, recv, rep, me, count):
        self.blocks, self.out, self.send, self.recv = blocks, out, send, recv
        self.rep, self.me, self.count = rep, me, count

    def copy(self, k):
        to = (self.me + k) % self.count
        return remote(
            self.blocks.at[to], self.out.at[self.me], self.send.at[k], self.recv.at[k], (self.rep, to)
        )

    def arrived(self, k):
        frm = (self.me + self.count - k) % self.count
        return remote(
            self.blocks.at[frm], self.out.at[frm], self.send.at[k], self.recv.at[k], (self.rep, frm)
        )

    def finish(self):
        for k in range(1, self.count):
            self.arrived(k).wait_recv()
        for k in range(1, self.count):
            self.copy(k).wait_send()


def near_devices(ring):
    across, beside = rep_partners(ring.rep)
    return [(ring.rep, (ring.me + k) % ring.count) for k in range(1, ring.count)] + [
        (across, ring.me),
        (beside, ring.me),
    ]


class Gather:
    def __init__(self, ring, block, out, send, recv):
        self.ring, self.block, self.out, self.send, self.recv = ring, block, out, send, recv
        self.rows = block.shape[0] // UNITS
        self.started = []

    def copy(self, way, hop, unit):
        ring = self.ring
        origin = ring.away(1 - way, hop - 1) if hop > 1 else ring.me
        span = pl.ds(unit * self.rows, self.rows)
        return remote(
            self.block.at[span] if hop == 1 else self.out.at[origin, span],
            self.out.at[origin, span],
            self.send.at[way, hop - 1, unit],
            self.recv.at[way, hop - 1, unit],
            ring.next[way],
        )

    def go(self, copy):
        copy.start()
        self.started.append(copy)

    def begin(self):
        for index in range(UNITS):
            for way in (0, 1):
                self.go(self.copy(way, 1, self.ring.units(way, 1)[index]))

    def steps(self):
        ring = self.ring

        def step(hop, index):
            for way in (0, 1):
                unit = ring.units(way, hop)[index]
                self.copy(way, hop, unit).wait_recv()
                if hop < ring.half and unit in ring.units(way, hop + 1):
                    self.go(self.copy(way, hop + 1, unit))

        return [
            functools.partial(step, hop, index)
            for hop in range(1, ring.half + 1)
            for index in range(len(ring.units(0, hop)))
        ]

    def finish(self):
        for copy in self.started:
            copy.wait_send()


def tn(left, right):
    return lax.dot_general(left, right, (((0,), (0,)), ((), ())), preferred_element_type=jnp.float32)


DN_PIECES = 3


def ffn_grads_kernel(
    reps, count, dattn_ref, h3_ref, hid_ref, dffn_ref, dgu_ref, all_ref, sum_ref, down_ref,
    g_part, g_core, g_to, g_from, d_part, d_core, d_to, d_from,
    t_send, t_recv, gc_s, gc_r, gx_s, gx_r, dc_s, dc_r, dx_s, dx_r, s_send, s_recv, loc
):
    bf16 = jnp.bfloat16
    ring = Ring(count)
    rep, me = ring.rep, ring.me
    d_rows, columns = sum_ref.shape[1:]
    part, width = d_part.shape
    block = part // reps
    wide = width // 3
    tall = part // 3
    meet(near_devices(ring))
    gather = Gather(ring, dattn_ref, all_ref, t_send, t_recv)
    gather.begin()
    own = pltpu.make_async_copy(dattn_ref, all_ref.at[me], loc)
    own.start()

    def d_at(owner, piece):
        rows = block // DN_PIECES
        return d_part.at[pl.ds(owner * block + piece * rows, rows)]

    down = RepSum(d_at, d_core, d_to, d_from, (dc_s, dc_r, dx_s, dx_r), rep, me)
    gate_up = RepSum(
        lambda owner, piece: g_part.at[owner, piece], g_core, g_to, g_from, (gc_s, gc_r, gx_s, gx_r), rep, me
    )
    spread = Spread(g_from, sum_ref, s_send, s_recv, rep, me, count)
    d_pieces = list(range(DN_PIECES))
    g_pieces = [(me + k) % count for k in range(1, count)] + [me]

    def make_down(j):
        def body(n, carry):
            cols = pl.ds(pl.multiple_of(n * wide, 128), wide)
            d_part[j * tall : (j + 1) * tall, cols] = tn(
                hid_ref[:, j * tall : (j + 1) * tall], dffn_ref[:, cols]
            ).astype(bf16)
            return carry

        lax.fori_loop(0, 3, body, 0)

    def make_gate_up(owner):
        rows = count * d_rows
        step = columns // 3

        def body(n, carry):
            cols = pl.ds(pl.multiple_of(n * step, 128), step)
            made = tn(h3_ref[:, owner * rows : (owner + 1) * rows], dgu_ref[:, cols])
            g_part[owner, :, :, cols] = made.reshape(count, d_rows, step).astype(bf16)
            return carry

        lax.fori_loop(0, 3, body, 0)

    work = [functools.partial(make_down, j) for j in range(3)]
    work.append(lambda: down.begin(d_pieces))
    work.append(functools.partial(make_gate_up, 0))
    work.append(lambda: [down.cross(piece) for piece in d_pieces])
    work += [functools.partial(make_gate_up, owner) for owner in range(1, reps)]
    work.append(lambda: gate_up.begin(g_pieces))
    steps = gather.steps()
    for step in steps:
        step()
        if work:
            work.pop(0)()
    for piece in work:
        piece()
    for piece in g_pieces:
        gate_up.cross(piece)
    for piece in d_pieces:
        rows = block // DN_PIECES
        down_ref[pl.ds(piece * rows, rows), :] = down.total(piece)
    for k, piece in enumerate(g_pieces):
        total = gate_up.total(piece).astype(bf16)
        if k < count - 1:
            g_from[piece] = total
            spread.copy(k + 1).start()
        else:
            sum_ref[me] = total
    spread.finish()
    down.finish(d_pieces)
    gate_up.finish(g_pieces)
    gather.finish()
    own.wait()


def ffn_grads(reps, count, d_attn, h3, hidden, d_ffn, d_gu, d_rows, collective_id):
    dma = pltpu.SemaphoreType.DMA
    low = jnp.bfloat16
    shape = jax.ShapeDtypeStruct
    width = d_attn.shape[1]
    columns = d_gu.shape[1]
    part = hidden.shape[1]
    block = part // reps
    blocks = (count, d_rows, columns)
    lots = (DN_PIECES, block // DN_PIECES, width)
    hops = dma((2, count // 2, UNITS))
    return pl.pallas_call(
        functools.partial(ffn_grads_kernel, reps, count),
        out_shape=[
            shape((count,) + d_attn.shape, low),
            shape(blocks, low),
            shape((block, width), jnp.float32),
        ],
        in_specs=[pl.BlockSpec(memory_space=VM)] * 5,
        out_specs=[pl.BlockSpec(memory_space=HB)] + [pl.BlockSpec(memory_space=VM)] * 2,
        scratch_shapes=[
            pltpu.VMEM((reps,) + blocks, low),
            pltpu.VMEM((2,) + blocks, low),
            pltpu.VMEM(blocks, low),
            pltpu.VMEM(blocks, low),
            pltpu.VMEM((part, width), low),
            pltpu.VMEM((2,) + lots, low),
            pltpu.VMEM(lots, low),
            pltpu.VMEM(lots, low),
            hops,
            hops,
            dma((2, count)),
            dma((2, count)),
            dma((count,)),
            dma((count,)),
            dma((2, DN_PIECES)),
            dma((2, DN_PIECES)),
            dma((DN_PIECES,)),
            dma((DN_PIECES,)),
            dma((count,)),
            dma((count,)),
            dma,
        ],
        compiler_params=pltpu.CompilerParams(
            collective_id=collective_id, has_side_effects=True, vmem_limit_bytes=VMEM_LIMIT
        ),
        name="ffn_grads",
    )(d_attn, h3, hidden, d_ffn, d_gu)


def closing_kernel(
    reps, count, x_ref, tokens_ref, dmid_ref, gains_ref, gg_ref, i_part, o_part, grad_ref, sum_ref, out_ref, gain_ref,
    held, landed, total_ref, tiles, i_core, i_to, i_from, o_core, o_to, o_from,
    r_send, r_recv, ic_s, ic_r, ix_s, ix_r, oc_s, oc_r, ox_s, ox_r, s_send, s_recv, p_send, p_recv, g_send, g_recv
):
    f32, bf16 = jnp.float32, jnp.bfloat16
    ring = Ring(count)
    rep, me = ring.rep, ring.me
    hops = ring.half
    here = rep * count + me
    others = everyone(rep, me, reps, count)
    rows = grad_ref.shape[0] // UNITS
    width = grad_ref.shape[1]
    full = o_part.shape[1]
    meet(others)

    o_pieces = list(range(full))
    i_pieces = [(me + k) % count for k in range(1, count)] + [me]
    ins = RepSum(lambda owner, piece: i_part.at[owner, piece], i_core, i_to, i_from, (ic_s, ic_r, ix_s, ix_r), rep, me)
    outs = RepSum(lambda owner, piece: o_part.at[owner, piece], o_core, o_to, o_from, (oc_s, oc_r, ox_s, ox_r), rep, me)
    spread = Spread(i_from, sum_ref, s_send, s_recv, rep, me, count)

    def o_owner(piece):
        where = me * full + piece
        return where // count, where % count

    def o_copy(piece):
        return remote(o_from.at[piece], out_ref.at[rep], p_send.at[piece], p_recv.at[rep], o_owner(piece))

    def o_self(piece):
        return me * full + piece == here

    def o_finish(piece):
        total = outs.total(piece).astype(bf16)
        o_from[piece] = total

        @pl.when(jnp.logical_not(o_self(piece)))
        def _():
            o_copy(piece).start()

        @pl.when(o_self(piece))
        def _():
            pltpu.make_async_copy(o_from.at[piece], out_ref.at[rep], p_recv.at[rep]).start()

    def i_finish(k):
        piece = i_pieces[k]
        total = ins.total(piece).astype(bf16)
        if k < count - 1:
            i_from[piece] = total
            spread.copy(k + 1).start()
        else:
            sum_ref[me] = total

    work = [functools.partial(ins.cross, piece) for piece in i_pieces]
    work += [functools.partial(outs.cross, piece) for piece in o_pieces]
    work += [functools.partial(i_finish, k) for k in range(count)]
    work += [functools.partial(o_finish, piece) for piece in o_pieces]

    started = []

    def part(unit):
        return pl.ds(unit * rows, rows)

    def step_copy(way, step, unit):
        return remote(
            held.at[way, step, part(unit)],
            landed.at[way, step, part(unit)],
            r_send.at[way, step, unit],
            r_recv.at[way, step, unit],
            ring.next[way],
        )

    for step in range(hops):
        order = ring.units(0, hops - step), ring.units(1, hops - step)
        before = [ring.units(way, hops - step + 1) if step else [] for way in (0, 1)]
        for index in range(len(order[0])):
            for way in (0, 1):
                unit = order[way][index]
                block = x_ref[ring.away(way, hops - step), part(unit), :].astype(f32)
                if unit in before[way]:
                    step_copy(way, step - 1, unit).wait_recv()
                    block += landed[way, step - 1, part(unit), :].astype(f32)
                held[way, step, part(unit), :] = block.astype(held.dtype)
                copy = step_copy(way, step, unit)
                copy.start()
                started.append(copy)
            if step == 0 and index == 0:
                ins.begin(i_pieces)
                outs.begin(o_pieces)
            elif step and work:
                work.pop(0)()
                if work:
                    work.pop(0)()
    gg = jnp.zeros((1, width), f32)
    gain = 1.0 + gains_ref[0:1, :]
    for unit in range(UNITS):
        span = part(unit)
        total = x_ref[me, span, :].astype(f32)
        for way in (0, 1):
            step_copy(way, hops - 1, unit).wait_recv()
            total += landed[way, hops - 1, span, :].astype(f32)
        value = tokens_ref[span, :].astype(f32)
        scale = lax.rsqrt(jnp.mean(value * value, axis=-1, keepdims=True) + 1e-06)
        normed = value * scale
        weighted = total * gain
        inner = jnp.mean(weighted * normed, axis=-1, keepdims=True)
        grad_ref[span, :] = dmid_ref[span, :] + scale * (weighted - normed * inner)
        gg += jnp.sum(total * normed, axis=0, keepdims=True)
    d_rows = sum_ref.shape[1]
    total_ref[...] = gg_ref[...]
    total_ref[0:1, :] = gg
    every = total_ref[...]
    for owner in range(reps * count):
        tiles[owner, :, 0:d_rows] = every[:, owner * d_rows : (owner + 1) * d_rows]
    for k, device in enumerate(others):
        to = (here + k + 1) % (reps * count)
        remote(tiles.at[to], gain_ref.at[here], g_send.at[k], g_recv.at[k], device).start()
    gain_ref[here] = tiles[here]
    for piece in work:
        piece()
    for k in range(len(others)):
        frm = (here + len(others) - k) % (reps * count)
        remote(tiles.at[frm], gain_ref.at[frm], g_send.at[k], g_recv.at[k], others[k]).wait_recv()
    for j in range(reps):
        remote(
            o_from.at[0], out_ref.at[j], p_send.at[0], p_recv.at[j], (rep, (me + 1) % count)
        ).wait_recv()
    for piece in o_pieces:
        @pl.when(jnp.logical_not(o_self(piece)))
        def _():
            o_copy(piece).wait_send()
    spread.finish()
    ins.finish(i_pieces)
    outs.finish(o_pieces)
    for k, device in enumerate(others):
        to = (here + k + 1) % (reps * count)
        remote(tiles.at[to], gain_ref.at[here], g_send.at[k], g_recv.at[k], device).wait_send()
    for copy in started:
        copy.wait_send()


def closing(reps, count, partial, tokens, d_middle, gain_rows, gain_terms, part_in, part_out, collective_id):
    dma = pltpu.SemaphoreType.DMA
    low, f32 = jnp.bfloat16, jnp.float32
    shape = jax.ShapeDtypeStruct
    rows, width = tokens.shape
    total = reps * count
    half = count // 2
    i_block = part_in.shape[1:]
    o_block = part_out.shape[1:]
    full = o_block[0]
    hops = dma((2, half, UNITS))
    return pl.pallas_call(
        functools.partial(closing_kernel, reps, count),
        out_shape=[
            shape((rows, width), f32),
            shape(i_block, low),
            shape((reps,) + o_block[1:], low),
            shape((total, 8, 128), f32),
        ],
        in_specs=[pl.BlockSpec(memory_space=VM)] * 7,
        out_specs=[pl.BlockSpec(memory_space=VM)] * 4,
        scratch_shapes=[
            pltpu.VMEM((2, half, rows, width), low),
            pltpu.VMEM((2, half, rows, width), low),
            pltpu.VMEM((8, width), f32),
            pltpu.VMEM((total, 8, 128), f32),
            pltpu.VMEM((2,) + i_block, low),
            pltpu.VMEM(i_block, low),
            pltpu.VMEM(i_block, low),
            pltpu.VMEM((2,) + o_block, low),
            pltpu.VMEM(o_block, low),
            pltpu.VMEM(o_block, low),
            hops,
            hops,
            dma((2, count)),
            dma((2, count)),
            dma((count,)),
            dma((count,)),
            dma((2, full)),
            dma((2, full)),
            dma((full,)),
            dma((full,)),
            dma((count,)),
            dma((count,)),
            dma((full,)),
            dma((reps,)),
            dma((total - 1,)),
            dma((total - 1,)),
        ],
        compiler_params=pltpu.CompilerParams(
            collective_id=collective_id, has_side_effects=True, vmem_limit_bytes=VMEM_LIMIT
        ),
        name="closing",
    )(partial.reshape(count, rows, width), tokens, d_middle, gain_rows, gain_terms, part_in, part_out)


def small_kernel(reps, count, spread, x_ref, out_ref, send, recv):
    rep = lax.axis_index("rep")
    me = lax.axis_index("shard")
    here = rep * count + me
    total = reps * count
    others = everyone(rep, me, reps, count)
    meet(others)
    copies = []
    for k, device in enumerate(others):
        to = (here + k + 1) % total
        src = x_ref.at[to] if spread else x_ref
        copy = remote(src, out_ref.at[here], send.at[k], recv.at[k], device)
        copy.start()
        copies.append(copy)
    out_ref[here] = x_ref[here] if spread else x_ref[...]
    for k in range(total - 1):
        frm = (here + total - k - 1) % total
        remote(out_ref.at[frm], out_ref.at[frm], send.at[k], recv.at[k], others[k]).wait_recv()
    for copy in copies:
        copy.wait_send()


def small_exchange(tiles, reps, count, spread, collective_id):
    total = reps * count
    return pl.pallas_call(
        functools.partial(small_kernel, reps, count, spread),
        out_shape=jax.ShapeDtypeStruct((total,) + tiles.shape[-2:], tiles.dtype),
        in_specs=[pl.BlockSpec(memory_space=VM)],
        out_specs=pl.BlockSpec(memory_space=VM),
        scratch_shapes=[pltpu.SemaphoreType.DMA((total - 1,)), pltpu.SemaphoreType.DMA((total - 1,))],
        compiler_params=pltpu.CompilerParams(
            collective_id=collective_id, has_side_effects=True, vmem_limit_bytes=VMEM_LIMIT
        ),
        name=f"small_exchange_{collective_id}",
    )(tiles)


def as_tile(flat):
    width = flat.shape[-1]
    filled = -(-width // 1024) * 1024
    padded = jnp.pad(flat, [(0, 0)] * (flat.ndim - 1) + [(0, filled - width)])
    return padded.reshape(flat.shape[:-1] + (filled // 128, 128))


def turn(flat, cosine, sine):
    half = flat.shape[1] // 2
    first, second = flat[:, :half], flat[:, half:]
    return jnp.concatenate([first * cosine - second * sine, second * cosine + first * sine], axis=1)


def norm_back(value, gain_col, grad):
    scale = lax.rsqrt(jnp.mean(value * value, axis=-1, keepdims=True) + 1e-06)
    normed = value * scale
    weighted = grad * (1.0 + gain_col)
    inner = jnp.mean(weighted * normed, axis=-1, keepdims=True)
    return scale * (weighted - normed * inner), jnp.sum(grad * normed, axis=0)


def dot_tn(left, right):
    return lax.dot_general(left, right, (((0,), (0,)), ((), ())), preferred_element_type=jnp.float32)


def split_device(
    tokens, cotangent, piece_starts, inproj, outproj, ffn_gate, ffn_up, ffn_down, norm_gains,
    mean_inproj, mean_outproj, mean_gate, mean_up, mean_down, mean_gains,
    square_inproj, square_outproj, square_gate, square_up, square_down, square_gains,
):
    bf16, f32 = jnp.bfloat16, jnp.float32
    reps, count = lax.axis_size("rep"), lax.axis_size("shard")
    rep = lax.axis_index("rep")
    me = lax.axis_index("shard")
    total = reps * count
    rows, width = tokens.shape
    seq_len = rows * count
    group = HEADS // KV_HEADS
    q_width, k_width = HEADS * HEAD_DIM, KV_HEADS * HEAD_DIM
    d_rows = inproj.shape[0]
    ff = ffn_gate.shape[1]
    ff_block = ff // total
    ff_part = ff // count
    o_rows = outproj.shape[0]
    per_head = HEAD_DIM // o_rows
    piece = o_rows // reps

    cut_in, cut_gu = cut_weights(reps, count, inproj, ffn_gate, ffn_up)
    cut_out = outproj.astype(bf16).reshape(reps, piece, width)
    gain_tile = as_tile(norm_gains.astype(bf16).astype(f32).reshape(-1))
    all_tokens, gain_tiles, got_in, got_gu, got_down, got_out = opening(
        reps, count, tokens, gain_tile, cut_in, cut_gu, ffn_down.astype(bf16), cut_out, 1
    )
    all_tokens = all_tokens.reshape(seq_len, width)
    w_in = got_in.reshape(width, -1)
    w_gu = got_gu.reshape(width, 2 * ff_part)
    w_down = got_down.reshape(ff_part, width)
    w_out = got_out.transpose(1, 0, 2, 3).reshape(HEAD_DIM, width)
    gains = gain_tiles.reshape(total, -1)[:, : d_rows * 4].reshape(width, 4)
    gain_rows = gains.T

    normed_in = rms_norm(all_tokens.astype(f32), gains[:, 0]).astype(bf16)
    projected = jnp.dot(normed_in, w_in, preferred_element_type=f32)
    half = HEAD_DIM // 2
    position = jnp.arange(seq_len, dtype=jnp.int32)
    freq = 10000.0 ** (-(jnp.arange(half, dtype=f32) * 2.0 / HEAD_DIM))
    angle = position.astype(f32)[:, None] * freq[None, :]
    cosine, sine = jnp.cos(angle), jnp.sin(angle)
    query_scale = HEAD_DIM ** (-0.5)
    queries = (turn(projected[:, :HEAD_DIM], cosine, sine) * query_scale).astype(bf16)
    keys = turn(projected[:, HEAD_DIM : 2 * HEAD_DIM], cosine, sine).astype(bf16)
    values = projected[:, 2 * HEAD_DIM :].astype(bf16)
    starts = lax.dynamic_slice_in_dim(piece_starts, rep, 1, 0)[0]
    inside = (position[:, None] >= starts[None, :]) & (position[:, None] < starts[None, :] + PIC)
    tag = jnp.sum(inside.astype(jnp.int32) * (jnp.arange(starts.shape[0], dtype=jnp.int32)[None, :] + 1), axis=1)
    visible = (position[None, :] <= position[:, None]) | ((tag[:, None] == tag[None, :]) & (tag[:, None] > 0))
    raw = lax.dot_general(queries, keys, (((1,), (1,)), ((), ())), preferred_element_type=f32)
    bent = jnp.tanh(raw / 50.0)
    masked = jnp.where(visible, 50.0 * bent, -1e30)
    top_score = jnp.max(masked, axis=-1, keepdims=True)
    expo = jnp.exp(masked - top_score)
    probs = expo / jnp.sum(expo, axis=-1, keepdims=True)
    probs_low = probs.astype(bf16)
    attended = jnp.dot(probs_low, values, preferred_element_type=f32).astype(bf16)
    attn_proj = ring_reduce(jnp.dot(attended, w_out, preferred_element_type=f32).astype(bf16), count, 4)

    layer_out, d_middle, d_attn, gain_terms, normed_mid, hidden, d_ffn, d_gu = feed_forward(
        attn_proj, tokens, cotangent, gain_rows, w_gu, w_down, count, 5
    )
    d_attn, sum_gu, grad_down = ffn_grads(
        reps, count, d_attn, normed_mid, hidden, d_ffn, d_gu, d_rows, 9
    )
    d_attn = d_attn.reshape(seq_len, width)
    grad_gate, grad_up = join_grads(reps, count, sum_gu)
    d_attended = back_dot(d_attn, w_out).astype(bf16)
    d_probs = back_dot(d_attended, values)
    d_values = dot_tn(probs_low, d_attended)
    d_scores = (
        probs * (d_probs - jnp.sum(probs * d_probs, axis=-1, keepdims=True)) * (1.0 - bent * bent)
    ).astype(bf16)
    d_queries = jnp.dot(d_scores, keys, preferred_element_type=f32)
    d_keys = dot_tn(d_scores, queries)
    d_projected = jnp.concatenate(
        [turn(d_queries, cosine, -sine) * query_scale, turn(d_keys, cosine, -sine), d_values], axis=1
    ).astype(bf16)
    part_in = dot_tn(normed_in, d_projected).astype(bf16).reshape(reps, count, d_rows, 3 * HEAD_DIM)
    part_out = (
        dot_tn(attended, d_attn).astype(bf16).reshape(per_head, reps, piece, width).transpose(1, 0, 2, 3)
    )
    input_grad, sum_in, sum_out, gain_tiles = closing(
        reps, count, back_dot(d_projected, w_in).astype(bf16), tokens, d_middle, gain_rows, gain_terms,
        part_in, part_out, 12,
    )
    sum_in = sum_in.astype(f32)
    grad_q = sum_in[:, :, :HEAD_DIM].transpose(1, 0, 2).reshape(d_rows, q_width)

    def join_kv(parts):
        return parts.reshape(KV_HEADS, group, d_rows, HEAD_DIM).sum(axis=1).transpose(1, 0, 2).reshape(d_rows, k_width)

    grad_inproj = jnp.concatenate(
        [grad_q, join_kv(sum_in[:, :, HEAD_DIM : 2 * HEAD_DIM]), join_kv(sum_in[:, :, 2 * HEAD_DIM :])], axis=1
    )
    grad_outproj = sum_out.reshape(o_rows, width).astype(f32)
    grad_gains = jnp.sum(gain_tiles, axis=0)[:4, :d_rows].T

    masters = (inproj, outproj, ffn_gate, ffn_up, ffn_down, norm_gains)
    gradients = (grad_inproj, grad_outproj, grad_gate, grad_up, grad_down, grad_gains)
    firsts = (mean_inproj, mean_outproj, mean_gate, mean_up, mean_down, mean_gains)
    seconds = (square_inproj, square_outproj, square_gate, square_up, square_down, square_gains)
    results = [lamb_local(*item) for item in zip(masters, gradients, firsts, seconds)]
    sums = jnp.stack(
        [jnp.sum(master * master) for master in masters] + [jnp.sum(item[2] * item[2]) for item in results]
    )
    totals = jnp.sum(small_exchange(as_tile(sums), reps, count, False, 14), axis=0)
    totals = totals.reshape(-1)[:12].reshape(2, 6)
    counts = jnp.array([float(master.size * total) for master in masters], f32)
    norm_table = jnp.sqrt(totals / counts[None, :] + 1e-06)
    fresh = [
        masters[index] - 0.3 * norm_table[0, index] / norm_table[1, index] * results[index][2]
        for index in range(6)
    ]
    return (
        layer_out,
        input_grad,
        *gradients,
        *[item[0] for item in results],
        *[item[1] for item in results],
        *fresh,
        norm_table,
    )


def fits(mesh, shapes):
    reps, count = mesh.shape["rep"], mesh.shape["shard"]
    total = reps * count
    tokens, piece_starts, outproj, ffn_gate = shapes
    o_rows = outproj[0] // total
    return (
        reps == 4
        and count == HEADS
        and piece_starts[0] == reps
        and tokens[0] % (total * UNITS * 16) == 0
        and HEAD_DIM % o_rows == 0
        and o_rows % (16 * reps) == 0
        and HEAD_DIM // o_rows == total // HEADS
        and ffn_gate[1] % (total * 96) == 0
    )


def solution(mesh):
    split = P(("rep", "shard"), None)

    def step(*args):
        shapes = args[0].shape, args[2].shape, args[4].shape, args[5].shape
        body = split_device if fits(mesh, shapes) else per_device
        return jax.shard_map(
            body,
            mesh=mesh,
            in_specs=(split, split, P()) + (split,) * 18,
            out_specs=(split,) * 26 + (P(),),
            check_vma=False,
        )(*args)

    return step
```

```python
import functools

import jax
import jax.numpy as jnp
from jax import lax
from jax.experimental import pallas as pl
from jax.experimental.pallas import tpu as pltpu
from jax.sharding import PartitionSpec as P

HEADS = 8
KV_HEADS = 4
HEAD_DIM = 256
PIC = 256


def rms_norm(values_in, gain_col):
    return (
        values_in
        * lax.rsqrt(jnp.mean(values_in * values_in, axis=-1, keepdims=True) + 1e-06)
        * (1.0 + gain_col)
    )


def geglu(gate_lin, up_lin):
    return jax.nn.gelu(gate_lin, approximate=True) * up_lin


def rotate(flat, position, head_count, sign):
    row_count = flat.shape[0]
    width = flat.shape[1] // head_count
    half = width // 2
    vectors = flat.reshape(row_count, head_count, width)
    freq = 10000.0 ** (-(jnp.arange(half, dtype=jnp.float32) * 2.0 / width))
    angle = position.astype(jnp.float32)[:, None] * freq[None, :]
    cosine = jnp.cos(angle)[:, None, :]
    sine = sign * jnp.sin(angle)[:, None, :]
    first = vectors[..., :half]
    second = vectors[..., half:]
    turned = jnp.concatenate(
        [first * cosine - second * sine, second * cosine + first * sine], axis=-1
    )
    return turned.reshape(row_count, head_count * width)


def owned_rows(activation, gradient, rep_index, width):
    piece = lax.dynamic_slice_in_dim(activation, rep_index * width, width, 1)
    return lax.dot_general(
        piece, gradient, (((0,), (0,)), ((), ())), preferred_element_type=jnp.float32
    )


def back_dot(gradient, weight):
    return lax.dot_general(
        gradient, weight, (((1,), (1,)), ((), ())), preferred_element_type=jnp.float32
    )


def describe(rows, piece_starts, seq_offset, seq_len):
    local_seq = rows // seq_len
    position = rows % seq_len
    global_seq = local_seq + seq_offset
    seq_total = piece_starts.shape[0]
    piece_count = piece_starts.shape[1]
    select = (global_seq[:, None] == jnp.arange(seq_total, dtype=jnp.int32)[None, :]).astype(
        jnp.int32
    )
    starts = jnp.sum(select[:, :, None] * piece_starts[None, :, :], axis=1)
    inside = ((position[:, None] >= starts) & (position[:, None] < starts + PIC)).astype(jnp.int32)
    labels = (
        global_seq[:, None] * piece_count + jnp.arange(piece_count, dtype=jnp.int32)[None, :] + 1
    )
    return (local_seq, position, jnp.sum(inside * labels, axis=1))


def visibility(piece_starts, query_rows, key_rows, seq_offset, seq_len):
    seq_q, pos_q, tag_q = describe(query_rows, piece_starts, seq_offset, seq_len)
    seq_k, pos_k, tag_k = describe(key_rows, piece_starts, seq_offset, seq_len)
    causal = pos_k[None, :] <= pos_q[:, None]
    same_piece = (tag_q[:, None] == tag_k[None, :]) & (tag_q[:, None] > 0)
    return (seq_q[:, None] == seq_k[None, :]) & (causal | same_piece)


def lamb_local(master, gradient, first, second):
    newmean = 0.5 * first + 0.5 * gradient
    newsquare = 0.5 * second + 0.5 * gradient * gradient
    step_dir = newmean / (jnp.sqrt(newsquare) + 1e-06) + 0.01 * master
    return (newmean, newsquare, step_dir)


def per_device(
    tokens,
    cotangent,
    piece_starts,
    inproj,
    outproj,
    ffn_gate,
    ffn_up,
    ffn_down,
    norm_gains,
    mean_inproj,
    mean_outproj,
    mean_gate,
    mean_up,
    mean_down,
    mean_gains,
    square_inproj,
    square_outproj,
    square_gate,
    square_up,
    square_down,
    square_gains,
):
    bf16 = jnp.bfloat16
    f32 = jnp.float32
    rep_count = lax.axis_size("rep")
    shard_count = lax.axis_size("shard")
    rep_index = lax.axis_index("rep")
    w_in, w_out, w_gate, w_up, w_down, gain_copy = (
        lax.all_gather(inproj.astype(bf16), ("rep", "shard"), axis=0, tiled=True),
        lax.all_gather(outproj.astype(bf16), ("rep", "shard"), axis=0, tiled=True),
        lax.all_gather(ffn_gate.astype(bf16), ("rep", "shard"), axis=0, tiled=True),
        lax.all_gather(ffn_up.astype(bf16), ("rep", "shard"), axis=0, tiled=True),
        lax.all_gather(ffn_down.astype(bf16), ("rep", "shard"), axis=0, tiled=True),
        lax.all_gather(norm_gains.astype(bf16), ("rep", "shard"), axis=0, tiled=True),
    )
    gains_used = gain_copy.astype(f32)
    residual = tokens.astype(f32)
    row_count = residual.shape[0]
    seq_len = row_count * shard_count
    q_width = HEADS * HEAD_DIM
    k_width = KV_HEADS * HEAD_DIM
    group_size = HEADS // KV_HEADS
    query_scale = HEAD_DIM ** (-0.5)
    local_rows = lax.axis_index("shard") * row_count + jnp.arange(row_count, dtype=jnp.int32)
    position = local_rows % seq_len
    normed_in = rms_norm(residual, gains_used[:, 0]).astype(bf16)
    projected = jnp.dot(normed_in, w_in, preferred_element_type=f32)
    queries = (rotate(projected[:, :q_width], position, HEADS, 1.0) * query_scale).astype(bf16)
    keys = rotate(projected[:, q_width : q_width + k_width], position, KV_HEADS, 1.0).astype(bf16)
    values = projected[:, q_width + k_width :].astype(bf16)
    all_keys, all_values = (
        lax.all_gather(keys, "shard", axis=0, tiled=True),
        lax.all_gather(values, "shard", axis=0, tiled=True),
    )
    key_rows = all_keys.shape[0]
    visible = visibility(
        piece_starts,
        local_rows,
        jnp.arange(key_rows, dtype=jnp.int32),
        rep_index * (key_rows // seq_len),
        seq_len,
    )
    query_heads = queries.reshape(row_count, KV_HEADS, group_size, HEAD_DIM)
    key_heads = all_keys.reshape(key_rows, KV_HEADS, HEAD_DIM)
    value_heads = all_values.reshape(key_rows, KV_HEADS, HEAD_DIM)

    def capped_scores():
        raw_scores = jnp.einsum(
            "tgrd,kgd->grtk", query_heads, key_heads, preferred_element_type=f32
        )
        bent_scores = jnp.tanh(raw_scores / 50.0)
        return (bent_scores, jnp.where(visible, 50.0 * bent_scores, -1e30))

    bent_scores, masked = capped_scores()
    top_score = jnp.max(masked, axis=-1, keepdims=True)
    log_total = top_score + jnp.log(jnp.sum(jnp.exp(masked - top_score), axis=-1, keepdims=True))
    probs_low = jnp.exp(masked - log_total).astype(bf16)
    attended = (
        jnp.einsum("grtk,kgd->tgrd", probs_low, value_heads, preferred_element_type=f32)
        .reshape(row_count, q_width)
        .astype(bf16)
    )
    attn_proj = jnp.dot(attended, w_out, preferred_element_type=f32)
    middle = residual + rms_norm(attn_proj, gains_used[:, 1])
    normed_mid = rms_norm(middle, gains_used[:, 2]).astype(bf16)
    gate_lin = jnp.dot(normed_mid, w_gate, preferred_element_type=f32)
    up_lin = jnp.dot(normed_mid, w_up, preferred_element_type=f32)
    hidden = geglu(gate_lin, up_lin).astype(bf16)
    ffn_proj = jnp.dot(hidden, w_down, preferred_element_type=f32)
    layer_out = (middle + rms_norm(ffn_proj, gains_used[:, 3])).astype(bf16)
    d_out = cotangent.astype(f32)
    _, post_back = jax.vjp(rms_norm, ffn_proj, gains_used[:, 3])
    d_ffn, d_gain3 = post_back(d_out)
    d_ffn_low = d_ffn.astype(bf16)
    hidden_all, d_ffn_all = (
        lax.all_gather(hidden, "rep", axis=0, tiled=True),
        lax.all_gather(d_ffn_low, "rep", axis=0, tiled=True),
    )
    part_down = owned_rows(hidden_all, d_ffn_all, rep_index, hidden.shape[1] // rep_count)
    d_hidden = back_dot(d_ffn_low, w_down)
    _, glu_back = jax.vjp(geglu, gate_lin, up_lin)
    d_gate, d_up = glu_back(d_hidden)
    d_gate_low = d_gate.astype(bf16)
    d_up_low = d_up.astype(bf16)
    gate_up_grad = jnp.concatenate([d_gate_low, d_up_low], axis=1)
    mid_all, gate_up_all = (
        lax.all_gather(normed_mid, "rep", axis=0, tiled=True),
        lax.all_gather(gate_up_grad, "rep", axis=0, tiled=True),
    )
    part_gate_up = owned_rows(mid_all, gate_up_all, rep_index, normed_mid.shape[1] // rep_count)
    d_mid_in = back_dot(d_gate_low, w_gate) + back_dot(d_up_low, w_up)
    _, pre_back = jax.vjp(rms_norm, middle, gains_used[:, 2])
    d_mid_part, d_gain2 = pre_back(d_mid_in)
    d_middle = d_out + d_mid_part
    _, attn_back = jax.vjp(rms_norm, attn_proj, gains_used[:, 1])
    d_attn, d_gain1 = attn_back(d_middle)
    d_attn_low = d_attn.astype(bf16)
    d_attended = back_dot(d_attn_low, w_out).astype(bf16)
    d_heads = d_attended.reshape(row_count, KV_HEADS, group_size, HEAD_DIM)
    bent_again, masked_again = capped_scores()
    attn_probs = jnp.exp(masked_again - log_total)
    probs_again = attn_probs.astype(bf16)
    d_probs = jnp.einsum("tgrd,kgd->grtk", d_heads, value_heads, preferred_element_type=f32)
    d_scores = (
        attn_probs
        * (d_probs - jnp.sum(attn_probs * d_probs, axis=-1, keepdims=True))
        * (1.0 - bent_again * bent_again)
    ).astype(bf16)
    d_queries = jnp.einsum(
        "grtk,kgd->tgrd", d_scores, key_heads, preferred_element_type=f32
    ).reshape(row_count, q_width)
    d_key = jnp.einsum("grtk,tgrd->kgd", d_scores, query_heads, preferred_element_type=f32).reshape(
        row_count * lax.axis_size("shard"), k_width
    )
    d_value = jnp.einsum(
        "grtk,tgrd->kgd", probs_again, d_heads, preferred_element_type=f32
    ).reshape(row_count * lax.axis_size("shard"), k_width)
    d_key_value = lax.psum_scatter(
        jnp.concatenate([d_key, d_value], axis=1), "shard", scatter_dimension=0, tiled=True
    )
    d_projected = jnp.concatenate(
        [
            rotate(d_queries, position, HEADS, -1.0) * query_scale,
            rotate(d_key_value[:, :k_width], position, KV_HEADS, -1.0),
            d_key_value[:, k_width:],
        ],
        axis=1,
    ).astype(bf16)
    d_normed_in = back_dot(d_projected, w_in)
    _, first_back = jax.vjp(rms_norm, residual, gains_used[:, 0])
    d_input_part, d_gain0 = first_back(d_normed_in)
    input_grad = d_middle + d_input_part
    gain_grad = jnp.stack([d_gain0, d_gain1, d_gain2, d_gain3], axis=1)
    attended_all, d_attn_all, normed_all, d_proj_all = (
        lax.all_gather(attended, "rep", axis=0, tiled=True),
        lax.all_gather(d_attn_low, "rep", axis=0, tiled=True),
        lax.all_gather(normed_in, "rep", axis=0, tiled=True),
        lax.all_gather(d_projected, "rep", axis=0, tiled=True),
    )
    part_out = owned_rows(attended_all, d_attn_all, rep_index, attended.shape[1] // rep_count)
    part_in = owned_rows(normed_all, d_proj_all, rep_index, normed_in.shape[1] // rep_count)
    part_gain = lax.psum_scatter(gain_grad, "rep", scatter_dimension=0, tiled=True)
    owned = (
        lax.psum_scatter(part_in, "shard", scatter_dimension=0, tiled=True),
        lax.psum_scatter(part_gain, "shard", scatter_dimension=0, tiled=True),
        lax.psum_scatter(part_out, "shard", scatter_dimension=0, tiled=True),
        lax.psum_scatter(part_gate_up, "shard", scatter_dimension=0, tiled=True),
        lax.psum_scatter(part_down, "shard", scatter_dimension=0, tiled=True),
    )
    grad_inproj, grad_gains, grad_outproj, grad_gate_up, grad_down = owned
    split_at = grad_gate_up.shape[1] // 2
    grad_gate = grad_gate_up[:, :split_at]
    grad_up = grad_gate_up[:, split_at:]
    masters = (inproj, outproj, ffn_gate, ffn_up, ffn_down, norm_gains)
    gradients = (grad_inproj, grad_outproj, grad_gate, grad_up, grad_down, grad_gains)
    firsts = (mean_inproj, mean_outproj, mean_gate, mean_up, mean_down, mean_gains)
    seconds = (square_inproj, square_outproj, square_gate, square_up, square_down, square_gains)
    results = [
        lamb_local(masters[index], gradients[index], firsts[index], seconds[index])
        for index in range(6)
    ]
    weight_sums = jnp.stack([jnp.sum(master * master) for master in masters])
    step_sums = jnp.stack([jnp.sum(item[2] * item[2]) for item in results])
    totals = lax.psum(jnp.stack([weight_sums, step_sums]), ("rep", "shard"))
    counts = jnp.array([float(master.size * rep_count * shard_count) for master in masters], f32)
    norm_table = jnp.sqrt(totals / counts[None, :] + 1e-06)
    fresh = [
        masters[index] - 0.3 * norm_table[0, index] / norm_table[1, index] * results[index][2]
        for index in range(6)
    ]
    return (
        layer_out,
        input_grad,
        grad_inproj,
        grad_outproj,
        grad_gate,
        grad_up,
        grad_down,
        grad_gains,
        results[0][0],
        results[1][0],
        results[2][0],
        results[3][0],
        results[4][0],
        results[5][0],
        results[0][1],
        results[1][1],
        results[2][1],
        results[3][1],
        results[4][1],
        results[5][1],
        fresh[0],
        fresh[1],
        fresh[2],
        fresh[3],
        fresh[4],
        fresh[5],
        norm_table,
    )


MESH = pl.DeviceIdType.MESH
VM = pltpu.VMEM
HB = pl.ANY
UNITS = 4
VMEM_LIMIT = 60 << 20


def ring_places(count):
    inner = 2 if count == 8 else 4
    outer = count // inner

    def place(shard):
        major = shard // inner
        minor = shard % inner
        return minor * outer + major + (minor % 2) * (outer - 1 - 2 * major)

    def shard_at(spot):
        minor = spot // outer
        major = spot % outer
        return (major + (minor % 2) * (outer - 1 - 2 * major)) * inner + minor

    return place, shard_at


def meet(devices):
    barrier = pltpu.get_barrier_semaphore()
    for device in devices:
        pl.semaphore_signal(barrier, inc=1, device_id=device, device_id_type=MESH)
    pl.semaphore_wait(barrier, len(devices))


def remote(src, dst, send_sem, recv_sem, device):
    return pltpu.make_async_remote_copy(
        src_ref=src,
        dst_ref=dst,
        send_sem=send_sem,
        recv_sem=recv_sem,
        device_id=device,
        device_id_type=MESH,
    )


class Ring:
    def __init__(self, count):
        place, shard_at = ring_places(count)
        self.count = count
        self.half = count // 2
        self.rep = lax.axis_index("rep")
        self.me = lax.axis_index("shard")
        self.spot = place(self.me)
        self.shard_at = shard_at
        self.next = [(self.rep, self.at(1)), (self.rep, self.at(count - 1))]

    def at(self, ahead):
        return self.shard_at((self.spot + ahead) % self.count)

    def away(self, way, hops):
        return self.at(hops if way == 0 else self.count - hops)

    def units(self, way, hop):
        order = list(range(UNITS)) if way == 0 else list(range(UNITS))[::-1]
        return order if hop < self.half else order[: UNITS // 2]


def reduce_on_ring(ring, rows, take, held, landed, send, recv, finish, pause):
    f32 = jnp.float32
    hops = ring.half
    started = []

    def part(unit):
        return pl.ds(unit * (rows // UNITS), rows // UNITS)

    def step_copy(way, step, unit):
        return remote(
            held.at[way, step, part(unit)],
            landed.at[way, step, part(unit)],
            send.at[way, step, unit],
            recv.at[way, step, unit],
            ring.next[way],
        )

    for step in range(hops):
        order = ring.units(0, hops - step), ring.units(1, hops - step)
        before = [ring.units(way, hops - step + 1) if step else [] for way in (0, 1)]
        for index in range(len(order[0])):
            for way in (0, 1):
                unit = order[way][index]
                block = take(ring.away(way, hops - step), part(unit)).astype(f32)
                if unit in before[way]:
                    step_copy(way, step - 1, unit).wait_recv()
                    block += landed[way, step - 1, part(unit), :].astype(f32)
                held[way, step, part(unit), :] = block.astype(held.dtype)
                copy = step_copy(way, step, unit)
                copy.start()
                started.append(copy)
            if step or index == len(order[0]) - 1:
                pause()
    for unit in range(UNITS):
        total = take(ring.me, part(unit)).astype(f32)
        for way in (0, 1):
            step_copy(way, hops - 1, unit).wait_recv()
            total += landed[way, hops - 1, part(unit), :].astype(f32)
        finish(part(unit), total)
    return started


class Flow:
    def __init__(self, ring, rows, send, recv):
        self.ring, self.rows, self.send, self.recv = ring, rows, send, recv
        self.unit_rows = rows // UNITS
        self.started = []

    def span(self, slot, unit):
        return pl.ds(slot * self.rows + unit * self.unit_rows, self.unit_rows)

    def slot(self, way, hops):
        if hops == 0:
            return 0
        return self.ring.count - 1 if hops == self.ring.half else 2 * hops - 1 + way

    def go(self, copy):
        copy.start()
        self.started.append(copy)

    def finish(self):
        for copy in self.started:
            copy.wait_send()

    def gather_copy(self, buffer, way, hop, unit):
        return remote(
            buffer.at[self.span(self.slot(way, hop - 1), unit)],
            buffer.at[self.span(self.slot(way, hop), unit)],
            self.send.at[way, hop - 1, unit],
            self.recv.at[way, hop - 1, unit],
            self.ring.next[way],
        )

    def gather(self, buffer, group_work):
        ring = self.ring
        for index in range(UNITS):
            for way in (0, 1):
                self.go(self.gather_copy(buffer, way, 1, ring.units(way, 1)[index]))
        queue = list(group_work(0, 1))
        for hop in range(1, ring.half + 1):
            length = len(ring.units(0, hop))
            for index in range(length):
                for way in (0, 1):
                    unit = ring.units(way, hop)[index]
                    self.gather_copy(buffer, way, hop, unit).wait_recv()
                    if hop < ring.half and unit in ring.units(way, hop + 1):
                        self.go(self.gather_copy(buffer, way, hop + 1, unit))
                if queue:
                    queue.pop(0)()
            for piece in queue:
                piece()
            queue = list(group_work(2 * hop - 1, 2) if hop < ring.half else group_work(ring.count - 1, 1))
        for piece in queue:
            piece()
        self.finish()

    def reduce_copy(self, first, landed, way, step, unit):
        span = pl.ds(unit * self.unit_rows, self.unit_rows)
        src = first.at[span] if step == 0 else landed.at[way, step - 1, span]
        return remote(
            src,
            landed.at[way, step, span],
            self.send.at[way, step, unit],
            self.recv.at[way, step, unit],
            self.ring.next[way],
        )

    def reduce(self, first, landed, partial, group_work, finish):
        ring = self.ring
        hops = ring.half
        f32 = jnp.float32
        for piece in group_work(ring.count - 1, 1, 0):
            piece()
        queue = list(group_work(2 * (hops - 1) - 1, 2, 1))
        for step in range(hops):
            order = ring.units(0, hops - step), ring.units(1, hops - step)
            before = [ring.units(way, hops - step + 1) if step else [] for way in (0, 1)]
            for index in range(len(order[0])):
                for way in (0, 1):
                    unit = order[way][index]
                    span = pl.ds(unit * self.unit_rows, self.unit_rows)
                    if step == 0:
                        first[span, :] = partial[0, pl.ds(unit * self.unit_rows, self.unit_rows), :].astype(first.dtype)
                    else:
                        side = 1 - way
                        block = partial[
                            step % 2, pl.ds(side * self.rows + unit * self.unit_rows, self.unit_rows), :
                        ]
                        if unit in before[way]:
                            self.reduce_copy(first, landed, way, step - 1, unit).wait_recv()
                            block = block + landed[way, step - 1, span, :].astype(f32)
                        landed[way, step - 1, span, :] = block.astype(landed.dtype)
                    self.go(self.reduce_copy(first, landed, way, step, unit))
                if queue:
                    queue.pop(0)()
            for piece in queue:
                piece()
            ahead = hops - step - 2
            queue = []
            if step < hops - 1:
                queue = list(group_work(2 * ahead - 1, 2, step % 2) if ahead > 0 else group_work(0, 1, step % 2))
        for unit in range(UNITS):
            span = pl.ds(unit * self.unit_rows, self.unit_rows)
            total = partial[hops % 2, span, :]
            for way in (0, 1):
                self.reduce_copy(first, landed, way, hops - 1, unit).wait_recv()
                total = total + landed[way, hops - 1, span, :].astype(f32)
            finish(unit, total)
        self.finish()


def looped(piece, count):
    def all_of_it():
        def body(j, carry):
            piece(j)
            return carry

        lax.fori_loop(0, count, body, 0)

    return [all_of_it]


def gelu_pair(gate):
    inner = 0.7978845608028654 * (gate + 0.044715 * gate * gate * gate)
    bend = jnp.tanh(inner)
    value = 0.5 * gate * (1.0 + bend)
    slope = 0.5 * (1.0 + bend) + 0.5 * gate * (1.0 - bend * bend) * 0.7978845608028654 * (
        1.0 + 0.134145 * gate * gate
    )
    return value, slope


def ffn_kernel(
    count, attn_ref, tokens_ref, cot_ref, gains_ref, gate_ref, up_ref, dn_ref,
    layer_ref, dmid_ref, dattn_ref, gg_ref, h3_ref, hid_ref, dffn_ref, dgu_ref,
    lin, partial, first, landed, middle, total_ref, s1, r1, s2, r2, s3, r3, s4, r4,
):
    f32, bf16 = jnp.float32, jnp.bfloat16
    ring = Ring(count)
    rows, width = attn_ref.shape
    part = hid_ref.shape[1]
    tile = part // 3
    wide = width // 3
    meet(ring.next)

    def gain(index):
        return 1.0 + gains_ref[index : index + 1, :]

    def scale_of(value):
        return lax.rsqrt(jnp.mean(value * value, axis=-1, keepdims=True) + 1e-06)

    half = rows // 2
    halves = [pl.ds(0, half), pl.ds(half, half)]
    for span in halves:
        proj = attn_ref[span, :]
        mid = tokens_ref[span, :].astype(f32) + proj * scale_of(proj) * gain(1)
        middle[span, :] = mid
        h3_ref[span, :] = (mid * scale_of(mid) * gain(2)).astype(bf16)

    def lin_work(slot, blocks):
        at = pl.ds(slot * rows, blocks * rows)

        def piece(j):
            lo = pl.ds(pl.multiple_of(j * tile, 128), tile)
            hi = pl.ds(pl.multiple_of(part + j * tile, 128), tile)
            gate = jnp.dot(h3_ref[at, :], gate_ref[:, lo], preferred_element_type=f32)
            up = jnp.dot(h3_ref[at, :], up_ref[:, lo], preferred_element_type=f32)
            value, slope = gelu_pair(gate)
            hid_ref[at, lo] = (value * up).astype(bf16)
            lin[at, lo] = (up * slope).astype(bf16)
            lin[at, hi] = value.astype(bf16)

        return looped(piece, 3)

    def down_work(slot, blocks, side):
        at = pl.ds(slot * rows, blocks * rows)

        def piece(j):
            cols = pl.ds(pl.multiple_of(j * wide, 128), wide)
            partial[side, pl.ds(0, blocks * rows), cols] = jnp.dot(
                hid_ref[at, :], dn_ref[:, cols], preferred_element_type=f32
            )

        return looped(piece, 3)

    def nt(left, right):
        return lax.dot_general(left, right, (((1,), (1,)), ((), ())), preferred_element_type=f32)

    def back_work(slot, blocks):
        at = pl.ds(slot * rows, blocks * rows)

        def piece(j):
            lo = pl.ds(pl.multiple_of(j * tile, 128), tile)
            hi = pl.ds(pl.multiple_of(part + j * tile, 128), tile)
            d_hidden = nt(dffn_ref[at, :], dn_ref[lo, :])
            dgu_ref[at, lo] = (d_hidden * lin[at, lo].astype(f32)).astype(bf16)
            dgu_ref[at, hi] = (d_hidden * lin[at, hi].astype(f32)).astype(bf16)

        return looped(piece, 3)

    def input_work(slot, blocks, side):
        at = pl.ds(slot * rows, blocks * rows)

        def piece(j):
            cols = pl.ds(pl.multiple_of(j * wide, 128), wide)
            partial[side, pl.ds(0, blocks * rows), cols] = nt(dgu_ref[at, :part], gate_ref[cols, :]) + nt(
                dgu_ref[at, part:], up_ref[cols, :]
            )

        return looped(piece, 3)

    def keep(unit, total):
        total_ref[pl.ds(unit * (rows // UNITS), rows // UNITS), :] = total

    Flow(ring, rows, s1, r1).gather(h3_ref, lin_work)
    Flow(ring, rows, s2, r2).reduce(first, landed, partial, down_work, keep)

    def back_norm(value, index, grad):
        scale = scale_of(value)
        normed = value * scale
        weighted = grad * gain(index)
        inner = jnp.mean(weighted * normed, axis=-1, keepdims=True)
        return scale * (weighted - normed * inner), jnp.sum(grad * normed, axis=0, keepdims=True)

    gg = jnp.zeros((1, width), f32)
    for span in halves:
        proj = total_ref[span, :]
        scale = scale_of(proj)
        layer_ref[span, :] = (middle[span, :] + proj * scale * gain(3)).astype(bf16)
        d_ffn, term = back_norm(proj, 3, cot_ref[span, :].astype(f32))
        gg += term
        dffn_ref[span, :] = d_ffn.astype(bf16)
    gg_ref[3:4, :] = gg

    Flow(ring, rows, s3, r3).gather(dffn_ref, back_work)
    Flow(ring, rows, s4, r4).reduce(first, landed, partial, input_work, keep)

    gg1 = jnp.zeros((1, width), f32)
    gg2 = jnp.zeros((1, width), f32)
    for span in halves:
        d_mid, term = back_norm(middle[span, :], 2, total_ref[span, :])
        gg2 += term
        d_mid = d_mid + cot_ref[span, :].astype(f32)
        dmid_ref[span, :] = d_mid
        d_attn, term = back_norm(attn_ref[span, :], 1, d_mid)
        gg1 += term
        dattn_ref[span, :] = d_attn.astype(bf16)
    gg_ref[1:2, :] = gg1
    gg_ref[2:3, :] = gg2
    gg_ref[0:1, :] = jnp.zeros((1, width), f32)
    gg_ref[4:8, :] = jnp.zeros((4, width), f32)


def feed_forward(attn_proj, tokens, cotangent, gain_rows, w_gate, w_up, w_down, count, collective_id):
    f32, bf16 = jnp.float32, jnp.bfloat16
    rows, width = attn_proj.shape
    part = w_down.shape[0]
    every = rows * count
    dma = pltpu.SemaphoreType.DMA
    shape = jax.ShapeDtypeStruct
    return pl.pallas_call(
        functools.partial(ffn_kernel, count),
        out_shape=[
            shape((rows, width), bf16),
            shape((rows, width), f32),
            shape((rows, width), bf16),
            shape((8, width), f32),
            shape((every, width), bf16),
            shape((every, part), bf16),
            shape((every, width), bf16),
            shape((every, 2 * part), bf16),
        ],
        in_specs=[pl.BlockSpec(memory_space=VM)] * 7,
        out_specs=[pl.BlockSpec(memory_space=VM)] * 8,
        scratch_shapes=[
            pltpu.VMEM((every, 2 * part), bf16),
            pltpu.VMEM((2, 2 * rows, width), f32),
            pltpu.VMEM((rows, width), bf16),
            pltpu.VMEM((2, count // 2, rows, width), bf16),
            pltpu.VMEM((rows, width), f32),
            pltpu.VMEM((rows, width), f32),
        ]
        + [dma((2, count // 2, UNITS))] * 8,
        compiler_params=pltpu.CompilerParams(
            collective_id=collective_id, has_side_effects=True, vmem_limit_bytes=VMEM_LIMIT
        ),
        name="feed_forward",
    )(attn_proj, tokens, cotangent, gain_rows, w_gate, w_up, w_down)


def attention_kernel(
    reps, count, h1_ref, in_ref, wo_ref, cos_ref, sin_ref, tagq_ref, tagk_ref, cut_ref,
    proj_ref, q_ref, k_ref, v_ref, att_ref, probs_ref, damp_ref, up_ref,
    part, held, landed, r_send, r_recv, w_sems, loc
):
    f32, bf16 = jnp.float32, jnp.bfloat16
    ring = Ring(count)
    rows = proj_ref.shape[0]
    seq_len = h1_ref.shape[0]
    tall = seq_len // 4
    half = HEAD_DIM // 2
    meet(near_devices(ring))
    weights = Fetch(ring, cut_ref, up_ref, w_sems)
    weights.begin()
    own = pltpu.make_async_copy(cut_ref.at[ring.me], up_ref.at[ring.rep, ring.me], loc)
    own.start()

    def project(i, carry):
        at = pl.ds(pl.multiple_of(i * tall, 16), tall)
        flat = jnp.dot(h1_ref[at, :], in_ref[...], preferred_element_type=f32)
        cosine, sine = cos_ref[at, :], sin_ref[at, :]

        def turned(start):
            first, second = flat[:, start : start + half], flat[:, start + half : start + HEAD_DIM]
            return jnp.concatenate([first * cosine - second * sine, second * cosine + first * sine], axis=1)

        q_ref[at, :] = (turned(0) * HEAD_DIM ** (-0.5)).astype(bf16)
        k_ref[at, :] = turned(HEAD_DIM).astype(bf16)
        v_ref[at, :] = flat[:, 2 * HEAD_DIM :].astype(bf16)
        return carry

    lax.fori_loop(0, 4, project, 0)

    def attend(i, carry):
        at = pl.ds(pl.multiple_of(i * tall, 16), tall)
        raw = lax.dot_general(q_ref[at, :], k_ref[...], (((1,), (1,)), ((), ())), preferred_element_type=f32)
        bent = jnp.tanh(raw * (1.0 / 50.0))
        query_at = i * tall + lax.broadcasted_iota(jnp.int32, (tall, seq_len), 0)
        key_at = lax.broadcasted_iota(jnp.int32, (tall, seq_len), 1)
        tag = tagq_ref[at, :]
        visible = (key_at <= query_at) | ((tag == tagk_ref[...]) & (tag > 0))
        masked = jnp.where(visible, 50.0 * bent, -1e30)
        expo = jnp.exp(masked - jnp.max(masked, axis=-1, keepdims=True))
        probs = expo / jnp.sum(expo, axis=-1, keepdims=True)
        low = probs.astype(bf16)
        probs_ref[at, :] = low
        damp_ref[at, :] = (probs * (1.0 - bent * bent)).astype(bf16)
        attended = jnp.dot(low, v_ref[...], preferred_element_type=f32).astype(bf16)
        att_ref[at, :] = attended
        part[at, :] = jnp.dot(attended, wo_ref[...], preferred_element_type=f32)
        return carry

    lax.fori_loop(0, 4, attend, 0)

    work = weights.steps()

    def pause():
        for _ in range(min(2, len(work))):
            work.pop(0)()

    def finish(span, total):
        proj_ref[span, :] = total

    def take(shard, span):
        return part[pl.ds(pl.multiple_of(shard * rows + span.start, 16), span.size), :]

    started = reduce_on_ring(ring, rows, take, held, landed, r_send, r_recv, finish, pause)
    for piece in work:
        piece()
    weights.finish()
    own.wait()
    for copy in started:
        copy.wait_send()


def attention(reps, count, normed, w_in, w_out, cosine, sine, tag, cut_up, collective_id):
    dma = pltpu.SemaphoreType.DMA
    low, f32 = jnp.bfloat16, jnp.float32
    shape = jax.ShapeDtypeStruct
    seq_len, width = normed.shape
    rows = seq_len // count
    hops = count // 2
    head = shape((seq_len, HEAD_DIM), low)
    square = shape((seq_len, seq_len), low)
    return pl.pallas_call(
        functools.partial(attention_kernel, reps, count),
        out_shape=[
            shape((rows, width), f32), head, head, head, head, square, square,
            shape((reps,) + cut_up.shape, low),
        ],
        in_specs=[pl.BlockSpec(memory_space=VM)] * 7 + [pl.BlockSpec(memory_space=HB)],
        out_specs=[pl.BlockSpec(memory_space=VM)] * 7 + [pl.BlockSpec(memory_space=HB)],
        scratch_shapes=[
            pltpu.VMEM((seq_len, width), f32),
            pltpu.VMEM((2, hops, rows, width), low),
            pltpu.VMEM((2, hops, rows, width), low),
            dma((2, hops, UNITS)),
            dma((2, hops, UNITS)),
            dma((8, count)),
            dma,
        ],
        compiler_params=pltpu.CompilerParams(
            collective_id=collective_id, has_side_effects=True, vmem_limit_bytes=VMEM_LIMIT
        ),
        name="attention",
    )(normed, w_in, w_out, cosine, sine, tag[:, None], tag[None, :], cut_up)


class Fetch:
    def __init__(self, ring, cut, out, sems):
        self.ring, self.cut, self.out = ring, cut, out
        self.rep, self.me, self.count = ring.rep, ring.me, ring.count
        self.across, self.beside = rep_partners(ring.rep)
        self.sems = sems
        self.started = []

    def go(self, copy):
        copy.start()
        self.started.append(copy)

    def spread(self, k):
        to = (self.me + k) % self.count
        return remote(
            self.cut.at[to], self.out.at[self.rep, self.me], self.sems.at[0, k], self.sems.at[1, k], (self.rep, to)
        )

    def arrived(self, k):
        frm = (self.me + self.count - k) % self.count
        return remote(
            self.cut.at[frm], self.out.at[self.rep, frm], self.sems.at[0, k], self.sems.at[1, k], (self.rep, frm)
        )

    def forward(self, k, hop):
        frm = (self.me + self.count - k) % self.count
        rep = self.across if hop == 2 else self.rep
        block = self.out.at[rep, frm] if k or hop == 2 else self.cut.at[self.me]
        to = self.across if hop == 0 else self.beside
        return remote(
            block,
            self.out.at[rep, frm],
            self.sems.at[2 + 2 * hop, k],
            self.sems.at[3 + 2 * hop, k],
            (to, self.me),
        )

    def pass_on(self, k):
        if k:
            self.arrived(k).wait_recv()
        self.go(self.forward(k, 0))
        self.go(self.forward(k, 1))

    def pass_beside(self, k):
        self.forward(k, 0).wait_recv()
        self.go(self.forward(k, 2))

    def begin(self):
        for k in range(1, self.count):
            self.go(self.spread(k))
        self.pass_on(0)

    def steps(self):
        work = [functools.partial(self.pass_on, k) for k in range(1, self.count)]
        return work + [functools.partial(self.pass_beside, k) for k in range(self.count)]

    def finish(self):
        for k in range(self.count):
            self.forward(k, 1).wait_recv()
            self.forward(k, 2).wait_recv()
        for copy in self.started:
            copy.wait_send()


def rep_partners(rep):
    return (rep + 2) % 4, rep + 1 - 2 * (rep % 2)


def everyone(rep, me, reps, count):
    here = rep * count + me
    total = reps * count
    return [
        (((here + k) % total) // count, ((here + k) % total) % count) for k in range(1, total)
    ]


def opening_kernel(
    reps, count, tok_ref, gain_ref, in_ref, gate_ref, dn_ref, ou_ref, h1_ref, gains_ref, w_in, w_gate, w_dn, w_ou,
    tok_all, gain_all, t_send, t_recv, g_send, g_recv, i_sems, u_sems, o_send, o_recv, n_send, n_recv, loc
):
    f32 = jnp.float32
    ring = Ring(count)
    rep, me = ring.rep, ring.me
    across, beside = rep_partners(rep)
    others = everyone(rep, me, reps, count)
    mine = rep * count + me
    d_rows = in_ref.shape[1]
    rows = tok_ref.shape[0]
    meet(others)
    started = []

    def go(copy):
        copy.start()
        started.append(copy)

    for k, device in enumerate(others):
        go(remote(gain_ref, gain_all.at[mine], g_send.at[k], g_recv.at[k], device))
    gain_all[mine] = gain_ref[...]
    ins = Fetch(ring, in_ref, w_in, i_sems)
    gates = Fetch(ring, gate_ref, w_gate, u_sems)
    gather = Gather(ring, tok_ref, tok_all, t_send, t_recv)
    ins.begin()
    gather.begin()

    per_head = count * reps // HEADS
    target = mine // per_head
    slot = mine % per_head

    def ou_copy(j):
        return remote(ou_ref.at[j], w_ou.at[j, slot], o_send.at[j], o_recv.at[slot], (j, target))

    def is_self(j):
        return (rep == j) & (me == target)

    for j in range(reps):
        @pl.when(jnp.logical_not(is_self(j)))
        def _():
            ou_copy(j).start()

        @pl.when(is_self(j))
        def _():
            pltpu.make_async_copy(ou_ref.at[j], w_ou.at[j, slot], o_recv.at[slot]).start()

    dn_x = remote(dn_ref, w_dn.at[rep], n_send.at[0], n_recv.at[0], (across, me))
    dn_c = remote(dn_ref, w_dn.at[rep], n_send.at[1], n_recv.at[1], (beside, me))
    dn_d = remote(w_dn.at[across], w_dn.at[across], n_send.at[2], n_recv.at[2], (beside, me))
    go(dn_x)
    go(dn_c)
    gates.begin()
    locals_ = []
    for index, (src, dst) in enumerate(
        ((in_ref.at[me], w_in.at[rep, me]), (gate_ref.at[me], w_gate.at[rep, me]), (dn_ref, w_dn.at[rep]))
    ):
        copy = pltpu.make_async_copy(src, dst, loc.at[index])
        copy.start()
        locals_.append(copy)

    for k in range(len(others)):
        frm = (mine + len(others) - k) % (reps * count)
        remote(gain_ref, gain_all.at[frm], g_send.at[k], g_recv.at[k], others[k]).wait_recv()
    gains_ref[...] = jnp.concatenate([gain_all[device, :, 0:d_rows] for device in range(reps * count)], axis=1)
    gain = 1.0 + gains_ref[0:1, :]

    def norm(value):
        value = value.astype(f32)
        return (value * lax.rsqrt(jnp.mean(value * value, axis=-1, keepdims=True) + 1e-06) * gain).astype(h1_ref.dtype)

    def norm_block(shard):
        for unit in range(UNITS):
            span = pl.ds(unit * (rows // UNITS), rows // UNITS)
            h1_ref[shard, span, :] = norm(tok_all[shard, span, :])

    for unit in range(UNITS):
        span = pl.ds(unit * (rows // UNITS), rows // UNITS)
        h1_ref[me, span, :] = norm(tok_ref[span, :])

    hops = gather.steps()

    def take_hop(hop):
        for _ in range(len(ring.units(0, hop))):
            hops.pop(0)()
        for way in (0, 1) if hop < ring.half else (0,):
            norm_block(ring.away(1 - way, hop))

    for k in range(1, count):
        ins.pass_on(k)
    take_hop(1)
    for k in range(count):
        ins.pass_beside(k)
    take_hop(2)
    for i in range(per_head):
        remote(
            ou_ref.at[0], w_ou.at[rep, i], o_send.at[0], o_recv.at[i], (across, me)
        ).wait_recv()
    ou_x = remote(w_ou.at[rep], w_ou.at[rep], n_send.at[3], n_recv.at[3], (across, me))
    ou_c = remote(w_ou.at[rep], w_ou.at[rep], n_send.at[4], n_recv.at[4], (beside, me))
    ou_d = remote(w_ou.at[across], w_ou.at[across], n_send.at[5], n_recv.at[5], (beside, me))
    go(ou_x)
    go(ou_c)
    dn_x.wait_recv()
    go(dn_d)
    for k in range(1, count // 2):
        gates.pass_on(k)
    take_hop(3)
    for k in range(count // 2, count):
        gates.pass_on(k)
    for hop in range(4, ring.half + 1):
        take_hop(hop)
    ou_x.wait_recv()
    go(ou_d)
    for k in range(count):
        gates.pass_beside(k)
    ins.finish()
    gates.finish()
    for copy in (dn_c, dn_d, ou_c, ou_d):
        copy.wait_recv()
    for copy in started:
        copy.wait_send()
    gather.finish()
    for j in range(reps):
        @pl.when(jnp.logical_not(is_self(j)))
        def _():
            ou_copy(j).wait_send()
    for copy in locals_:
        copy.wait()


def opening(reps, count, tokens, gain_tile, w_in, w_gate, w_dn, w_ou, collective_id):
    dma = pltpu.SemaphoreType.DMA
    per_head = count * reps // HEADS
    total = reps * count
    low = jnp.bfloat16
    shape = jax.ShapeDtypeStruct
    hops = dma((2, count // 2, UNITS))
    width = tokens.shape[1]
    gathered = (count,) + tokens.shape
    return pl.pallas_call(
        functools.partial(opening_kernel, reps, count),
        out_shape=[
            shape(gathered, low),
            shape((8, width), jnp.float32),
            shape((reps,) + w_in.shape, low),
            shape((reps,) + w_gate.shape, low),
            shape((reps,) + w_dn.shape, low),
            shape((reps, per_head) + w_ou.shape[1:], low),
        ],
        in_specs=[pl.BlockSpec(memory_space=VM)] * 2 + [pl.BlockSpec(memory_space=HB)] * 4,
        out_specs=[pl.BlockSpec(memory_space=VM)] * 2 + [pl.BlockSpec(memory_space=HB)] * 4,
        scratch_shapes=[
            pltpu.VMEM(gathered, low),
            pltpu.VMEM((total,) + gain_tile.shape, jnp.float32),
            hops,
            hops,
            dma((total - 1,)),
            dma((total - 1,)),
            dma((8, count)),
            dma((8, count)),
            dma((reps,)),
            dma((per_head,)),
            dma((6,)),
            dma((6,)),
            dma((3,)),
        ],
        compiler_params=pltpu.CompilerParams(
            collective_id=collective_id, has_side_effects=True, vmem_limit_bytes=VMEM_LIMIT
        ),
        name="opening",
    )(tokens, gain_tile, w_in, w_gate, w_dn, w_ou)


def cut_kernel(reps, count, in_ref, gate_ref, up_ref, cut_in, cut_gate, cut_up):
    low = jnp.bfloat16
    group = HEADS // KV_HEADS
    block = gate_ref.shape[1] // (reps * count)
    for shard in range(count):
        for ref, cut in ((gate_ref, cut_gate), (up_ref, cut_up)):
            pieces = [ref[:, (r * count + shard) * block : (r * count + shard + 1) * block] for r in range(reps)]
            cut[shard] = jnp.concatenate(pieces, axis=1).astype(low)
        heads = shard, HEADS + shard // group, HEADS + KV_HEADS + shard // group
        for index, head in enumerate(heads):
            cut_in[shard, :, index * HEAD_DIM : (index + 1) * HEAD_DIM] = in_ref[
                :, head * HEAD_DIM : (head + 1) * HEAD_DIM
            ].astype(low)


def cut_weights(reps, count, inproj, ffn_gate, ffn_up):
    rows = inproj.shape[0]
    shape = jax.ShapeDtypeStruct
    return pl.pallas_call(
        functools.partial(cut_kernel, reps, count),
        out_shape=[
            shape((count, rows, 3 * HEAD_DIM), jnp.bfloat16),
            shape((count, rows, ffn_gate.shape[1] // count), jnp.bfloat16),
            shape((count, rows, ffn_up.shape[1] // count), jnp.bfloat16),
        ],
        in_specs=[pl.BlockSpec(memory_space=VM)] * 3,
        out_specs=[pl.BlockSpec(memory_space=VM)] * 3,
        compiler_params=pltpu.CompilerParams(vmem_limit_bytes=VMEM_LIMIT),
        name="cut_weights",
    )(inproj, ffn_gate, ffn_up)


def join_kernel(reps, count, sum_ref, gate_ref, up_ref):
    block = gate_ref.shape[1] // (reps * count)
    part = block * reps
    per = 4
    for index, ref in enumerate((gate_ref, up_ref)):
        for first in range(0, reps * count, per):
            pieces = []
            for b in range(first, first + per):
                r, shard = b // count, b % count
                start = index * part + r * block
                pieces.append(sum_ref[shard, :, start : start + block].astype(jnp.float32))
            ref[:, first * block : (first + per) * block] = jnp.concatenate(pieces, axis=1)


def join_grads(reps, count, sums):
    rows = sums.shape[1]
    shape = jax.ShapeDtypeStruct((rows, sums.shape[2] * count // 2), jnp.float32)
    return pl.pallas_call(
        functools.partial(join_kernel, reps, count),
        out_shape=[shape, shape],
        in_specs=[pl.BlockSpec(memory_space=VM)],
        out_specs=[pl.BlockSpec(memory_space=VM)] * 2,
        compiler_params=pltpu.CompilerParams(vmem_limit_bytes=VMEM_LIMIT),
        name="join_grads",
    )(sums)


class RepSum:
    def __init__(self, part, from_core, to_across, from_across, sems, rep, me):
        self.part, self.from_core = part, from_core
        self.to_across, self.from_across = to_across, from_across
        self.c_send, self.c_recv, self.x_send, self.x_recv = sems
        self.across, self.beside = rep_partners(rep)
        self.rep, self.me = rep, me
        self.core = rep % 2
        self.chip = rep // 2

    def core_copy(self, side, piece):
        chip = 1 - self.chip if side == 0 else self.chip
        return remote(
            self.part(chip * 2 + 1 - self.core, piece),
            self.from_core.at[side, piece],
            self.c_send.at[side, piece],
            self.c_recv.at[side, piece],
            (self.beside, self.me),
        )

    def cross_copy(self, piece):
        return remote(
            self.to_across.at[piece],
            self.from_across.at[piece],
            self.x_send.at[piece],
            self.x_recv.at[piece],
            (self.across, self.me),
        )

    def begin(self, pieces):
        for side in (0, 1):
            for piece in pieces:
                self.core_copy(side, piece).start()

    def cross(self, piece):
        f32 = jnp.float32
        self.core_copy(0, piece).wait_recv()
        mine = self.part((1 - self.chip) * 2 + self.core, piece)[...].astype(f32)
        self.to_across[piece] = (mine + self.from_core[0, piece].astype(f32)).astype(jnp.bfloat16)
        self.cross_copy(piece).start()

    def total(self, piece):
        f32 = jnp.float32
        self.core_copy(1, piece).wait_recv()
        mine = self.part(self.rep, piece)[...].astype(f32) + self.from_core[1, piece].astype(f32)
        self.cross_copy(piece).wait_recv()
        return mine + self.from_across[piece].astype(f32)

    def finish(self, pieces):
        for piece in pieces:
            self.core_copy(0, piece).wait_send()
            self.core_copy(1, piece).wait_send()
            self.cross_copy(piece).wait_send()


class Spread:
    def __init__(self, blocks, out, send, recv, rep, me, count):
        self.blocks, self.out, self.send, self.recv = blocks, out, send, recv
        self.rep, self.me, self.count = rep, me, count

    def copy(self, k):
        to = (self.me + k) % self.count
        return remote(
            self.blocks.at[to], self.out.at[self.me], self.send.at[k], self.recv.at[k], (self.rep, to)
        )

    def arrived(self, k):
        frm = (self.me + self.count - k) % self.count
        return remote(
            self.blocks.at[frm], self.out.at[frm], self.send.at[k], self.recv.at[k], (self.rep, frm)
        )

    def finish(self):
        for k in range(1, self.count):
            self.arrived(k).wait_recv()
        for k in range(1, self.count):
            self.copy(k).wait_send()


def near_devices(ring):
    across, beside = rep_partners(ring.rep)
    return [(ring.rep, (ring.me + k) % ring.count) for k in range(1, ring.count)] + [
        (across, ring.me),
        (beside, ring.me),
    ]


class Gather:
    def __init__(self, ring, block, out, send, recv):
        self.ring, self.block, self.out, self.send, self.recv = ring, block, out, send, recv
        self.rows = block.shape[0] // UNITS
        self.started = []

    def copy(self, way, hop, unit):
        ring = self.ring
        origin = ring.away(1 - way, hop - 1) if hop > 1 else ring.me
        span = pl.ds(unit * self.rows, self.rows)
        return remote(
            self.block.at[span] if hop == 1 else self.out.at[origin, span],
            self.out.at[origin, span],
            self.send.at[way, hop - 1, unit],
            self.recv.at[way, hop - 1, unit],
            ring.next[way],
        )

    def go(self, copy):
        copy.start()
        self.started.append(copy)

    def begin(self):
        for index in range(UNITS):
            for way in (0, 1):
                self.go(self.copy(way, 1, self.ring.units(way, 1)[index]))

    def steps(self):
        ring = self.ring

        def step(hop, index):
            for way in (0, 1):
                unit = ring.units(way, hop)[index]
                self.copy(way, hop, unit).wait_recv()
                if hop < ring.half and unit in ring.units(way, hop + 1):
                    self.go(self.copy(way, hop + 1, unit))

        return [
            functools.partial(step, hop, index)
            for hop in range(1, ring.half + 1)
            for index in range(len(ring.units(0, hop)))
        ]

    def finish(self):
        for copy in self.started:
            copy.wait_send()


def tn(left, right):
    return lax.dot_general(left, right, (((0,), (0,)), ((), ())), preferred_element_type=jnp.float32)


DN_PIECES = 3


def ffn_grads_kernel(
    reps, count, dattn_ref, h3_ref, hid_ref, dffn_ref, dgu_ref, all_ref, sum_ref, down_ref,
    g_part, g_core, g_to, g_from, d_part, d_core, d_to, d_from,
    t_send, t_recv, gc_s, gc_r, gx_s, gx_r, dc_s, dc_r, dx_s, dx_r, s_send, s_recv, loc
):
    bf16 = jnp.bfloat16
    ring = Ring(count)
    rep, me = ring.rep, ring.me
    d_rows, columns = sum_ref.shape[1:]
    part, width = d_part.shape
    block = part // reps
    wide = width // 3
    tall = part // 3
    meet(near_devices(ring))
    gather = Gather(ring, dattn_ref, all_ref, t_send, t_recv)
    gather.begin()
    own = pltpu.make_async_copy(dattn_ref, all_ref.at[me], loc)
    own.start()

    def d_at(owner, piece):
        rows = block // DN_PIECES
        return d_part.at[pl.ds(owner * block + piece * rows, rows)]

    down = RepSum(d_at, d_core, d_to, d_from, (dc_s, dc_r, dx_s, dx_r), rep, me)
    gate_up = RepSum(
        lambda owner, piece: g_part.at[owner, piece], g_core, g_to, g_from, (gc_s, gc_r, gx_s, gx_r), rep, me
    )
    spread = Spread(g_from, sum_ref, s_send, s_recv, rep, me, count)
    d_pieces = list(range(DN_PIECES))
    g_pieces = [(me + k) % count for k in range(1, count)] + [me]

    def make_down(j):
        def body(n, carry):
            cols = pl.ds(pl.multiple_of(n * wide, 128), wide)
            d_part[j * tall : (j + 1) * tall, cols] = tn(
                hid_ref[:, j * tall : (j + 1) * tall], dffn_ref[:, cols]
            ).astype(bf16)
            return carry

        lax.fori_loop(0, 3, body, 0)

    def make_gate_up(owner):
        rows = count * d_rows
        step = columns // 3

        def body(n, carry):
            cols = pl.ds(pl.multiple_of(n * step, 128), step)
            made = tn(h3_ref[:, owner * rows : (owner + 1) * rows], dgu_ref[:, cols])
            g_part[owner, :, :, cols] = made.reshape(count, d_rows, step).astype(bf16)
            return carry

        lax.fori_loop(0, 3, body, 0)

    work = [functools.partial(make_down, j) for j in range(3)]
    work.append(lambda: down.begin(d_pieces))
    work.append(functools.partial(make_gate_up, 0))
    work.append(lambda: [down.cross(piece) for piece in d_pieces])
    work += [functools.partial(make_gate_up, owner) for owner in range(1, reps)]
    work.append(lambda: gate_up.begin(g_pieces))
    steps = gather.steps()
    for step in steps:
        step()
        if work:
            work.pop(0)()
    for piece in work:
        piece()
    for piece in g_pieces:
        gate_up.cross(piece)
    for piece in d_pieces:
        rows = block // DN_PIECES
        down_ref[pl.ds(piece * rows, rows), :] = down.total(piece)
    for k, piece in enumerate(g_pieces):
        total = gate_up.total(piece).astype(bf16)
        if k < count - 1:
            g_from[piece] = total
            spread.copy(k + 1).start()
        else:
            sum_ref[me] = total
    spread.finish()
    down.finish(d_pieces)
    gate_up.finish(g_pieces)
    gather.finish()
    own.wait()


def ffn_grads(reps, count, d_attn, h3, hidden, d_ffn, d_gu, d_rows, collective_id):
    dma = pltpu.SemaphoreType.DMA
    low = jnp.bfloat16
    shape = jax.ShapeDtypeStruct
    width = d_attn.shape[1]
    columns = d_gu.shape[1]
    part = hidden.shape[1]
    block = part // reps
    blocks = (count, d_rows, columns)
    lots = (DN_PIECES, block // DN_PIECES, width)
    hops = dma((2, count // 2, UNITS))
    return pl.pallas_call(
        functools.partial(ffn_grads_kernel, reps, count),
        out_shape=[
            shape((count,) + d_attn.shape, low),
            shape(blocks, low),
            shape((block, width), jnp.float32),
        ],
        in_specs=[pl.BlockSpec(memory_space=VM)] * 5,
        out_specs=[pl.BlockSpec(memory_space=HB)] + [pl.BlockSpec(memory_space=VM)] * 2,
        scratch_shapes=[
            pltpu.VMEM((reps,) + blocks, low),
            pltpu.VMEM((2,) + blocks, low),
            pltpu.VMEM(blocks, low),
            pltpu.VMEM(blocks, low),
            pltpu.VMEM((part, width), low),
            pltpu.VMEM((2,) + lots, low),
            pltpu.VMEM(lots, low),
            pltpu.VMEM(lots, low),
            hops,
            hops,
            dma((2, count)),
            dma((2, count)),
            dma((count,)),
            dma((count,)),
            dma((2, DN_PIECES)),
            dma((2, DN_PIECES)),
            dma((DN_PIECES,)),
            dma((DN_PIECES,)),
            dma((count,)),
            dma((count,)),
            dma,
        ],
        compiler_params=pltpu.CompilerParams(
            collective_id=collective_id, has_side_effects=True, vmem_limit_bytes=VMEM_LIMIT
        ),
        name="ffn_grads",
    )(d_attn, h3, hidden, d_ffn, d_gu)


def closing_kernel(
    reps, count, x_ref, tokens_ref, dmid_ref, gains_ref, gg_ref, i_part, o_part, grad_ref, sum_ref, out_ref, gain_ref,
    held, landed, total_ref, tiles, i_core, i_to, i_from, o_core, o_to, o_from,
    r_send, r_recv, ic_s, ic_r, ix_s, ix_r, oc_s, oc_r, ox_s, ox_r, s_send, s_recv, p_send, p_recv, g_send, g_recv
):
    f32, bf16 = jnp.float32, jnp.bfloat16
    ring = Ring(count)
    rep, me = ring.rep, ring.me
    here = rep * count + me
    others = everyone(rep, me, reps, count)
    full = o_part.shape[1]
    meet(others)

    o_pieces = list(range(full))
    i_pieces = [(me + k) % count for k in range(1, count)] + [me]
    ins = RepSum(lambda owner, piece: i_part.at[owner, piece], i_core, i_to, i_from, (ic_s, ic_r, ix_s, ix_r), rep, me)
    outs = RepSum(lambda owner, piece: o_part.at[owner, piece], o_core, o_to, o_from, (oc_s, oc_r, ox_s, ox_r), rep, me)
    spread = Spread(i_from, sum_ref, s_send, s_recv, rep, me, count)

    def o_owner(piece):
        where = me * full + piece
        return where // count, where % count

    def o_copy(piece):
        return remote(o_from.at[piece], out_ref.at[rep], p_send.at[piece], p_recv.at[rep], o_owner(piece))

    def o_self(piece):
        return me * full + piece == here

    def o_finish(piece):
        total = outs.total(piece).astype(bf16)
        o_from[piece] = total

        @pl.when(jnp.logical_not(o_self(piece)))
        def _():
            o_copy(piece).start()

        @pl.when(o_self(piece))
        def _():
            pltpu.make_async_copy(o_from.at[piece], out_ref.at[rep], p_recv.at[rep]).start()

    def i_finish(k):
        piece = i_pieces[k]
        total = ins.total(piece).astype(bf16)
        if k < count - 1:
            i_from[piece] = total
            spread.copy(k + 1).start()
        else:
            sum_ref[me] = total

    work = [functools.partial(ins.cross, piece) for piece in i_pieces]
    work += [functools.partial(outs.cross, piece) for piece in o_pieces]
    work += [functools.partial(i_finish, k) for k in range(count)]
    work += [functools.partial(o_finish, piece) for piece in o_pieces]

    terms = []
    gain = 1.0 + gains_ref[0:1, :]
    opened = []

    def pause():
        if not opened:
            opened.append(True)
            ins.begin(i_pieces)
            outs.begin(o_pieces)
            return
        for _ in range(min(2, len(work))):
            work.pop(0)()

    def finish(span, total):
        value = tokens_ref[span, :].astype(f32)
        scale = lax.rsqrt(jnp.mean(value * value, axis=-1, keepdims=True) + 1e-06)
        normed = value * scale
        weighted = total * gain
        inner = jnp.mean(weighted * normed, axis=-1, keepdims=True)
        grad_ref[span, :] = dmid_ref[span, :] + scale * (weighted - normed * inner)
        terms.append(jnp.sum(total * normed, axis=0, keepdims=True))

    started = reduce_on_ring(
        ring, grad_ref.shape[0], lambda shard, span: x_ref[shard, span, :], held, landed, r_send, r_recv, finish, pause
    )
    gg = functools.reduce(jnp.add, terms)
    d_rows = sum_ref.shape[1]
    total_ref[...] = gg_ref[...]
    total_ref[0:1, :] = gg
    every = total_ref[...]
    for owner in range(reps * count):
        tiles[owner, :, 0:d_rows] = every[:, owner * d_rows : (owner + 1) * d_rows]
    for k, device in enumerate(others):
        to = (here + k + 1) % (reps * count)
        remote(tiles.at[to], gain_ref.at[here], g_send.at[k], g_recv.at[k], device).start()
    gain_ref[here] = tiles[here]
    for piece in work:
        piece()
    for k in range(len(others)):
        frm = (here + len(others) - k) % (reps * count)
        remote(tiles.at[frm], gain_ref.at[frm], g_send.at[k], g_recv.at[k], others[k]).wait_recv()
    for j in range(reps):
        remote(
            o_from.at[0], out_ref.at[j], p_send.at[0], p_recv.at[j], (rep, (me + 1) % count)
        ).wait_recv()
    for piece in o_pieces:
        @pl.when(jnp.logical_not(o_self(piece)))
        def _():
            o_copy(piece).wait_send()
    spread.finish()
    ins.finish(i_pieces)
    outs.finish(o_pieces)
    for k, device in enumerate(others):
        to = (here + k + 1) % (reps * count)
        remote(tiles.at[to], gain_ref.at[here], g_send.at[k], g_recv.at[k], device).wait_send()
    for copy in started:
        copy.wait_send()


def closing(reps, count, partial, tokens, d_middle, gain_rows, gain_terms, part_in, part_out, collective_id):
    dma = pltpu.SemaphoreType.DMA
    low, f32 = jnp.bfloat16, jnp.float32
    shape = jax.ShapeDtypeStruct
    rows, width = tokens.shape
    total = reps * count
    half = count // 2
    i_block = part_in.shape[1:]
    o_block = part_out.shape[1:]
    full = o_block[0]
    hops = dma((2, half, UNITS))
    return pl.pallas_call(
        functools.partial(closing_kernel, reps, count),
        out_shape=[
            shape((rows, width), f32),
            shape(i_block, low),
            shape((reps,) + o_block[1:], low),
            shape((total, 8, 128), f32),
        ],
        in_specs=[pl.BlockSpec(memory_space=VM)] * 7,
        out_specs=[pl.BlockSpec(memory_space=VM)] * 4,
        scratch_shapes=[
            pltpu.VMEM((2, half, rows, width), low),
            pltpu.VMEM((2, half, rows, width), low),
            pltpu.VMEM((8, width), f32),
            pltpu.VMEM((total, 8, 128), f32),
            pltpu.VMEM((2,) + i_block, low),
            pltpu.VMEM(i_block, low),
            pltpu.VMEM(i_block, low),
            pltpu.VMEM((2,) + o_block, low),
            pltpu.VMEM(o_block, low),
            pltpu.VMEM(o_block, low),
            hops,
            hops,
            dma((2, count)),
            dma((2, count)),
            dma((count,)),
            dma((count,)),
            dma((2, full)),
            dma((2, full)),
            dma((full,)),
            dma((full,)),
            dma((count,)),
            dma((count,)),
            dma((full,)),
            dma((reps,)),
            dma((total - 1,)),
            dma((total - 1,)),
        ],
        compiler_params=pltpu.CompilerParams(
            collective_id=collective_id, has_side_effects=True, vmem_limit_bytes=VMEM_LIMIT
        ),
        name="closing",
    )(partial.reshape(count, rows, width), tokens, d_middle, gain_rows, gain_terms, part_in, part_out)


def small_kernel(reps, count, spread, x_ref, out_ref, send, recv):
    rep = lax.axis_index("rep")
    me = lax.axis_index("shard")
    here = rep * count + me
    total = reps * count
    others = everyone(rep, me, reps, count)
    meet(others)
    copies = []
    for k, device in enumerate(others):
        to = (here + k + 1) % total
        src = x_ref.at[to] if spread else x_ref
        copy = remote(src, out_ref.at[here], send.at[k], recv.at[k], device)
        copy.start()
        copies.append(copy)
    out_ref[here] = x_ref[here] if spread else x_ref[...]
    for k in range(total - 1):
        frm = (here + total - k - 1) % total
        remote(out_ref.at[frm], out_ref.at[frm], send.at[k], recv.at[k], others[k]).wait_recv()
    for copy in copies:
        copy.wait_send()


def small_exchange(tiles, reps, count, spread, collective_id):
    total = reps * count
    return pl.pallas_call(
        functools.partial(small_kernel, reps, count, spread),
        out_shape=jax.ShapeDtypeStruct((total,) + tiles.shape[-2:], tiles.dtype),
        in_specs=[pl.BlockSpec(memory_space=VM)],
        out_specs=pl.BlockSpec(memory_space=VM),
        scratch_shapes=[pltpu.SemaphoreType.DMA((total - 1,)), pltpu.SemaphoreType.DMA((total - 1,))],
        compiler_params=pltpu.CompilerParams(
            collective_id=collective_id, has_side_effects=True, vmem_limit_bytes=VMEM_LIMIT
        ),
        name=f"small_exchange_{collective_id}",
    )(tiles)


def as_tile(flat):
    width = flat.shape[-1]
    filled = -(-width // 1024) * 1024
    padded = jnp.pad(flat, [(0, 0)] * (flat.ndim - 1) + [(0, filled - width)])
    return padded.reshape(flat.shape[:-1] + (filled // 128, 128))


def turn(flat, cosine, sine):
    half = flat.shape[1] // 2
    first, second = flat[:, :half], flat[:, half:]
    return jnp.concatenate([first * cosine - second * sine, second * cosine + first * sine], axis=1)


def norm_back(value, gain_col, grad):
    scale = lax.rsqrt(jnp.mean(value * value, axis=-1, keepdims=True) + 1e-06)
    normed = value * scale
    weighted = grad * (1.0 + gain_col)
    inner = jnp.mean(weighted * normed, axis=-1, keepdims=True)
    return scale * (weighted - normed * inner), jnp.sum(grad * normed, axis=0)


def dot_tn(left, right):
    return lax.dot_general(left, right, (((0,), (0,)), ((), ())), preferred_element_type=jnp.float32)


def split_device(
    tokens, cotangent, piece_starts, inproj, outproj, ffn_gate, ffn_up, ffn_down, norm_gains,
    mean_inproj, mean_outproj, mean_gate, mean_up, mean_down, mean_gains,
    square_inproj, square_outproj, square_gate, square_up, square_down, square_gains,
):
    bf16, f32 = jnp.bfloat16, jnp.float32
    reps, count = lax.axis_size("rep"), lax.axis_size("shard")
    rep = lax.axis_index("rep")
    me = lax.axis_index("shard")
    total = reps * count
    rows, width = tokens.shape
    seq_len = rows * count
    group = HEADS // KV_HEADS
    q_width, k_width = HEADS * HEAD_DIM, KV_HEADS * HEAD_DIM
    d_rows = inproj.shape[0]
    ff = ffn_gate.shape[1]
    ff_block = ff // total
    ff_part = ff // count
    o_rows = outproj.shape[0]
    per_head = HEAD_DIM // o_rows
    piece = o_rows // reps

    cut_in, cut_gate, cut_up = cut_weights(reps, count, inproj, ffn_gate, ffn_up)
    cut_out = outproj.astype(bf16).reshape(reps, piece, width)
    gain_tile = jnp.pad(norm_gains.astype(bf16).astype(f32).T, ((0, 4), (0, 128 - d_rows)))
    normed_in, gain_rows, got_in, got_gate, got_down, got_out = opening(
        reps, count, tokens, gain_tile, cut_in, cut_gate, ffn_down.astype(bf16), cut_out, 1
    )
    normed_in = normed_in.reshape(seq_len, width)
    w_in = got_in.reshape(width, -1)
    w_gate = got_gate.reshape(width, ff_part)
    w_down = got_down.reshape(ff_part, width)
    w_out = got_out.transpose(1, 0, 2, 3).reshape(HEAD_DIM, width)

    half = HEAD_DIM // 2
    position = jnp.arange(seq_len, dtype=jnp.int32)
    freq = 10000.0 ** (-(jnp.arange(half, dtype=f32) * 2.0 / HEAD_DIM))
    angle = position.astype(f32)[:, None] * freq[None, :]
    cosine, sine = jnp.cos(angle), jnp.sin(angle)
    query_scale = HEAD_DIM ** (-0.5)
    starts = lax.dynamic_slice_in_dim(piece_starts, rep, 1, 0)[0]
    inside = (position[:, None] >= starts[None, :]) & (position[:, None] < starts[None, :] + PIC)
    tag = jnp.sum(inside.astype(jnp.int32) * (jnp.arange(starts.shape[0], dtype=jnp.int32)[None, :] + 1), axis=1)
    attn_proj, queries, keys, values, attended, probs, damp, got_up = attention(
        reps, count, normed_in, w_in, w_out, cosine, sine, tag, cut_up, 4
    )
    w_up = got_up.reshape(width, ff_part)

    layer_out, d_middle, d_attn, gain_terms, normed_mid, hidden, d_ffn, d_gu = feed_forward(
        attn_proj, tokens, cotangent, gain_rows, w_gate, w_up, w_down, count, 5
    )
    d_attn, sum_gu, grad_down = ffn_grads(
        reps, count, d_attn, normed_mid, hidden, d_ffn, d_gu, d_rows, 9
    )
    d_attn = d_attn.reshape(seq_len, width)
    grad_gate, grad_up = join_grads(reps, count, sum_gu)
    d_attended = back_dot(d_attn, w_out).astype(bf16)
    d_probs = back_dot(d_attended, values)
    d_values = dot_tn(probs, d_attended)
    inner = jnp.sum(probs.astype(f32) * d_probs, axis=-1, keepdims=True)
    d_scores = (damp.astype(f32) * (d_probs - inner)).astype(bf16)
    d_queries = jnp.dot(d_scores, keys, preferred_element_type=f32)
    d_keys = dot_tn(d_scores, queries)
    d_projected = jnp.concatenate(
        [turn(d_queries, cosine, -sine) * query_scale, turn(d_keys, cosine, -sine), d_values], axis=1
    ).astype(bf16)
    part_in = dot_tn(normed_in, d_projected).astype(bf16).reshape(reps, count, d_rows, 3 * HEAD_DIM)
    part_out = (
        dot_tn(attended, d_attn).astype(bf16).reshape(per_head, reps, piece, width).transpose(1, 0, 2, 3)
    )
    input_grad, sum_in, sum_out, gain_tiles = closing(
        reps, count, back_dot(d_projected, w_in).astype(bf16), tokens, d_middle, gain_rows, gain_terms,
        part_in, part_out, 12,
    )
    sum_in = sum_in.astype(f32)
    grad_q = sum_in[:, :, :HEAD_DIM].transpose(1, 0, 2).reshape(d_rows, q_width)

    def join_kv(parts):
        return parts.reshape(KV_HEADS, group, d_rows, HEAD_DIM).sum(axis=1).transpose(1, 0, 2).reshape(d_rows, k_width)

    grad_inproj = jnp.concatenate(
        [grad_q, join_kv(sum_in[:, :, HEAD_DIM : 2 * HEAD_DIM]), join_kv(sum_in[:, :, 2 * HEAD_DIM :])], axis=1
    )
    grad_outproj = sum_out.reshape(o_rows, width).astype(f32)
    grad_gains = jnp.sum(gain_tiles, axis=0)[:4, :d_rows].T

    masters = (inproj, outproj, ffn_gate, ffn_up, ffn_down, norm_gains)
    gradients = (grad_inproj, grad_outproj, grad_gate, grad_up, grad_down, grad_gains)
    firsts = (mean_inproj, mean_outproj, mean_gate, mean_up, mean_down, mean_gains)
    seconds = (square_inproj, square_outproj, square_gate, square_up, square_down, square_gains)
    results = [lamb_local(*item) for item in zip(masters, gradients, firsts, seconds)]
    sums = jnp.stack(
        [jnp.sum(master * master) for master in masters] + [jnp.sum(item[2] * item[2]) for item in results]
    )
    totals = jnp.sum(small_exchange(as_tile(sums), reps, count, False, 14), axis=0)
    totals = totals.reshape(-1)[:12].reshape(2, 6)
    counts = jnp.array([float(master.size * total) for master in masters], f32)
    norm_table = jnp.sqrt(totals / counts[None, :] + 1e-06)
    fresh = [
        masters[index] - 0.3 * norm_table[0, index] / norm_table[1, index] * results[index][2]
        for index in range(6)
    ]
    return (
        layer_out,
        input_grad,
        *gradients,
        *[item[0] for item in results],
        *[item[1] for item in results],
        *fresh,
        norm_table,
    )


def fits(mesh, shapes):
    reps, count = mesh.shape["rep"], mesh.shape["shard"]
    total = reps * count
    tokens, piece_starts, outproj, ffn_gate = shapes
    o_rows = outproj[0] // total
    return (
        reps == 4
        and count == HEADS
        and piece_starts[0] == reps
        and tokens[0] % (total * UNITS * 16) == 0
        and HEAD_DIM % o_rows == 0
        and o_rows % (16 * reps) == 0
        and HEAD_DIM // o_rows == total // HEADS
        and ffn_gate[1] % (total * 96) == 0
    )


def solution(mesh):
    split = P(("rep", "shard"), None)

    def step(*args):
        shapes = args[0].shape, args[2].shape, args[4].shape, args[5].shape
        body = split_device if fits(mesh, shapes) else per_device
        return jax.shard_map(
            body,
            mesh=mesh,
            in_specs=(split, split, P()) + (split,) * 18,
            out_specs=(split,) * 26 + (P(),),
            check_vma=False,
        )(*args)

    return step
```

```python
import functools

import jax
import jax.numpy as jnp
from jax import lax
from jax.experimental import pallas as pl
from jax.experimental.pallas import tpu as pltpu
from jax.sharding import PartitionSpec as P

HEADS = 8
KV_HEADS = 4
HEAD_DIM = 256
PIC = 256


def rms_norm(values_in, gain_col):
    return (
        values_in
        * lax.rsqrt(jnp.mean(values_in * values_in, axis=-1, keepdims=True) + 1e-06)
        * (1.0 + gain_col)
    )


def geglu(gate_lin, up_lin):
    return jax.nn.gelu(gate_lin, approximate=True) * up_lin


def rotate(flat, position, head_count, sign):
    row_count = flat.shape[0]
    width = flat.shape[1] // head_count
    half = width // 2
    vectors = flat.reshape(row_count, head_count, width)
    freq = 10000.0 ** (-(jnp.arange(half, dtype=jnp.float32) * 2.0 / width))
    angle = position.astype(jnp.float32)[:, None] * freq[None, :]
    cosine = jnp.cos(angle)[:, None, :]
    sine = sign * jnp.sin(angle)[:, None, :]
    first = vectors[..., :half]
    second = vectors[..., half:]
    turned = jnp.concatenate(
        [first * cosine - second * sine, second * cosine + first * sine], axis=-1
    )
    return turned.reshape(row_count, head_count * width)


def owned_rows(activation, gradient, rep_index, width):
    piece = lax.dynamic_slice_in_dim(activation, rep_index * width, width, 1)
    return lax.dot_general(
        piece, gradient, (((0,), (0,)), ((), ())), preferred_element_type=jnp.float32
    )


def back_dot(gradient, weight):
    return lax.dot_general(
        gradient, weight, (((1,), (1,)), ((), ())), preferred_element_type=jnp.float32
    )


def describe(rows, piece_starts, seq_offset, seq_len):
    local_seq = rows // seq_len
    position = rows % seq_len
    global_seq = local_seq + seq_offset
    seq_total = piece_starts.shape[0]
    piece_count = piece_starts.shape[1]
    select = (global_seq[:, None] == jnp.arange(seq_total, dtype=jnp.int32)[None, :]).astype(
        jnp.int32
    )
    starts = jnp.sum(select[:, :, None] * piece_starts[None, :, :], axis=1)
    inside = ((position[:, None] >= starts) & (position[:, None] < starts + PIC)).astype(jnp.int32)
    labels = (
        global_seq[:, None] * piece_count + jnp.arange(piece_count, dtype=jnp.int32)[None, :] + 1
    )
    return (local_seq, position, jnp.sum(inside * labels, axis=1))


def visibility(piece_starts, query_rows, key_rows, seq_offset, seq_len):
    seq_q, pos_q, tag_q = describe(query_rows, piece_starts, seq_offset, seq_len)
    seq_k, pos_k, tag_k = describe(key_rows, piece_starts, seq_offset, seq_len)
    causal = pos_k[None, :] <= pos_q[:, None]
    same_piece = (tag_q[:, None] == tag_k[None, :]) & (tag_q[:, None] > 0)
    return (seq_q[:, None] == seq_k[None, :]) & (causal | same_piece)


def lamb_local(master, gradient, first, second):
    newmean = 0.5 * first + 0.5 * gradient
    newsquare = 0.5 * second + 0.5 * gradient * gradient
    step_dir = newmean / (jnp.sqrt(newsquare) + 1e-06) + 0.01 * master
    return (newmean, newsquare, step_dir)


def per_device(
    tokens,
    cotangent,
    piece_starts,
    inproj,
    outproj,
    ffn_gate,
    ffn_up,
    ffn_down,
    norm_gains,
    mean_inproj,
    mean_outproj,
    mean_gate,
    mean_up,
    mean_down,
    mean_gains,
    square_inproj,
    square_outproj,
    square_gate,
    square_up,
    square_down,
    square_gains,
):
    bf16 = jnp.bfloat16
    f32 = jnp.float32
    rep_count = lax.axis_size("rep")
    shard_count = lax.axis_size("shard")
    rep_index = lax.axis_index("rep")
    w_in, w_out, w_gate, w_up, w_down, gain_copy = (
        lax.all_gather(inproj.astype(bf16), ("rep", "shard"), axis=0, tiled=True),
        lax.all_gather(outproj.astype(bf16), ("rep", "shard"), axis=0, tiled=True),
        lax.all_gather(ffn_gate.astype(bf16), ("rep", "shard"), axis=0, tiled=True),
        lax.all_gather(ffn_up.astype(bf16), ("rep", "shard"), axis=0, tiled=True),
        lax.all_gather(ffn_down.astype(bf16), ("rep", "shard"), axis=0, tiled=True),
        lax.all_gather(norm_gains.astype(bf16), ("rep", "shard"), axis=0, tiled=True),
    )
    gains_used = gain_copy.astype(f32)
    residual = tokens.astype(f32)
    row_count = residual.shape[0]
    seq_len = row_count * shard_count
    q_width = HEADS * HEAD_DIM
    k_width = KV_HEADS * HEAD_DIM
    group_size = HEADS // KV_HEADS
    query_scale = HEAD_DIM ** (-0.5)
    local_rows = lax.axis_index("shard") * row_count + jnp.arange(row_count, dtype=jnp.int32)
    position = local_rows % seq_len
    normed_in = rms_norm(residual, gains_used[:, 0]).astype(bf16)
    projected = jnp.dot(normed_in, w_in, preferred_element_type=f32)
    queries = (rotate(projected[:, :q_width], position, HEADS, 1.0) * query_scale).astype(bf16)
    keys = rotate(projected[:, q_width : q_width + k_width], position, KV_HEADS, 1.0).astype(bf16)
    values = projected[:, q_width + k_width :].astype(bf16)
    all_keys, all_values = (
        lax.all_gather(keys, "shard", axis=0, tiled=True),
        lax.all_gather(values, "shard", axis=0, tiled=True),
    )
    key_rows = all_keys.shape[0]
    visible = visibility(
        piece_starts,
        local_rows,
        jnp.arange(key_rows, dtype=jnp.int32),
        rep_index * (key_rows // seq_len),
        seq_len,
    )
    query_heads = queries.reshape(row_count, KV_HEADS, group_size, HEAD_DIM)
    key_heads = all_keys.reshape(key_rows, KV_HEADS, HEAD_DIM)
    value_heads = all_values.reshape(key_rows, KV_HEADS, HEAD_DIM)

    def capped_scores():
        raw_scores = jnp.einsum(
            "tgrd,kgd->grtk", query_heads, key_heads, preferred_element_type=f32
        )
        bent_scores = jnp.tanh(raw_scores / 50.0)
        return (bent_scores, jnp.where(visible, 50.0 * bent_scores, -1e30))

    bent_scores, masked = capped_scores()
    top_score = jnp.max(masked, axis=-1, keepdims=True)
    log_total = top_score + jnp.log(jnp.sum(jnp.exp(masked - top_score), axis=-1, keepdims=True))
    probs_low = jnp.exp(masked - log_total).astype(bf16)
    attended = (
        jnp.einsum("grtk,kgd->tgrd", probs_low, value_heads, preferred_element_type=f32)
        .reshape(row_count, q_width)
        .astype(bf16)
    )
    attn_proj = jnp.dot(attended, w_out, preferred_element_type=f32)
    middle = residual + rms_norm(attn_proj, gains_used[:, 1])
    normed_mid = rms_norm(middle, gains_used[:, 2]).astype(bf16)
    gate_lin = jnp.dot(normed_mid, w_gate, preferred_element_type=f32)
    up_lin = jnp.dot(normed_mid, w_up, preferred_element_type=f32)
    hidden = geglu(gate_lin, up_lin).astype(bf16)
    ffn_proj = jnp.dot(hidden, w_down, preferred_element_type=f32)
    layer_out = (middle + rms_norm(ffn_proj, gains_used[:, 3])).astype(bf16)
    d_out = cotangent.astype(f32)
    _, post_back = jax.vjp(rms_norm, ffn_proj, gains_used[:, 3])
    d_ffn, d_gain3 = post_back(d_out)
    d_ffn_low = d_ffn.astype(bf16)
    hidden_all, d_ffn_all = (
        lax.all_gather(hidden, "rep", axis=0, tiled=True),
        lax.all_gather(d_ffn_low, "rep", axis=0, tiled=True),
    )
    part_down = owned_rows(hidden_all, d_ffn_all, rep_index, hidden.shape[1] // rep_count)
    d_hidden = back_dot(d_ffn_low, w_down)
    _, glu_back = jax.vjp(geglu, gate_lin, up_lin)
    d_gate, d_up = glu_back(d_hidden)
    d_gate_low = d_gate.astype(bf16)
    d_up_low = d_up.astype(bf16)
    gate_up_grad = jnp.concatenate([d_gate_low, d_up_low], axis=1)
    mid_all, gate_up_all = (
        lax.all_gather(normed_mid, "rep", axis=0, tiled=True),
        lax.all_gather(gate_up_grad, "rep", axis=0, tiled=True),
    )
    part_gate_up = owned_rows(mid_all, gate_up_all, rep_index, normed_mid.shape[1] // rep_count)
    d_mid_in = back_dot(d_gate_low, w_gate) + back_dot(d_up_low, w_up)
    _, pre_back = jax.vjp(rms_norm, middle, gains_used[:, 2])
    d_mid_part, d_gain2 = pre_back(d_mid_in)
    d_middle = d_out + d_mid_part
    _, attn_back = jax.vjp(rms_norm, attn_proj, gains_used[:, 1])
    d_attn, d_gain1 = attn_back(d_middle)
    d_attn_low = d_attn.astype(bf16)
    d_attended = back_dot(d_attn_low, w_out).astype(bf16)
    d_heads = d_attended.reshape(row_count, KV_HEADS, group_size, HEAD_DIM)
    bent_again, masked_again = capped_scores()
    attn_probs = jnp.exp(masked_again - log_total)
    probs_again = attn_probs.astype(bf16)
    d_probs = jnp.einsum("tgrd,kgd->grtk", d_heads, value_heads, preferred_element_type=f32)
    d_scores = (
        attn_probs
        * (d_probs - jnp.sum(attn_probs * d_probs, axis=-1, keepdims=True))
        * (1.0 - bent_again * bent_again)
    ).astype(bf16)
    d_queries = jnp.einsum(
        "grtk,kgd->tgrd", d_scores, key_heads, preferred_element_type=f32
    ).reshape(row_count, q_width)
    d_key = jnp.einsum("grtk,tgrd->kgd", d_scores, query_heads, preferred_element_type=f32).reshape(
        row_count * lax.axis_size("shard"), k_width
    )
    d_value = jnp.einsum(
        "grtk,tgrd->kgd", probs_again, d_heads, preferred_element_type=f32
    ).reshape(row_count * lax.axis_size("shard"), k_width)
    d_key_value = lax.psum_scatter(
        jnp.concatenate([d_key, d_value], axis=1), "shard", scatter_dimension=0, tiled=True
    )
    d_projected = jnp.concatenate(
        [
            rotate(d_queries, position, HEADS, -1.0) * query_scale,
            rotate(d_key_value[:, :k_width], position, KV_HEADS, -1.0),
            d_key_value[:, k_width:],
        ],
        axis=1,
    ).astype(bf16)
    d_normed_in = back_dot(d_projected, w_in)
    _, first_back = jax.vjp(rms_norm, residual, gains_used[:, 0])
    d_input_part, d_gain0 = first_back(d_normed_in)
    input_grad = d_middle + d_input_part
    gain_grad = jnp.stack([d_gain0, d_gain1, d_gain2, d_gain3], axis=1)
    attended_all, d_attn_all, normed_all, d_proj_all = (
        lax.all_gather(attended, "rep", axis=0, tiled=True),
        lax.all_gather(d_attn_low, "rep", axis=0, tiled=True),
        lax.all_gather(normed_in, "rep", axis=0, tiled=True),
        lax.all_gather(d_projected, "rep", axis=0, tiled=True),
    )
    part_out = owned_rows(attended_all, d_attn_all, rep_index, attended.shape[1] // rep_count)
    part_in = owned_rows(normed_all, d_proj_all, rep_index, normed_in.shape[1] // rep_count)
    part_gain = lax.psum_scatter(gain_grad, "rep", scatter_dimension=0, tiled=True)
    owned = (
        lax.psum_scatter(part_in, "shard", scatter_dimension=0, tiled=True),
        lax.psum_scatter(part_gain, "shard", scatter_dimension=0, tiled=True),
        lax.psum_scatter(part_out, "shard", scatter_dimension=0, tiled=True),
        lax.psum_scatter(part_gate_up, "shard", scatter_dimension=0, tiled=True),
        lax.psum_scatter(part_down, "shard", scatter_dimension=0, tiled=True),
    )
    grad_inproj, grad_gains, grad_outproj, grad_gate_up, grad_down = owned
    split_at = grad_gate_up.shape[1] // 2
    grad_gate = grad_gate_up[:, :split_at]
    grad_up = grad_gate_up[:, split_at:]
    masters = (inproj, outproj, ffn_gate, ffn_up, ffn_down, norm_gains)
    gradients = (grad_inproj, grad_outproj, grad_gate, grad_up, grad_down, grad_gains)
    firsts = (mean_inproj, mean_outproj, mean_gate, mean_up, mean_down, mean_gains)
    seconds = (square_inproj, square_outproj, square_gate, square_up, square_down, square_gains)
    results = [
        lamb_local(masters[index], gradients[index], firsts[index], seconds[index])
        for index in range(6)
    ]
    weight_sums = jnp.stack([jnp.sum(master * master) for master in masters])
    step_sums = jnp.stack([jnp.sum(item[2] * item[2]) for item in results])
    totals = lax.psum(jnp.stack([weight_sums, step_sums]), ("rep", "shard"))
    counts = jnp.array([float(master.size * rep_count * shard_count) for master in masters], f32)
    norm_table = jnp.sqrt(totals / counts[None, :] + 1e-06)
    fresh = [
        masters[index] - 0.3 * norm_table[0, index] / norm_table[1, index] * results[index][2]
        for index in range(6)
    ]
    return (
        layer_out,
        input_grad,
        grad_inproj,
        grad_outproj,
        grad_gate,
        grad_up,
        grad_down,
        grad_gains,
        results[0][0],
        results[1][0],
        results[2][0],
        results[3][0],
        results[4][0],
        results[5][0],
        results[0][1],
        results[1][1],
        results[2][1],
        results[3][1],
        results[4][1],
        results[5][1],
        fresh[0],
        fresh[1],
        fresh[2],
        fresh[3],
        fresh[4],
        fresh[5],
        norm_table,
    )


MESH = pl.DeviceIdType.MESH
VM = pltpu.VMEM
HB = pl.ANY
UNITS = 4
VMEM_LIMIT = 60 << 20


def ring_places(count):
    inner = 2 if count == 8 else 4
    outer = count // inner

    def place(shard):
        major = shard // inner
        minor = shard % inner
        return minor * outer + major + (minor % 2) * (outer - 1 - 2 * major)

    def shard_at(spot):
        minor = spot // outer
        major = spot % outer
        return (major + (minor % 2) * (outer - 1 - 2 * major)) * inner + minor

    return place, shard_at


def meet(devices):
    barrier = pltpu.get_barrier_semaphore()
    for device in devices:
        pl.semaphore_signal(barrier, inc=1, device_id=device, device_id_type=MESH)
    pl.semaphore_wait(barrier, len(devices))


def remote(src, dst, send_sem, recv_sem, device):
    return pltpu.make_async_remote_copy(
        src_ref=src,
        dst_ref=dst,
        send_sem=send_sem,
        recv_sem=recv_sem,
        device_id=device,
        device_id_type=MESH,
    )


class Ring:
    def __init__(self, count):
        place, shard_at = ring_places(count)
        self.count = count
        self.half = count // 2
        self.rep = lax.axis_index("rep")
        self.me = lax.axis_index("shard")
        self.spot = place(self.me)
        self.shard_at = shard_at
        self.next = [(self.rep, self.at(1)), (self.rep, self.at(count - 1))]

    def at(self, ahead):
        return self.shard_at((self.spot + ahead) % self.count)

    def away(self, way, hops):
        return self.at(hops if way == 0 else self.count - hops)

    def units(self, way, hop):
        order = list(range(UNITS)) if way == 0 else list(range(UNITS))[::-1]
        return order if hop < self.half else order[: UNITS // 2]


def reduce_on_ring(ring, rows, take, first, landed, send, recv, finish, pause):
    f32 = jnp.float32
    hops = ring.half
    started = []

    def part(unit):
        return pl.ds(unit * (rows // UNITS), rows // UNITS)

    def step_copy(way, step, unit):
        return remote(
            landed.at[way, step - 1, part(unit)] if step else first.at[part(unit)],
            landed.at[way, step, part(unit)],
            send.at[way, step, unit],
            recv.at[way, step, unit],
            ring.next[way],
        )

    for step in range(hops):
        order = ring.units(0, hops - step), ring.units(1, hops - step)
        before = [ring.units(way, hops - step + 1) if step else [] for way in (0, 1)]
        for index in range(len(order[0])):
            for way in (0, 1):
                unit = order[way][index]
                block = take(ring.away(way, hops - step), part(unit)).astype(f32)
                if unit in before[way]:
                    step_copy(way, step - 1, unit).wait_recv()
                    block += landed[way, step - 1, part(unit), :].astype(f32)
                if step:
                    landed[way, step - 1, part(unit), :] = block.astype(landed.dtype)
                else:
                    first[part(unit), :] = block.astype(first.dtype)
                copy = step_copy(way, step, unit)
                copy.start()
                started.append(copy)
            if step or index == len(order[0]) - 1:
                pause()
    for unit in range(UNITS):
        total = take(ring.me, part(unit)).astype(f32)
        for way in (0, 1):
            step_copy(way, hops - 1, unit).wait_recv()
            total += landed[way, hops - 1, part(unit), :].astype(f32)
        finish(part(unit), total)
    return started


class Flow:
    def __init__(self, ring, rows, send, recv):
        self.ring, self.rows, self.send, self.recv = ring, rows, send, recv
        self.unit_rows = rows // UNITS
        self.started = []

    def span(self, slot, unit):
        return pl.ds(slot * self.rows + unit * self.unit_rows, self.unit_rows)

    def slot(self, way, hops):
        if hops == 0:
            return 0
        return self.ring.count - 1 if hops == self.ring.half else 2 * hops - 1 + way

    def go(self, copy):
        copy.start()
        self.started.append(copy)

    def finish(self):
        for copy in self.started:
            copy.wait_send()

    def gather_copy(self, buffer, way, hop, unit):
        return remote(
            buffer.at[self.span(self.slot(way, hop - 1), unit)],
            buffer.at[self.span(self.slot(way, hop), unit)],
            self.send.at[way, hop - 1, unit],
            self.recv.at[way, hop - 1, unit],
            self.ring.next[way],
        )

    def gather(self, buffer, group_work):
        ring = self.ring
        for index in range(UNITS):
            for way in (0, 1):
                self.go(self.gather_copy(buffer, way, 1, ring.units(way, 1)[index]))
        queue = list(group_work(0, 1))
        for hop in range(1, ring.half + 1):
            length = len(ring.units(0, hop))
            for index in range(length):
                for way in (0, 1):
                    unit = ring.units(way, hop)[index]
                    self.gather_copy(buffer, way, hop, unit).wait_recv()
                    if hop < ring.half and unit in ring.units(way, hop + 1):
                        self.go(self.gather_copy(buffer, way, hop + 1, unit))
                if queue:
                    queue.pop(0)()
            for piece in queue:
                piece()
            queue = list(group_work(2 * hop - 1, 2) if hop < ring.half else group_work(ring.count - 1, 1))
        for piece in queue:
            piece()
        self.finish()

    def reduce_copy(self, first, landed, way, step, unit):
        span = pl.ds(unit * self.unit_rows, self.unit_rows)
        src = first.at[span] if step == 0 else landed.at[way, step - 1, span]
        return remote(
            src,
            landed.at[way, step, span],
            self.send.at[way, step, unit],
            self.recv.at[way, step, unit],
            self.ring.next[way],
        )

    def reduce(self, first, landed, partial, group_work, finish):
        ring = self.ring
        hops = ring.half
        f32 = jnp.float32
        for piece in group_work(ring.count - 1, 1, 0):
            piece()
        queue = list(group_work(2 * (hops - 1) - 1, 2, 1))
        for step in range(hops):
            order = ring.units(0, hops - step), ring.units(1, hops - step)
            before = [ring.units(way, hops - step + 1) if step else [] for way in (0, 1)]
            for index in range(len(order[0])):
                for way in (0, 1):
                    unit = order[way][index]
                    span = pl.ds(unit * self.unit_rows, self.unit_rows)
                    if step == 0:
                        first[span, :] = partial[0, pl.ds(unit * self.unit_rows, self.unit_rows), :].astype(first.dtype)
                    else:
                        side = 1 - way
                        block = partial[
                            step % 2, pl.ds(side * self.rows + unit * self.unit_rows, self.unit_rows), :
                        ]
                        if unit in before[way]:
                            self.reduce_copy(first, landed, way, step - 1, unit).wait_recv()
                            block = block + landed[way, step - 1, span, :].astype(f32)
                        landed[way, step - 1, span, :] = block.astype(landed.dtype)
                    self.go(self.reduce_copy(first, landed, way, step, unit))
                if queue:
                    queue.pop(0)()
            for piece in queue:
                piece()
            ahead = hops - step - 2
            queue = []
            if step < hops - 1:
                queue = list(group_work(2 * ahead - 1, 2, step % 2) if ahead > 0 else group_work(0, 1, step % 2))
        for unit in range(UNITS):
            span = pl.ds(unit * self.unit_rows, self.unit_rows)
            total = partial[hops % 2, span, :]
            for way in (0, 1):
                self.reduce_copy(first, landed, way, hops - 1, unit).wait_recv()
                total = total + landed[way, hops - 1, span, :].astype(f32)
            finish(unit, total)
        self.finish()


def looped(piece, count):
    def all_of_it():
        def body(j, carry):
            piece(j)
            return carry

        lax.fori_loop(0, count, body, 0)

    return [all_of_it]


def gelu_pair(gate):
    inner = 0.7978845608028654 * (gate + 0.044715 * gate * gate * gate)
    bend = jnp.tanh(inner)
    value = 0.5 * gate * (1.0 + bend)
    slope = 0.5 * (1.0 + bend) + 0.5 * gate * (1.0 - bend * bend) * 0.7978845608028654 * (
        1.0 + 0.134145 * gate * gate
    )
    return value, slope


def ffn_kernel(
    count, attn_ref, tokens_ref, cot_ref, gains_ref, gate_ref, up_ref, dn_ref,
    layer_ref, dmid_ref, dattn_ref, gg_ref, h3_ref, hid_ref, dffn_ref, dgu_ref,
    lin, partial, first, landed, middle, total_ref, s1, r1, s2, r2, s3, r3, s4, r4,
):
    f32, bf16 = jnp.float32, jnp.bfloat16
    ring = Ring(count)
    rows, width = attn_ref.shape
    part = hid_ref.shape[1]
    tile = part // 3
    wide = width // 3
    meet(ring.next)

    def gain(index):
        return 1.0 + gains_ref[index : index + 1, :]

    def scale_of(value):
        return lax.rsqrt(jnp.mean(value * value, axis=-1, keepdims=True) + 1e-06)

    half = rows // 2
    halves = [pl.ds(0, half), pl.ds(half, half)]
    for span in halves:
        proj = attn_ref[span, :]
        mid = tokens_ref[span, :].astype(f32) + proj * scale_of(proj) * gain(1)
        middle[span, :] = mid
        h3_ref[span, :] = (mid * scale_of(mid) * gain(2)).astype(bf16)

    def lin_work(slot, blocks):
        at = pl.ds(slot * rows, blocks * rows)

        def piece(j):
            lo = pl.ds(pl.multiple_of(j * tile, 128), tile)
            hi = pl.ds(pl.multiple_of(part + j * tile, 128), tile)
            gate = jnp.dot(h3_ref[at, :], gate_ref[:, lo], preferred_element_type=f32)
            up = jnp.dot(h3_ref[at, :], up_ref[:, lo], preferred_element_type=f32)
            value, slope = gelu_pair(gate)
            hid_ref[at, lo] = (value * up).astype(bf16)
            lin[at, lo] = (up * slope).astype(bf16)
            lin[at, hi] = value.astype(bf16)

        return looped(piece, 3)

    def down_work(slot, blocks, side):
        at = pl.ds(slot * rows, blocks * rows)

        def piece(j):
            cols = pl.ds(pl.multiple_of(j * wide, 128), wide)
            partial[side, pl.ds(0, blocks * rows), cols] = jnp.dot(
                hid_ref[at, :], dn_ref[:, cols], preferred_element_type=f32
            )

        return looped(piece, 3)

    def nt(left, right):
        return lax.dot_general(left, right, (((1,), (1,)), ((), ())), preferred_element_type=f32)

    def back_work(slot, blocks):
        at = pl.ds(slot * rows, blocks * rows)

        def piece(j):
            lo = pl.ds(pl.multiple_of(j * tile, 128), tile)
            hi = pl.ds(pl.multiple_of(part + j * tile, 128), tile)
            d_hidden = nt(dffn_ref[at, :], dn_ref[lo, :])
            dgu_ref[at, lo] = (d_hidden * lin[at, lo].astype(f32)).astype(bf16)
            dgu_ref[at, hi] = (d_hidden * lin[at, hi].astype(f32)).astype(bf16)

        return looped(piece, 3)

    def input_work(slot, blocks, side):
        at = pl.ds(slot * rows, blocks * rows)

        def piece(j):
            cols = pl.ds(pl.multiple_of(j * wide, 128), wide)
            partial[side, pl.ds(0, blocks * rows), cols] = nt(dgu_ref[at, :part], gate_ref[cols, :]) + nt(
                dgu_ref[at, part:], up_ref[cols, :]
            )

        return looped(piece, 3)

    def keep(unit, total):
        total_ref[pl.ds(unit * (rows // UNITS), rows // UNITS), :] = total

    Flow(ring, rows, s1, r1).gather(h3_ref, lin_work)
    Flow(ring, rows, s2, r2).reduce(first, landed, partial, down_work, keep)

    def back_norm(value, index, grad):
        scale = scale_of(value)
        normed = value * scale
        weighted = grad * gain(index)
        inner = jnp.mean(weighted * normed, axis=-1, keepdims=True)
        return scale * (weighted - normed * inner), jnp.sum(grad * normed, axis=0, keepdims=True)

    gg = jnp.zeros((1, width), f32)
    for span in halves:
        proj = total_ref[span, :]
        scale = scale_of(proj)
        layer_ref[span, :] = (middle[span, :] + proj * scale * gain(3)).astype(bf16)
        d_ffn, term = back_norm(proj, 3, cot_ref[span, :].astype(f32))
        gg += term
        dffn_ref[span, :] = d_ffn.astype(bf16)
    gg_ref[3:4, :] = gg

    Flow(ring, rows, s3, r3).gather(dffn_ref, back_work)
    Flow(ring, rows, s4, r4).reduce(first, landed, partial, input_work, keep)

    gg1 = jnp.zeros((1, width), f32)
    gg2 = jnp.zeros((1, width), f32)
    for span in halves:
        d_mid, term = back_norm(middle[span, :], 2, total_ref[span, :])
        gg2 += term
        d_mid = d_mid + cot_ref[span, :].astype(f32)
        dmid_ref[span, :] = d_mid
        d_attn, term = back_norm(attn_ref[span, :], 1, d_mid)
        gg1 += term
        dattn_ref[span, :] = d_attn.astype(bf16)
    gg_ref[1:2, :] = gg1
    gg_ref[2:3, :] = gg2
    gg_ref[0:1, :] = jnp.zeros((1, width), f32)
    gg_ref[4:8, :] = jnp.zeros((4, width), f32)


def feed_forward(attn_proj, tokens, cotangent, gain_rows, w_gate, w_up, w_down, count, collective_id):
    f32, bf16 = jnp.float32, jnp.bfloat16
    rows, width = attn_proj.shape
    part = w_down.shape[0]
    every = rows * count
    dma = pltpu.SemaphoreType.DMA
    shape = jax.ShapeDtypeStruct
    return pl.pallas_call(
        functools.partial(ffn_kernel, count),
        out_shape=[
            shape((rows, width), bf16),
            shape((rows, width), f32),
            shape((rows, width), bf16),
            shape((8, width), f32),
            shape((every, width), bf16),
            shape((every, part), bf16),
            shape((every, width), bf16),
            shape((every, 2 * part), bf16),
        ],
        in_specs=[pl.BlockSpec(memory_space=VM)] * 7,
        out_specs=[pl.BlockSpec(memory_space=VM)] * 8,
        scratch_shapes=[
            pltpu.VMEM((every, 2 * part), bf16),
            pltpu.VMEM((2, 2 * rows, width), f32),
            pltpu.VMEM((rows, width), bf16),
            pltpu.VMEM((2, count // 2, rows, width), bf16),
            pltpu.VMEM((rows, width), f32),
            pltpu.VMEM((rows, width), f32),
        ]
        + [dma((2, count // 2, UNITS))] * 8,
        compiler_params=pltpu.CompilerParams(
            collective_id=collective_id, has_side_effects=True, vmem_limit_bytes=VMEM_LIMIT
        ),
        name="feed_forward",
    )(attn_proj, tokens, cotangent, gain_rows, w_gate, w_up, w_down)


def attention_kernel(
    reps, count, h1_ref, in_ref, wo_ref, cos_ref, sin_ref, tagq_ref, tagk_ref, cut_ref,
    proj_ref, q_ref, k_ref, v_ref, att_ref, probs_ref, damp_ref, up_ref,
    part, first, landed, r_send, r_recv, w_sems, loc
):
    f32, bf16 = jnp.float32, jnp.bfloat16
    ring = Ring(count)
    rows = proj_ref.shape[0]
    seq_len = h1_ref.shape[0]
    tall = seq_len // 4
    half = HEAD_DIM // 2
    meet(near_devices(ring))
    weights = Fetch(ring, cut_ref, up_ref, w_sems)
    weights.begin()
    own = pltpu.make_async_copy(cut_ref.at[ring.me], up_ref.at[ring.rep, ring.me], loc)
    own.start()

    def project(i, carry):
        at = pl.ds(pl.multiple_of(i * tall, 16), tall)
        flat = jnp.dot(h1_ref[at, :], in_ref[...], preferred_element_type=f32)
        cosine, sine = cos_ref[at, :], sin_ref[at, :]

        def turned(start):
            first, second = flat[:, start : start + half], flat[:, start + half : start + HEAD_DIM]
            return jnp.concatenate([first * cosine - second * sine, second * cosine + first * sine], axis=1)

        q_ref[at, :] = (turned(0) * HEAD_DIM ** (-0.5)).astype(bf16)
        k_ref[at, :] = turned(HEAD_DIM).astype(bf16)
        v_ref[at, :] = flat[:, 2 * HEAD_DIM :].astype(bf16)
        return carry

    lax.fori_loop(0, 4, project, 0)

    def attend(i, carry):
        at = pl.ds(pl.multiple_of(i * tall, 16), tall)
        raw = lax.dot_general(q_ref[at, :], k_ref[...], (((1,), (1,)), ((), ())), preferred_element_type=f32)
        bent = jnp.tanh(raw * (1.0 / 50.0))
        query_at = i * tall + lax.broadcasted_iota(jnp.int32, (tall, seq_len), 0)
        key_at = lax.broadcasted_iota(jnp.int32, (tall, seq_len), 1)
        tag = tagq_ref[at, :]
        visible = (key_at <= query_at) | ((tag == tagk_ref[...]) & (tag > 0))
        masked = jnp.where(visible, 50.0 * bent, -1e30)
        expo = jnp.exp(masked - jnp.max(masked, axis=-1, keepdims=True))
        probs = expo / jnp.sum(expo, axis=-1, keepdims=True)
        low = probs.astype(bf16)
        probs_ref[at, :] = low
        damp_ref[at, :] = (probs * (1.0 - bent * bent)).astype(bf16)
        attended = jnp.dot(low, v_ref[...], preferred_element_type=f32).astype(bf16)
        att_ref[at, :] = attended
        part[at, :] = jnp.dot(attended, wo_ref[...], preferred_element_type=f32)
        return carry

    lax.fori_loop(0, 4, attend, 0)

    work = weights.steps()

    def pause():
        for _ in range(min(2, len(work))):
            work.pop(0)()

    def finish(span, total):
        proj_ref[span, :] = total

    def take(shard, span):
        return part[pl.ds(pl.multiple_of(shard * rows + span.start, 16), span.size), :]

    started = reduce_on_ring(ring, rows, take, first, landed, r_send, r_recv, finish, pause)
    for piece in work:
        piece()
    weights.finish()
    own.wait()
    for copy in started:
        copy.wait_send()


def attention(reps, count, normed, w_in, w_out, cosine, sine, tag, cut_up, collective_id):
    dma = pltpu.SemaphoreType.DMA
    low, f32 = jnp.bfloat16, jnp.float32
    shape = jax.ShapeDtypeStruct
    seq_len, width = normed.shape
    rows = seq_len // count
    hops = count // 2
    head = shape((seq_len, HEAD_DIM), low)
    square = shape((seq_len, seq_len), low)
    return pl.pallas_call(
        functools.partial(attention_kernel, reps, count),
        out_shape=[
            shape((rows, width), f32), head, head, head, head, square, square,
            shape((reps,) + cut_up.shape, low),
        ],
        in_specs=[pl.BlockSpec(memory_space=VM)] * 7 + [pl.BlockSpec(memory_space=HB)],
        out_specs=[pl.BlockSpec(memory_space=VM)] * 7 + [pl.BlockSpec(memory_space=HB)],
        scratch_shapes=[
            pltpu.VMEM((seq_len, width), f32),
            pltpu.VMEM((rows, width), low),
            pltpu.VMEM((2, hops, rows, width), low),
            dma((2, hops, UNITS)),
            dma((2, hops, UNITS)),
            dma((8, count)),
            dma,
        ],
        compiler_params=pltpu.CompilerParams(
            collective_id=collective_id, has_side_effects=True, vmem_limit_bytes=VMEM_LIMIT
        ),
        name="attention",
    )(normed, w_in, w_out, cosine, sine, tag[:, None], tag[None, :], cut_up)


class Fetch:
    def __init__(self, ring, cut, out, sems):
        self.ring, self.cut, self.out = ring, cut, out
        self.rep, self.me, self.count = ring.rep, ring.me, ring.count
        self.across, self.beside = rep_partners(ring.rep)
        self.sems = sems
        self.started = []

    def go(self, copy):
        copy.start()
        self.started.append(copy)

    def spread(self, k):
        to = (self.me + k) % self.count
        return remote(
            self.cut.at[to], self.out.at[self.rep, self.me], self.sems.at[0, k], self.sems.at[1, k], (self.rep, to)
        )

    def arrived(self, k):
        frm = (self.me + self.count - k) % self.count
        return remote(
            self.cut.at[frm], self.out.at[self.rep, frm], self.sems.at[0, k], self.sems.at[1, k], (self.rep, frm)
        )

    def forward(self, k, hop):
        frm = (self.me + self.count - k) % self.count
        rep = self.across if hop == 2 else self.rep
        block = self.out.at[rep, frm] if k or hop == 2 else self.cut.at[self.me]
        to = self.across if hop == 0 else self.beside
        return remote(
            block,
            self.out.at[rep, frm],
            self.sems.at[2 + 2 * hop, k],
            self.sems.at[3 + 2 * hop, k],
            (to, self.me),
        )

    def pass_on(self, k):
        if k:
            self.arrived(k).wait_recv()
        self.go(self.forward(k, 0))
        self.go(self.forward(k, 1))

    def pass_beside(self, k):
        self.forward(k, 0).wait_recv()
        self.go(self.forward(k, 2))

    def begin(self):
        for k in range(1, self.count):
            self.go(self.spread(k))
        self.pass_on(0)

    def steps(self):
        work = [functools.partial(self.pass_on, k) for k in range(1, self.count)]
        return work + [functools.partial(self.pass_beside, k) for k in range(self.count)]

    def finish(self):
        for k in range(self.count):
            self.forward(k, 1).wait_recv()
            self.forward(k, 2).wait_recv()
        for copy in self.started:
            copy.wait_send()


def rep_partners(rep):
    return (rep + 2) % 4, rep + 1 - 2 * (rep % 2)


def everyone(rep, me, reps, count):
    here = rep * count + me
    total = reps * count
    return [
        (((here + k) % total) // count, ((here + k) % total) % count) for k in range(1, total)
    ]


def opening_kernel(
    reps, count, tok_ref, gain_ref, in_ref, gate_ref, dn_ref, ou_ref, h1_ref, gains_ref, w_in, w_gate, w_dn, w_ou,
    tok_all, gain_all, t_send, t_recv, g_send, g_recv, i_sems, u_sems, o_send, o_recv, n_send, n_recv, loc
):
    f32 = jnp.float32
    ring = Ring(count)
    rep, me = ring.rep, ring.me
    across, beside = rep_partners(rep)
    others = everyone(rep, me, reps, count)
    mine = rep * count + me
    d_rows = in_ref.shape[1]
    rows = tok_ref.shape[0]
    meet(others)
    started = []

    def go(copy):
        copy.start()
        started.append(copy)

    for k, device in enumerate(others):
        go(remote(gain_ref, gain_all.at[mine], g_send.at[k], g_recv.at[k], device))
    gain_all[mine] = gain_ref[...]
    ins = Fetch(ring, in_ref, w_in, i_sems)
    gates = Fetch(ring, gate_ref, w_gate, u_sems)
    gather = Gather(ring, tok_ref, tok_all, t_send, t_recv)
    ins.begin()
    gather.begin()

    per_head = count * reps // HEADS
    target = mine // per_head
    slot = mine % per_head

    def ou_copy(j):
        return remote(ou_ref.at[j], w_ou.at[j, slot], o_send.at[j], o_recv.at[slot], (j, target))

    def is_self(j):
        return (rep == j) & (me == target)

    for j in range(reps):
        @pl.when(jnp.logical_not(is_self(j)))
        def _():
            ou_copy(j).start()

        @pl.when(is_self(j))
        def _():
            pltpu.make_async_copy(ou_ref.at[j], w_ou.at[j, slot], o_recv.at[slot]).start()

    dn_x = remote(dn_ref, w_dn.at[rep], n_send.at[0], n_recv.at[0], (across, me))
    dn_c = remote(dn_ref, w_dn.at[rep], n_send.at[1], n_recv.at[1], (beside, me))
    dn_d = remote(w_dn.at[across], w_dn.at[across], n_send.at[2], n_recv.at[2], (beside, me))
    go(dn_x)
    go(dn_c)
    gates.begin()
    locals_ = []
    for index, (src, dst) in enumerate(
        ((in_ref.at[me], w_in.at[rep, me]), (gate_ref.at[me], w_gate.at[rep, me]), (dn_ref, w_dn.at[rep]))
    ):
        copy = pltpu.make_async_copy(src, dst, loc.at[index])
        copy.start()
        locals_.append(copy)

    for k in range(len(others)):
        frm = (mine + len(others) - k) % (reps * count)
        remote(gain_ref, gain_all.at[frm], g_send.at[k], g_recv.at[k], others[k]).wait_recv()
    gains_ref[...] = jnp.concatenate([gain_all[device, :, 0:d_rows] for device in range(reps * count)], axis=1)
    gain = 1.0 + gains_ref[0:1, :]

    def norm(value):
        value = value.astype(f32)
        return (value * lax.rsqrt(jnp.mean(value * value, axis=-1, keepdims=True) + 1e-06) * gain).astype(h1_ref.dtype)

    def norm_block(shard):
        for unit in range(UNITS):
            span = pl.ds(unit * (rows // UNITS), rows // UNITS)
            h1_ref[shard, span, :] = norm(tok_all[shard, span, :])

    for unit in range(UNITS):
        span = pl.ds(unit * (rows // UNITS), rows // UNITS)
        h1_ref[me, span, :] = norm(tok_ref[span, :])

    hops = gather.steps()

    def take_hop(hop):
        for _ in range(len(ring.units(0, hop))):
            hops.pop(0)()
        for way in (0, 1) if hop < ring.half else (0,):
            norm_block(ring.away(1 - way, hop))

    for k in range(1, count):
        ins.pass_on(k)
    take_hop(1)
    for k in range(count):
        ins.pass_beside(k)
    take_hop(2)
    for i in range(per_head):
        remote(
            ou_ref.at[0], w_ou.at[rep, i], o_send.at[0], o_recv.at[i], (across, me)
        ).wait_recv()
    ou_x = remote(w_ou.at[rep], w_ou.at[rep], n_send.at[3], n_recv.at[3], (across, me))
    ou_c = remote(w_ou.at[rep], w_ou.at[rep], n_send.at[4], n_recv.at[4], (beside, me))
    ou_d = remote(w_ou.at[across], w_ou.at[across], n_send.at[5], n_recv.at[5], (beside, me))
    go(ou_x)
    go(ou_c)
    dn_x.wait_recv()
    go(dn_d)
    for k in range(1, count // 2):
        gates.pass_on(k)
    take_hop(3)
    for k in range(count // 2, count):
        gates.pass_on(k)
    for hop in range(4, ring.half + 1):
        take_hop(hop)
    ou_x.wait_recv()
    go(ou_d)
    for k in range(count):
        gates.pass_beside(k)
    ins.finish()
    gates.finish()
    for copy in (dn_c, dn_d, ou_c, ou_d):
        copy.wait_recv()
    for copy in started:
        copy.wait_send()
    gather.finish()
    for j in range(reps):
        @pl.when(jnp.logical_not(is_self(j)))
        def _():
            ou_copy(j).wait_send()
    for copy in locals_:
        copy.wait()


def opening(reps, count, tokens, gain_tile, w_in, w_gate, w_dn, w_ou, collective_id):
    dma = pltpu.SemaphoreType.DMA
    per_head = count * reps // HEADS
    total = reps * count
    low = jnp.bfloat16
    shape = jax.ShapeDtypeStruct
    hops = dma((2, count // 2, UNITS))
    width = tokens.shape[1]
    gathered = (count,) + tokens.shape
    return pl.pallas_call(
        functools.partial(opening_kernel, reps, count),
        out_shape=[
            shape(gathered, low),
            shape((8, width), jnp.float32),
            shape((reps,) + w_in.shape, low),
            shape((reps,) + w_gate.shape, low),
            shape((reps,) + w_dn.shape, low),
            shape((reps, per_head) + w_ou.shape[1:], low),
        ],
        in_specs=[pl.BlockSpec(memory_space=VM)] * 2 + [pl.BlockSpec(memory_space=HB)] * 4,
        out_specs=[pl.BlockSpec(memory_space=VM)] * 2 + [pl.BlockSpec(memory_space=HB)] * 4,
        scratch_shapes=[
            pltpu.VMEM(gathered, low),
            pltpu.VMEM((total,) + gain_tile.shape, jnp.float32),
            hops,
            hops,
            dma((total - 1,)),
            dma((total - 1,)),
            dma((8, count)),
            dma((8, count)),
            dma((reps,)),
            dma((per_head,)),
            dma((6,)),
            dma((6,)),
            dma((3,)),
        ],
        compiler_params=pltpu.CompilerParams(
            collective_id=collective_id, has_side_effects=True, vmem_limit_bytes=VMEM_LIMIT
        ),
        name="opening",
    )(tokens, gain_tile, w_in, w_gate, w_dn, w_ou)


def cut_kernel(reps, count, in_ref, gate_ref, up_ref, cut_in, cut_gate, cut_up):
    low = jnp.bfloat16
    group = HEADS // KV_HEADS
    block = gate_ref.shape[1] // (reps * count)
    for shard in range(count):
        for ref, cut in ((gate_ref, cut_gate), (up_ref, cut_up)):
            pieces = [ref[:, (r * count + shard) * block : (r * count + shard + 1) * block] for r in range(reps)]
            cut[shard] = jnp.concatenate(pieces, axis=1).astype(low)
        heads = shard, HEADS + shard // group, HEADS + KV_HEADS + shard // group
        for index, head in enumerate(heads):
            cut_in[shard, :, index * HEAD_DIM : (index + 1) * HEAD_DIM] = in_ref[
                :, head * HEAD_DIM : (head + 1) * HEAD_DIM
            ].astype(low)


def cut_weights(reps, count, inproj, ffn_gate, ffn_up):
    rows = inproj.shape[0]
    shape = jax.ShapeDtypeStruct
    return pl.pallas_call(
        functools.partial(cut_kernel, reps, count),
        out_shape=[
            shape((count, rows, 3 * HEAD_DIM), jnp.bfloat16),
            shape((count, rows, ffn_gate.shape[1] // count), jnp.bfloat16),
            shape((count, rows, ffn_up.shape[1] // count), jnp.bfloat16),
        ],
        in_specs=[pl.BlockSpec(memory_space=VM)] * 3,
        out_specs=[pl.BlockSpec(memory_space=VM)] * 3,
        compiler_params=pltpu.CompilerParams(vmem_limit_bytes=VMEM_LIMIT),
        name="cut_weights",
    )(inproj, ffn_gate, ffn_up)


class RepSum:
    def __init__(self, part, from_core, to_across, from_across, sems, rep, me):
        self.part, self.from_core = part, from_core
        self.to_across, self.from_across = to_across, from_across
        self.c_send, self.c_recv, self.x_send, self.x_recv = sems
        self.across, self.beside = rep_partners(rep)
        self.rep, self.me = rep, me
        self.core = rep % 2
        self.chip = rep // 2

    def core_copy(self, side, piece):
        chip = 1 - self.chip if side == 0 else self.chip
        return remote(
            self.part(chip * 2 + 1 - self.core, piece),
            self.from_core.at[side, piece],
            self.c_send.at[side, piece],
            self.c_recv.at[side, piece],
            (self.beside, self.me),
        )

    def cross_copy(self, piece):
        return remote(
            self.to_across.at[piece],
            self.from_across.at[piece],
            self.x_send.at[piece],
            self.x_recv.at[piece],
            (self.across, self.me),
        )

    def begin(self, pieces):
        for side in (0, 1):
            for piece in pieces:
                self.core_copy(side, piece).start()

    def cross(self, piece):
        f32 = jnp.float32
        self.core_copy(0, piece).wait_recv()
        mine = self.part((1 - self.chip) * 2 + self.core, piece)[...].astype(f32)
        self.to_across[piece] = (mine + self.from_core[0, piece].astype(f32)).astype(jnp.bfloat16)
        self.cross_copy(piece).start()

    def total(self, piece):
        f32 = jnp.float32
        self.core_copy(1, piece).wait_recv()
        mine = self.part(self.rep, piece)[...].astype(f32) + self.from_core[1, piece].astype(f32)
        self.cross_copy(piece).wait_recv()
        return mine + self.from_across[piece].astype(f32)

    def finish(self, pieces):
        for piece in pieces:
            self.core_copy(0, piece).wait_send()
            self.core_copy(1, piece).wait_send()
            self.cross_copy(piece).wait_send()


class Spread:
    def __init__(self, blocks, out, send, recv, rep, me, count):
        self.blocks, self.out, self.send, self.recv = blocks, out, send, recv
        self.rep, self.me, self.count = rep, me, count

    def copy(self, k):
        to = (self.me + k) % self.count
        return remote(
            self.blocks.at[to], self.out.at[self.me], self.send.at[k], self.recv.at[k], (self.rep, to)
        )

    def arrived(self, k):
        frm = (self.me + self.count - k) % self.count
        return remote(
            self.blocks.at[frm], self.out.at[frm], self.send.at[k], self.recv.at[k], (self.rep, frm)
        )

    def finish(self):
        for k in range(1, self.count):
            self.arrived(k).wait_recv()
        for k in range(1, self.count):
            self.copy(k).wait_send()


def near_devices(ring):
    across, beside = rep_partners(ring.rep)
    return [(ring.rep, (ring.me + k) % ring.count) for k in range(1, ring.count)] + [
        (across, ring.me),
        (beside, ring.me),
    ]


class Gather:
    def __init__(self, ring, block, out, send, recv):
        self.ring, self.block, self.out, self.send, self.recv = ring, block, out, send, recv
        self.rows = block.shape[0] // UNITS
        self.started = []

    def copy(self, way, hop, unit):
        ring = self.ring
        origin = ring.away(1 - way, hop - 1) if hop > 1 else ring.me
        span = pl.ds(unit * self.rows, self.rows)
        return remote(
            self.block.at[span] if hop == 1 else self.out.at[origin, span],
            self.out.at[origin, span],
            self.send.at[way, hop - 1, unit],
            self.recv.at[way, hop - 1, unit],
            ring.next[way],
        )

    def go(self, copy):
        copy.start()
        self.started.append(copy)

    def begin(self):
        for index in range(UNITS):
            for way in (0, 1):
                self.go(self.copy(way, 1, self.ring.units(way, 1)[index]))

    def steps(self):
        ring = self.ring

        def step(hop, index):
            for way in (0, 1):
                unit = ring.units(way, hop)[index]
                self.copy(way, hop, unit).wait_recv()
                if hop < ring.half and unit in ring.units(way, hop + 1):
                    self.go(self.copy(way, hop + 1, unit))

        return [
            functools.partial(step, hop, index)
            for hop in range(1, ring.half + 1)
            for index in range(len(ring.units(0, hop)))
        ]

    def finish(self):
        for copy in self.started:
            copy.wait_send()


def tn(left, right):
    return lax.dot_general(left, right, (((0,), (0,)), ((), ())), preferred_element_type=jnp.float32)


DN_PIECES = 3


def ffn_grads_kernel(
    reps, count, dattn_ref, h3_ref, hid_ref, dffn_ref, dgu_ref, all_ref, sum_ref, down_ref,
    g_part, g_core, g_to, g_from, d_part, d_core, d_to, d_from,
    t_send, t_recv, gc_s, gc_r, gx_s, gx_r, dc_s, dc_r, dx_s, dx_r, s_send, s_recv, loc
):
    bf16 = jnp.bfloat16
    ring = Ring(count)
    rep, me = ring.rep, ring.me
    d_rows, columns = sum_ref.shape[1:]
    part, width = d_part.shape
    block = part // reps
    wide = width // 3
    tall = part // 3
    meet(near_devices(ring))
    gather = Gather(ring, dattn_ref, all_ref, t_send, t_recv)
    gather.begin()
    own = pltpu.make_async_copy(dattn_ref, all_ref.at[me], loc)
    own.start()

    def d_at(owner, piece):
        rows = block // DN_PIECES
        return d_part.at[pl.ds(owner * block + piece * rows, rows)]

    down = RepSum(d_at, d_core, d_to, d_from, (dc_s, dc_r, dx_s, dx_r), rep, me)
    gate_up = RepSum(
        lambda owner, piece: g_part.at[owner, piece], g_core, g_to, g_from, (gc_s, gc_r, gx_s, gx_r), rep, me
    )
    spread = Spread(g_from, sum_ref, s_send, s_recv, rep, me, count)
    d_pieces = list(range(DN_PIECES))
    g_pieces = [(me + k) % count for k in range(1, count)] + [me]

    def make_down(j):
        def body(n, carry):
            cols = pl.ds(pl.multiple_of(n * wide, 128), wide)
            d_part[j * tall : (j + 1) * tall, cols] = tn(
                hid_ref[:, j * tall : (j + 1) * tall], dffn_ref[:, cols]
            ).astype(bf16)
            return carry

        lax.fori_loop(0, 3, body, 0)

    def make_gate_up(owner):
        rows = count * d_rows
        step = columns // 3

        def body(n, carry):
            cols = pl.ds(pl.multiple_of(n * step, 128), step)
            made = tn(h3_ref[:, owner * rows : (owner + 1) * rows], dgu_ref[:, cols])
            g_part[owner, :, :, cols] = made.reshape(count, d_rows, step).astype(bf16)
            return carry

        lax.fori_loop(0, 3, body, 0)

    work = [functools.partial(make_down, j) for j in range(3)]
    work.append(lambda: down.begin(d_pieces))
    work.append(functools.partial(make_gate_up, 0))
    work.append(lambda: [down.cross(piece) for piece in d_pieces])
    work += [functools.partial(make_gate_up, owner) for owner in range(1, reps)]
    work.append(lambda: gate_up.begin(g_pieces))
    steps = gather.steps()
    for step in steps:
        step()
        if work:
            work.pop(0)()
    for piece in work:
        piece()
    for piece in g_pieces:
        gate_up.cross(piece)
    for piece in d_pieces:
        rows = block // DN_PIECES
        down_ref[pl.ds(piece * rows, rows), :] = down.total(piece)
    for k, piece in enumerate(g_pieces):
        total = gate_up.total(piece).astype(bf16)
        if k < count - 1:
            g_from[piece] = total
            spread.copy(k + 1).start()
        else:
            sum_ref[me] = total
    spread.finish()
    down.finish(d_pieces)
    gate_up.finish(g_pieces)
    gather.finish()
    own.wait()


def ffn_grads(reps, count, d_attn, h3, hidden, d_ffn, d_gu, d_rows, collective_id):
    dma = pltpu.SemaphoreType.DMA
    low = jnp.bfloat16
    shape = jax.ShapeDtypeStruct
    width = d_attn.shape[1]
    columns = d_gu.shape[1]
    part = hidden.shape[1]
    block = part // reps
    blocks = (count, d_rows, columns)
    lots = (DN_PIECES, block // DN_PIECES, width)
    hops = dma((2, count // 2, UNITS))
    return pl.pallas_call(
        functools.partial(ffn_grads_kernel, reps, count),
        out_shape=[
            shape((count,) + d_attn.shape, low),
            shape(blocks, low),
            shape((block, width), jnp.float32),
        ],
        in_specs=[pl.BlockSpec(memory_space=VM)] * 5,
        out_specs=[pl.BlockSpec(memory_space=HB)] + [pl.BlockSpec(memory_space=VM)] * 2,
        scratch_shapes=[
            pltpu.VMEM((reps,) + blocks, low),
            pltpu.VMEM((2,) + blocks, low),
            pltpu.VMEM(blocks, low),
            pltpu.VMEM(blocks, low),
            pltpu.VMEM((part, width), low),
            pltpu.VMEM((2,) + lots, low),
            pltpu.VMEM(lots, low),
            pltpu.VMEM(lots, low),
            hops,
            hops,
            dma((2, count)),
            dma((2, count)),
            dma((count,)),
            dma((count,)),
            dma((2, DN_PIECES)),
            dma((2, DN_PIECES)),
            dma((DN_PIECES,)),
            dma((DN_PIECES,)),
            dma((count,)),
            dma((count,)),
            dma,
        ],
        compiler_params=pltpu.CompilerParams(
            collective_id=collective_id, has_side_effects=True, vmem_limit_bytes=VMEM_LIMIT
        ),
        name="ffn_grads",
    )(d_attn, h3, hidden, d_ffn, d_gu)


def closing_kernel(
    reps, count, dattn_ref, h1_ref, in_ref, wo_ref, q_ref, k_ref, v_ref, att_ref, probs_ref, damp_ref, cos_ref, sin_ref,
    tokens_ref, dmid_ref, gains_ref, gg_ref, grad_ref, sum_ref, out_ref, gain_ref,
    x_part, dproj, d_key, d_value, i_part, o_part, first, landed, total_ref, tiles, i_core, i_to, i_from,
    o_core, o_to, o_from,
    r_send, r_recv, ic_s, ic_r, ix_s, ix_r, oc_s, oc_r, ox_s, ox_r, s_send, s_recv, p_send, p_recv,
    g_send, g_recv
):
    f32, bf16 = jnp.float32, jnp.bfloat16
    ring = Ring(count)
    rep, me = ring.rep, ring.me
    here = rep * count + me
    others = everyone(rep, me, reps, count)
    full = o_part.shape[1]
    d_rows = sum_ref.shape[1]
    seq_len, width = dattn_ref.shape
    rows = grad_ref.shape[0]
    half = HEAD_DIM // 2
    meet(others)

    def nt(left, right):
        return lax.dot_general(left, right, (((1,), (1,)), ((), ())), preferred_element_type=f32)

    def unturned(flat, at):
        cosine, sine = cos_ref[at, :], sin_ref[at, :]
        low, high = flat[:, :half], flat[:, half:]
        return jnp.concatenate([low * cosine + high * sine, high * cosine - low * sine], axis=1)

    tall = seq_len // 4
    d_key[...] = jnp.zeros_like(d_key)
    d_value[...] = jnp.zeros_like(d_value)

    def attend(i, carry):
        at = pl.ds(pl.multiple_of(i * tall, 16), tall)
        d_att = nt(dattn_ref[at, :], wo_ref[...]).astype(bf16)
        d_probs = nt(d_att, v_ref[...])
        probs = probs_ref[at, :]
        inner = jnp.sum(probs.astype(f32) * d_probs, axis=-1, keepdims=True)
        d_scores = (damp_ref[at, :].astype(f32) * (d_probs - inner)).astype(bf16)
        d_query = jnp.dot(d_scores, k_ref[...], preferred_element_type=f32)
        dproj[at, :HEAD_DIM] = (unturned(d_query, at) * HEAD_DIM ** (-0.5)).astype(bf16)
        d_key[...] += tn(d_scores, q_ref[at, :])
        d_value[...] += tn(probs, d_att)
        return carry

    lax.fori_loop(0, 4, attend, 0)

    def project(i, carry):
        at = pl.ds(pl.multiple_of(i * tall, 16), tall)
        dproj[at, HEAD_DIM : 2 * HEAD_DIM] = unturned(d_key[at, :], at).astype(bf16)
        dproj[at, 2 * HEAD_DIM :] = d_value[at, :].astype(bf16)
        x_part[at, :] = nt(dproj[at, :], in_ref[...]).astype(bf16)
        return carry

    lax.fori_loop(0, 4, project, 0)

    def make_out():
        per = width // 3

        def body(n, carry):
            cols = pl.ds(pl.multiple_of(n * per, 128), per)
            made = tn(att_ref[...], dattn_ref[:, cols]).reshape(full, reps, HEAD_DIM // full // reps, per)
            for owner in range(reps):
                o_part[owner, :, :, cols] = made[:, owner].astype(bf16)
            return carry

        lax.fori_loop(0, 3, body, 0)

    def make_in(owner):
        deep = count * d_rows
        made = tn(h1_ref[:, owner * deep : (owner + 1) * deep], dproj[...])
        i_part[owner] = made.reshape(count, d_rows, 3 * HEAD_DIM).astype(bf16)

    o_pieces = list(range(full))
    i_pieces = [(me + k) % count for k in range(1, count)] + [me]
    ins = RepSum(lambda owner, piece: i_part.at[owner, piece], i_core, i_to, i_from, (ic_s, ic_r, ix_s, ix_r), rep, me)
    outs = RepSum(lambda owner, piece: o_part.at[owner, piece], o_core, o_to, o_from, (oc_s, oc_r, ox_s, ox_r), rep, me)
    spread = Spread(i_from, sum_ref, s_send, s_recv, rep, me, count)

    def o_owner(piece):
        where = me * full + piece
        return where // count, where % count

    def o_copy(piece):
        return remote(o_from.at[piece], out_ref.at[rep], p_send.at[piece], p_recv.at[rep], o_owner(piece))

    def o_self(piece):
        return me * full + piece == here

    def o_finish(piece):
        total = outs.total(piece).astype(bf16)
        o_from[piece] = total

        @pl.when(jnp.logical_not(o_self(piece)))
        def _():
            o_copy(piece).start()

        @pl.when(o_self(piece))
        def _():
            pltpu.make_async_copy(o_from.at[piece], out_ref.at[rep], p_recv.at[rep]).start()

    def i_finish(k):
        piece = i_pieces[k]
        total = ins.total(piece).astype(bf16)
        if k < count - 1:
            i_from[piece] = total
            spread.copy(k + 1).start()
        else:
            sum_ref[me] = total

    work = [functools.partial(make_in, owner) for owner in range(reps)]
    work += [lambda: ins.begin(i_pieces), make_out, lambda: outs.begin(o_pieces)]
    work += [functools.partial(ins.cross, piece) for piece in i_pieces]
    work += [functools.partial(outs.cross, piece) for piece in o_pieces]
    work += [functools.partial(i_finish, k) for k in range(count)]
    work += [functools.partial(o_finish, piece) for piece in o_pieces]

    terms = []
    gain = 1.0 + gains_ref[0:1, :]

    def pause():
        for _ in range(min(2, len(work))):
            work.pop(0)()

    def take(shard, span):
        return x_part[pl.ds(pl.multiple_of(shard * rows + span.start, 16), span.size), :]

    def finish(span, total):
        value = tokens_ref[span, :].astype(f32)
        scale = lax.rsqrt(jnp.mean(value * value, axis=-1, keepdims=True) + 1e-06)
        normed = value * scale
        weighted = total * gain
        inner = jnp.mean(weighted * normed, axis=-1, keepdims=True)
        grad_ref[span, :] = dmid_ref[span, :] + scale * (weighted - normed * inner)
        terms.append(jnp.sum(total * normed, axis=0, keepdims=True))

    started = reduce_on_ring(ring, rows, take, first, landed, r_send, r_recv, finish, pause)
    total_ref[...] = gg_ref[...]
    total_ref[0:1, :] = functools.reduce(jnp.add, terms)
    every = total_ref[...]
    for owner in range(reps * count):
        tiles[owner, :, 0:d_rows] = every[:, owner * d_rows : (owner + 1) * d_rows]
        tiles[owner, :, d_rows:] = jnp.zeros((8, 128 - d_rows), f32)
    for k, device in enumerate(others):
        to = (here + k + 1) % (reps * count)
        remote(tiles.at[to], gain_ref.at[here], g_send.at[k], g_recv.at[k], device).start()
    gain_ref[here] = tiles[here]
    for piece in work:
        piece()
    for k in range(len(others)):
        frm = (here + len(others) - k) % (reps * count)
        remote(tiles.at[frm], gain_ref.at[frm], g_send.at[k], g_recv.at[k], others[k]).wait_recv()
    for j in range(reps):
        remote(
            o_from.at[0], out_ref.at[j], p_send.at[0], p_recv.at[j], (rep, (me + 1) % count)
        ).wait_recv()
    for piece in o_pieces:
        @pl.when(jnp.logical_not(o_self(piece)))
        def _():
            o_copy(piece).wait_send()
    spread.finish()
    ins.finish(i_pieces)
    outs.finish(o_pieces)
    for k, device in enumerate(others):
        to = (here + k + 1) % (reps * count)
        remote(tiles.at[to], gain_ref.at[here], g_send.at[k], g_recv.at[k], device).wait_send()
    for copy in started:
        copy.wait_send()


def closing(
    reps, count, d_attn, normed, w_in, w_out, queries, keys, values, attended, probs, damp, cosine, sine,
    tokens, d_middle, gain_rows, gain_terms, piece, collective_id
):
    dma = pltpu.SemaphoreType.DMA
    low, f32 = jnp.bfloat16, jnp.float32
    shape = jax.ShapeDtypeStruct
    rows, width = tokens.shape
    seq_len = normed.shape[0]
    total = reps * count
    half = count // 2
    d_rows = width // total
    full = HEAD_DIM // (reps * piece)
    i_block = (count, d_rows, 3 * HEAD_DIM)
    o_block = (full, piece, width)
    hops = dma((2, half, UNITS))
    return pl.pallas_call(
        functools.partial(closing_kernel, reps, count),
        out_shape=[
            shape((rows, width), f32),
            shape(i_block, low),
            shape((reps, piece, width), low),
            shape((total, 8, 128), f32),
        ],
        in_specs=[pl.BlockSpec(memory_space=VM)] * 16,
        out_specs=[pl.BlockSpec(memory_space=VM)] * 4,
        scratch_shapes=[
            pltpu.VMEM((seq_len, width), low),
            pltpu.VMEM((seq_len, 3 * HEAD_DIM), low),
            pltpu.VMEM((seq_len, HEAD_DIM), f32),
            pltpu.VMEM((seq_len, HEAD_DIM), f32),
            pltpu.VMEM((reps,) + i_block, low),
            pltpu.VMEM((reps,) + o_block, low),
            pltpu.VMEM((rows, width), low),
            pltpu.VMEM((2, half, rows, width), low),
            pltpu.VMEM((8, width), f32),
            pltpu.VMEM((total, 8, 128), f32),
            pltpu.VMEM((2,) + i_block, low),
            pltpu.VMEM(i_block, low),
            pltpu.VMEM(i_block, low),
            pltpu.VMEM((2,) + o_block, low),
            pltpu.VMEM(o_block, low),
            pltpu.VMEM(o_block, low),
            hops,
            hops,
            dma((2, count)),
            dma((2, count)),
            dma((count,)),
            dma((count,)),
            dma((2, full)),
            dma((2, full)),
            dma((full,)),
            dma((full,)),
            dma((count,)),
            dma((count,)),
            dma((full,)),
            dma((reps,)),
            dma((total - 1,)),
            dma((total - 1,)),
        ],
        compiler_params=pltpu.CompilerParams(
            collective_id=collective_id, has_side_effects=True, vmem_limit_bytes=VMEM_LIMIT
        ),
        name="closing",
    )(
        d_attn, normed, w_in, w_out, queries, keys, values, attended, probs, damp, cosine, sine,
        tokens, d_middle, gain_rows, gain_terms,
    )


def tiles_of(ref):
    rows, columns = ref.shape
    tall = 72 if rows % 72 == 0 else 64 if rows % 64 == 0 else 8
    wide = 384 if columns % 384 == 0 else 256
    return rows // tall, columns // wide, tall, wide


def tile_at(ref, n):
    _, across, tall, wide = tiles_of(ref)
    down, right = n // across, n % across
    return pl.ds(pl.multiple_of(down * tall, 8), tall), pl.ds(pl.multiple_of(right * wide, 128), wide)


LAMB_ORDER = (4, 2, 3, 0, 1)


def lamb_kernel(reps, count, sum_in, sum_out, sum_gu, gain_tiles, g_master, g_mean, g_square, *refs):
    f32 = jnp.float32
    names = 5
    hbm_in, refs = [refs[3 * i : 3 * i + 3] for i in range(names)], refs[3 * names :]
    grad_dn, refs = refs[0], refs[1:]
    (sums_out, gg_out, gm_out, gs_out, gp_out), refs = refs[:5], refs[5:]
    hbm_out, refs = [refs[4 * i : 4 * i + 4] for i in range(names)], refs[4 * names :]
    masters, means, squares, grads = (refs[names * i : names * (i + 1)] for i in range(4))
    in_sem, out_sem, dn_sem = refs[4 * names :]
    total = reps * count
    group = HEADS // KV_HEADS

    def fetch(i, j):
        return pltpu.make_async_copy(hbm_in[i][j], (masters, means, squares)[j][i], in_sem.at[i, j])

    fetch_dn = pltpu.make_async_copy(grad_dn, grads[4], dn_sem)
    fetch_dn.start()
    for i in LAMB_ORDER:
        for j in range(3):
            fetch(i, j).start()

    def store(i, j):
        return pltpu.make_async_copy((grads, means, squares, masters)[j][i], hbm_out[i][j], out_sem.at[i, j])

    def join(index, ref):
        block = ref.shape[1] // total
        part = block * reps
        for first in range(0, total, 4):
            pieces = []
            for b in range(first, first + 4):
                start = index * part + (b // count) * block
                pieces.append(sum_gu[b % count, :, start : start + block].astype(f32))
            ref[:, first * block : (first + 4) * block] = jnp.concatenate(pieces, axis=1)

    def make_grad(i):
        if i == 0:
            for head in range(HEADS):
                grads[0][:, head * HEAD_DIM : (head + 1) * HEAD_DIM] = sum_in[head, :, :HEAD_DIM].astype(f32)
            for kind in (1, 2):
                for head in range(KV_HEADS):
                    start = (HEADS + (kind - 1) * KV_HEADS + head) * HEAD_DIM
                    parts = [
                        sum_in[head * group + g, :, kind * HEAD_DIM : (kind + 1) * HEAD_DIM].astype(f32)
                        for g in range(group)
                    ]
                    grads[0][:, start : start + HEAD_DIM] = functools.reduce(jnp.add, parts)
        elif i == 1:
            rows = sum_out.shape[1]
            for j in range(reps):
                grads[1][j * rows : (j + 1) * rows, :] = sum_out[j].astype(f32)
        elif i in (2, 3):
            join(i - 2, grads[i])
        else:
            fetch_dn.wait()

    def lamb(master, grad, mean, square):
        new_mean = 0.5 * mean + 0.5 * grad
        new_square = 0.5 * square + 0.5 * grad * grad
        return new_mean, new_square, new_mean / (jnp.sqrt(new_square) + 1e-06) + 0.01 * master

    def sweep(i):
        down, across, tall, wide = tiles_of(masters[i])

        def body(n, carry):
            at = tile_at(masters[i], n)
            master = masters[i][at]
            new_mean, new_square, step = lamb(master, grads[i][at], means[i][at], squares[i][at])
            means[i][at] = new_mean
            squares[i][at] = new_square
            masters[i][at] = step

            def fold(value):
                return jnp.sum((value * value).reshape(tall // 8, 8, wide), axis=0)

            return carry[0] + fold(master), carry[1] + fold(step)

        zero = jnp.zeros((8, wide), f32)
        return lax.fori_loop(0, down * across, body, (zero, zero))

    at_row = lax.broadcasted_iota(jnp.int32, (8, 128), 0)
    at_lane = lax.broadcasted_iota(jnp.int32, (8, 128), 1)

    def note(sums, i, pair):
        for row in (0, 1):
            sums = sums + jnp.where((at_row == row) & (at_lane == i), jnp.sum(pair[row]), 0.0)
        return sums

    sums = jnp.zeros((8, 128), f32)
    for i in LAMB_ORDER:
        make_grad(i)
        for j in range(3):
            fetch(i, j).wait()
        pair = sweep(i)
        for j in range(4):
            store(i, j).start()
        sums = note(sums, i, pair)
    gain_total = functools.reduce(jnp.add, [gain_tiles[device] for device in range(total)])
    d_rows, kinds = g_master.shape
    gain_grad = gain_total.T[:d_rows, :kinds]
    gain_master = g_master[...]
    new_mean, new_square, gain_step = lamb(gain_master, gain_grad, g_mean[...], g_square[...])
    gg_out[...] = gain_grad
    gm_out[...] = new_mean
    gs_out[...] = new_square
    gp_out[...] = gain_step
    sums_out[...] = note(sums, 5, (gain_master * gain_master, gain_step * gain_step))
    for i in LAMB_ORDER:
        for j in range(4):
            store(i, j).wait()


def table_kernel(reps, count, sizes, x_ref, out_ref, near, far, held, n_send, n_recv, f_send, f_recv):
    f32 = jnp.float32
    rep = lax.axis_index("rep")
    me = lax.axis_index("shard")
    meet(
        [(rep, (me + k) % count) for k in range(1, count)] + [((rep + k) % reps, me) for k in range(1, reps)]
    )
    copies = []
    for k in range(1, count):
        copies.append(remote(x_ref, near.at[me], n_send.at[k], n_recv.at[k], (rep, (me + k) % count)))
    for copy in copies:
        copy.start()
    near[me] = x_ref[...]
    for k in range(1, count):
        frm = (me + count - k) % count
        remote(x_ref, near.at[frm], n_send.at[k], n_recv.at[k], (rep, frm)).wait_recv()
    sums = functools.reduce(jnp.add, [near[shard] for shard in range(count)])
    held[...] = sums
    more = []
    for k in range(1, reps):
        more.append(remote(held, far.at[rep], f_send.at[k], f_recv.at[k], ((rep + k) % reps, me)))
    for copy in more:
        copy.start()
    far[rep] = sums
    for k in range(1, reps):
        frm = (rep + reps - k) % reps
        remote(held, far.at[frm], f_send.at[k], f_recv.at[k], (frm, me)).wait_recv()
    totals = functools.reduce(jnp.add, [far[other] for other in range(reps)])
    at_lane = lax.broadcasted_iota(jnp.int32, (8, 128), 1)
    counts = jnp.ones((8, 128), f32)
    for i, size in enumerate(sizes):
        counts = jnp.where(at_lane == i, float(size), counts)
    out_ref[...] = jnp.sqrt(totals / counts + 1e-06)
    for copy in copies + more:
        copy.wait_send()


def fresh_kernel(table_ref, g_master, g_step, *refs):
    names = 5
    hbm_in, refs = [refs[2 * i : 2 * i + 2] for i in range(names)], refs[2 * names :]
    gp_out, refs = refs[0], refs[1:]
    hbm_out, refs = refs[:names], refs[names:]
    masters, steps, refs = refs[:names], refs[names : 2 * names], refs[2 * names :]
    in_sem, out_sem = refs

    def fetch(i, j):
        return pltpu.make_async_copy(hbm_in[i][j], (masters, steps)[j][i], in_sem.at[i, j])

    def store(i):
        return pltpu.make_async_copy(masters[i], hbm_out[i], out_sem.at[i])

    for i in LAMB_ORDER:
        for j in (0, 1):
            fetch(i, j).start()
    rate = 0.3 * table_ref[0:1, :] / table_ref[1:2, :]
    gp_out[...] = g_master[...] - rate[:, 5:6] * g_step[...]
    for i in LAMB_ORDER:
        down, across, _, _ = tiles_of(masters[i])
        scale = rate[:, i : i + 1]
        for j in (0, 1):
            fetch(i, j).wait()

        def body(n, carry):
            at = tile_at(masters[i], n)
            masters[i][at] = masters[i][at] - scale * steps[i][at]
            return carry

        lax.fori_loop(0, down * across, body, 0)
        store(i).start()
    for i in LAMB_ORDER:
        store(i).wait()


def lamb_step(reps, count, sums, grad_down, gains, states, collective_id):
    dma = pltpu.SemaphoreType.DMA
    f32 = jnp.float32
    shape = jax.ShapeDtypeStruct
    shapes = [state[0].shape for state in states]
    like_gains = shape(gains[0].shape, f32)
    tile = shape((8, 128), f32)
    vm, hb = pl.BlockSpec(memory_space=VM), pl.BlockSpec(memory_space=HB)
    local = pltpu.CompilerParams(vmem_limit_bytes=VMEM_LIMIT)
    outs = pl.pallas_call(
        functools.partial(lamb_kernel, reps, count),
        out_shape=[tile] + [like_gains] * 4 + [shape(item, f32) for item in shapes for _ in range(4)],
        in_specs=[vm] * 7 + [hb] * 16,
        out_specs=[vm] * 5 + [hb] * 20,
        scratch_shapes=[pltpu.VMEM(item, f32) for _ in range(4) for item in shapes] + [dma((5, 3)), dma((5, 4)), dma],
        compiler_params=local,
        name="lamb_moments",
    )(*sums, *gains, *[item for state in states for item in state], grad_down)
    sums, gain_parts, parts = outs[0], outs[1:5], [outs[5 + 4 * i : 9 + 4 * i] for i in range(5)]
    sizes = [item[0] * item[1] * reps * count for item in shapes + [like_gains.shape]]
    table = pl.pallas_call(
        functools.partial(table_kernel, reps, count, sizes),
        out_shape=tile,
        in_specs=[vm],
        out_specs=vm,
        scratch_shapes=[
            pltpu.VMEM((count, 8, 128), f32),
            pltpu.VMEM((reps, 8, 128), f32),
            pltpu.VMEM((8, 128), f32),
            dma((count,)),
            dma((count,)),
            dma((reps,)),
            dma((reps,)),
        ],
        compiler_params=pltpu.CompilerParams(collective_id=collective_id, has_side_effects=True),
        name="norm_table",
    )(sums)
    fresh = pl.pallas_call(
        fresh_kernel,
        out_shape=[like_gains] + [shape(item, f32) for item in shapes],
        in_specs=[vm] * 3 + [hb] * 10,
        out_specs=[vm] + [hb] * 5,
        scratch_shapes=[pltpu.VMEM(item, f32) for _ in range(2) for item in shapes] + [dma((5, 2)), dma((5,))],
        compiler_params=local,
        name="lamb_masters",
    )(table, gains[0], gain_parts[3], *[item for i in range(5) for item in (states[i][0], parts[i][3])])
    rest = [[parts[i][j] for i in range(5)] + [gain_parts[j]] for j in range(3)]
    return table[:2, :6], rest[0], rest[1], rest[2], list(fresh[1:]) + [fresh[0]]


def split_device(
    tokens, cotangent, piece_starts, inproj, outproj, ffn_gate, ffn_up, ffn_down, norm_gains,
    mean_inproj, mean_outproj, mean_gate, mean_up, mean_down, mean_gains,
    square_inproj, square_outproj, square_gate, square_up, square_down, square_gains,
):
    bf16, f32 = jnp.bfloat16, jnp.float32
    reps, count = lax.axis_size("rep"), lax.axis_size("shard")
    rep = lax.axis_index("rep")
    me = lax.axis_index("shard")
    total = reps * count
    rows, width = tokens.shape
    seq_len = rows * count
    group = HEADS // KV_HEADS
    q_width, k_width = HEADS * HEAD_DIM, KV_HEADS * HEAD_DIM
    d_rows = inproj.shape[0]
    ff = ffn_gate.shape[1]
    ff_block = ff // total
    ff_part = ff // count
    o_rows = outproj.shape[0]
    per_head = HEAD_DIM // o_rows
    piece = o_rows // reps

    cut_in, cut_gate, cut_up = cut_weights(reps, count, inproj, ffn_gate, ffn_up)
    cut_out = outproj.astype(bf16).reshape(reps, piece, width)
    gain_tile = jnp.pad(norm_gains.astype(bf16).astype(f32).T, ((0, 4), (0, 128 - d_rows)))
    normed_in, gain_rows, got_in, got_gate, got_down, got_out = opening(
        reps, count, tokens, gain_tile, cut_in, cut_gate, ffn_down.astype(bf16), cut_out, 1
    )
    normed_in = normed_in.reshape(seq_len, width)
    w_in = got_in.reshape(width, -1)
    w_gate = got_gate.reshape(width, ff_part)
    w_down = got_down.reshape(ff_part, width)
    w_out = got_out.transpose(1, 0, 2, 3).reshape(HEAD_DIM, width)

    half = HEAD_DIM // 2
    position = jnp.arange(seq_len, dtype=jnp.int32)
    freq = 10000.0 ** (-(jnp.arange(half, dtype=f32) * 2.0 / HEAD_DIM))
    angle = position.astype(f32)[:, None] * freq[None, :]
    cosine, sine = jnp.cos(angle), jnp.sin(angle)
    starts = lax.dynamic_slice_in_dim(piece_starts, rep, 1, 0)[0]
    inside = (position[:, None] >= starts[None, :]) & (position[:, None] < starts[None, :] + PIC)
    tag = jnp.sum(inside.astype(jnp.int32) * (jnp.arange(starts.shape[0], dtype=jnp.int32)[None, :] + 1), axis=1)
    attn_proj, queries, keys, values, attended, probs, damp, got_up = attention(
        reps, count, normed_in, w_in, w_out, cosine, sine, tag, cut_up, 4
    )
    w_up = got_up.reshape(width, ff_part)

    layer_out, d_middle, d_attn, gain_terms, normed_mid, hidden, d_ffn, d_gu = feed_forward(
        attn_proj, tokens, cotangent, gain_rows, w_gate, w_up, w_down, count, 5
    )
    d_attn, sum_gu, grad_down = ffn_grads(
        reps, count, d_attn, normed_mid, hidden, d_ffn, d_gu, d_rows, 9
    )
    d_attn = d_attn.reshape(seq_len, width)
    input_grad, sum_in, sum_out, gain_tiles = closing(
        reps, count, d_attn, normed_in, w_in, w_out, queries, keys, values, attended, probs, damp, cosine, sine,
        tokens, d_middle, gain_rows, gain_terms, piece, 12,
    )
    norm_table, gradients, new_means, new_squares, fresh = lamb_step(
        reps,
        count,
        (sum_in, sum_out, sum_gu, gain_tiles),
        grad_down,
        (norm_gains, mean_gains, square_gains),
        (
            (inproj, mean_inproj, square_inproj),
            (outproj, mean_outproj, square_outproj),
            (ffn_gate, mean_gate, square_gate),
            (ffn_up, mean_up, square_up),
            (ffn_down, mean_down, square_down),
        ),
        14,
    )
    return (
        layer_out,
        input_grad,
        *gradients,
        *new_means,
        *new_squares,
        *fresh,
        norm_table,
    )


def fits(mesh, shapes):
    reps, count = mesh.shape["rep"], mesh.shape["shard"]
    total = reps * count
    tokens, piece_starts, outproj, ffn_gate = shapes
    o_rows = outproj[0] // total
    return (
        reps == 4
        and count == HEADS
        and piece_starts[0] == reps
        and tokens[0] % (total * UNITS * 16) == 0
        and HEAD_DIM % o_rows == 0
        and o_rows % (16 * reps) == 0
        and HEAD_DIM // o_rows == total // HEADS
        and ffn_gate[1] % (total * 96) == 0
    )


def solution(mesh):
    split = P(("rep", "shard"), None)

    def step(*args):
        shapes = args[0].shape, args[2].shape, args[4].shape, args[5].shape
        body = split_device if fits(mesh, shapes) else per_device
        return jax.shard_map(
            body,
            mesh=mesh,
            in_specs=(split, split, P()) + (split,) * 18,
            out_specs=(split,) * 26 + (P(),),
            check_vma=False,
        )(*args)

    return step
```

```python
import functools

import jax
import jax.numpy as jnp
from jax import lax
from jax.experimental import pallas as pl
from jax.experimental.pallas import tpu as pltpu
import numpy as np
from jax.sharding import PartitionSpec as P

HEADS = 8
KV_HEADS = 4
HEAD_DIM = 256
PIC = 256


def rms_norm(values_in, gain_col):
    return (
        values_in
        * lax.rsqrt(jnp.mean(values_in * values_in, axis=-1, keepdims=True) + 1e-06)
        * (1.0 + gain_col)
    )


def geglu(gate_lin, up_lin):
    return jax.nn.gelu(gate_lin, approximate=True) * up_lin


def rotate(flat, position, head_count, sign):
    row_count = flat.shape[0]
    width = flat.shape[1] // head_count
    half = width // 2
    vectors = flat.reshape(row_count, head_count, width)
    freq = 10000.0 ** (-(jnp.arange(half, dtype=jnp.float32) * 2.0 / width))
    angle = position.astype(jnp.float32)[:, None] * freq[None, :]
    cosine = jnp.cos(angle)[:, None, :]
    sine = sign * jnp.sin(angle)[:, None, :]
    first = vectors[..., :half]
    second = vectors[..., half:]
    turned = jnp.concatenate(
        [first * cosine - second * sine, second * cosine + first * sine], axis=-1
    )
    return turned.reshape(row_count, head_count * width)


def owned_rows(activation, gradient, rep_index, width):
    piece = lax.dynamic_slice_in_dim(activation, rep_index * width, width, 1)
    return lax.dot_general(
        piece, gradient, (((0,), (0,)), ((), ())), preferred_element_type=jnp.float32
    )


def back_dot(gradient, weight):
    return lax.dot_general(
        gradient, weight, (((1,), (1,)), ((), ())), preferred_element_type=jnp.float32
    )


def describe(rows, piece_starts, seq_offset, seq_len):
    local_seq = rows // seq_len
    position = rows % seq_len
    global_seq = local_seq + seq_offset
    seq_total = piece_starts.shape[0]
    piece_count = piece_starts.shape[1]
    select = (global_seq[:, None] == jnp.arange(seq_total, dtype=jnp.int32)[None, :]).astype(
        jnp.int32
    )
    starts = jnp.sum(select[:, :, None] * piece_starts[None, :, :], axis=1)
    inside = ((position[:, None] >= starts) & (position[:, None] < starts + PIC)).astype(jnp.int32)
    labels = (
        global_seq[:, None] * piece_count + jnp.arange(piece_count, dtype=jnp.int32)[None, :] + 1
    )
    return (local_seq, position, jnp.sum(inside * labels, axis=1))


def visibility(piece_starts, query_rows, key_rows, seq_offset, seq_len):
    seq_q, pos_q, tag_q = describe(query_rows, piece_starts, seq_offset, seq_len)
    seq_k, pos_k, tag_k = describe(key_rows, piece_starts, seq_offset, seq_len)
    causal = pos_k[None, :] <= pos_q[:, None]
    same_piece = (tag_q[:, None] == tag_k[None, :]) & (tag_q[:, None] > 0)
    return (seq_q[:, None] == seq_k[None, :]) & (causal | same_piece)


def lamb_local(master, gradient, first, second):
    newmean = 0.5 * first + 0.5 * gradient
    newsquare = 0.5 * second + 0.5 * gradient * gradient
    step_dir = newmean / (jnp.sqrt(newsquare) + 1e-06) + 0.01 * master
    return (newmean, newsquare, step_dir)


def per_device(
    tokens,
    cotangent,
    piece_starts,
    inproj,
    outproj,
    ffn_gate,
    ffn_up,
    ffn_down,
    norm_gains,
    mean_inproj,
    mean_outproj,
    mean_gate,
    mean_up,
    mean_down,
    mean_gains,
    square_inproj,
    square_outproj,
    square_gate,
    square_up,
    square_down,
    square_gains,
):
    bf16 = jnp.bfloat16
    f32 = jnp.float32
    rep_count = lax.axis_size("rep")
    shard_count = lax.axis_size("shard")
    rep_index = lax.axis_index("rep")
    w_in, w_out, w_gate, w_up, w_down, gain_copy = (
        lax.all_gather(inproj.astype(bf16), ("rep", "shard"), axis=0, tiled=True),
        lax.all_gather(outproj.astype(bf16), ("rep", "shard"), axis=0, tiled=True),
        lax.all_gather(ffn_gate.astype(bf16), ("rep", "shard"), axis=0, tiled=True),
        lax.all_gather(ffn_up.astype(bf16), ("rep", "shard"), axis=0, tiled=True),
        lax.all_gather(ffn_down.astype(bf16), ("rep", "shard"), axis=0, tiled=True),
        lax.all_gather(norm_gains.astype(bf16), ("rep", "shard"), axis=0, tiled=True),
    )
    gains_used = gain_copy.astype(f32)
    residual = tokens.astype(f32)
    row_count = residual.shape[0]
    seq_len = row_count * shard_count
    q_width = HEADS * HEAD_DIM
    k_width = KV_HEADS * HEAD_DIM
    group_size = HEADS // KV_HEADS
    query_scale = HEAD_DIM ** (-0.5)
    local_rows = lax.axis_index("shard") * row_count + jnp.arange(row_count, dtype=jnp.int32)
    position = local_rows % seq_len
    normed_in = rms_norm(residual, gains_used[:, 0]).astype(bf16)
    projected = jnp.dot(normed_in, w_in, preferred_element_type=f32)
    queries = (rotate(projected[:, :q_width], position, HEADS, 1.0) * query_scale).astype(bf16)
    keys = rotate(projected[:, q_width : q_width + k_width], position, KV_HEADS, 1.0).astype(bf16)
    values = projected[:, q_width + k_width :].astype(bf16)
    all_keys, all_values = (
        lax.all_gather(keys, "shard", axis=0, tiled=True),
        lax.all_gather(values, "shard", axis=0, tiled=True),
    )
    key_rows = all_keys.shape[0]
    visible = visibility(
        piece_starts,
        local_rows,
        jnp.arange(key_rows, dtype=jnp.int32),
        rep_index * (key_rows // seq_len),
        seq_len,
    )
    query_heads = queries.reshape(row_count, KV_HEADS, group_size, HEAD_DIM)
    key_heads = all_keys.reshape(key_rows, KV_HEADS, HEAD_DIM)
    value_heads = all_values.reshape(key_rows, KV_HEADS, HEAD_DIM)

    def capped_scores():
        raw_scores = jnp.einsum(
            "tgrd,kgd->grtk", query_heads, key_heads, preferred_element_type=f32
        )
        bent_scores = jnp.tanh(raw_scores / 50.0)
        return (bent_scores, jnp.where(visible, 50.0 * bent_scores, -1e30))

    bent_scores, masked = capped_scores()
    top_score = jnp.max(masked, axis=-1, keepdims=True)
    log_total = top_score + jnp.log(jnp.sum(jnp.exp(masked - top_score), axis=-1, keepdims=True))
    probs_low = jnp.exp(masked - log_total).astype(bf16)
    attended = (
        jnp.einsum("grtk,kgd->tgrd", probs_low, value_heads, preferred_element_type=f32)
        .reshape(row_count, q_width)
        .astype(bf16)
    )
    attn_proj = jnp.dot(attended, w_out, preferred_element_type=f32)
    middle = residual + rms_norm(attn_proj, gains_used[:, 1])
    normed_mid = rms_norm(middle, gains_used[:, 2]).astype(bf16)
    gate_lin = jnp.dot(normed_mid, w_gate, preferred_element_type=f32)
    up_lin = jnp.dot(normed_mid, w_up, preferred_element_type=f32)
    hidden = geglu(gate_lin, up_lin).astype(bf16)
    ffn_proj = jnp.dot(hidden, w_down, preferred_element_type=f32)
    layer_out = (middle + rms_norm(ffn_proj, gains_used[:, 3])).astype(bf16)
    d_out = cotangent.astype(f32)
    _, post_back = jax.vjp(rms_norm, ffn_proj, gains_used[:, 3])
    d_ffn, d_gain3 = post_back(d_out)
    d_ffn_low = d_ffn.astype(bf16)
    hidden_all, d_ffn_all = (
        lax.all_gather(hidden, "rep", axis=0, tiled=True),
        lax.all_gather(d_ffn_low, "rep", axis=0, tiled=True),
    )
    part_down = owned_rows(hidden_all, d_ffn_all, rep_index, hidden.shape[1] // rep_count)
    d_hidden = back_dot(d_ffn_low, w_down)
    _, glu_back = jax.vjp(geglu, gate_lin, up_lin)
    d_gate, d_up = glu_back(d_hidden)
    d_gate_low = d_gate.astype(bf16)
    d_up_low = d_up.astype(bf16)
    gate_up_grad = jnp.concatenate([d_gate_low, d_up_low], axis=1)
    mid_all, gate_up_all = (
        lax.all_gather(normed_mid, "rep", axis=0, tiled=True),
        lax.all_gather(gate_up_grad, "rep", axis=0, tiled=True),
    )
    part_gate_up = owned_rows(mid_all, gate_up_all, rep_index, normed_mid.shape[1] // rep_count)
    d_mid_in = back_dot(d_gate_low, w_gate) + back_dot(d_up_low, w_up)
    _, pre_back = jax.vjp(rms_norm, middle, gains_used[:, 2])
    d_mid_part, d_gain2 = pre_back(d_mid_in)
    d_middle = d_out + d_mid_part
    _, attn_back = jax.vjp(rms_norm, attn_proj, gains_used[:, 1])
    d_attn, d_gain1 = attn_back(d_middle)
    d_attn_low = d_attn.astype(bf16)
    d_attended = back_dot(d_attn_low, w_out).astype(bf16)
    d_heads = d_attended.reshape(row_count, KV_HEADS, group_size, HEAD_DIM)
    bent_again, masked_again = capped_scores()
    attn_probs = jnp.exp(masked_again - log_total)
    probs_again = attn_probs.astype(bf16)
    d_probs = jnp.einsum("tgrd,kgd->grtk", d_heads, value_heads, preferred_element_type=f32)
    d_scores = (
        attn_probs
        * (d_probs - jnp.sum(attn_probs * d_probs, axis=-1, keepdims=True))
        * (1.0 - bent_again * bent_again)
    ).astype(bf16)
    d_queries = jnp.einsum(
        "grtk,kgd->tgrd", d_scores, key_heads, preferred_element_type=f32
    ).reshape(row_count, q_width)
    d_key = jnp.einsum("grtk,tgrd->kgd", d_scores, query_heads, preferred_element_type=f32).reshape(
        row_count * lax.axis_size("shard"), k_width
    )
    d_value = jnp.einsum(
        "grtk,tgrd->kgd", probs_again, d_heads, preferred_element_type=f32
    ).reshape(row_count * lax.axis_size("shard"), k_width)
    d_key_value = lax.psum_scatter(
        jnp.concatenate([d_key, d_value], axis=1), "shard", scatter_dimension=0, tiled=True
    )
    d_projected = jnp.concatenate(
        [
            rotate(d_queries, position, HEADS, -1.0) * query_scale,
            rotate(d_key_value[:, :k_width], position, KV_HEADS, -1.0),
            d_key_value[:, k_width:],
        ],
        axis=1,
    ).astype(bf16)
    d_normed_in = back_dot(d_projected, w_in)
    _, first_back = jax.vjp(rms_norm, residual, gains_used[:, 0])
    d_input_part, d_gain0 = first_back(d_normed_in)
    input_grad = d_middle + d_input_part
    gain_grad = jnp.stack([d_gain0, d_gain1, d_gain2, d_gain3], axis=1)
    attended_all, d_attn_all, normed_all, d_proj_all = (
        lax.all_gather(attended, "rep", axis=0, tiled=True),
        lax.all_gather(d_attn_low, "rep", axis=0, tiled=True),
        lax.all_gather(normed_in, "rep", axis=0, tiled=True),
        lax.all_gather(d_projected, "rep", axis=0, tiled=True),
    )
    part_out = owned_rows(attended_all, d_attn_all, rep_index, attended.shape[1] // rep_count)
    part_in = owned_rows(normed_all, d_proj_all, rep_index, normed_in.shape[1] // rep_count)
    part_gain = lax.psum_scatter(gain_grad, "rep", scatter_dimension=0, tiled=True)
    owned = (
        lax.psum_scatter(part_in, "shard", scatter_dimension=0, tiled=True),
        lax.psum_scatter(part_gain, "shard", scatter_dimension=0, tiled=True),
        lax.psum_scatter(part_out, "shard", scatter_dimension=0, tiled=True),
        lax.psum_scatter(part_gate_up, "shard", scatter_dimension=0, tiled=True),
        lax.psum_scatter(part_down, "shard", scatter_dimension=0, tiled=True),
    )
    grad_inproj, grad_gains, grad_outproj, grad_gate_up, grad_down = owned
    split_at = grad_gate_up.shape[1] // 2
    grad_gate = grad_gate_up[:, :split_at]
    grad_up = grad_gate_up[:, split_at:]
    masters = (inproj, outproj, ffn_gate, ffn_up, ffn_down, norm_gains)
    gradients = (grad_inproj, grad_outproj, grad_gate, grad_up, grad_down, grad_gains)
    firsts = (mean_inproj, mean_outproj, mean_gate, mean_up, mean_down, mean_gains)
    seconds = (square_inproj, square_outproj, square_gate, square_up, square_down, square_gains)
    results = [
        lamb_local(masters[index], gradients[index], firsts[index], seconds[index])
        for index in range(6)
    ]
    weight_sums = jnp.stack([jnp.sum(master * master) for master in masters])
    step_sums = jnp.stack([jnp.sum(item[2] * item[2]) for item in results])
    totals = lax.psum(jnp.stack([weight_sums, step_sums]), ("rep", "shard"))
    counts = jnp.array([float(master.size * rep_count * shard_count) for master in masters], f32)
    norm_table = jnp.sqrt(totals / counts[None, :] + 1e-06)
    fresh = [
        masters[index] - 0.3 * norm_table[0, index] / norm_table[1, index] * results[index][2]
        for index in range(6)
    ]
    return (
        layer_out,
        input_grad,
        grad_inproj,
        grad_outproj,
        grad_gate,
        grad_up,
        grad_down,
        grad_gains,
        results[0][0],
        results[1][0],
        results[2][0],
        results[3][0],
        results[4][0],
        results[5][0],
        results[0][1],
        results[1][1],
        results[2][1],
        results[3][1],
        results[4][1],
        results[5][1],
        fresh[0],
        fresh[1],
        fresh[2],
        fresh[3],
        fresh[4],
        fresh[5],
        norm_table,
    )


MESH = pl.DeviceIdType.MESH
VM = pltpu.VMEM
HB = pl.ANY
UNITS = 4
VMEM_LIMIT = 60 << 20


def ring_places(count):
    inner = 2 if count == 8 else 4
    outer = count // inner

    def place(shard):
        major = shard // inner
        minor = shard % inner
        return minor * outer + major + (minor % 2) * (outer - 1 - 2 * major)

    def shard_at(spot):
        minor = spot // outer
        major = spot % outer
        return (major + (minor % 2) * (outer - 1 - 2 * major)) * inner + minor

    return place, shard_at


def meet(devices):
    barrier = pltpu.get_barrier_semaphore()
    for device in devices:
        pl.semaphore_signal(barrier, inc=1, device_id=device, device_id_type=MESH)
    pl.semaphore_wait(barrier, len(devices))


def remote(src, dst, send_sem, recv_sem, device):
    return pltpu.make_async_remote_copy(
        src_ref=src,
        dst_ref=dst,
        send_sem=send_sem,
        recv_sem=recv_sem,
        device_id=device,
        device_id_type=MESH,
    )


class Ring:
    def __init__(self, count):
        place, shard_at = ring_places(count)
        self.count = count
        self.half = count // 2
        self.rep = lax.axis_index("rep")
        self.me = lax.axis_index("shard")
        self.spot = place(self.me)
        self.shard_at = shard_at
        self.next = [(self.rep, self.at(1)), (self.rep, self.at(count - 1))]

    def at(self, ahead):
        return self.shard_at((self.spot + ahead) % self.count)

    def away(self, way, hops):
        return self.at(hops if way == 0 else self.count - hops)

    def units(self, way, hop):
        order = list(range(UNITS)) if way == 0 else list(range(UNITS))[::-1]
        return order if hop < self.half else order[: UNITS // 2]


def reduce_on_ring(ring, rows, take, first, landed, send, recv, finish, pause):
    f32 = jnp.float32
    hops = ring.half
    started = []

    def part(unit):
        return pl.ds(unit * (rows // UNITS), rows // UNITS)

    def step_copy(way, step, unit):
        return remote(
            landed.at[way, step - 1, part(unit)] if step else first.at[part(unit)],
            landed.at[way, step, part(unit)],
            send.at[way, step, unit],
            recv.at[way, step, unit],
            ring.next[way],
        )

    for step in range(hops):
        order = ring.units(0, hops - step), ring.units(1, hops - step)
        before = [ring.units(way, hops - step + 1) if step else [] for way in (0, 1)]
        for index in range(len(order[0])):
            for way in (0, 1):
                unit = order[way][index]
                block = take(ring.away(way, hops - step), part(unit)).astype(f32)
                if unit in before[way]:
                    step_copy(way, step - 1, unit).wait_recv()
                    block += landed[way, step - 1, part(unit), :].astype(f32)
                if step:
                    landed[way, step - 1, part(unit), :] = block.astype(landed.dtype)
                else:
                    first[part(unit), :] = block.astype(first.dtype)
                copy = step_copy(way, step, unit)
                copy.start()
                started.append(copy)
            if step or index == len(order[0]) - 1:
                pause()
    for unit in range(UNITS):
        total = take(ring.me, part(unit)).astype(f32)
        for way in (0, 1):
            step_copy(way, hops - 1, unit).wait_recv()
            total += landed[way, hops - 1, part(unit), :].astype(f32)
        finish(part(unit), total)
    return started


class Flow:
    def __init__(self, ring, rows, send, recv):
        self.ring, self.rows, self.send, self.recv = ring, rows, send, recv
        self.unit_rows = rows // UNITS
        self.started = []

    def span(self, slot, unit):
        return pl.ds(slot * self.rows + unit * self.unit_rows, self.unit_rows)

    def slot(self, way, hops):
        if hops == 0:
            return 0
        return self.ring.count - 1 if hops == self.ring.half else 2 * hops - 1 + way

    def go(self, copy):
        copy.start()
        self.started.append(copy)

    def finish(self):
        for copy in self.started:
            copy.wait_send()

    def gather_copy(self, buffer, way, hop, unit):
        return remote(
            buffer.at[self.span(self.slot(way, hop - 1), unit)],
            buffer.at[self.span(self.slot(way, hop), unit)],
            self.send.at[way, hop - 1, unit],
            self.recv.at[way, hop - 1, unit],
            self.ring.next[way],
        )

    def gather(self, buffer, group_work):
        ring = self.ring
        for index in range(UNITS):
            for way in (0, 1):
                self.go(self.gather_copy(buffer, way, 1, ring.units(way, 1)[index]))
        queue = list(group_work(0, 1))
        for hop in range(1, ring.half + 1):
            length = len(ring.units(0, hop))
            for index in range(length):
                for way in (0, 1):
                    unit = ring.units(way, hop)[index]
                    self.gather_copy(buffer, way, hop, unit).wait_recv()
                    if hop < ring.half and unit in ring.units(way, hop + 1):
                        self.go(self.gather_copy(buffer, way, hop + 1, unit))
                if queue:
                    queue.pop(0)()
            for piece in queue:
                piece()
            queue = list(group_work(2 * hop - 1, 2) if hop < ring.half else group_work(ring.count - 1, 1))
        for piece in queue:
            piece()
        self.finish()

    def reduce_copy(self, first, landed, way, step, unit):
        span = pl.ds(unit * self.unit_rows, self.unit_rows)
        src = first.at[span] if step == 0 else landed.at[way, step - 1, span]
        return remote(
            src,
            landed.at[way, step, span],
            self.send.at[way, step, unit],
            self.recv.at[way, step, unit],
            self.ring.next[way],
        )

    def reduce(self, first, landed, partial, group_work, finish, extra=()):
        extra = list(extra)
        ring = self.ring
        hops = ring.half
        f32 = jnp.float32
        for piece in group_work(ring.count - 1, 1, 0):
            piece()
        queue = list(group_work(2 * (hops - 1) - 1, 2, 1))
        for step in range(hops):
            order = ring.units(0, hops - step), ring.units(1, hops - step)
            before = [ring.units(way, hops - step + 1) if step else [] for way in (0, 1)]
            for index in range(len(order[0])):
                for way in (0, 1):
                    unit = order[way][index]
                    span = pl.ds(unit * self.unit_rows, self.unit_rows)
                    if step == 0:
                        first[span, :] = partial[0, pl.ds(unit * self.unit_rows, self.unit_rows), :].astype(first.dtype)
                    else:
                        side = 1 - way
                        block = partial[
                            step % 2, pl.ds(side * self.rows + unit * self.unit_rows, self.unit_rows), :
                        ]
                        if unit in before[way]:
                            self.reduce_copy(first, landed, way, step - 1, unit).wait_recv()
                            block = block + landed[way, step - 1, span, :].astype(f32)
                        landed[way, step - 1, span, :] = block.astype(landed.dtype)
                    self.go(self.reduce_copy(first, landed, way, step, unit))
                if queue:
                    queue.pop(0)()
                elif extra:
                    extra.pop(0)()
            for piece in queue:
                piece()
            ahead = hops - step - 2
            queue = []
            if step < hops - 1:
                queue = list(group_work(2 * ahead - 1, 2, step % 2) if ahead > 0 else group_work(0, 1, step % 2))
        for piece in extra:
            piece()
        for unit in range(UNITS):
            span = pl.ds(unit * self.unit_rows, self.unit_rows)
            total = partial[hops % 2, span, :]
            for way in (0, 1):
                self.reduce_copy(first, landed, way, hops - 1, unit).wait_recv()
                total = total + landed[way, hops - 1, span, :].astype(f32)
            finish(unit, total)
        self.finish()


def looped(piece, count):
    def all_of_it():
        def body(j, carry):
            piece(j)
            return carry

        lax.fori_loop(0, count, body, 0)

    return [all_of_it]


def gelu_pair(gate):
    inner = 0.7978845608028654 * (gate + 0.044715 * gate * gate * gate)
    bend = jnp.tanh(inner)
    value = 0.5 * gate * (1.0 + bend)
    slope = 0.5 * (1.0 + bend) + 0.5 * gate * (1.0 - bend * bend) * 0.7978845608028654 * (
        1.0 + 0.134145 * gate * gate
    )
    return value, slope


def ffn_kernel(
    count, attn_ref, tokens_ref, cot_ref, gains_ref, gate_hbm, up_hbm, dn_hbm,
    layer_ref, dmid_ref, dattn_ref, gg_ref, h3_hbm, dgu_hbm, part_hbm,
    gate_ref, up_ref, dn_ref, h3_ref, hid_ref, dffn_ref, dgu_ref,
    lin, partial, first, landed, middle, total_ref, s1, r1, s2, r2, s3, r3, s4, r4, loads, stores,
):
    f32, bf16 = jnp.float32, jnp.bfloat16
    ring = Ring(count)
    rows, width = attn_ref.shape
    part = hid_ref.shape[1]
    tile = part // 3
    wide = width // 3
    fetched = [
        pltpu.make_async_copy(src, dst, loads.at[index])
        for index, (src, dst) in enumerate(((gate_hbm, gate_ref), (up_hbm, up_ref), (dn_hbm, dn_ref)))
    ]
    for copy in fetched:
        copy.start()
    kept = []

    def keep_out(src, dst):
        copy = pltpu.make_async_copy(src, dst, stores.at[len(kept)])
        copy.start()
        kept.append(copy)

    meet(ring.next)

    def gain(index):
        return 1.0 + gains_ref[index : index + 1, :]

    def scale_of(value):
        return lax.rsqrt(jnp.mean(value * value, axis=-1, keepdims=True) + 1e-06)

    half = rows // 2
    halves = [pl.ds(0, half), pl.ds(half, half)]
    for span in halves:
        proj = attn_ref[span, :]
        mid = tokens_ref[span, :].astype(f32) + proj * scale_of(proj) * gain(1)
        middle[span, :] = mid
        h3_ref[span, :] = (mid * scale_of(mid) * gain(2)).astype(bf16)

    def lin_work(slot, blocks):
        at = pl.ds(slot * rows, blocks * rows)

        def piece(j):
            lo = pl.ds(pl.multiple_of(j * tile, 128), tile)
            hi = pl.ds(pl.multiple_of(part + j * tile, 128), tile)
            gate = jnp.dot(h3_ref[at, :], gate_ref[:, lo], preferred_element_type=f32)
            up = jnp.dot(h3_ref[at, :], up_ref[:, lo], preferred_element_type=f32)
            value, slope = gelu_pair(gate)
            hid_ref[at, lo] = (value * up).astype(bf16)
            lin[at, lo] = (up * slope).astype(bf16)
            lin[at, hi] = value.astype(bf16)

        return looped(piece, 3)

    def down_work(slot, blocks, side):
        at = pl.ds(slot * rows, blocks * rows)

        def piece(j):
            cols = pl.ds(pl.multiple_of(j * wide, 128), wide)
            partial[side, pl.ds(0, blocks * rows), cols] = jnp.dot(
                hid_ref[at, :], dn_ref[:, cols], preferred_element_type=f32
            )

        return looped(piece, 3)

    def nt(left, right):
        return lax.dot_general(left, right, (((1,), (1,)), ((), ())), preferred_element_type=f32)

    def back_work(slot, blocks):
        at = pl.ds(slot * rows, blocks * rows)

        def piece(j):
            lo = pl.ds(pl.multiple_of(j * tile, 128), tile)
            hi = pl.ds(pl.multiple_of(part + j * tile, 128), tile)
            d_hidden = nt(dffn_ref[at, :], dn_ref[lo, :])
            dgu_ref[at, lo] = (d_hidden * lin[at, lo].astype(f32)).astype(bf16)
            dgu_ref[at, hi] = (d_hidden * lin[at, hi].astype(f32)).astype(bf16)

        return looped(piece, 3)

    def input_work(slot, blocks, side):
        at = pl.ds(slot * rows, blocks * rows)

        def piece(j):
            cols = pl.ds(pl.multiple_of(j * wide, 128), wide)
            partial[side, pl.ds(0, blocks * rows), cols] = nt(dgu_ref[at, :part], gate_ref[cols, :]) + nt(
                dgu_ref[at, part:], up_ref[cols, :]
            )

        return looped(piece, 3)

    def keep(unit, total):
        total_ref[pl.ds(unit * (rows // UNITS), rows // UNITS), :] = total

    def lin_first(slot, blocks):
        work = lin_work(slot, blocks)
        return [lambda: (fetched[0].wait(), fetched[1].wait())] + work if slot == 0 else work

    Flow(ring, rows, s1, r1).gather(h3_ref, lin_first)
    keep_out(h3_ref, h3_hbm)
    fetched[2].wait()
    Flow(ring, rows, s2, r2).reduce(first, landed, partial, down_work, keep)

    def back_norm(value, index, grad):
        scale = scale_of(value)
        normed = value * scale
        weighted = grad * gain(index)
        inner = jnp.mean(weighted * normed, axis=-1, keepdims=True)
        return scale * (weighted - normed * inner), jnp.sum(grad * normed, axis=0, keepdims=True)

    gg = jnp.zeros((1, width), f32)
    for span in halves:
        proj = total_ref[span, :]
        scale = scale_of(proj)
        layer_ref[span, :] = (middle[span, :] + proj * scale * gain(3)).astype(bf16)
        d_ffn, term = back_norm(proj, 3, cot_ref[span, :].astype(f32))
        gg += term
        dffn_ref[span, :] = d_ffn.astype(bf16)
    gg_ref[3:4, :] = gg

    Flow(ring, rows, s3, r3).gather(dffn_ref, back_work)
    keep_out(dgu_ref, dgu_hbm)

    def make_down(j):
        span = pl.ds(j * tile, tile)

        def body(n, carry):
            cols = pl.ds(pl.multiple_of(n * wide, 128), wide)
            lin[span, cols] = tn(hid_ref[:, span], dffn_ref[:, cols]).astype(bf16)
            return carry

        lax.fori_loop(0, 3, body, 0)
        keep_out(lin.at[span, pl.ds(0, width)], part_hbm.at[span])

    Flow(ring, rows, s4, r4).reduce(
        first, landed, partial, input_work, keep, [functools.partial(make_down, j) for j in range(3)]
    )

    gg1 = jnp.zeros((1, width), f32)
    gg2 = jnp.zeros((1, width), f32)
    for span in halves:
        d_mid, term = back_norm(middle[span, :], 2, total_ref[span, :])
        gg2 += term
        d_mid = d_mid + cot_ref[span, :].astype(f32)
        dmid_ref[span, :] = d_mid
        d_attn, term = back_norm(attn_ref[span, :], 1, d_mid)
        gg1 += term
        dattn_ref[span, :] = d_attn.astype(bf16)
    gg_ref[1:2, :] = gg1
    gg_ref[2:3, :] = gg2
    gg_ref[0:1, :] = jnp.zeros((1, width), f32)
    gg_ref[4:8, :] = jnp.zeros((4, width), f32)
    for copy in kept:
        copy.wait()


def feed_forward(attn_proj, tokens, cotangent, gain_rows, w_gate, w_up, w_down, count, collective_id):
    f32, bf16 = jnp.float32, jnp.bfloat16
    rows, width = attn_proj.shape
    part = w_down.shape[0]
    every = rows * count
    dma = pltpu.SemaphoreType.DMA
    shape = jax.ShapeDtypeStruct
    return pl.pallas_call(
        functools.partial(ffn_kernel, count),
        out_shape=[
            shape((rows, width), bf16),
            shape((rows, width), f32),
            shape((rows, width), bf16),
            shape((8, width), f32),
            shape((every, width), bf16),
            shape((every, 2 * part), bf16),
            shape((part, width), bf16),
        ],
        in_specs=[pl.BlockSpec(memory_space=VM)] * 4 + [pl.BlockSpec(memory_space=HB)] * 3,
        out_specs=[pl.BlockSpec(memory_space=VM)] * 4 + [pl.BlockSpec(memory_space=HB)] * 3,
        scratch_shapes=[
            pltpu.VMEM(w_gate.shape, bf16),
            pltpu.VMEM(w_up.shape, bf16),
            pltpu.VMEM(w_down.shape, bf16),
            pltpu.VMEM((every, width), bf16),
            pltpu.VMEM((every, part), bf16),
            pltpu.VMEM((every, width), bf16),
            pltpu.VMEM((every, 2 * part), bf16),
            pltpu.VMEM((max(every, part), max(2 * part, width)), bf16),
            pltpu.VMEM((2, 2 * rows, width), f32),
            pltpu.VMEM((rows, width), bf16),
            pltpu.VMEM((2, count // 2, rows, width), bf16),
            pltpu.VMEM((rows, width), f32),
            pltpu.VMEM((rows, width), f32),
        ]
        + [dma((2, count // 2, UNITS))] * 8
        + [dma((3,)), dma((5,))],
        compiler_params=pltpu.CompilerParams(
            collective_id=collective_id, has_side_effects=True, vmem_limit_bytes=VMEM_LIMIT
        ),
        name="feed_forward",
    )(attn_proj, tokens, cotangent, gain_rows, w_gate, w_up, w_down)


def attention_kernel(
    reps, count, h1_ref, in_ref, got_ref, cos_ref, sin_ref, tagq_ref, tagk_ref, cut_ref,
    proj_ref, q_ref, k_ref, v_ref, att_ref, probs_ref, damp_ref, wo_ref, up_ref,
    part, first, landed, r_send, r_recv, w_sems, loc
):
    f32, bf16 = jnp.float32, jnp.bfloat16
    ring = Ring(count)
    rows = proj_ref.shape[0]
    seq_len = h1_ref.shape[0]
    tall = seq_len // 4
    half = HEAD_DIM // 2
    meet(near_devices(ring))
    weights = Fetch(ring, cut_ref, up_ref, w_sems)
    weights.begin()
    own = pltpu.make_async_copy(cut_ref.at[ring.me], up_ref.at[ring.rep, ring.me], loc)
    own.start()
    piece = got_ref.shape[2]
    for block in range(got_ref.shape[1]):
        for j in range(reps):
            start = (block * reps + j) * piece
            wo_ref[start : start + piece, :] = got_ref[j, block]

    def project(i, carry):
        at = pl.ds(pl.multiple_of(i * tall, 16), tall)
        flat = jnp.dot(h1_ref[at, :], in_ref[...], preferred_element_type=f32)
        cosine, sine = cos_ref[at, :], sin_ref[at, :]

        def turned(start):
            first, second = flat[:, start : start + half], flat[:, start + half : start + HEAD_DIM]
            return jnp.concatenate([first * cosine - second * sine, second * cosine + first * sine], axis=1)

        q_ref[at, :] = (turned(0) * HEAD_DIM ** (-0.5)).astype(bf16)
        k_ref[at, :] = turned(HEAD_DIM).astype(bf16)
        v_ref[at, :] = flat[:, 2 * HEAD_DIM :].astype(bf16)
        return carry

    lax.fori_loop(0, 4, project, 0)

    def attend(i, carry):
        at = pl.ds(pl.multiple_of(i * tall, 16), tall)
        raw = lax.dot_general(q_ref[at, :], k_ref[...], (((1,), (1,)), ((), ())), preferred_element_type=f32)
        bent = jnp.tanh(raw * (1.0 / 50.0))
        query_at = i * tall + lax.broadcasted_iota(jnp.int32, (tall, seq_len), 0)
        key_at = lax.broadcasted_iota(jnp.int32, (tall, seq_len), 1)
        tag = tagq_ref[at, :]
        visible = (key_at <= query_at) | ((tag == tagk_ref[...]) & (tag > 0))
        masked = jnp.where(visible, 50.0 * bent, -1e30)
        expo = jnp.exp(masked - jnp.max(masked, axis=-1, keepdims=True))
        probs = expo / jnp.sum(expo, axis=-1, keepdims=True)
        low = probs.astype(bf16)
        probs_ref[at, :] = low
        damp_ref[at, :] = (probs * (1.0 - bent * bent)).astype(bf16)
        attended = jnp.dot(low, v_ref[...], preferred_element_type=f32).astype(bf16)
        att_ref[at, :] = attended
        part[at, :] = jnp.dot(attended, wo_ref[...], preferred_element_type=f32)
        return carry

    lax.fori_loop(0, 4, attend, 0)

    work = weights.steps()

    def pause():
        for _ in range(min(2, len(work))):
            work.pop(0)()

    def finish(span, total):
        proj_ref[span, :] = total

    def take(shard, span):
        return part[pl.ds(pl.multiple_of(shard * rows + span.start, 16), span.size), :]

    started = reduce_on_ring(ring, rows, take, first, landed, r_send, r_recv, finish, pause)
    for piece in work:
        piece()
    weights.finish()
    own.wait()
    for copy in started:
        copy.wait_send()


def attention(reps, count, normed, w_in, w_out, cosine, sine, tag, cut_up, collective_id):
    dma = pltpu.SemaphoreType.DMA
    low, f32 = jnp.bfloat16, jnp.float32
    shape = jax.ShapeDtypeStruct
    seq_len, width = normed.shape
    rows = seq_len // count
    hops = count // 2
    head = shape((seq_len, HEAD_DIM), low)
    square = shape((seq_len, seq_len), low)
    return pl.pallas_call(
        functools.partial(attention_kernel, reps, count),
        out_shape=[
            shape((rows, width), f32), head, head, head, head, square, square, shape((HEAD_DIM, width), low),
            shape((reps,) + cut_up.shape, low),
        ],
        in_specs=[pl.BlockSpec(memory_space=VM)] * 7 + [pl.BlockSpec(memory_space=HB)],
        out_specs=[pl.BlockSpec(memory_space=VM)] * 8 + [pl.BlockSpec(memory_space=HB)],
        scratch_shapes=[
            pltpu.VMEM((seq_len, width), f32),
            pltpu.VMEM((rows, width), low),
            pltpu.VMEM((2, hops, rows, width), low),
            dma((2, hops, UNITS)),
            dma((2, hops, UNITS)),
            dma((8, count)),
            dma,
        ],
        compiler_params=pltpu.CompilerParams(
            collective_id=collective_id, has_side_effects=True, vmem_limit_bytes=VMEM_LIMIT
        ),
        name="attention",
    )(normed, w_in, w_out, cosine, sine, tag[:, None], tag[None, :], cut_up)


class Fetch:
    def __init__(self, ring, cut, out, sems):
        self.ring, self.cut, self.out = ring, cut, out
        self.rep, self.me, self.count = ring.rep, ring.me, ring.count
        self.across, self.beside = rep_partners(ring.rep)
        self.sems = sems
        self.started = []

    def go(self, copy):
        copy.start()
        self.started.append(copy)

    def spread(self, k):
        to = (self.me + k) % self.count
        return remote(
            self.cut.at[to], self.out.at[self.rep, self.me], self.sems.at[0, k], self.sems.at[1, k], (self.rep, to)
        )

    def arrived(self, k):
        frm = (self.me + self.count - k) % self.count
        return remote(
            self.cut.at[frm], self.out.at[self.rep, frm], self.sems.at[0, k], self.sems.at[1, k], (self.rep, frm)
        )

    def forward(self, k, hop):
        frm = (self.me + self.count - k) % self.count
        rep = self.across if hop == 2 else self.rep
        block = self.out.at[rep, frm] if k or hop == 2 else self.cut.at[self.me]
        to = self.across if hop == 0 else self.beside
        return remote(
            block,
            self.out.at[rep, frm],
            self.sems.at[2 + 2 * hop, k],
            self.sems.at[3 + 2 * hop, k],
            (to, self.me),
        )

    def pass_on(self, k):
        if k:
            self.arrived(k).wait_recv()
        self.go(self.forward(k, 0))
        self.go(self.forward(k, 1))

    def pass_beside(self, k):
        self.forward(k, 0).wait_recv()
        self.go(self.forward(k, 2))

    def begin(self):
        for k in range(1, self.count):
            self.go(self.spread(k))
        self.pass_on(0)

    def steps(self):
        work = [functools.partial(self.pass_on, k) for k in range(1, self.count)]
        return work + [functools.partial(self.pass_beside, k) for k in range(self.count)]

    def finish(self):
        for k in range(self.count):
            self.forward(k, 1).wait_recv()
            self.forward(k, 2).wait_recv()
        for copy in self.started:
            copy.wait_send()


def rep_partners(rep):
    return (rep + 2) % 4, rep + 1 - 2 * (rep % 2)


def everyone(rep, me, reps, count):
    here = rep * count + me
    total = reps * count
    return [
        (((here + k) % total) // count, ((here + k) % total) % count) for k in range(1, total)
    ]


def opening_kernel(
    reps, count, tok_ref, gain_ref, in_ref, gate_ref, dn_ref, ou_ref, h1_ref, gains_ref, w_in, w_gate, w_dn, w_ou,
    tok_all, gain_all, t_send, t_recv, g_send, g_recv, i_sems, u_sems, o_send, o_recv, n_send, n_recv, loc
):
    f32 = jnp.float32
    ring = Ring(count)
    rep, me = ring.rep, ring.me
    across, beside = rep_partners(rep)
    others = everyone(rep, me, reps, count)
    mine = rep * count + me
    d_rows = in_ref.shape[1]
    rows = tok_ref.shape[0]
    meet(others)
    started = []

    def go(copy):
        copy.start()
        started.append(copy)

    for k, device in enumerate(others):
        go(remote(gain_ref, gain_all.at[mine], g_send.at[k], g_recv.at[k], device))
    gain_all[mine] = gain_ref[...]
    ins = Fetch(ring, in_ref, w_in, i_sems)
    gates = Fetch(ring, gate_ref, w_gate, u_sems)
    gather = Gather(ring, tok_ref, tok_all, t_send, t_recv)
    ins.begin()
    gather.begin()

    per_head = count * reps // HEADS
    target = mine // per_head
    slot = mine % per_head

    def ou_copy(j):
        return remote(ou_ref.at[j], w_ou.at[j, slot], o_send.at[j], o_recv.at[slot], (j, target))

    def is_self(j):
        return (rep == j) & (me == target)

    for j in range(reps):
        @pl.when(jnp.logical_not(is_self(j)))
        def _():
            ou_copy(j).start()

        @pl.when(is_self(j))
        def _():
            pltpu.make_async_copy(ou_ref.at[j], w_ou.at[j, slot], o_recv.at[slot]).start()

    dn_x = remote(dn_ref, w_dn.at[rep], n_send.at[0], n_recv.at[0], (across, me))
    dn_c = remote(dn_ref, w_dn.at[rep], n_send.at[1], n_recv.at[1], (beside, me))
    dn_d = remote(w_dn.at[across], w_dn.at[across], n_send.at[2], n_recv.at[2], (beside, me))
    go(dn_x)
    go(dn_c)
    gates.begin()
    locals_ = []
    for index, (src, dst) in enumerate(
        ((in_ref.at[me], w_in.at[rep, me]), (gate_ref.at[me], w_gate.at[rep, me]), (dn_ref, w_dn.at[rep]))
    ):
        copy = pltpu.make_async_copy(src, dst, loc.at[index])
        copy.start()
        locals_.append(copy)

    for k in range(len(others)):
        frm = (mine + len(others) - k) % (reps * count)
        remote(gain_ref, gain_all.at[frm], g_send.at[k], g_recv.at[k], others[k]).wait_recv()
    gains_ref[...] = jnp.concatenate([gain_all[device, :, 0:d_rows] for device in range(reps * count)], axis=1)
    gain = 1.0 + gains_ref[0:1, :]

    def norm(value):
        value = value.astype(f32)
        return (value * lax.rsqrt(jnp.mean(value * value, axis=-1, keepdims=True) + 1e-06) * gain).astype(h1_ref.dtype)

    def norm_block(shard):
        for unit in range(UNITS):
            span = pl.ds(unit * (rows // UNITS), rows // UNITS)
            h1_ref[shard, span, :] = norm(tok_all[shard, span, :])

    for unit in range(UNITS):
        span = pl.ds(unit * (rows // UNITS), rows // UNITS)
        h1_ref[me, span, :] = norm(tok_ref[span, :])

    hops = gather.steps()

    def take_hop(hop):
        for _ in range(len(ring.units(0, hop))):
            hops.pop(0)()
        for way in (0, 1) if hop < ring.half else (0,):
            norm_block(ring.away(1 - way, hop))

    for k in range(1, count):
        ins.pass_on(k)
    take_hop(1)
    for k in range(count):
        ins.pass_beside(k)
    take_hop(2)
    for i in range(per_head):
        remote(
            ou_ref.at[0], w_ou.at[rep, i], o_send.at[0], o_recv.at[i], (across, me)
        ).wait_recv()
    ou_x = remote(w_ou.at[rep], w_ou.at[rep], n_send.at[3], n_recv.at[3], (across, me))
    ou_c = remote(w_ou.at[rep], w_ou.at[rep], n_send.at[4], n_recv.at[4], (beside, me))
    ou_d = remote(w_ou.at[across], w_ou.at[across], n_send.at[5], n_recv.at[5], (beside, me))
    go(ou_x)
    go(ou_c)
    dn_x.wait_recv()
    go(dn_d)
    for k in range(1, count // 2):
        gates.pass_on(k)
    take_hop(3)
    for k in range(count // 2, count):
        gates.pass_on(k)
    for hop in range(4, ring.half + 1):
        take_hop(hop)
    ou_x.wait_recv()
    go(ou_d)
    for k in range(count):
        gates.pass_beside(k)
    ins.finish()
    gates.finish()
    for copy in (dn_c, dn_d, ou_c, ou_d):
        copy.wait_recv()
    for copy in started:
        copy.wait_send()
    gather.finish()
    for j in range(reps):
        @pl.when(jnp.logical_not(is_self(j)))
        def _():
            ou_copy(j).wait_send()
    for copy in locals_:
        copy.wait()


def opening(reps, count, tokens, gain_tile, w_in, w_gate, w_dn, w_ou, collective_id):
    dma = pltpu.SemaphoreType.DMA
    per_head = count * reps // HEADS
    total = reps * count
    low = jnp.bfloat16
    shape = jax.ShapeDtypeStruct
    hops = dma((2, count // 2, UNITS))
    width = tokens.shape[1]
    gathered = (count,) + tokens.shape
    return pl.pallas_call(
        functools.partial(opening_kernel, reps, count),
        out_shape=[
            shape(gathered, low),
            shape((8, width), jnp.float32),
            shape((reps,) + w_in.shape, low),
            shape((reps,) + w_gate.shape, low),
            shape((reps,) + w_dn.shape, low),
            shape((reps, per_head) + w_ou.shape[1:], low),
        ],
        in_specs=[pl.BlockSpec(memory_space=VM)] * 2 + [pl.BlockSpec(memory_space=HB)] * 4,
        out_specs=[pl.BlockSpec(memory_space=VM)] * 2 + [pl.BlockSpec(memory_space=HB)] * 4,
        scratch_shapes=[
            pltpu.VMEM(gathered, low),
            pltpu.VMEM((total,) + gain_tile.shape, jnp.float32),
            hops,
            hops,
            dma((total - 1,)),
            dma((total - 1,)),
            dma((8, count)),
            dma((8, count)),
            dma((reps,)),
            dma((per_head,)),
            dma((6,)),
            dma((6,)),
            dma((3,)),
        ],
        compiler_params=pltpu.CompilerParams(
            collective_id=collective_id, has_side_effects=True, vmem_limit_bytes=VMEM_LIMIT
        ),
        name="opening",
    )(tokens, gain_tile, w_in, w_gate, w_dn, w_ou)


def cut_kernel(reps, count, in_ref, gate_ref, up_ref, cut_in, cut_gate, cut_up):
    low = jnp.bfloat16
    group = HEADS // KV_HEADS
    block = gate_ref.shape[1] // (reps * count)
    for shard in range(count):
        for ref, cut in ((gate_ref, cut_gate), (up_ref, cut_up)):
            pieces = [ref[:, (r * count + shard) * block : (r * count + shard + 1) * block] for r in range(reps)]
            cut[shard] = jnp.concatenate(pieces, axis=1).astype(low)
        heads = shard, HEADS + shard // group, HEADS + KV_HEADS + shard // group
        for index, head in enumerate(heads):
            cut_in[shard, :, index * HEAD_DIM : (index + 1) * HEAD_DIM] = in_ref[
                :, head * HEAD_DIM : (head + 1) * HEAD_DIM
            ].astype(low)


def cut_weights(reps, count, inproj, ffn_gate, ffn_up):
    rows = inproj.shape[0]
    shape = jax.ShapeDtypeStruct
    return pl.pallas_call(
        functools.partial(cut_kernel, reps, count),
        out_shape=[
            shape((count, rows, 3 * HEAD_DIM), jnp.bfloat16),
            shape((count, rows, ffn_gate.shape[1] // count), jnp.bfloat16),
            shape((count, rows, ffn_up.shape[1] // count), jnp.bfloat16),
        ],
        in_specs=[pl.BlockSpec(memory_space=VM)] * 3,
        out_specs=[pl.BlockSpec(memory_space=VM)] * 3,
        compiler_params=pltpu.CompilerParams(vmem_limit_bytes=VMEM_LIMIT),
        name="cut_weights",
    )(inproj, ffn_gate, ffn_up)


class RepSum:
    def __init__(self, part, from_core, from_across, sems, rep, me):
        self.part, self.from_core, self.from_across = part, from_core, from_across
        self.c_send, self.c_recv, self.x_send, self.x_recv = sems
        self.across, self.beside = rep_partners(rep)
        self.rep, self.me = rep, me
        self.core = rep % 2
        self.chip = rep // 2

    def core_copy(self, side, piece):
        chip = 1 - self.chip if side == 0 else self.chip
        return remote(
            self.part(chip * 2 + 1 - self.core, piece),
            self.from_core.at[side, piece],
            self.c_send.at[side, piece],
            self.c_recv.at[side, piece],
            (self.beside, self.me),
        )

    def cross_copy(self, piece):
        return remote(
            self.from_core.at[0, piece],
            self.from_across.at[piece],
            self.x_send.at[piece],
            self.x_recv.at[piece],
            (self.across, self.me),
        )

    def begin(self, pieces):
        for side in (0, 1):
            for piece in pieces:
                self.core_copy(side, piece).start()

    def cross(self, piece):
        f32 = jnp.float32
        self.core_copy(0, piece).wait_recv()
        mine = self.part((1 - self.chip) * 2 + self.core, piece)[...].astype(f32)
        self.from_core[0, piece] = (mine + self.from_core[0, piece].astype(f32)).astype(jnp.bfloat16)
        self.cross_copy(piece).start()

    def total(self, piece):
        f32 = jnp.float32
        self.core_copy(1, piece).wait_recv()
        mine = self.part(self.rep, piece)[...].astype(f32) + self.from_core[1, piece].astype(f32)
        self.cross_copy(piece).wait_recv()
        return mine + self.from_across[piece].astype(f32)

    def finish(self, pieces):
        for piece in pieces:
            self.core_copy(0, piece).wait_send()
            self.core_copy(1, piece).wait_send()
            self.cross_copy(piece).wait_send()


class Spread:
    def __init__(self, blocks, out, send, recv, rep, me, count):
        self.blocks, self.out, self.send, self.recv = blocks, out, send, recv
        self.rep, self.me, self.count = rep, me, count

    def copy(self, k):
        to = (self.me + k) % self.count
        return remote(
            self.blocks.at[to], self.out.at[self.me], self.send.at[k], self.recv.at[k], (self.rep, to)
        )

    def arrived(self, k):
        frm = (self.me + self.count - k) % self.count
        return remote(
            self.blocks.at[frm], self.out.at[frm], self.send.at[k], self.recv.at[k], (self.rep, frm)
        )

    def finish(self):
        for k in range(1, self.count):
            self.arrived(k).wait_recv()
        for k in range(1, self.count):
            self.copy(k).wait_send()


def near_devices(ring):
    across, beside = rep_partners(ring.rep)
    return [(ring.rep, (ring.me + k) % ring.count) for k in range(1, ring.count)] + [
        (across, ring.me),
        (beside, ring.me),
    ]


class Gather:
    def __init__(self, ring, block, out, send, recv):
        self.ring, self.block, self.out, self.send, self.recv = ring, block, out, send, recv
        self.rows = block.shape[0] // UNITS
        self.started = []

    def copy(self, way, hop, unit):
        ring = self.ring
        origin = ring.away(1 - way, hop - 1) if hop > 1 else ring.me
        span = pl.ds(unit * self.rows, self.rows)
        return remote(
            self.block.at[span] if hop == 1 else self.out.at[origin, span],
            self.out.at[origin, span],
            self.send.at[way, hop - 1, unit],
            self.recv.at[way, hop - 1, unit],
            ring.next[way],
        )

    def go(self, copy):
        copy.start()
        self.started.append(copy)

    def begin(self):
        for index in range(UNITS):
            for way in (0, 1):
                self.go(self.copy(way, 1, self.ring.units(way, 1)[index]))

    def steps(self):
        ring = self.ring

        def step(hop, index):
            for way in (0, 1):
                unit = ring.units(way, hop)[index]
                self.copy(way, hop, unit).wait_recv()
                if hop < ring.half and unit in ring.units(way, hop + 1):
                    self.go(self.copy(way, hop + 1, unit))

        return [
            functools.partial(step, hop, index)
            for hop in range(1, ring.half + 1)
            for index in range(len(ring.units(0, hop)))
        ]

    def finish(self):
        for copy in self.started:
            copy.wait_send()


def tn(left, right):
    return lax.dot_general(left, right, (((0,), (0,)), ((), ())), preferred_element_type=jnp.float32)


DN_PIECES = 3


def ffn_grads_kernel(
    reps, count, dattn_ref, wo_ref, q_ref, k_ref, v_ref, cos_ref, sin_ref, h3_hbm, dgu_hbm, part_hbm, probs_hbm, damp_hbm,
    all_ref, sum_ref, down_ref, dproj,
    h3_ref, dgu_ref, g_part, g_core, g_from, d_part, d_core, d_from, probs_ref, damp_ref, d_key, d_value,
    t_send, t_recv, gc_s, gc_r, gx_s, gx_r, dc_s, dc_r, dx_s, dx_r, s_send, s_recv, loc, loads, square
):
    f32, bf16 = jnp.float32, jnp.bfloat16
    ring = Ring(count)
    rep, me = ring.rep, ring.me
    d_rows, columns = sum_ref.shape[1:]
    part, width = d_part.shape
    block = part // reps
    seq_len = q_ref.shape[0]
    blocks = 4
    tall = seq_len // blocks
    half = HEAD_DIM // 2
    fetched = [
        pltpu.make_async_copy(src, dst, loads.at[index])
        for index, (src, dst) in enumerate(((part_hbm, d_part), (h3_hbm, h3_ref), (dgu_hbm, dgu_ref)))
    ]
    for copy in fetched:
        copy.start()

    def squares(i):
        span = pl.ds(i * tall, tall)
        return [
            pltpu.make_async_copy(probs_hbm.at[span], probs_ref, square.at[0]),
            pltpu.make_async_copy(damp_hbm.at[span], damp_ref, square.at[1]),
        ]

    for copy in squares(0):
        copy.start()
    meet(near_devices(ring))
    gather = Gather(ring, dattn_ref, all_ref, t_send, t_recv)
    gather.begin()
    own = pltpu.make_async_copy(dattn_ref, all_ref.at[me], loc)
    own.start()

    def d_at(owner, piece):
        rows = block // DN_PIECES
        return d_part.at[pl.ds(owner * block + piece * rows, rows)]

    down = RepSum(d_at, d_core, d_from, (dc_s, dc_r, dx_s, dx_r), rep, me)
    gate_up = RepSum(
        lambda owner, piece: g_part.at[owner, piece], g_core, g_from, (gc_s, gc_r, gx_s, gx_r), rep, me
    )
    spread = Spread(g_from, sum_ref, s_send, s_recv, rep, me, count)
    d_pieces = list(range(DN_PIECES))
    g_pieces = [(me + k) % count for k in range(1, count)] + [me]

    def make_gate_up(owner):
        rows = count * d_rows
        step = columns // 3

        def body(n, carry):
            cols = pl.ds(pl.multiple_of(n * step, 128), step)
            made = tn(h3_ref[:, owner * rows : (owner + 1) * rows], dgu_ref[:, cols])
            g_part[owner, :, :, cols] = made.reshape(count, d_rows, step).astype(bf16)
            return carry

        lax.fori_loop(0, 3, body, 0)

    def nt(left, right):
        return lax.dot_general(left, right, (((1,), (1,)), ((), ())), preferred_element_type=f32)

    def unturned(flat, at):
        cosine, sine = cos_ref[at, :], sin_ref[at, :]
        low, high = flat[:, :half], flat[:, half:]
        return jnp.concatenate([low * cosine + high * sine, high * cosine - low * sine], axis=1)

    d_key[...] = jnp.zeros_like(d_key)
    d_value[...] = jnp.zeros_like(d_value)

    def attend(i):
        at = pl.ds(i * tall, tall)
        per = count // blocks
        d_out = all_ref[i * per : (i + 1) * per].reshape(tall, width)
        d_att = nt(d_out, wo_ref[...]).astype(bf16)
        d_probs = nt(d_att, v_ref[...])
        for copy in squares(i):
            copy.wait()
        probs = probs_ref[...]
        inner = jnp.sum(probs.astype(f32) * d_probs, axis=-1, keepdims=True)
        d_scores = (damp_ref[...].astype(f32) * (d_probs - inner)).astype(bf16)
        d_query = jnp.dot(d_scores, k_ref[...], preferred_element_type=f32)
        dproj[at, :HEAD_DIM] = (unturned(d_query, at) * HEAD_DIM ** (-0.5)).astype(bf16)
        d_key[...] += tn(d_scores, q_ref[at, :])
        d_value[...] += tn(probs, d_att)
        if i < blocks - 1:
            for copy in squares(i + 1):
                copy.start()

    def project():
        for i in range(blocks):
            at = pl.ds(i * tall, tall)
            dproj[at, HEAD_DIM : 2 * HEAD_DIM] = unturned(d_key[at, :], at).astype(bf16)
            dproj[at, 2 * HEAD_DIM :] = d_value[at, :].astype(bf16)

    def finish_gate_up(k):
        piece = g_pieces[k]
        total = gate_up.total(piece).astype(bf16)
        if k < count - 1:
            g_from[piece] = total
            spread.copy(k + 1).start()
        else:
            sum_ref[me] = total

    def finish_down(piece):
        rows = block // DN_PIECES
        down_ref[pl.ds(piece * rows, rows), :] = down.total(piece)

    fetched[0].wait()
    down.begin(d_pieces)
    for copy in fetched[1:]:
        copy.wait()
    work = [functools.partial(make_gate_up, 0)]
    work += [functools.partial(down.cross, piece) for piece in d_pieces]
    work += [functools.partial(make_gate_up, owner) for owner in range(1, reps)]
    work += [lambda: gate_up.begin(g_pieces)]
    work += [functools.partial(gate_up.cross, piece) for piece in g_pieces]
    for step in gather.steps():
        step()
        if work:
            work.pop(0)()
    for piece in work:
        piece()
    own.wait()
    after = [functools.partial(finish_gate_up, k) for k in range(count)]
    per = max(1, count // blocks)
    for i in range(blocks):
        attend(i)
        for _ in range(min(per, len(after) - 2)):
            after.pop(0)()
    project()
    for piece in d_pieces:
        finish_down(piece)
    for piece in after:
        piece()
    spread.finish()
    down.finish(d_pieces)
    gate_up.finish(g_pieces)
    gather.finish()


def ffn_grads(
    reps, count, d_attn, w_out, queries, keys, values, cosine, sine, h3, d_gu, part_down, probs, damp, d_rows, collective_id
):
    dma = pltpu.SemaphoreType.DMA
    low, f32 = jnp.bfloat16, jnp.float32
    shape = jax.ShapeDtypeStruct
    width = d_attn.shape[1]
    columns = d_gu.shape[1]
    part = part_down.shape[0]
    seq_len = h3.shape[0]
    block = part // reps
    blocks = (count, d_rows, columns)
    lots = (DN_PIECES, block // DN_PIECES, width)
    hops = dma((2, count // 2, UNITS))
    vm, hb = pl.BlockSpec(memory_space=VM), pl.BlockSpec(memory_space=HB)
    return pl.pallas_call(
        functools.partial(ffn_grads_kernel, reps, count),
        out_shape=[
            shape((count,) + d_attn.shape, low),
            shape(blocks, low),
            shape((block, width), f32),
            shape((seq_len, 3 * HEAD_DIM), low),
        ],
        in_specs=[vm] * 7 + [hb] * 5,
        out_specs=[vm] * 4,
        scratch_shapes=[
            pltpu.VMEM(h3.shape, low),
            pltpu.VMEM(d_gu.shape, low),
            pltpu.VMEM((reps,) + blocks, low),
            pltpu.VMEM((2,) + blocks, low),
            pltpu.VMEM(blocks, low),
            pltpu.VMEM((part, width), low),
            pltpu.VMEM((2,) + lots, low),
            pltpu.VMEM(lots, low),
            pltpu.VMEM((seq_len // 4, seq_len), low),
            pltpu.VMEM((seq_len // 4, seq_len), low),
            pltpu.VMEM((seq_len, HEAD_DIM), f32),
            pltpu.VMEM((seq_len, HEAD_DIM), f32),
            hops,
            hops,
            dma((2, count)),
            dma((2, count)),
            dma((count,)),
            dma((count,)),
            dma((2, DN_PIECES)),
            dma((2, DN_PIECES)),
            dma((DN_PIECES,)),
            dma((DN_PIECES,)),
            dma((count,)),
            dma((count,)),
            dma,
            dma((3,)),
            dma((2,)),
        ],
        compiler_params=pltpu.CompilerParams(
            collective_id=collective_id, has_side_effects=True, vmem_limit_bytes=VMEM_LIMIT
        ),
        name="ffn_grads",
    )(d_attn, w_out, queries, keys, values, cosine, sine, h3, d_gu, part_down, probs, damp)


def closing_kernel(
    reps, count, dproj, in_ref, att_ref, h1_hbm, dattn_hbm, tokens_ref, dmid_ref, gains_ref, gg_ref,
    grad_ref, sum_ref, out_ref, gain_ref,
    h1_ref, dattn_ref, x_part, i_part, o_part, first, landed, total_ref, tiles, i_core, i_from, o_core, o_from,
    r_send, r_recv, ic_s, ic_r, ix_s, ix_r, oc_s, oc_r, ox_s, ox_r, s_send, s_recv, p_send, p_recv,
    g_send, g_recv, loads
):
    f32, bf16 = jnp.float32, jnp.bfloat16
    ring = Ring(count)
    rep, me = ring.rep, ring.me
    here = rep * count + me
    others = everyone(rep, me, reps, count)
    full = o_part.shape[1]
    d_rows = sum_ref.shape[1]
    seq_len, width = dattn_ref.shape
    rows = grad_ref.shape[0]
    fetched = [
        pltpu.make_async_copy(h1_hbm, h1_ref, loads.at[0]),
        pltpu.make_async_copy(dattn_hbm, dattn_ref, loads.at[1]),
    ]
    for copy in fetched:
        copy.start()
    meet(others)
    tall = seq_len // 4

    def project(i, carry):
        at = pl.ds(pl.multiple_of(i * tall, 16), tall)
        x_part[at, :] = lax.dot_general(
            dproj[at, :], in_ref[...], (((1,), (1,)), ((), ())), preferred_element_type=f32
        ).astype(bf16)
        return carry

    lax.fori_loop(0, 4, project, 0)

    def make_out():
        fetched[1].wait()
        per = width // 3

        def body(n, carry):
            cols = pl.ds(pl.multiple_of(n * per, 128), per)
            made = tn(att_ref[...], dattn_ref[:, cols]).reshape(full, reps, HEAD_DIM // full // reps, per)
            for owner in range(reps):
                o_part[owner, :, :, cols] = made[:, owner].astype(bf16)
            return carry

        lax.fori_loop(0, 3, body, 0)

    def make_in(owner):
        if owner == 0:
            fetched[0].wait()
        deep = count * d_rows
        made = tn(h1_ref[:, owner * deep : (owner + 1) * deep], dproj[...])
        i_part[owner] = made.reshape(count, d_rows, 3 * HEAD_DIM).astype(bf16)

    o_pieces = list(range(full))
    i_pieces = [(me + k) % count for k in range(1, count)] + [me]
    ins = RepSum(lambda owner, piece: i_part.at[owner, piece], i_core, i_from, (ic_s, ic_r, ix_s, ix_r), rep, me)
    outs = RepSum(lambda owner, piece: o_part.at[owner, piece], o_core, o_from, (oc_s, oc_r, ox_s, ox_r), rep, me)
    spread = Spread(i_from, sum_ref, s_send, s_recv, rep, me, count)

    def o_owner(piece):
        where = me * full + piece
        return where // count, where % count

    def o_copy(piece):
        return remote(o_from.at[piece], out_ref.at[rep], p_send.at[piece], p_recv.at[rep], o_owner(piece))

    def o_self(piece):
        return me * full + piece == here

    def o_finish(piece):
        total = outs.total(piece).astype(bf16)
        o_from[piece] = total

        @pl.when(jnp.logical_not(o_self(piece)))
        def _():
            o_copy(piece).start()

        @pl.when(o_self(piece))
        def _():
            pltpu.make_async_copy(o_from.at[piece], out_ref.at[rep], p_recv.at[rep]).start()

    def i_finish(k):
        piece = i_pieces[k]
        total = ins.total(piece).astype(bf16)
        if k < count - 1:
            i_from[piece] = total
            spread.copy(k + 1).start()
        else:
            sum_ref[me] = total

    work = [functools.partial(make_in, owner) for owner in range(reps)]
    work += [lambda: ins.begin(i_pieces), make_out, lambda: outs.begin(o_pieces)]
    work += [functools.partial(ins.cross, piece) for piece in i_pieces]
    work += [functools.partial(outs.cross, piece) for piece in o_pieces]
    work += [functools.partial(i_finish, k) for k in range(count)]
    work += [functools.partial(o_finish, piece) for piece in o_pieces]

    terms = []
    gain = 1.0 + gains_ref[0:1, :]

    def pause():
        for _ in range(min(2, len(work))):
            work.pop(0)()

    def take(shard, span):
        return x_part[pl.ds(pl.multiple_of(shard * rows + span.start, 16), span.size), :]

    def finish(span, total):
        value = tokens_ref[span, :].astype(f32)
        scale = lax.rsqrt(jnp.mean(value * value, axis=-1, keepdims=True) + 1e-06)
        normed = value * scale
        weighted = total * gain
        inner = jnp.mean(weighted * normed, axis=-1, keepdims=True)
        grad_ref[span, :] = dmid_ref[span, :] + scale * (weighted - normed * inner)
        terms.append(jnp.sum(total * normed, axis=0, keepdims=True))

    started = reduce_on_ring(ring, rows, take, first, landed, r_send, r_recv, finish, pause)
    total_ref[...] = gg_ref[...]
    total_ref[0:1, :] = functools.reduce(jnp.add, terms)
    every = total_ref[...]
    for owner in range(reps * count):
        tiles[owner, :, 0:d_rows] = every[:, owner * d_rows : (owner + 1) * d_rows]
        tiles[owner, :, d_rows:] = jnp.zeros((8, 128 - d_rows), f32)
    for k, device in enumerate(others):
        to = (here + k + 1) % (reps * count)
        remote(tiles.at[to], gain_ref.at[here], g_send.at[k], g_recv.at[k], device).start()
    gain_ref[here] = tiles[here]
    for piece in work:
        piece()
    for k in range(len(others)):
        frm = (here + len(others) - k) % (reps * count)
        remote(tiles.at[frm], gain_ref.at[frm], g_send.at[k], g_recv.at[k], others[k]).wait_recv()
    for j in range(reps):
        remote(
            o_from.at[0], out_ref.at[j], p_send.at[0], p_recv.at[j], (rep, (me + 1) % count)
        ).wait_recv()
    for piece in o_pieces:
        @pl.when(jnp.logical_not(o_self(piece)))
        def _():
            o_copy(piece).wait_send()
    spread.finish()
    ins.finish(i_pieces)
    outs.finish(o_pieces)
    for k, device in enumerate(others):
        to = (here + k + 1) % (reps * count)
        remote(tiles.at[to], gain_ref.at[here], g_send.at[k], g_recv.at[k], device).wait_send()
    for copy in started:
        copy.wait_send()


def closing(
    reps, count, d_projected, w_in, attended, normed, d_attn, tokens, d_middle, gain_rows, gain_terms, piece, collective_id
):
    dma = pltpu.SemaphoreType.DMA
    low, f32 = jnp.bfloat16, jnp.float32
    shape = jax.ShapeDtypeStruct
    rows, width = tokens.shape
    seq_len = normed.shape[0]
    total = reps * count
    half = count // 2
    d_rows = width // total
    full = HEAD_DIM // (reps * piece)
    i_block = (count, d_rows, 3 * HEAD_DIM)
    o_block = (full, piece, width)
    hops = dma((2, half, UNITS))
    vm, hb = pl.BlockSpec(memory_space=VM), pl.BlockSpec(memory_space=HB)
    return pl.pallas_call(
        functools.partial(closing_kernel, reps, count),
        out_shape=[
            shape((rows, width), f32),
            shape(i_block, low),
            shape((reps, piece, width), low),
            shape((total, 8, 128), f32),
        ],
        in_specs=[vm] * 3 + [hb] * 2 + [vm] * 4,
        out_specs=[vm] * 4,
        scratch_shapes=[
            pltpu.VMEM((seq_len, width), low),
            pltpu.VMEM((seq_len, width), low),
            pltpu.VMEM((seq_len, width), low),
            pltpu.VMEM((reps,) + i_block, low),
            pltpu.VMEM((reps,) + o_block, low),
            pltpu.VMEM((rows, width), low),
            pltpu.VMEM((2, half, rows, width), low),
            pltpu.VMEM((8, width), f32),
            pltpu.VMEM((total, 8, 128), f32),
            pltpu.VMEM((2,) + i_block, low),
            pltpu.VMEM(i_block, low),
            pltpu.VMEM((2,) + o_block, low),
            pltpu.VMEM(o_block, low),
            hops,
            hops,
            dma((2, count)),
            dma((2, count)),
            dma((count,)),
            dma((count,)),
            dma((2, full)),
            dma((2, full)),
            dma((full,)),
            dma((full,)),
            dma((count,)),
            dma((count,)),
            dma((full,)),
            dma((reps,)),
            dma((total - 1,)),
            dma((total - 1,)),
            dma((2,)),
        ],
        compiler_params=pltpu.CompilerParams(
            collective_id=collective_id, has_side_effects=True, vmem_limit_bytes=VMEM_LIMIT
        ),
        name="closing",
    )(d_projected, w_in, attended, normed, d_attn, tokens, d_middle, gain_rows, gain_terms)


def tiles_of(ref):
    rows, columns = ref.shape
    tall = 72 if rows % 72 == 0 else 64 if rows % 64 == 0 else 8
    wide = 384 if columns % 384 == 0 else 256
    return rows // tall, columns // wide, tall, wide


def tile_at(ref, n):
    _, across, tall, wide = tiles_of(ref)
    down, right = n // across, n % across
    return pl.ds(pl.multiple_of(down * tall, 8), tall), pl.ds(pl.multiple_of(right * wide, 128), wide)


LAMB_ORDER = (4, 2, 3, 0, 1)


def lamb_kernel(reps, count, sum_in, sum_out, sum_gu, gain_tiles, g_master, g_mean, g_square, *refs):
    f32 = jnp.float32
    names = 5
    hbm_in, refs = [refs[3 * i : 3 * i + 3] for i in range(names)], refs[3 * names :]
    grad_dn, refs = refs[0], refs[1:]
    (sums_out, gg_out, gm_out, gs_out, gp_out), refs = refs[:5], refs[5:]
    hbm_out, refs = [refs[4 * i : 4 * i + 4] for i in range(names)], refs[4 * names :]
    masters, means, squares, grads = (refs[names * i : names * (i + 1)] for i in range(4))
    in_sem, out_sem, dn_sem = refs[4 * names :]
    total = reps * count
    group = HEADS // KV_HEADS

    def fetch(i, j):
        return pltpu.make_async_copy(hbm_in[i][j], (masters, means, squares)[j][i], in_sem.at[i, j])

    fetch_dn = pltpu.make_async_copy(grad_dn, grads[4], dn_sem)
    fetch_dn.start()
    for i in LAMB_ORDER:
        for j in range(3):
            fetch(i, j).start()

    def store(i, j):
        return pltpu.make_async_copy((grads, means, squares, masters)[j][i], hbm_out[i][j], out_sem.at[i, j])

    def join(index, ref):
        block = ref.shape[1] // total
        part = block * reps
        for first in range(0, total, 4):
            pieces = []
            for b in range(first, first + 4):
                start = index * part + (b // count) * block
                pieces.append(sum_gu[b % count, :, start : start + block].astype(f32))
            ref[:, first * block : (first + 4) * block] = jnp.concatenate(pieces, axis=1)

    def make_grad(i):
        if i == 0:
            for head in range(HEADS):
                grads[0][:, head * HEAD_DIM : (head + 1) * HEAD_DIM] = sum_in[head, :, :HEAD_DIM].astype(f32)
            for kind in (1, 2):
                for head in range(KV_HEADS):
                    start = (HEADS + (kind - 1) * KV_HEADS + head) * HEAD_DIM
                    parts = [
                        sum_in[head * group + g, :, kind * HEAD_DIM : (kind + 1) * HEAD_DIM].astype(f32)
                        for g in range(group)
                    ]
                    grads[0][:, start : start + HEAD_DIM] = functools.reduce(jnp.add, parts)
        elif i == 1:
            rows = sum_out.shape[1]
            for j in range(reps):
                grads[1][j * rows : (j + 1) * rows, :] = sum_out[j].astype(f32)
        elif i in (2, 3):
            join(i - 2, grads[i])
        else:
            fetch_dn.wait()

    def lamb(master, grad, mean, square):
        new_mean = 0.5 * mean + 0.5 * grad
        new_square = 0.5 * square + 0.5 * grad * grad
        return new_mean, new_square, new_mean / (jnp.sqrt(new_square) + 1e-06) + 0.01 * master

    def sweep(i):
        down, across, tall, wide = tiles_of(masters[i])

        def body(n, carry):
            at = tile_at(masters[i], n)
            master = masters[i][at]
            new_mean, new_square, step = lamb(master, grads[i][at], means[i][at], squares[i][at])
            means[i][at] = new_mean
            squares[i][at] = new_square
            masters[i][at] = step

            def fold(value):
                return jnp.sum((value * value).reshape(tall // 8, 8, wide), axis=0)

            return carry[0] + fold(master), carry[1] + fold(step)

        zero = jnp.zeros((8, wide), f32)
        return lax.fori_loop(0, down * across, body, (zero, zero))

    at_row = lax.broadcasted_iota(jnp.int32, (8, 128), 0)
    at_lane = lax.broadcasted_iota(jnp.int32, (8, 128), 1)

    def note(sums, i, pair):
        for row in (0, 1):
            sums = sums + jnp.where((at_row == row) & (at_lane == i), jnp.sum(pair[row]), 0.0)
        return sums

    sums = jnp.zeros((8, 128), f32)
    for i in LAMB_ORDER:
        make_grad(i)
        for j in range(3):
            fetch(i, j).wait()
        pair = sweep(i)
        for j in range(4):
            store(i, j).start()
        sums = note(sums, i, pair)
    gain_total = functools.reduce(jnp.add, [gain_tiles[device] for device in range(total)])
    d_rows, kinds = g_master.shape
    gain_grad = gain_total.T[:d_rows, :kinds]
    gain_master = g_master[...]
    new_mean, new_square, gain_step = lamb(gain_master, gain_grad, g_mean[...], g_square[...])
    gg_out[...] = gain_grad
    gm_out[...] = new_mean
    gs_out[...] = new_square
    gp_out[...] = gain_step
    sums_out[...] = note(sums, 5, (gain_master * gain_master, gain_step * gain_step))
    for i in LAMB_ORDER:
        for j in range(4):
            store(i, j).wait()


def table_kernel(reps, count, sizes, x_ref, out_ref, near, far, held, n_send, n_recv, f_send, f_recv):
    f32 = jnp.float32
    rep = lax.axis_index("rep")
    me = lax.axis_index("shard")
    meet(
        [(rep, (me + k) % count) for k in range(1, count)] + [((rep + k) % reps, me) for k in range(1, reps)]
    )
    copies = []
    for k in range(1, count):
        copies.append(remote(x_ref, near.at[me], n_send.at[k], n_recv.at[k], (rep, (me + k) % count)))
    for copy in copies:
        copy.start()
    near[me] = x_ref[...]
    for k in range(1, count):
        frm = (me + count - k) % count
        remote(x_ref, near.at[frm], n_send.at[k], n_recv.at[k], (rep, frm)).wait_recv()
    sums = functools.reduce(jnp.add, [near[shard] for shard in range(count)])
    held[...] = sums
    more = []
    for k in range(1, reps):
        more.append(remote(held, far.at[rep], f_send.at[k], f_recv.at[k], ((rep + k) % reps, me)))
    for copy in more:
        copy.start()
    far[rep] = sums
    for k in range(1, reps):
        frm = (rep + reps - k) % reps
        remote(held, far.at[frm], f_send.at[k], f_recv.at[k], (frm, me)).wait_recv()
    totals = functools.reduce(jnp.add, [far[other] for other in range(reps)])
    at_lane = lax.broadcasted_iota(jnp.int32, (8, 128), 1)
    counts = jnp.ones((8, 128), f32)
    for i, size in enumerate(sizes):
        counts = jnp.where(at_lane == i, float(size), counts)
    out_ref[...] = jnp.sqrt(totals / counts + 1e-06)
    for copy in copies + more:
        copy.wait_send()


def fresh_kernel(table_ref, g_master, g_step, *refs):
    names = 5
    hbm_in, refs = [refs[2 * i : 2 * i + 2] for i in range(names)], refs[2 * names :]
    gp_out, refs = refs[0], refs[1:]
    hbm_out, refs = refs[:names], refs[names:]
    masters, steps, refs = refs[:names], refs[names : 2 * names], refs[2 * names :]
    in_sem, out_sem = refs

    def fetch(i, j):
        return pltpu.make_async_copy(hbm_in[i][j], (masters, steps)[j][i], in_sem.at[i, j])

    def store(i):
        return pltpu.make_async_copy(masters[i], hbm_out[i], out_sem.at[i])

    for i in LAMB_ORDER:
        for j in (0, 1):
            fetch(i, j).start()
    rate = 0.3 * table_ref[0:1, :] / table_ref[1:2, :]
    gp_out[...] = g_master[...] - rate[:, 5:6] * g_step[...]
    for i in LAMB_ORDER:
        down, across, _, _ = tiles_of(masters[i])
        scale = rate[:, i : i + 1]
        for j in (0, 1):
            fetch(i, j).wait()

        def body(n, carry):
            at = tile_at(masters[i], n)
            masters[i][at] = masters[i][at] - scale * steps[i][at]
            return carry

        lax.fori_loop(0, down * across, body, 0)
        store(i).start()
    for i in LAMB_ORDER:
        store(i).wait()


def lamb_step(reps, count, sums, grad_down, gains, states, collective_id):
    dma = pltpu.SemaphoreType.DMA
    f32 = jnp.float32
    shape = jax.ShapeDtypeStruct
    shapes = [state[0].shape for state in states]
    like_gains = shape(gains[0].shape, f32)
    tile = shape((8, 128), f32)
    vm, hb = pl.BlockSpec(memory_space=VM), pl.BlockSpec(memory_space=HB)
    local = pltpu.CompilerParams(vmem_limit_bytes=VMEM_LIMIT)
    outs = pl.pallas_call(
        functools.partial(lamb_kernel, reps, count),
        out_shape=[tile] + [like_gains] * 4 + [shape(item, f32) for item in shapes for _ in range(4)],
        in_specs=[vm] * 7 + [hb] * 16,
        out_specs=[vm] * 5 + [hb] * 20,
        scratch_shapes=[pltpu.VMEM(item, f32) for _ in range(4) for item in shapes] + [dma((5, 3)), dma((5, 4)), dma],
        compiler_params=local,
        name="lamb_moments",
    )(*sums, *gains, *[item for state in states for item in state], grad_down)
    sums, gain_parts, parts = outs[0], outs[1:5], [outs[5 + 4 * i : 9 + 4 * i] for i in range(5)]
    sizes = [item[0] * item[1] * reps * count for item in shapes + [like_gains.shape]]
    table = pl.pallas_call(
        functools.partial(table_kernel, reps, count, sizes),
        out_shape=tile,
        in_specs=[vm],
        out_specs=vm,
        scratch_shapes=[
            pltpu.VMEM((count, 8, 128), f32),
            pltpu.VMEM((reps, 8, 128), f32),
            pltpu.VMEM((8, 128), f32),
            dma((count,)),
            dma((count,)),
            dma((reps,)),
            dma((reps,)),
        ],
        compiler_params=pltpu.CompilerParams(collective_id=collective_id, has_side_effects=True),
        name="norm_table",
    )(sums)
    fresh = pl.pallas_call(
        fresh_kernel,
        out_shape=[like_gains] + [shape(item, f32) for item in shapes],
        in_specs=[vm] * 3 + [hb] * 10,
        out_specs=[vm] + [hb] * 5,
        scratch_shapes=[pltpu.VMEM(item, f32) for _ in range(2) for item in shapes] + [dma((5, 2)), dma((5,))],
        compiler_params=local,
        name="lamb_masters",
    )(table, gains[0], gain_parts[3], *[item for i in range(5) for item in (states[i][0], parts[i][3])])
    rest = [[parts[i][j] for i in range(5)] + [gain_parts[j]] for j in range(3)]
    return table[:2, :6], rest[0], rest[1], rest[2], list(fresh[1:]) + [fresh[0]]


def rope_tables(seq_len):
    exponent = -np.arange(HEAD_DIM // 2, dtype=np.float32) * np.float32(2.0) / np.float32(HEAD_DIM)
    freq = np.float32(10000.0) ** exponent
    angle = (np.arange(seq_len, dtype=np.float32)[:, None] * freq[None, :]).astype(np.float64)
    return jnp.asarray(np.cos(angle).astype(np.float32)), jnp.asarray(np.sin(angle).astype(np.float32))


def split_device(
    tokens, cotangent, piece_starts, inproj, outproj, ffn_gate, ffn_up, ffn_down, norm_gains,
    mean_inproj, mean_outproj, mean_gate, mean_up, mean_down, mean_gains,
    square_inproj, square_outproj, square_gate, square_up, square_down, square_gains,
):
    bf16, f32 = jnp.bfloat16, jnp.float32
    reps, count = lax.axis_size("rep"), lax.axis_size("shard")
    rep = lax.axis_index("rep")
    me = lax.axis_index("shard")
    total = reps * count
    rows, width = tokens.shape
    seq_len = rows * count
    group = HEADS // KV_HEADS
    q_width, k_width = HEADS * HEAD_DIM, KV_HEADS * HEAD_DIM
    d_rows = inproj.shape[0]
    ff = ffn_gate.shape[1]
    ff_block = ff // total
    ff_part = ff // count
    o_rows = outproj.shape[0]
    per_head = HEAD_DIM // o_rows
    piece = o_rows // reps

    cut_in, cut_gate, cut_up = cut_weights(reps, count, inproj, ffn_gate, ffn_up)
    cut_out = outproj.astype(bf16).reshape(reps, piece, width)
    gain_tile = jnp.pad(norm_gains.astype(bf16).astype(f32).T, ((0, 4), (0, 128 - d_rows)))
    normed_in, gain_rows, got_in, got_gate, got_down, got_out = opening(
        reps, count, tokens, gain_tile, cut_in, cut_gate, ffn_down.astype(bf16), cut_out, 1
    )
    normed_in = normed_in.reshape(seq_len, width)
    w_in = got_in.reshape(width, -1)
    w_gate = got_gate.reshape(width, ff_part)
    w_down = got_down.reshape(ff_part, width)

    position = jnp.arange(seq_len, dtype=jnp.int32)
    cosine, sine = rope_tables(seq_len)
    starts = lax.dynamic_slice_in_dim(piece_starts, rep, 1, 0)[0]
    inside = (position[:, None] >= starts[None, :]) & (position[:, None] < starts[None, :] + PIC)
    tag = jnp.sum(inside.astype(jnp.int32) * (jnp.arange(starts.shape[0], dtype=jnp.int32)[None, :] + 1), axis=1)
    attn_proj, queries, keys, values, attended, probs, damp, w_out, got_up = attention(
        reps, count, normed_in, w_in, got_out, cosine, sine, tag, cut_up, 4
    )
    w_up = got_up.reshape(width, ff_part)

    layer_out, d_middle, d_attn, gain_terms, normed_mid, d_gu, part_down = feed_forward(
        attn_proj, tokens, cotangent, gain_rows, w_gate, w_up, w_down, count, 5
    )
    d_attn, sum_gu, grad_down, d_projected = ffn_grads(
        reps, count, d_attn, w_out, queries, keys, values, cosine, sine, normed_mid, d_gu, part_down, probs, damp, d_rows, 9
    )
    input_grad, sum_in, sum_out, gain_tiles = closing(
        reps, count, d_projected, w_in, attended, normed_in, d_attn.reshape(seq_len, width), tokens, d_middle,
        gain_rows, gain_terms, piece, 12,
    )
    norm_table, gradients, new_means, new_squares, fresh = lamb_step(
        reps,
        count,
        (sum_in, sum_out, sum_gu, gain_tiles),
        grad_down,
        (norm_gains, mean_gains, square_gains),
        (
            (inproj, mean_inproj, square_inproj),
            (outproj, mean_outproj, square_outproj),
            (ffn_gate, mean_gate, square_gate),
            (ffn_up, mean_up, square_up),
            (ffn_down, mean_down, square_down),
        ),
        14,
    )
    return (
        layer_out,
        input_grad,
        *gradients,
        *new_means,
        *new_squares,
        *fresh,
        norm_table,
    )


def fits(mesh, shapes):
    reps, count = mesh.shape["rep"], mesh.shape["shard"]
    total = reps * count
    tokens, piece_starts, outproj, ffn_gate = shapes
    o_rows = outproj[0] // total
    return (
        reps == 4
        and count == HEADS
        and piece_starts[0] == reps
        and tokens[0] % (total * UNITS * 16) == 0
        and HEAD_DIM % o_rows == 0
        and o_rows % (16 * reps) == 0
        and HEAD_DIM // o_rows == total // HEADS
        and ffn_gate[1] % (total * 96) == 0
    )


def solution(mesh):
    split = P(("rep", "shard"), None)

    def step(*args):
        shapes = args[0].shape, args[2].shape, args[4].shape, args[5].shape
        body = split_device if fits(mesh, shapes) else per_device
        return jax.shard_map(
            body,
            mesh=mesh,
            in_specs=(split, split, P()) + (split,) * 18,
            out_specs=(split,) * 26 + (P(),),
            check_vma=False,
        )(*args)

    return step
```

```python
import functools

import jax
import jax.numpy as jnp
from jax import lax
from jax.experimental import pallas as pl
from jax.experimental.pallas import tpu as pltpu
import numpy as np
from jax.sharding import PartitionSpec as P

HEADS = 8
KV_HEADS = 4
HEAD_DIM = 256
PIC = 256


def rms_norm(values_in, gain_col):
    return (
        values_in
        * lax.rsqrt(jnp.mean(values_in * values_in, axis=-1, keepdims=True) + 1e-06)
        * (1.0 + gain_col)
    )


def geglu(gate_lin, up_lin):
    return jax.nn.gelu(gate_lin, approximate=True) * up_lin


def rotate(flat, position, head_count, sign):
    row_count = flat.shape[0]
    width = flat.shape[1] // head_count
    half = width // 2
    vectors = flat.reshape(row_count, head_count, width)
    freq = 10000.0 ** (-(jnp.arange(half, dtype=jnp.float32) * 2.0 / width))
    angle = position.astype(jnp.float32)[:, None] * freq[None, :]
    cosine = jnp.cos(angle)[:, None, :]
    sine = sign * jnp.sin(angle)[:, None, :]
    first = vectors[..., :half]
    second = vectors[..., half:]
    turned = jnp.concatenate(
        [first * cosine - second * sine, second * cosine + first * sine], axis=-1
    )
    return turned.reshape(row_count, head_count * width)


def owned_rows(activation, gradient, rep_index, width):
    piece = lax.dynamic_slice_in_dim(activation, rep_index * width, width, 1)
    return lax.dot_general(
        piece, gradient, (((0,), (0,)), ((), ())), preferred_element_type=jnp.float32
    )


def back_dot(gradient, weight):
    return lax.dot_general(
        gradient, weight, (((1,), (1,)), ((), ())), preferred_element_type=jnp.float32
    )


def describe(rows, piece_starts, seq_offset, seq_len):
    local_seq = rows // seq_len
    position = rows % seq_len
    global_seq = local_seq + seq_offset
    seq_total = piece_starts.shape[0]
    piece_count = piece_starts.shape[1]
    select = (global_seq[:, None] == jnp.arange(seq_total, dtype=jnp.int32)[None, :]).astype(
        jnp.int32
    )
    starts = jnp.sum(select[:, :, None] * piece_starts[None, :, :], axis=1)
    inside = ((position[:, None] >= starts) & (position[:, None] < starts + PIC)).astype(jnp.int32)
    labels = (
        global_seq[:, None] * piece_count + jnp.arange(piece_count, dtype=jnp.int32)[None, :] + 1
    )
    return (local_seq, position, jnp.sum(inside * labels, axis=1))


def visibility(piece_starts, query_rows, key_rows, seq_offset, seq_len):
    seq_q, pos_q, tag_q = describe(query_rows, piece_starts, seq_offset, seq_len)
    seq_k, pos_k, tag_k = describe(key_rows, piece_starts, seq_offset, seq_len)
    causal = pos_k[None, :] <= pos_q[:, None]
    same_piece = (tag_q[:, None] == tag_k[None, :]) & (tag_q[:, None] > 0)
    return (seq_q[:, None] == seq_k[None, :]) & (causal | same_piece)


def lamb_local(master, gradient, first, second):
    newmean = 0.5 * first + 0.5 * gradient
    newsquare = 0.5 * second + 0.5 * gradient * gradient
    step_dir = newmean / (jnp.sqrt(newsquare) + 1e-06) + 0.01 * master
    return (newmean, newsquare, step_dir)


def per_device(
    tokens,
    cotangent,
    piece_starts,
    inproj,
    outproj,
    ffn_gate,
    ffn_up,
    ffn_down,
    norm_gains,
    mean_inproj,
    mean_outproj,
    mean_gate,
    mean_up,
    mean_down,
    mean_gains,
    square_inproj,
    square_outproj,
    square_gate,
    square_up,
    square_down,
    square_gains,
):
    bf16 = jnp.bfloat16
    f32 = jnp.float32
    rep_count = lax.axis_size("rep")
    shard_count = lax.axis_size("shard")
    rep_index = lax.axis_index("rep")
    w_in, w_out, w_gate, w_up, w_down, gain_copy = (
        lax.all_gather(inproj.astype(bf16), ("rep", "shard"), axis=0, tiled=True),
        lax.all_gather(outproj.astype(bf16), ("rep", "shard"), axis=0, tiled=True),
        lax.all_gather(ffn_gate.astype(bf16), ("rep", "shard"), axis=0, tiled=True),
        lax.all_gather(ffn_up.astype(bf16), ("rep", "shard"), axis=0, tiled=True),
        lax.all_gather(ffn_down.astype(bf16), ("rep", "shard"), axis=0, tiled=True),
        lax.all_gather(norm_gains.astype(bf16), ("rep", "shard"), axis=0, tiled=True),
    )
    gains_used = gain_copy.astype(f32)
    residual = tokens.astype(f32)
    row_count = residual.shape[0]
    seq_len = row_count * shard_count
    q_width = HEADS * HEAD_DIM
    k_width = KV_HEADS * HEAD_DIM
    group_size = HEADS // KV_HEADS
    query_scale = HEAD_DIM ** (-0.5)
    local_rows = lax.axis_index("shard") * row_count + jnp.arange(row_count, dtype=jnp.int32)
    position = local_rows % seq_len
    normed_in = rms_norm(residual, gains_used[:, 0]).astype(bf16)
    projected = jnp.dot(normed_in, w_in, preferred_element_type=f32)
    queries = (rotate(projected[:, :q_width], position, HEADS, 1.0) * query_scale).astype(bf16)
    keys = rotate(projected[:, q_width : q_width + k_width], position, KV_HEADS, 1.0).astype(bf16)
    values = projected[:, q_width + k_width :].astype(bf16)
    all_keys, all_values = (
        lax.all_gather(keys, "shard", axis=0, tiled=True),
        lax.all_gather(values, "shard", axis=0, tiled=True),
    )
    key_rows = all_keys.shape[0]
    visible = visibility(
        piece_starts,
        local_rows,
        jnp.arange(key_rows, dtype=jnp.int32),
        rep_index * (key_rows // seq_len),
        seq_len,
    )
    query_heads = queries.reshape(row_count, KV_HEADS, group_size, HEAD_DIM)
    key_heads = all_keys.reshape(key_rows, KV_HEADS, HEAD_DIM)
    value_heads = all_values.reshape(key_rows, KV_HEADS, HEAD_DIM)

    def capped_scores():
        raw_scores = jnp.einsum(
            "tgrd,kgd->grtk", query_heads, key_heads, preferred_element_type=f32
        )
        bent_scores = jnp.tanh(raw_scores / 50.0)
        return (bent_scores, jnp.where(visible, 50.0 * bent_scores, -1e30))

    bent_scores, masked = capped_scores()
    top_score = jnp.max(masked, axis=-1, keepdims=True)
    log_total = top_score + jnp.log(jnp.sum(jnp.exp(masked - top_score), axis=-1, keepdims=True))
    probs_low = jnp.exp(masked - log_total).astype(bf16)
    attended = (
        jnp.einsum("grtk,kgd->tgrd", probs_low, value_heads, preferred_element_type=f32)
        .reshape(row_count, q_width)
        .astype(bf16)
    )
    attn_proj = jnp.dot(attended, w_out, preferred_element_type=f32)
    middle = residual + rms_norm(attn_proj, gains_used[:, 1])
    normed_mid = rms_norm(middle, gains_used[:, 2]).astype(bf16)
    gate_lin = jnp.dot(normed_mid, w_gate, preferred_element_type=f32)
    up_lin = jnp.dot(normed_mid, w_up, preferred_element_type=f32)
    hidden = geglu(gate_lin, up_lin).astype(bf16)
    ffn_proj = jnp.dot(hidden, w_down, preferred_element_type=f32)
    layer_out = (middle + rms_norm(ffn_proj, gains_used[:, 3])).astype(bf16)
    d_out = cotangent.astype(f32)
    _, post_back = jax.vjp(rms_norm, ffn_proj, gains_used[:, 3])
    d_ffn, d_gain3 = post_back(d_out)
    d_ffn_low = d_ffn.astype(bf16)
    hidden_all, d_ffn_all = (
        lax.all_gather(hidden, "rep", axis=0, tiled=True),
        lax.all_gather(d_ffn_low, "rep", axis=0, tiled=True),
    )
    part_down = owned_rows(hidden_all, d_ffn_all, rep_index, hidden.shape[1] // rep_count)
    d_hidden = back_dot(d_ffn_low, w_down)
    _, glu_back = jax.vjp(geglu, gate_lin, up_lin)
    d_gate, d_up = glu_back(d_hidden)
    d_gate_low = d_gate.astype(bf16)
    d_up_low = d_up.astype(bf16)
    gate_up_grad = jnp.concatenate([d_gate_low, d_up_low], axis=1)
    mid_all, gate_up_all = (
        lax.all_gather(normed_mid, "rep", axis=0, tiled=True),
        lax.all_gather(gate_up_grad, "rep", axis=0, tiled=True),
    )
    part_gate_up = owned_rows(mid_all, gate_up_all, rep_index, normed_mid.shape[1] // rep_count)
    d_mid_in = back_dot(d_gate_low, w_gate) + back_dot(d_up_low, w_up)
    _, pre_back = jax.vjp(rms_norm, middle, gains_used[:, 2])
    d_mid_part, d_gain2 = pre_back(d_mid_in)
    d_middle = d_out + d_mid_part
    _, attn_back = jax.vjp(rms_norm, attn_proj, gains_used[:, 1])
    d_attn, d_gain1 = attn_back(d_middle)
    d_attn_low = d_attn.astype(bf16)
    d_attended = back_dot(d_attn_low, w_out).astype(bf16)
    d_heads = d_attended.reshape(row_count, KV_HEADS, group_size, HEAD_DIM)
    bent_again, masked_again = capped_scores()
    attn_probs = jnp.exp(masked_again - log_total)
    probs_again = attn_probs.astype(bf16)
    d_probs = jnp.einsum("tgrd,kgd->grtk", d_heads, value_heads, preferred_element_type=f32)
    d_scores = (
        attn_probs
        * (d_probs - jnp.sum(attn_probs * d_probs, axis=-1, keepdims=True))
        * (1.0 - bent_again * bent_again)
    ).astype(bf16)
    d_queries = jnp.einsum(
        "grtk,kgd->tgrd", d_scores, key_heads, preferred_element_type=f32
    ).reshape(row_count, q_width)
    d_key = jnp.einsum("grtk,tgrd->kgd", d_scores, query_heads, preferred_element_type=f32).reshape(
        row_count * lax.axis_size("shard"), k_width
    )
    d_value = jnp.einsum(
        "grtk,tgrd->kgd", probs_again, d_heads, preferred_element_type=f32
    ).reshape(row_count * lax.axis_size("shard"), k_width)
    d_key_value = lax.psum_scatter(
        jnp.concatenate([d_key, d_value], axis=1), "shard", scatter_dimension=0, tiled=True
    )
    d_projected = jnp.concatenate(
        [
            rotate(d_queries, position, HEADS, -1.0) * query_scale,
            rotate(d_key_value[:, :k_width], position, KV_HEADS, -1.0),
            d_key_value[:, k_width:],
        ],
        axis=1,
    ).astype(bf16)
    d_normed_in = back_dot(d_projected, w_in)
    _, first_back = jax.vjp(rms_norm, residual, gains_used[:, 0])
    d_input_part, d_gain0 = first_back(d_normed_in)
    input_grad = d_middle + d_input_part
    gain_grad = jnp.stack([d_gain0, d_gain1, d_gain2, d_gain3], axis=1)
    attended_all, d_attn_all, normed_all, d_proj_all = (
        lax.all_gather(attended, "rep", axis=0, tiled=True),
        lax.all_gather(d_attn_low, "rep", axis=0, tiled=True),
        lax.all_gather(normed_in, "rep", axis=0, tiled=True),
        lax.all_gather(d_projected, "rep", axis=0, tiled=True),
    )
    part_out = owned_rows(attended_all, d_attn_all, rep_index, attended.shape[1] // rep_count)
    part_in = owned_rows(normed_all, d_proj_all, rep_index, normed_in.shape[1] // rep_count)
    part_gain = lax.psum_scatter(gain_grad, "rep", scatter_dimension=0, tiled=True)
    owned = (
        lax.psum_scatter(part_in, "shard", scatter_dimension=0, tiled=True),
        lax.psum_scatter(part_gain, "shard", scatter_dimension=0, tiled=True),
        lax.psum_scatter(part_out, "shard", scatter_dimension=0, tiled=True),
        lax.psum_scatter(part_gate_up, "shard", scatter_dimension=0, tiled=True),
        lax.psum_scatter(part_down, "shard", scatter_dimension=0, tiled=True),
    )
    grad_inproj, grad_gains, grad_outproj, grad_gate_up, grad_down = owned
    split_at = grad_gate_up.shape[1] // 2
    grad_gate = grad_gate_up[:, :split_at]
    grad_up = grad_gate_up[:, split_at:]
    masters = (inproj, outproj, ffn_gate, ffn_up, ffn_down, norm_gains)
    gradients = (grad_inproj, grad_outproj, grad_gate, grad_up, grad_down, grad_gains)
    firsts = (mean_inproj, mean_outproj, mean_gate, mean_up, mean_down, mean_gains)
    seconds = (square_inproj, square_outproj, square_gate, square_up, square_down, square_gains)
    results = [
        lamb_local(masters[index], gradients[index], firsts[index], seconds[index])
        for index in range(6)
    ]
    weight_sums = jnp.stack([jnp.sum(master * master) for master in masters])
    step_sums = jnp.stack([jnp.sum(item[2] * item[2]) for item in results])
    totals = lax.psum(jnp.stack([weight_sums, step_sums]), ("rep", "shard"))
    counts = jnp.array([float(master.size * rep_count * shard_count) for master in masters], f32)
    norm_table = jnp.sqrt(totals / counts[None, :] + 1e-06)
    fresh = [
        masters[index] - 0.3 * norm_table[0, index] / norm_table[1, index] * results[index][2]
        for index in range(6)
    ]
    return (
        layer_out,
        input_grad,
        grad_inproj,
        grad_outproj,
        grad_gate,
        grad_up,
        grad_down,
        grad_gains,
        results[0][0],
        results[1][0],
        results[2][0],
        results[3][0],
        results[4][0],
        results[5][0],
        results[0][1],
        results[1][1],
        results[2][1],
        results[3][1],
        results[4][1],
        results[5][1],
        fresh[0],
        fresh[1],
        fresh[2],
        fresh[3],
        fresh[4],
        fresh[5],
        norm_table,
    )


MESH = pl.DeviceIdType.MESH
VM = pltpu.VMEM
HB = pl.ANY
UNITS = 4
VMEM_LIMIT = 60 << 20


def ring_places(count):
    inner = 2 if count == 8 else 4
    outer = count // inner

    def place(shard):
        major = shard // inner
        minor = shard % inner
        return minor * outer + major + (minor % 2) * (outer - 1 - 2 * major)

    def shard_at(spot):
        minor = spot // outer
        major = spot % outer
        return (major + (minor % 2) * (outer - 1 - 2 * major)) * inner + minor

    return place, shard_at


def meet(devices):
    barrier = pltpu.get_barrier_semaphore()
    for device in devices:
        pl.semaphore_signal(barrier, inc=1, device_id=device, device_id_type=MESH)
    pl.semaphore_wait(barrier, len(devices))


def remote(src, dst, send_sem, recv_sem, device):
    return pltpu.make_async_remote_copy(
        src_ref=src,
        dst_ref=dst,
        send_sem=send_sem,
        recv_sem=recv_sem,
        device_id=device,
        device_id_type=MESH,
    )


class Ring:
    def __init__(self, count):
        place, shard_at = ring_places(count)
        self.count = count
        self.half = count // 2
        self.rep = lax.axis_index("rep")
        self.me = lax.axis_index("shard")
        self.spot = place(self.me)
        self.shard_at = shard_at
        self.next = [(self.rep, self.at(1)), (self.rep, self.at(count - 1))]

    def at(self, ahead):
        return self.shard_at((self.spot + ahead) % self.count)

    def away(self, way, hops):
        return self.at(hops if way == 0 else self.count - hops)

    def units(self, way, hop):
        order = list(range(UNITS)) if way == 0 else list(range(UNITS))[::-1]
        return order if hop < self.half else order[: UNITS // 2]


def reduce_on_ring(ring, rows, take, first, landed, send, recv, finish, pause):
    f32 = jnp.float32
    hops = ring.half
    started = []

    def part(unit):
        return pl.ds(unit * (rows // UNITS), rows // UNITS)

    def step_copy(way, step, unit):
        return remote(
            landed.at[way, step - 1, part(unit)] if step else first.at[part(unit)],
            landed.at[way, step, part(unit)],
            send.at[way, step, unit],
            recv.at[way, step, unit],
            ring.next[way],
        )

    for step in range(hops):
        order = ring.units(0, hops - step), ring.units(1, hops - step)
        before = [ring.units(way, hops - step + 1) if step else [] for way in (0, 1)]
        for index in range(len(order[0])):
            for way in (0, 1):
                unit = order[way][index]
                block = take(ring.away(way, hops - step), part(unit)).astype(f32)
                if unit in before[way]:
                    step_copy(way, step - 1, unit).wait_recv()
                    block += landed[way, step - 1, part(unit), :].astype(f32)
                if step:
                    landed[way, step - 1, part(unit), :] = block.astype(landed.dtype)
                else:
                    first[part(unit), :] = block.astype(first.dtype)
                copy = step_copy(way, step, unit)
                copy.start()
                started.append(copy)
            if step or index == len(order[0]) - 1:
                pause()
    for unit in range(UNITS):
        total = take(ring.me, part(unit)).astype(f32)
        for way in (0, 1):
            step_copy(way, hops - 1, unit).wait_recv()
            total += landed[way, hops - 1, part(unit), :].astype(f32)
        finish(part(unit), total)
    return started


class Flow:
    def __init__(self, ring, rows, send, recv):
        self.ring, self.rows, self.send, self.recv = ring, rows, send, recv
        self.unit_rows = rows // UNITS
        self.started = []

    def span(self, slot, unit):
        return pl.ds(slot * self.rows + unit * self.unit_rows, self.unit_rows)

    def slot(self, way, hops):
        if hops == 0:
            return 0
        return self.ring.count - 1 if hops == self.ring.half else 2 * hops - 1 + way

    def go(self, copy):
        copy.start()
        self.started.append(copy)

    def finish(self):
        for copy in self.started:
            copy.wait_send()

    def gather_copy(self, buffer, way, hop, unit):
        return remote(
            buffer.at[self.span(self.slot(way, hop - 1), unit)],
            buffer.at[self.span(self.slot(way, hop), unit)],
            self.send.at[way, hop - 1, unit],
            self.recv.at[way, hop - 1, unit],
            self.ring.next[way],
        )

    def gather(self, buffer, group_work):
        ring = self.ring
        for index in range(UNITS):
            for way in (0, 1):
                self.go(self.gather_copy(buffer, way, 1, ring.units(way, 1)[index]))
        queue = list(group_work(0, 1))
        for hop in range(1, ring.half + 1):
            length = len(ring.units(0, hop))
            for index in range(length):
                for way in (0, 1):
                    unit = ring.units(way, hop)[index]
                    self.gather_copy(buffer, way, hop, unit).wait_recv()
                    if hop < ring.half and unit in ring.units(way, hop + 1):
                        self.go(self.gather_copy(buffer, way, hop + 1, unit))
                if queue:
                    queue.pop(0)()
            for piece in queue:
                piece()
            queue = list(group_work(2 * hop - 1, 2) if hop < ring.half else group_work(ring.count - 1, 1))
        for piece in queue:
            piece()
        self.finish()

    def reduce_copy(self, first, landed, way, step, unit):
        span = pl.ds(unit * self.unit_rows, self.unit_rows)
        src = first.at[span] if step == 0 else landed.at[way, step - 1, span]
        return remote(
            src,
            landed.at[way, step, span],
            self.send.at[way, step, unit],
            self.recv.at[way, step, unit],
            self.ring.next[way],
        )

    def reduce(self, first, landed, partial, group_work, finish, extra=()):
        extra = list(extra)
        ring = self.ring
        hops = ring.half
        f32 = jnp.float32
        for piece in group_work(ring.count - 1, 1, 0):
            piece()
        queue = list(group_work(2 * (hops - 1) - 1, 2, 1))
        for step in range(hops):
            order = ring.units(0, hops - step), ring.units(1, hops - step)
            before = [ring.units(way, hops - step + 1) if step else [] for way in (0, 1)]
            for index in range(len(order[0])):
                for way in (0, 1):
                    unit = order[way][index]
                    span = pl.ds(unit * self.unit_rows, self.unit_rows)
                    if step == 0:
                        first[span, :] = partial[0, pl.ds(unit * self.unit_rows, self.unit_rows), :].astype(first.dtype)
                    else:
                        side = 1 - way
                        block = partial[
                            step % 2, pl.ds(side * self.rows + unit * self.unit_rows, self.unit_rows), :
                        ]
                        if unit in before[way]:
                            self.reduce_copy(first, landed, way, step - 1, unit).wait_recv()
                            block = block + landed[way, step - 1, span, :].astype(f32)
                        landed[way, step - 1, span, :] = block.astype(landed.dtype)
                    self.go(self.reduce_copy(first, landed, way, step, unit))
                if queue:
                    queue.pop(0)()
                elif extra:
                    extra.pop(0)()
            for piece in queue:
                piece()
            ahead = hops - step - 2
            queue = []
            if step < hops - 1:
                queue = list(group_work(2 * ahead - 1, 2, step % 2) if ahead > 0 else group_work(0, 1, step % 2))
        for piece in extra:
            piece()
        for unit in range(UNITS):
            span = pl.ds(unit * self.unit_rows, self.unit_rows)
            total = partial[hops % 2, span, :]
            for way in (0, 1):
                self.reduce_copy(first, landed, way, hops - 1, unit).wait_recv()
                total = total + landed[way, hops - 1, span, :].astype(f32)
            finish(unit, total)
        self.finish()


def looped(piece, count):
    def all_of_it():
        def body(j, carry):
            piece(j)
            return carry

        lax.fori_loop(0, count, body, 0)

    return [all_of_it]


def gelu_pair(gate):
    inner = 0.7978845608028654 * (gate + 0.044715 * gate * gate * gate)
    bend = jnp.tanh(inner)
    value = 0.5 * gate * (1.0 + bend)
    slope = 0.5 * (1.0 + bend) + 0.5 * gate * (1.0 - bend * bend) * 0.7978845608028654 * (
        1.0 + 0.134145 * gate * gate
    )
    return value, slope


def ffn_kernel(
    count, attn_ref, tokens_ref, cot_ref, gains_ref, gate_hbm, up_hbm, dn_hbm,
    layer_ref, dmid_ref, dattn_ref, gg_ref, h3_hbm, dgu_hbm, part_hbm,
    gate_ref, up_ref, dn_ref, h3_ref, hid_ref, dffn_ref, dgu_ref,
    lin, partial, first, landed, middle, total_ref, s1, r1, s2, r2, s3, r3, s4, r4, loads, stores,
):
    f32, bf16 = jnp.float32, jnp.bfloat16
    ring = Ring(count)
    rows, width = attn_ref.shape
    part = hid_ref.shape[1]
    tile = part // 3
    wide = width // 3
    fetched = [
        pltpu.make_async_copy(src, dst, loads.at[index])
        for index, (src, dst) in enumerate(((gate_hbm, gate_ref), (up_hbm, up_ref), (dn_hbm, dn_ref)))
    ]
    for copy in fetched:
        copy.start()
    kept = []

    def keep_out(src, dst):
        copy = pltpu.make_async_copy(src, dst, stores.at[len(kept)])
        copy.start()
        kept.append(copy)

    meet(ring.next)

    def gain(index):
        return 1.0 + gains_ref[index : index + 1, :]

    def scale_of(value):
        return lax.rsqrt(jnp.mean(value * value, axis=-1, keepdims=True) + 1e-06)

    half = rows // 2
    halves = [pl.ds(0, half), pl.ds(half, half)]
    for span in halves:
        proj = attn_ref[span, :]
        mid = tokens_ref[span, :].astype(f32) + proj * scale_of(proj) * gain(1)
        middle[span, :] = mid
        h3_ref[span, :] = (mid * scale_of(mid) * gain(2)).astype(bf16)

    def lin_work(slot, blocks):
        at = pl.ds(slot * rows, blocks * rows)

        def piece(j):
            lo = pl.ds(pl.multiple_of(j * tile, 128), tile)
            hi = pl.ds(pl.multiple_of(part + j * tile, 128), tile)
            gate = jnp.dot(h3_ref[at, :], gate_ref[:, lo], preferred_element_type=f32)
            up = jnp.dot(h3_ref[at, :], up_ref[:, lo], preferred_element_type=f32)
            value, slope = gelu_pair(gate)
            hid_ref[at, lo] = (value * up).astype(bf16)
            lin[at, lo] = (up * slope).astype(bf16)
            lin[at, hi] = value.astype(bf16)

        return looped(piece, 3)

    def down_work(slot, blocks, side):
        at = pl.ds(slot * rows, blocks * rows)

        def piece(j):
            cols = pl.ds(pl.multiple_of(j * wide, 128), wide)
            partial[side, pl.ds(0, blocks * rows), cols] = jnp.dot(
                hid_ref[at, :], dn_ref[:, cols], preferred_element_type=f32
            )

        return looped(piece, 3)

    def nt(left, right):
        return lax.dot_general(left, right, (((1,), (1,)), ((), ())), preferred_element_type=f32)

    def back_work(slot, blocks):
        at = pl.ds(slot * rows, blocks * rows)

        def piece(j):
            lo = pl.ds(pl.multiple_of(j * tile, 128), tile)
            hi = pl.ds(pl.multiple_of(part + j * tile, 128), tile)
            d_hidden = nt(dffn_ref[at, :], dn_ref[lo, :])
            dgu_ref[at, lo] = (d_hidden * lin[at, lo].astype(f32)).astype(bf16)
            dgu_ref[at, hi] = (d_hidden * lin[at, hi].astype(f32)).astype(bf16)

        return looped(piece, 3)

    def input_work(slot, blocks, side):
        at = pl.ds(slot * rows, blocks * rows)

        def piece(j):
            cols = pl.ds(pl.multiple_of(j * wide, 128), wide)
            partial[side, pl.ds(0, blocks * rows), cols] = nt(dgu_ref[at, :part], gate_ref[cols, :]) + nt(
                dgu_ref[at, part:], up_ref[cols, :]
            )

        return looped(piece, 3)

    def keep(unit, total):
        total_ref[pl.ds(unit * (rows // UNITS), rows // UNITS), :] = total

    def lin_first(slot, blocks):
        work = lin_work(slot, blocks)
        return [lambda: (fetched[0].wait(), fetched[1].wait())] + work if slot == 0 else work

    Flow(ring, rows, s1, r1).gather(h3_ref, lin_first)
    keep_out(h3_ref, h3_hbm)
    fetched[2].wait()
    Flow(ring, rows, s2, r2).reduce(first, landed, partial, down_work, keep)

    def back_norm(value, index, grad):
        scale = scale_of(value)
        normed = value * scale
        weighted = grad * gain(index)
        inner = jnp.mean(weighted * normed, axis=-1, keepdims=True)
        return scale * (weighted - normed * inner), jnp.sum(grad * normed, axis=0, keepdims=True)

    gg = jnp.zeros((1, width), f32)
    for span in halves:
        proj = total_ref[span, :]
        scale = scale_of(proj)
        layer_ref[span, :] = (middle[span, :] + proj * scale * gain(3)).astype(bf16)
        d_ffn, term = back_norm(proj, 3, cot_ref[span, :].astype(f32))
        gg += term
        dffn_ref[span, :] = d_ffn.astype(bf16)
    gg_ref[3:4, :] = gg

    Flow(ring, rows, s3, r3).gather(dffn_ref, back_work)
    keep_out(dgu_ref, dgu_hbm)

    def make_down(j):
        span = pl.ds(j * tile, tile)

        def body(n, carry):
            cols = pl.ds(pl.multiple_of(n * wide, 128), wide)
            lin[span, cols] = tn(hid_ref[:, span], dffn_ref[:, cols]).astype(bf16)
            return carry

        lax.fori_loop(0, 3, body, 0)
        keep_out(lin.at[span, pl.ds(0, width)], part_hbm.at[span])

    Flow(ring, rows, s4, r4).reduce(
        first, landed, partial, input_work, keep, [functools.partial(make_down, j) for j in range(3)]
    )

    gg1 = jnp.zeros((1, width), f32)
    gg2 = jnp.zeros((1, width), f32)
    for span in halves:
        d_mid, term = back_norm(middle[span, :], 2, total_ref[span, :])
        gg2 += term
        d_mid = d_mid + cot_ref[span, :].astype(f32)
        dmid_ref[span, :] = d_mid
        d_attn, term = back_norm(attn_ref[span, :], 1, d_mid)
        gg1 += term
        dattn_ref[span, :] = d_attn.astype(bf16)
    gg_ref[1:2, :] = gg1
    gg_ref[2:3, :] = gg2
    gg_ref[0:1, :] = jnp.zeros((1, width), f32)
    gg_ref[4:8, :] = jnp.zeros((4, width), f32)
    for copy in kept:
        copy.wait()


def feed_forward(attn_proj, tokens, cotangent, gain_rows, w_gate, w_up, w_down, count, collective_id):
    f32, bf16 = jnp.float32, jnp.bfloat16
    rows, width = attn_proj.shape
    part = w_down.shape[0]
    every = rows * count
    dma = pltpu.SemaphoreType.DMA
    shape = jax.ShapeDtypeStruct
    return pl.pallas_call(
        functools.partial(ffn_kernel, count),
        out_shape=[
            shape((rows, width), bf16),
            shape((rows, width), f32),
            shape((rows, width), bf16),
            shape((8, width), f32),
            shape((every, width), bf16),
            shape((every, 2 * part), bf16),
            shape((part, width), bf16),
        ],
        in_specs=[pl.BlockSpec(memory_space=VM)] * 4 + [pl.BlockSpec(memory_space=HB)] * 3,
        out_specs=[pl.BlockSpec(memory_space=VM)] * 4 + [pl.BlockSpec(memory_space=HB)] * 3,
        scratch_shapes=[
            pltpu.VMEM(w_gate.shape, bf16),
            pltpu.VMEM(w_up.shape, bf16),
            pltpu.VMEM(w_down.shape, bf16),
            pltpu.VMEM((every, width), bf16),
            pltpu.VMEM((every, part), bf16),
            pltpu.VMEM((every, width), bf16),
            pltpu.VMEM((every, 2 * part), bf16),
            pltpu.VMEM((max(every, part), max(2 * part, width)), bf16),
            pltpu.VMEM((2, 2 * rows, width), f32),
            pltpu.VMEM((rows, width), bf16),
            pltpu.VMEM((2, count // 2, rows, width), bf16),
            pltpu.VMEM((rows, width), f32),
            pltpu.VMEM((rows, width), f32),
        ]
        + [dma((2, count // 2, UNITS))] * 8
        + [dma((3,)), dma((5,))],
        compiler_params=pltpu.CompilerParams(
            collective_id=collective_id, has_side_effects=True, vmem_limit_bytes=VMEM_LIMIT
        ),
        name="feed_forward",
    )(attn_proj, tokens, cotangent, gain_rows, w_gate, w_up, w_down)


def attention_kernel(
    reps, count, h1_ref, in_ref, got_ref, cos_ref, sin_ref, tagq_ref, tagk_ref, cut_ref,
    proj_ref, q_ref, k_ref, v_ref, att_ref, probs_ref, damp_ref, wo_ref, up_ref,
    part, first, landed, r_send, r_recv, w_sems, loc
):
    f32, bf16 = jnp.float32, jnp.bfloat16
    ring = Ring(count)
    rows = proj_ref.shape[0]
    seq_len = h1_ref.shape[0]
    tall = seq_len // 4
    half = HEAD_DIM // 2
    meet(near_devices(ring))
    weights = Fetch(ring, cut_ref, up_ref, w_sems)
    weights.begin()
    own = pltpu.make_async_copy(cut_ref.at[ring.me], up_ref.at[ring.rep, ring.me], loc)
    own.start()
    piece = got_ref.shape[2]
    for block in range(got_ref.shape[1]):
        for j in range(reps):
            start = (block * reps + j) * piece
            wo_ref[start : start + piece, :] = got_ref[j, block]

    def project(i, carry):
        at = pl.ds(pl.multiple_of(i * tall, 16), tall)
        flat = jnp.dot(h1_ref[at, :], in_ref[...], preferred_element_type=f32)
        cosine, sine = cos_ref[at, :], sin_ref[at, :]

        def turned(start):
            first, second = flat[:, start : start + half], flat[:, start + half : start + HEAD_DIM]
            return jnp.concatenate([first * cosine - second * sine, second * cosine + first * sine], axis=1)

        q_ref[at, :] = (turned(0) * HEAD_DIM ** (-0.5)).astype(bf16)
        k_ref[at, :] = turned(HEAD_DIM).astype(bf16)
        v_ref[at, :] = flat[:, 2 * HEAD_DIM :].astype(bf16)
        return carry

    lax.fori_loop(0, 4, project, 0)

    def attend(shard):
        at = pl.ds(pl.multiple_of(shard * rows, 16), rows)
        raw = lax.dot_general(q_ref[at, :], k_ref[...], (((1,), (1,)), ((), ())), preferred_element_type=f32)
        bent = jnp.tanh(raw * (1.0 / 50.0))
        query_at = shard * rows + lax.broadcasted_iota(jnp.int32, (rows, seq_len), 0)
        key_at = lax.broadcasted_iota(jnp.int32, (rows, seq_len), 1)
        tag = tagq_ref[at, :]
        visible = (key_at <= query_at) | ((tag == tagk_ref[...]) & (tag > 0))
        masked = jnp.where(visible, 50.0 * bent, -1e30)
        expo = jnp.exp(masked - jnp.max(masked, axis=-1, keepdims=True))
        probs = expo / jnp.sum(expo, axis=-1, keepdims=True)
        low = probs.astype(bf16)
        probs_ref[at, :] = low
        damp_ref[at, :] = (probs * (1.0 - bent * bent)).astype(bf16)
        attended = jnp.dot(low, v_ref[...], preferred_element_type=f32).astype(bf16)
        att_ref[at, :] = attended
        part[at, :] = jnp.dot(attended, wo_ref[...], preferred_element_type=f32)

    def attend_both(hop):
        def body(way, carry):
            attend(ring.at(hop + way * (count - 2 * hop)))
            return carry

        lax.fori_loop(0, 2 if hop else 1, body, 0)

    work = weights.steps()
    first_of_step = [0] + [1 + UNITS * step for step in range(ring.half - 1)]
    calls = []

    def pause():
        call = len(calls)
        calls.append(call)
        if call in first_of_step:
            attend_both(ring.half - 1 - first_of_step.index(call))
            return
        for _ in range(min(3, len(work))):
            work.pop(0)()

    def finish(span, total):
        proj_ref[span, :] = total

    def take(shard, span):
        return part[pl.ds(pl.multiple_of(shard * rows + span.start, 16), span.size), :]

    attend(ring.at(ring.half))
    started = reduce_on_ring(ring, rows, take, first, landed, r_send, r_recv, finish, pause)
    for piece in work:
        piece()
    weights.finish()
    own.wait()
    for copy in started:
        copy.wait_send()


def attention(reps, count, normed, w_in, w_out, cosine, sine, tag, cut_up, collective_id):
    dma = pltpu.SemaphoreType.DMA
    low, f32 = jnp.bfloat16, jnp.float32
    shape = jax.ShapeDtypeStruct
    seq_len, width = normed.shape
    rows = seq_len // count
    hops = count // 2
    head = shape((seq_len, HEAD_DIM), low)
    square = shape((seq_len, seq_len), low)
    return pl.pallas_call(
        functools.partial(attention_kernel, reps, count),
        out_shape=[
            shape((rows, width), f32), head, head, head, head, square, square, shape((HEAD_DIM, width), low),
            shape((reps,) + cut_up.shape, low),
        ],
        in_specs=[pl.BlockSpec(memory_space=VM)] * 7 + [pl.BlockSpec(memory_space=HB)],
        out_specs=[pl.BlockSpec(memory_space=VM)] * 8 + [pl.BlockSpec(memory_space=HB)],
        scratch_shapes=[
            pltpu.VMEM((seq_len, width), f32),
            pltpu.VMEM((rows, width), low),
            pltpu.VMEM((2, hops, rows, width), low),
            dma((2, hops, UNITS)),
            dma((2, hops, UNITS)),
            dma((8, count)),
            dma,
        ],
        compiler_params=pltpu.CompilerParams(
            collective_id=collective_id, has_side_effects=True, vmem_limit_bytes=VMEM_LIMIT
        ),
        name="attention",
    )(normed, w_in, w_out, cosine, sine, tag[:, None], tag[None, :], cut_up)


class Fetch:
    def __init__(self, ring, cut, out, sems):
        self.ring, self.cut, self.out = ring, cut, out
        self.rep, self.me, self.count = ring.rep, ring.me, ring.count
        self.across, self.beside = rep_partners(ring.rep)
        self.sems = sems
        self.started = []

    def go(self, copy):
        copy.start()
        self.started.append(copy)

    def spread(self, k):
        to = (self.me + k) % self.count
        return remote(
            self.cut.at[to], self.out.at[self.rep, self.me], self.sems.at[0, k], self.sems.at[1, k], (self.rep, to)
        )

    def arrived(self, k):
        frm = (self.me + self.count - k) % self.count
        return remote(
            self.cut.at[frm], self.out.at[self.rep, frm], self.sems.at[0, k], self.sems.at[1, k], (self.rep, frm)
        )

    def forward(self, k, hop):
        frm = (self.me + self.count - k) % self.count
        rep = self.across if hop == 2 else self.rep
        block = self.out.at[rep, frm] if k or hop == 2 else self.cut.at[self.me]
        to = self.across if hop == 0 else self.beside
        return remote(
            block,
            self.out.at[rep, frm],
            self.sems.at[2 + 2 * hop, k],
            self.sems.at[3 + 2 * hop, k],
            (to, self.me),
        )

    def pass_on(self, k):
        if k:
            self.arrived(k).wait_recv()
        self.go(self.forward(k, 0))
        self.go(self.forward(k, 1))

    def pass_beside(self, k):
        self.forward(k, 0).wait_recv()
        self.go(self.forward(k, 2))

    def begin(self):
        for k in range(1, self.count):
            self.go(self.spread(k))
        self.pass_on(0)

    def steps(self):
        work = [functools.partial(self.pass_on, k) for k in range(1, self.count)]
        return work + [functools.partial(self.pass_beside, k) for k in range(self.count)]

    def finish(self):
        for k in range(self.count):
            self.forward(k, 1).wait_recv()
            self.forward(k, 2).wait_recv()
        for copy in self.started:
            copy.wait_send()


def rep_partners(rep):
    return (rep + 2) % 4, rep + 1 - 2 * (rep % 2)


def everyone(rep, me, reps, count):
    here = rep * count + me
    total = reps * count
    return [
        (((here + k) % total) // count, ((here + k) % total) % count) for k in range(1, total)
    ]


def opening_kernel(
    reps, count, tok_ref, gain_ref, in_hbm, dn_hbm, ou_hbm, gate_hbm, up_hbm,
    h1_ref, gains_ref, w_in, w_gate, w_dn, w_ou, cut_up,
    in_f, dn_f, ou_f, gate_f, up_f, in_ref, dn_ref, ou_ref, gate_ref, tok_all, gain_all,
    t_send, t_recv, g_send, g_recv, i_sems, u_sems, o_send, o_recv, n_send, n_recv, loc, loads
):
    f32 = jnp.float32
    ring = Ring(count)
    rep, me = ring.rep, ring.me
    across, beside = rep_partners(rep)
    others = everyone(rep, me, reps, count)
    mine = rep * count + me
    d_rows = in_ref.shape[1]
    rows = tok_ref.shape[0]
    fetched = [
        pltpu.make_async_copy(src, dst, loads.at[index])
        for index, (src, dst) in enumerate(
            ((in_hbm, in_f), (dn_hbm, dn_f), (ou_hbm, ou_f), (gate_hbm, gate_f), (up_hbm, up_f))
        )
    ]
    for copy in fetched:
        copy.start()
    meet(others)
    started = []

    def go(copy):
        copy.start()
        started.append(copy)

    for k, device in enumerate(others):
        go(remote(gain_ref, gain_all.at[mine], g_send.at[k], g_recv.at[k], device))
    gain_all[mine] = gain_ref[...]
    ins = Fetch(ring, in_ref, w_in, i_sems)
    gates = Fetch(ring, gate_ref, w_gate, u_sems)
    gather = Gather(ring, tok_ref, tok_all, t_send, t_recv)
    gather.begin()
    fetched[0].wait()
    cut_heads(count, in_f, in_ref)
    ins.begin()
    fetched[1].wait()
    dn_ref[...] = dn_f[...].astype(dn_ref.dtype)
    dn_x = remote(dn_ref, w_dn.at[rep], n_send.at[0], n_recv.at[0], (across, me))
    dn_c = remote(dn_ref, w_dn.at[rep], n_send.at[1], n_recv.at[1], (beside, me))
    dn_d = remote(w_dn.at[across], w_dn.at[across], n_send.at[2], n_recv.at[2], (beside, me))
    go(dn_x)
    go(dn_c)
    fetched[2].wait()
    for j in range(reps):
        ou_ref[j] = ou_f[j * ou_ref.shape[1] : (j + 1) * ou_ref.shape[1], :].astype(ou_ref.dtype)

    per_head = count * reps // HEADS
    target = mine // per_head
    slot = mine % per_head

    def ou_copy(j):
        return remote(ou_ref.at[j], w_ou.at[j, slot], o_send.at[j], o_recv.at[slot], (j, target))

    def is_self(j):
        return (rep == j) & (me == target)

    for j in range(reps):
        @pl.when(jnp.logical_not(is_self(j)))
        def _():
            ou_copy(j).start()

        @pl.when(is_self(j))
        def _():
            pltpu.make_async_copy(ou_ref.at[j], w_ou.at[j, slot], o_recv.at[slot]).start()

    fetched[3].wait()
    cut_units(reps, count, gate_f, gate_ref)
    gates.begin()
    locals_ = []
    for index, (src, dst) in enumerate(
        ((in_ref.at[me], w_in.at[rep, me]), (gate_ref.at[me], w_gate.at[rep, me]), (dn_ref, w_dn.at[rep]))
    ):
        copy = pltpu.make_async_copy(src, dst, loc.at[index])
        copy.start()
        locals_.append(copy)

    for k in range(len(others)):
        frm = (mine + len(others) - k) % (reps * count)
        remote(gain_ref, gain_all.at[frm], g_send.at[k], g_recv.at[k], others[k]).wait_recv()
    gains_ref[...] = jnp.concatenate([gain_all[device, :, 0:d_rows] for device in range(reps * count)], axis=1)
    gain = 1.0 + gains_ref[0:1, :]

    def norm(value):
        value = value.astype(f32)
        return (value * lax.rsqrt(jnp.mean(value * value, axis=-1, keepdims=True) + 1e-06) * gain).astype(h1_ref.dtype)

    def norm_block(shard):
        for unit in range(UNITS):
            span = pl.ds(unit * (rows // UNITS), rows // UNITS)
            h1_ref[shard, span, :] = norm(tok_all[shard, span, :])

    for unit in range(UNITS):
        span = pl.ds(unit * (rows // UNITS), rows // UNITS)
        h1_ref[me, span, :] = norm(tok_ref[span, :])

    hops = gather.steps()

    def take_hop(hop):
        for _ in range(len(ring.units(0, hop))):
            hops.pop(0)()
        for way in (0, 1) if hop < ring.half else (0,):
            norm_block(ring.away(1 - way, hop))

    for k in range(1, count):
        ins.pass_on(k)
    take_hop(1)
    fetched[4].wait()
    cut_units(reps, count, up_f, cut_up)
    for k in range(count):
        ins.pass_beside(k)
    take_hop(2)
    for i in range(per_head):
        remote(
            ou_ref.at[0], w_ou.at[rep, i], o_send.at[0], o_recv.at[i], (across, me)
        ).wait_recv()
    ou_x = remote(w_ou.at[rep], w_ou.at[rep], n_send.at[3], n_recv.at[3], (across, me))
    ou_c = remote(w_ou.at[rep], w_ou.at[rep], n_send.at[4], n_recv.at[4], (beside, me))
    ou_d = remote(w_ou.at[across], w_ou.at[across], n_send.at[5], n_recv.at[5], (beside, me))
    go(ou_x)
    go(ou_c)
    dn_x.wait_recv()
    go(dn_d)
    for k in range(1, count // 2):
        gates.pass_on(k)
    take_hop(3)
    for k in range(count // 2, count):
        gates.pass_on(k)
    for hop in range(4, ring.half + 1):
        take_hop(hop)
    ou_x.wait_recv()
    go(ou_d)
    for k in range(count):
        gates.pass_beside(k)
    ins.finish()
    gates.finish()
    for copy in (dn_c, dn_d, ou_c, ou_d):
        copy.wait_recv()
    for copy in started:
        copy.wait_send()
    gather.finish()
    for j in range(reps):
        @pl.when(jnp.logical_not(is_self(j)))
        def _():
            ou_copy(j).wait_send()
    for copy in locals_:
        copy.wait()


def opening(reps, count, tokens, gain_tile, inproj, outproj, ffn_gate, ffn_up, ffn_down, collective_id):
    dma = pltpu.SemaphoreType.DMA
    per_head = count * reps // HEADS
    total = reps * count
    low, f32 = jnp.bfloat16, jnp.float32
    shape = jax.ShapeDtypeStruct
    hops = dma((2, count // 2, UNITS))
    width = tokens.shape[1]
    gathered = (count,) + tokens.shape
    d_rows = inproj.shape[0]
    heads = (count, d_rows, 3 * HEAD_DIM)
    units = (count, d_rows, ffn_gate.shape[1] // count)
    outs = (reps, outproj.shape[0] // reps, width)
    vm, hb = pl.BlockSpec(memory_space=VM), pl.BlockSpec(memory_space=HB)
    return pl.pallas_call(
        functools.partial(opening_kernel, reps, count),
        out_shape=[
            shape(gathered, low),
            shape((8, width), f32),
            shape((reps,) + heads, low),
            shape((reps,) + units, low),
            shape((reps,) + ffn_down.shape, low),
            shape((reps, per_head) + outs[1:], low),
            shape(units, low),
        ],
        in_specs=[vm] * 2 + [hb] * 5,
        out_specs=[vm] * 2 + [hb] * 4 + [vm],
        scratch_shapes=[
            pltpu.VMEM(inproj.shape, f32),
            pltpu.VMEM(ffn_down.shape, f32),
            pltpu.VMEM(outproj.shape, f32),
            pltpu.VMEM(ffn_gate.shape, f32),
            pltpu.VMEM(ffn_up.shape, f32),
            pltpu.VMEM(heads, low),
            pltpu.VMEM(ffn_down.shape, low),
            pltpu.VMEM(outs, low),
            pltpu.VMEM(units, low),
            pltpu.VMEM(gathered, low),
            pltpu.VMEM((total,) + gain_tile.shape, f32),
            hops,
            hops,
            dma((total - 1,)),
            dma((total - 1,)),
            dma((8, count)),
            dma((8, count)),
            dma((reps,)),
            dma((per_head,)),
            dma((6,)),
            dma((6,)),
            dma((3,)),
            dma((5,)),
        ],
        compiler_params=pltpu.CompilerParams(
            collective_id=collective_id, has_side_effects=True, vmem_limit_bytes=VMEM_LIMIT
        ),
        name="opening",
    )(tokens, gain_tile, inproj, ffn_down, outproj, ffn_gate, ffn_up)


def cut_units(reps, count, ref, cut):
    block = ref.shape[1] // (reps * count)
    for shard in range(count):
        pieces = [ref[:, (r * count + shard) * block : (r * count + shard + 1) * block] for r in range(reps)]
        cut[shard] = jnp.concatenate(pieces, axis=1).astype(cut.dtype)


def cut_heads(count, ref, cut):
    group = HEADS // KV_HEADS
    for shard in range(count):
        heads = shard, HEADS + shard // group, HEADS + KV_HEADS + shard // group
        for index, head in enumerate(heads):
            cut[shard, :, index * HEAD_DIM : (index + 1) * HEAD_DIM] = ref[
                :, head * HEAD_DIM : (head + 1) * HEAD_DIM
            ].astype(cut.dtype)


class RepSum:
    def __init__(self, part, from_core, from_across, sems, rep, me):
        self.part, self.from_core, self.from_across = part, from_core, from_across
        self.c_send, self.c_recv, self.x_send, self.x_recv = sems
        self.across, self.beside = rep_partners(rep)
        self.rep, self.me = rep, me
        self.core = rep % 2
        self.chip = rep // 2

    def core_copy(self, side, piece):
        chip = 1 - self.chip if side == 0 else self.chip
        return remote(
            self.part(chip * 2 + 1 - self.core, piece),
            self.from_core.at[side, piece],
            self.c_send.at[side, piece],
            self.c_recv.at[side, piece],
            (self.beside, self.me),
        )

    def cross_copy(self, piece):
        return remote(
            self.from_core.at[0, piece],
            self.from_across.at[piece],
            self.x_send.at[piece],
            self.x_recv.at[piece],
            (self.across, self.me),
        )

    def begin(self, pieces):
        for side in (0, 1):
            for piece in pieces:
                self.core_copy(side, piece).start()

    def cross(self, piece):
        f32 = jnp.float32
        self.core_copy(0, piece).wait_recv()
        mine = self.part((1 - self.chip) * 2 + self.core, piece)[...].astype(f32)
        self.from_core[0, piece] = (mine + self.from_core[0, piece].astype(f32)).astype(jnp.bfloat16)
        self.cross_copy(piece).start()

    def total(self, piece):
        f32 = jnp.float32
        self.core_copy(1, piece).wait_recv()
        mine = self.part(self.rep, piece)[...].astype(f32) + self.from_core[1, piece].astype(f32)
        self.cross_copy(piece).wait_recv()
        return mine + self.from_across[piece].astype(f32)

    def finish(self, pieces):
        for piece in pieces:
            self.core_copy(0, piece).wait_send()
            self.core_copy(1, piece).wait_send()
            self.cross_copy(piece).wait_send()


class Spread:
    def __init__(self, blocks, out, send, recv, rep, me, count):
        self.blocks, self.out, self.send, self.recv = blocks, out, send, recv
        self.rep, self.me, self.count = rep, me, count

    def copy(self, k):
        to = (self.me + k) % self.count
        return remote(
            self.blocks.at[to], self.out.at[self.me], self.send.at[k], self.recv.at[k], (self.rep, to)
        )

    def arrived(self, k):
        frm = (self.me + self.count - k) % self.count
        return remote(
            self.blocks.at[frm], self.out.at[frm], self.send.at[k], self.recv.at[k], (self.rep, frm)
        )

    def finish(self):
        for k in range(1, self.count):
            self.arrived(k).wait_recv()
        for k in range(1, self.count):
            self.copy(k).wait_send()


def near_devices(ring):
    across, beside = rep_partners(ring.rep)
    return [(ring.rep, (ring.me + k) % ring.count) for k in range(1, ring.count)] + [
        (across, ring.me),
        (beside, ring.me),
    ]


class Gather:
    def __init__(self, ring, block, out, send, recv):
        self.ring, self.block, self.out, self.send, self.recv = ring, block, out, send, recv
        self.rows = block.shape[0] // UNITS
        self.started = []

    def copy(self, way, hop, unit):
        ring = self.ring
        origin = ring.away(1 - way, hop - 1) if hop > 1 else ring.me
        span = pl.ds(unit * self.rows, self.rows)
        return remote(
            self.block.at[span] if hop == 1 else self.out.at[origin, span],
            self.out.at[origin, span],
            self.send.at[way, hop - 1, unit],
            self.recv.at[way, hop - 1, unit],
            ring.next[way],
        )

    def go(self, copy):
        copy.start()
        self.started.append(copy)

    def begin(self):
        for index in range(UNITS):
            for way in (0, 1):
                self.go(self.copy(way, 1, self.ring.units(way, 1)[index]))

    def steps(self):
        ring = self.ring

        def step(hop, index):
            for way in (0, 1):
                unit = ring.units(way, hop)[index]
                self.copy(way, hop, unit).wait_recv()
                if hop < ring.half and unit in ring.units(way, hop + 1):
                    self.go(self.copy(way, hop + 1, unit))

        return [
            functools.partial(step, hop, index)
            for hop in range(1, ring.half + 1)
            for index in range(len(ring.units(0, hop)))
        ]

    def finish(self):
        for copy in self.started:
            copy.wait_send()


def tn(left, right):
    return lax.dot_general(left, right, (((0,), (0,)), ((), ())), preferred_element_type=jnp.float32)


DN_PIECES = 3


def ffn_grads_kernel(
    reps, count, dattn_ref, wo_ref, q_ref, k_ref, v_ref, cos_ref, sin_ref, h3_hbm, dgu_hbm, part_hbm, probs_hbm, damp_hbm,
    all_ref, sum_ref, down_ref, dproj,
    h3_ref, dgu_ref, g_part, g_core, g_from, d_part, d_core, d_from, probs_ref, damp_ref, d_key, d_value,
    t_send, t_recv, gc_s, gc_r, gx_s, gx_r, dc_s, dc_r, dx_s, dx_r, s_send, s_recv, loc, loads, square
):
    f32, bf16 = jnp.float32, jnp.bfloat16
    ring = Ring(count)
    rep, me = ring.rep, ring.me
    d_rows, columns = sum_ref.shape[1:]
    part, width = d_part.shape
    block = part // reps
    seq_len = q_ref.shape[0]
    blocks = 4
    tall = seq_len // blocks
    half = HEAD_DIM // 2
    fetched = [
        pltpu.make_async_copy(src, dst, loads.at[index])
        for index, (src, dst) in enumerate(((part_hbm, d_part), (h3_hbm, h3_ref), (dgu_hbm, dgu_ref)))
    ]
    for copy in fetched:
        copy.start()

    def squares(i):
        span = pl.ds(i * tall, tall)
        return [
            pltpu.make_async_copy(probs_hbm.at[span], probs_ref, square.at[0]),
            pltpu.make_async_copy(damp_hbm.at[span], damp_ref, square.at[1]),
        ]

    for copy in squares(0):
        copy.start()
    meet(near_devices(ring))
    gather = Gather(ring, dattn_ref, all_ref, t_send, t_recv)
    gather.begin()
    own = pltpu.make_async_copy(dattn_ref, all_ref.at[me], loc)
    own.start()

    def d_at(owner, piece):
        rows = block // DN_PIECES
        return d_part.at[pl.ds(owner * block + piece * rows, rows)]

    down = RepSum(d_at, d_core, d_from, (dc_s, dc_r, dx_s, dx_r), rep, me)
    gate_up = RepSum(
        lambda owner, piece: g_part.at[owner, piece], g_core, g_from, (gc_s, gc_r, gx_s, gx_r), rep, me
    )
    spread = Spread(g_from, sum_ref, s_send, s_recv, rep, me, count)
    d_pieces = list(range(DN_PIECES))
    g_pieces = [(me + k) % count for k in range(1, count)] + [me]

    def make_gate_up(owner):
        rows = count * d_rows
        step = columns // 3

        def body(n, carry):
            cols = pl.ds(pl.multiple_of(n * step, 128), step)
            made = tn(h3_ref[:, owner * rows : (owner + 1) * rows], dgu_ref[:, cols])
            g_part[owner, :, :, cols] = made.reshape(count, d_rows, step).astype(bf16)
            return carry

        lax.fori_loop(0, 3, body, 0)

    def nt(left, right):
        return lax.dot_general(left, right, (((1,), (1,)), ((), ())), preferred_element_type=f32)

    def unturned(flat, at):
        cosine, sine = cos_ref[at, :], sin_ref[at, :]
        low, high = flat[:, :half], flat[:, half:]
        return jnp.concatenate([low * cosine + high * sine, high * cosine - low * sine], axis=1)

    d_key[...] = jnp.zeros_like(d_key)
    d_value[...] = jnp.zeros_like(d_value)

    def attend(i):
        at = pl.ds(i * tall, tall)
        per = count // blocks
        d_out = all_ref[i * per : (i + 1) * per].reshape(tall, width)
        d_att = nt(d_out, wo_ref[...]).astype(bf16)
        d_probs = nt(d_att, v_ref[...])
        for copy in squares(i):
            copy.wait()
        probs = probs_ref[...]
        inner = jnp.sum(probs.astype(f32) * d_probs, axis=-1, keepdims=True)
        d_scores = (damp_ref[...].astype(f32) * (d_probs - inner)).astype(bf16)
        d_query = jnp.dot(d_scores, k_ref[...], preferred_element_type=f32)
        dproj[at, :HEAD_DIM] = (unturned(d_query, at) * HEAD_DIM ** (-0.5)).astype(bf16)
        d_key[...] += tn(d_scores, q_ref[at, :])
        d_value[...] += tn(probs, d_att)
        if i < blocks - 1:
            for copy in squares(i + 1):
                copy.start()

    def project():
        for i in range(blocks):
            at = pl.ds(i * tall, tall)
            dproj[at, HEAD_DIM : 2 * HEAD_DIM] = unturned(d_key[at, :], at).astype(bf16)
            dproj[at, 2 * HEAD_DIM :] = d_value[at, :].astype(bf16)

    def finish_gate_up(k):
        piece = g_pieces[k]
        total = gate_up.total(piece).astype(bf16)
        if k < count - 1:
            g_from[piece] = total
            spread.copy(k + 1).start()
        else:
            sum_ref[me] = total

    def finish_down(piece):
        rows = block // DN_PIECES
        down_ref[pl.ds(piece * rows, rows), :] = down.total(piece)

    fetched[0].wait()
    down.begin(d_pieces)
    for copy in fetched[1:]:
        copy.wait()
    work = [functools.partial(make_gate_up, 0)]
    work += [functools.partial(down.cross, piece) for piece in d_pieces]
    work += [functools.partial(make_gate_up, owner) for owner in range(1, reps)]
    work += [lambda: gate_up.begin(g_pieces)]
    work += [functools.partial(gate_up.cross, piece) for piece in g_pieces]
    for step in gather.steps():
        step()
        if work:
            work.pop(0)()
    for piece in work:
        piece()
    own.wait()
    after = [functools.partial(finish_gate_up, k) for k in range(count)]
    per = max(1, count // blocks)
    for i in range(blocks):
        attend(i)
        for _ in range(min(per, len(after) - 2)):
            after.pop(0)()
    project()
    for piece in d_pieces:
        finish_down(piece)
    for piece in after:
        piece()
    spread.finish()
    down.finish(d_pieces)
    gate_up.finish(g_pieces)
    gather.finish()


def ffn_grads(
    reps, count, d_attn, w_out, queries, keys, values, cosine, sine, h3, d_gu, part_down, probs, damp, d_rows, collective_id
):
    dma = pltpu.SemaphoreType.DMA
    low, f32 = jnp.bfloat16, jnp.float32
    shape = jax.ShapeDtypeStruct
    width = d_attn.shape[1]
    columns = d_gu.shape[1]
    part = part_down.shape[0]
    seq_len = h3.shape[0]
    block = part // reps
    blocks = (count, d_rows, columns)
    lots = (DN_PIECES, block // DN_PIECES, width)
    hops = dma((2, count // 2, UNITS))
    vm, hb = pl.BlockSpec(memory_space=VM), pl.BlockSpec(memory_space=HB)
    return pl.pallas_call(
        functools.partial(ffn_grads_kernel, reps, count),
        out_shape=[
            shape((count,) + d_attn.shape, low),
            shape(blocks, low),
            shape((block, width), f32),
            shape((seq_len, 3 * HEAD_DIM), low),
        ],
        in_specs=[vm] * 7 + [hb] * 5,
        out_specs=[vm] * 4,
        scratch_shapes=[
            pltpu.VMEM(h3.shape, low),
            pltpu.VMEM(d_gu.shape, low),
            pltpu.VMEM((reps,) + blocks, low),
            pltpu.VMEM((2,) + blocks, low),
            pltpu.VMEM(blocks, low),
            pltpu.VMEM((part, width), low),
            pltpu.VMEM((2,) + lots, low),
            pltpu.VMEM(lots, low),
            pltpu.VMEM((seq_len // 4, seq_len), low),
            pltpu.VMEM((seq_len // 4, seq_len), low),
            pltpu.VMEM((seq_len, HEAD_DIM), f32),
            pltpu.VMEM((seq_len, HEAD_DIM), f32),
            hops,
            hops,
            dma((2, count)),
            dma((2, count)),
            dma((count,)),
            dma((count,)),
            dma((2, DN_PIECES)),
            dma((2, DN_PIECES)),
            dma((DN_PIECES,)),
            dma((DN_PIECES,)),
            dma((count,)),
            dma((count,)),
            dma,
            dma((3,)),
            dma((2,)),
        ],
        compiler_params=pltpu.CompilerParams(
            collective_id=collective_id, has_side_effects=True, vmem_limit_bytes=VMEM_LIMIT
        ),
        name="ffn_grads",
    )(d_attn, w_out, queries, keys, values, cosine, sine, h3, d_gu, part_down, probs, damp)


def closing_kernel(
    reps, count, dproj, in_ref, att_ref, h1_hbm, dattn_hbm, tokens_ref, dmid_ref, gains_ref, gg_ref,
    grad_ref, sum_ref, out_ref, gain_ref,
    h1_ref, dattn_ref, x_part, i_part, o_part, first, landed, total_ref, tiles, i_core, i_from, o_core, o_from,
    r_send, r_recv, ic_s, ic_r, ix_s, ix_r, oc_s, oc_r, ox_s, ox_r, s_send, s_recv, p_send, p_recv,
    g_send, g_recv, loads
):
    f32, bf16 = jnp.float32, jnp.bfloat16
    ring = Ring(count)
    rep, me = ring.rep, ring.me
    here = rep * count + me
    others = everyone(rep, me, reps, count)
    full = o_part.shape[1]
    d_rows = sum_ref.shape[1]
    seq_len, width = dattn_ref.shape
    rows = grad_ref.shape[0]
    fetched = [
        pltpu.make_async_copy(h1_hbm, h1_ref, loads.at[0]),
        pltpu.make_async_copy(dattn_hbm, dattn_ref, loads.at[1]),
    ]
    for copy in fetched:
        copy.start()
    meet(others)
    tall = seq_len // 4

    def project(i, carry):
        at = pl.ds(pl.multiple_of(i * tall, 16), tall)
        x_part[at, :] = lax.dot_general(
            dproj[at, :], in_ref[...], (((1,), (1,)), ((), ())), preferred_element_type=f32
        ).astype(bf16)
        return carry

    lax.fori_loop(0, 4, project, 0)

    def make_out():
        fetched[1].wait()
        per = width // 3

        def body(n, carry):
            cols = pl.ds(pl.multiple_of(n * per, 128), per)
            made = tn(att_ref[...], dattn_ref[:, cols]).reshape(full, reps, HEAD_DIM // full // reps, per)
            for owner in range(reps):
                o_part[owner, :, :, cols] = made[:, owner].astype(bf16)
            return carry

        lax.fori_loop(0, 3, body, 0)

    def make_in(owner):
        if owner == 0:
            fetched[0].wait()
        deep = count * d_rows
        made = tn(h1_ref[:, owner * deep : (owner + 1) * deep], dproj[...])
        i_part[owner] = made.reshape(count, d_rows, 3 * HEAD_DIM).astype(bf16)

    o_pieces = list(range(full))
    i_pieces = [(me + k) % count for k in range(1, count)] + [me]
    ins = RepSum(lambda owner, piece: i_part.at[owner, piece], i_core, i_from, (ic_s, ic_r, ix_s, ix_r), rep, me)
    outs = RepSum(lambda owner, piece: o_part.at[owner, piece], o_core, o_from, (oc_s, oc_r, ox_s, ox_r), rep, me)
    spread = Spread(i_from, sum_ref, s_send, s_recv, rep, me, count)

    def o_owner(piece):
        where = me * full + piece
        return where // count, where % count

    def o_copy(piece):
        return remote(o_from.at[piece], out_ref.at[rep], p_send.at[piece], p_recv.at[rep], o_owner(piece))

    def o_self(piece):
        return me * full + piece == here

    def o_finish(piece):
        total = outs.total(piece).astype(bf16)
        o_from[piece] = total

        @pl.when(jnp.logical_not(o_self(piece)))
        def _():
            o_copy(piece).start()

        @pl.when(o_self(piece))
        def _():
            pltpu.make_async_copy(o_from.at[piece], out_ref.at[rep], p_recv.at[rep]).start()

    def i_finish(k):
        piece = i_pieces[k]
        total = ins.total(piece).astype(bf16)
        if k < count - 1:
            i_from[piece] = total
            spread.copy(k + 1).start()
        else:
            sum_ref[me] = total

    work = [functools.partial(make_in, owner) for owner in range(reps)]
    work += [lambda: ins.begin(i_pieces), make_out, lambda: outs.begin(o_pieces)]
    work += [functools.partial(ins.cross, piece) for piece in i_pieces]
    work += [functools.partial(outs.cross, piece) for piece in o_pieces]
    work += [functools.partial(i_finish, k) for k in range(count)]
    work += [functools.partial(o_finish, piece) for piece in o_pieces]

    terms = []
    gain = 1.0 + gains_ref[0:1, :]

    def pause():
        for _ in range(min(2, len(work))):
            work.pop(0)()

    def take(shard, span):
        return x_part[pl.ds(pl.multiple_of(shard * rows + span.start, 16), span.size), :]

    def finish(span, total):
        value = tokens_ref[span, :].astype(f32)
        scale = lax.rsqrt(jnp.mean(value * value, axis=-1, keepdims=True) + 1e-06)
        normed = value * scale
        weighted = total * gain
        inner = jnp.mean(weighted * normed, axis=-1, keepdims=True)
        grad_ref[span, :] = dmid_ref[span, :] + scale * (weighted - normed * inner)
        terms.append(jnp.sum(total * normed, axis=0, keepdims=True))

    started = reduce_on_ring(ring, rows, take, first, landed, r_send, r_recv, finish, pause)
    total_ref[...] = gg_ref[...]
    total_ref[0:1, :] = functools.reduce(jnp.add, terms)
    every = total_ref[...]
    for owner in range(reps * count):
        tiles[owner, :, 0:d_rows] = every[:, owner * d_rows : (owner + 1) * d_rows]
        tiles[owner, :, d_rows:] = jnp.zeros((8, 128 - d_rows), f32)
    for k, device in enumerate(others):
        to = (here + k + 1) % (reps * count)
        remote(tiles.at[to], gain_ref.at[here], g_send.at[k], g_recv.at[k], device).start()
    gain_ref[here] = tiles[here]
    for piece in work:
        piece()
    for k in range(len(others)):
        frm = (here + len(others) - k) % (reps * count)
        remote(tiles.at[frm], gain_ref.at[frm], g_send.at[k], g_recv.at[k], others[k]).wait_recv()
    for j in range(reps):
        remote(
            o_from.at[0], out_ref.at[j], p_send.at[0], p_recv.at[j], (rep, (me + 1) % count)
        ).wait_recv()
    for piece in o_pieces:
        @pl.when(jnp.logical_not(o_self(piece)))
        def _():
            o_copy(piece).wait_send()
    spread.finish()
    ins.finish(i_pieces)
    outs.finish(o_pieces)
    for k, device in enumerate(others):
        to = (here + k + 1) % (reps * count)
        remote(tiles.at[to], gain_ref.at[here], g_send.at[k], g_recv.at[k], device).wait_send()
    for copy in started:
        copy.wait_send()


def closing(
    reps, count, d_projected, w_in, attended, normed, d_attn, tokens, d_middle, gain_rows, gain_terms, piece, collective_id
):
    dma = pltpu.SemaphoreType.DMA
    low, f32 = jnp.bfloat16, jnp.float32
    shape = jax.ShapeDtypeStruct
    rows, width = tokens.shape
    seq_len = normed.shape[0]
    total = reps * count
    half = count // 2
    d_rows = width // total
    full = HEAD_DIM // (reps * piece)
    i_block = (count, d_rows, 3 * HEAD_DIM)
    o_block = (full, piece, width)
    hops = dma((2, half, UNITS))
    vm, hb = pl.BlockSpec(memory_space=VM), pl.BlockSpec(memory_space=HB)
    return pl.pallas_call(
        functools.partial(closing_kernel, reps, count),
        out_shape=[
            shape((rows, width), f32),
            shape(i_block, low),
            shape((reps, piece, width), low),
            shape((total, 8, 128), f32),
        ],
        in_specs=[vm] * 3 + [hb] * 2 + [vm] * 4,
        out_specs=[vm] * 4,
        scratch_shapes=[
            pltpu.VMEM((seq_len, width), low),
            pltpu.VMEM((seq_len, width), low),
            pltpu.VMEM((seq_len, width), low),
            pltpu.VMEM((reps,) + i_block, low),
            pltpu.VMEM((reps,) + o_block, low),
            pltpu.VMEM((rows, width), low),
            pltpu.VMEM((2, half, rows, width), low),
            pltpu.VMEM((8, width), f32),
            pltpu.VMEM((total, 8, 128), f32),
            pltpu.VMEM((2,) + i_block, low),
            pltpu.VMEM(i_block, low),
            pltpu.VMEM((2,) + o_block, low),
            pltpu.VMEM(o_block, low),
            hops,
            hops,
            dma((2, count)),
            dma((2, count)),
            dma((count,)),
            dma((count,)),
            dma((2, full)),
            dma((2, full)),
            dma((full,)),
            dma((full,)),
            dma((count,)),
            dma((count,)),
            dma((full,)),
            dma((reps,)),
            dma((total - 1,)),
            dma((total - 1,)),
            dma((2,)),
        ],
        compiler_params=pltpu.CompilerParams(
            collective_id=collective_id, has_side_effects=True, vmem_limit_bytes=VMEM_LIMIT
        ),
        name="closing",
    )(d_projected, w_in, attended, normed, d_attn, tokens, d_middle, gain_rows, gain_terms)


def tiles_of(ref):
    rows, columns = ref.shape
    tall = 72 if rows % 72 == 0 else 64 if rows % 64 == 0 else 8
    wide = 384 if columns % 384 == 0 else 256
    return rows // tall, columns // wide, tall, wide


def tile_at(ref, n):
    _, across, tall, wide = tiles_of(ref)
    down, right = n // across, n % across
    return pl.ds(pl.multiple_of(down * tall, 8), tall), pl.ds(pl.multiple_of(right * wide, 128), wide)


LAMB_ORDER = (4, 2, 3, 0, 1)


def lamb_kernel(reps, count, sum_in, sum_out, sum_gu, gain_tiles, g_master, g_mean, g_square, *refs):
    f32 = jnp.float32
    names = 5
    hbm_in, refs = [refs[3 * i : 3 * i + 3] for i in range(names)], refs[3 * names :]
    grad_dn, refs = refs[0], refs[1:]
    (sums_out, gg_out, gm_out, gs_out, gp_out), refs = refs[:5], refs[5:]
    hbm_out, refs = [refs[4 * i : 4 * i + 4] for i in range(names)], refs[4 * names :]
    masters, means, squares, grads = (refs[names * i : names * (i + 1)] for i in range(4))
    in_sem, out_sem, dn_sem = refs[4 * names :]
    total = reps * count
    group = HEADS // KV_HEADS

    def fetch(i, j):
        return pltpu.make_async_copy(hbm_in[i][j], (masters, means, squares)[j][i], in_sem.at[i, j])

    fetch_dn = pltpu.make_async_copy(grad_dn, grads[4], dn_sem)
    fetch_dn.start()
    for i in LAMB_ORDER:
        for j in range(3):
            fetch(i, j).start()

    def store(i, j):
        return pltpu.make_async_copy((grads, means, squares, masters)[j][i], hbm_out[i][j], out_sem.at[i, j])

    def join(index, ref):
        block = ref.shape[1] // total
        part = block * reps
        for first in range(0, total, 4):
            pieces = []
            for b in range(first, first + 4):
                start = index * part + (b // count) * block
                pieces.append(sum_gu[b % count, :, start : start + block].astype(f32))
            ref[:, first * block : (first + 4) * block] = jnp.concatenate(pieces, axis=1)

    def make_grad(i):
        if i == 0:
            for head in range(HEADS):
                grads[0][:, head * HEAD_DIM : (head + 1) * HEAD_DIM] = sum_in[head, :, :HEAD_DIM].astype(f32)
            for kind in (1, 2):
                for head in range(KV_HEADS):
                    start = (HEADS + (kind - 1) * KV_HEADS + head) * HEAD_DIM
                    parts = [
                        sum_in[head * group + g, :, kind * HEAD_DIM : (kind + 1) * HEAD_DIM].astype(f32)
                        for g in range(group)
                    ]
                    grads[0][:, start : start + HEAD_DIM] = functools.reduce(jnp.add, parts)
        elif i == 1:
            rows = sum_out.shape[1]
            for j in range(reps):
                grads[1][j * rows : (j + 1) * rows, :] = sum_out[j].astype(f32)
        elif i in (2, 3):
            join(i - 2, grads[i])
        else:
            fetch_dn.wait()

    def lamb(master, grad, mean, square):
        new_mean = 0.5 * mean + 0.5 * grad
        new_square = 0.5 * square + 0.5 * grad * grad
        return new_mean, new_square, new_mean / (jnp.sqrt(new_square) + 1e-06) + 0.01 * master

    def sweep(i):
        down, across, tall, wide = tiles_of(masters[i])

        def body(n, carry):
            at = tile_at(masters[i], n)
            master = masters[i][at]
            new_mean, new_square, step = lamb(master, grads[i][at], means[i][at], squares[i][at])
            means[i][at] = new_mean
            squares[i][at] = new_square
            masters[i][at] = step

            def fold(value):
                return jnp.sum((value * value).reshape(tall // 8, 8, wide), axis=0)

            return carry[0] + fold(master), carry[1] + fold(step)

        zero = jnp.zeros((8, wide), f32)
        return lax.fori_loop(0, down * across, body, (zero, zero))

    at_row = lax.broadcasted_iota(jnp.int32, (8, 128), 0)
    at_lane = lax.broadcasted_iota(jnp.int32, (8, 128), 1)

    def note(sums, i, pair):
        for row in (0, 1):
            sums = sums + jnp.where((at_row == row) & (at_lane == i), jnp.sum(pair[row]), 0.0)
        return sums

    sums = jnp.zeros((8, 128), f32)
    for i in LAMB_ORDER:
        make_grad(i)
        for j in range(3):
            fetch(i, j).wait()
        pair = sweep(i)
        for j in range(4):
            store(i, j).start()
        sums = note(sums, i, pair)
    gain_total = functools.reduce(jnp.add, [gain_tiles[device] for device in range(total)])
    kinds, d_rows = g_master.shape
    gain_grad = gain_total[:kinds, :d_rows]
    gain_master = g_master[...]
    new_mean, new_square, gain_step = lamb(gain_master, gain_grad, g_mean[...], g_square[...])
    gg_out[...] = gain_grad
    gm_out[...] = new_mean
    gs_out[...] = new_square
    gp_out[...] = gain_step
    sums_out[...] = note(sums, 5, (gain_master * gain_master, gain_step * gain_step))
    for i in LAMB_ORDER:
        for j in range(4):
            store(i, j).wait()


def table_kernel(reps, count, sizes, x_ref, out_ref, near, far, held, n_send, n_recv, f_send, f_recv):
    f32 = jnp.float32
    rep = lax.axis_index("rep")
    me = lax.axis_index("shard")
    meet(
        [(rep, (me + k) % count) for k in range(1, count)] + [((rep + k) % reps, me) for k in range(1, reps)]
    )
    copies = []
    for k in range(1, count):
        copies.append(remote(x_ref, near.at[me], n_send.at[k], n_recv.at[k], (rep, (me + k) % count)))
    for copy in copies:
        copy.start()
    near[me] = x_ref[...]
    for k in range(1, count):
        frm = (me + count - k) % count
        remote(x_ref, near.at[frm], n_send.at[k], n_recv.at[k], (rep, frm)).wait_recv()
    sums = functools.reduce(jnp.add, [near[shard] for shard in range(count)])
    held[...] = sums
    more = []
    for k in range(1, reps):
        more.append(remote(held, far.at[rep], f_send.at[k], f_recv.at[k], ((rep + k) % reps, me)))
    for copy in more:
        copy.start()
    far[rep] = sums
    for k in range(1, reps):
        frm = (rep + reps - k) % reps
        remote(held, far.at[frm], f_send.at[k], f_recv.at[k], (frm, me)).wait_recv()
    totals = functools.reduce(jnp.add, [far[other] for other in range(reps)])
    at_lane = lax.broadcasted_iota(jnp.int32, (8, 128), 1)
    counts = jnp.ones((8, 128), f32)
    for i, size in enumerate(sizes):
        counts = jnp.where(at_lane == i, float(size), counts)
    out_ref[...] = jnp.sqrt(totals / counts + 1e-06)
    for copy in copies + more:
        copy.wait_send()


def fresh_kernel(table_ref, g_master, g_step, *refs):
    names = 5
    hbm_in, refs = [refs[2 * i : 2 * i + 2] for i in range(names)], refs[2 * names :]
    (gp_out, table_out), refs = refs[:2], refs[2:]
    hbm_out, refs = refs[:names], refs[names:]
    masters, steps, refs = refs[:names], refs[names : 2 * names], refs[2 * names :]
    in_sem, out_sem = refs

    def fetch(i, j):
        return pltpu.make_async_copy(hbm_in[i][j], (masters, steps)[j][i], in_sem.at[i, j])

    def store(i):
        return pltpu.make_async_copy(masters[i], hbm_out[i], out_sem.at[i])

    for i in LAMB_ORDER:
        for j in (0, 1):
            fetch(i, j).start()
    table_out[...] = table_ref[0:2, 0 : names + 1]
    rate = 0.3 * table_ref[0:1, :] / table_ref[1:2, :]
    gp_out[...] = g_master[...] - rate[:, 5:6] * g_step[...]
    for i in LAMB_ORDER:
        down, across, _, _ = tiles_of(masters[i])
        scale = rate[:, i : i + 1]
        for j in (0, 1):
            fetch(i, j).wait()

        def body(n, carry):
            at = tile_at(masters[i], n)
            masters[i][at] = masters[i][at] - scale * steps[i][at]
            return carry

        lax.fori_loop(0, down * across, body, 0)
        store(i).start()
    for i in LAMB_ORDER:
        store(i).wait()


def lamb_step(reps, count, sums, grad_down, gains, states, collective_id):
    dma = pltpu.SemaphoreType.DMA
    f32 = jnp.float32
    shape = jax.ShapeDtypeStruct
    shapes = [state[0].shape for state in states]
    like_gains = shape(gains[0].shape, f32)
    tile = shape((8, 128), f32)
    vm, hb = pl.BlockSpec(memory_space=VM), pl.BlockSpec(memory_space=HB)
    local = pltpu.CompilerParams(vmem_limit_bytes=VMEM_LIMIT)
    outs = pl.pallas_call(
        functools.partial(lamb_kernel, reps, count),
        out_shape=[tile] + [like_gains] * 4 + [shape(item, f32) for item in shapes for _ in range(4)],
        in_specs=[vm] * 7 + [hb] * 16,
        out_specs=[vm] * 5 + [hb] * 20,
        scratch_shapes=[pltpu.VMEM(item, f32) for _ in range(4) for item in shapes] + [dma((5, 3)), dma((5, 4)), dma],
        compiler_params=local,
        name="lamb_moments",
    )(*sums, *gains, *[item for state in states for item in state], grad_down)
    sums, gain_parts, parts = outs[0], outs[1:5], [outs[5 + 4 * i : 9 + 4 * i] for i in range(5)]
    sizes = [item[0] * item[1] * reps * count for item in shapes + [like_gains.shape]]
    table = pl.pallas_call(
        functools.partial(table_kernel, reps, count, sizes),
        out_shape=tile,
        in_specs=[vm],
        out_specs=vm,
        scratch_shapes=[
            pltpu.VMEM((count, 8, 128), f32),
            pltpu.VMEM((reps, 8, 128), f32),
            pltpu.VMEM((8, 128), f32),
            dma((count,)),
            dma((count,)),
            dma((reps,)),
            dma((reps,)),
        ],
        compiler_params=pltpu.CompilerParams(collective_id=collective_id, has_side_effects=True),
        name="norm_table",
    )(sums)
    fresh = pl.pallas_call(
        fresh_kernel,
        out_shape=[like_gains, shape((2, 6), f32)] + [shape(item, f32) for item in shapes],
        in_specs=[vm] * 3 + [hb] * 10,
        out_specs=[vm] * 2 + [hb] * 5,
        scratch_shapes=[pltpu.VMEM(item, f32) for _ in range(2) for item in shapes] + [dma((5, 2)), dma((5,))],
        compiler_params=local,
        name="lamb_masters",
    )(table, gains[0], gain_parts[3], *[item for i in range(5) for item in (states[i][0], parts[i][3])])
    rest = [[parts[i][j] for i in range(5)] + [gain_parts[j].T] for j in range(3)]
    return fresh[1], rest[0], rest[1], rest[2], list(fresh[2:]) + [fresh[0].T]


def rope_tables(seq_len):
    exponent = -np.arange(HEAD_DIM // 2, dtype=np.float32) * np.float32(2.0) / np.float32(HEAD_DIM)
    freq = np.float32(10000.0) ** exponent
    angle = (np.arange(seq_len, dtype=np.float32)[:, None] * freq[None, :]).astype(np.float64)
    return jnp.asarray(np.cos(angle).astype(np.float32)), jnp.asarray(np.sin(angle).astype(np.float32))


def split_device(
    tokens, cotangent, piece_starts, inproj, outproj, ffn_gate, ffn_up, ffn_down, norm_gains,
    mean_inproj, mean_outproj, mean_gate, mean_up, mean_down, mean_gains,
    square_inproj, square_outproj, square_gate, square_up, square_down, square_gains,
):
    bf16, f32 = jnp.bfloat16, jnp.float32
    reps, count = lax.axis_size("rep"), lax.axis_size("shard")
    rep = lax.axis_index("rep")
    me = lax.axis_index("shard")
    total = reps * count
    rows, width = tokens.shape
    seq_len = rows * count
    group = HEADS // KV_HEADS
    q_width, k_width = HEADS * HEAD_DIM, KV_HEADS * HEAD_DIM
    d_rows = inproj.shape[0]
    ff = ffn_gate.shape[1]
    ff_block = ff // total
    ff_part = ff // count
    o_rows = outproj.shape[0]
    per_head = HEAD_DIM // o_rows
    piece = o_rows // reps

    gain_tile = jnp.pad(norm_gains.T.astype(bf16).astype(f32), ((0, 4), (0, 128 - d_rows)))
    normed_in, gain_rows, got_in, got_gate, got_down, got_out, cut_up = opening(
        reps, count, tokens, gain_tile, inproj, outproj, ffn_gate, ffn_up, ffn_down, 1
    )
    normed_in = normed_in.reshape(seq_len, width)
    w_in = got_in.reshape(width, -1)
    w_gate = got_gate.reshape(width, ff_part)
    w_down = got_down.reshape(ff_part, width)

    position = jnp.arange(seq_len, dtype=jnp.int32)
    cosine, sine = rope_tables(seq_len)
    starts = lax.dynamic_slice_in_dim(piece_starts, rep, 1, 0)[0]
    inside = (position[:, None] >= starts[None, :]) & (position[:, None] < starts[None, :] + PIC)
    tag = jnp.sum(inside.astype(jnp.int32) * (jnp.arange(starts.shape[0], dtype=jnp.int32)[None, :] + 1), axis=1)
    attn_proj, queries, keys, values, attended, probs, damp, w_out, got_up = attention(
        reps, count, normed_in, w_in, got_out, cosine, sine, tag, cut_up, 4
    )
    w_up = got_up.reshape(width, ff_part)

    layer_out, d_middle, d_attn, gain_terms, normed_mid, d_gu, part_down = feed_forward(
        attn_proj, tokens, cotangent, gain_rows, w_gate, w_up, w_down, count, 5
    )
    d_attn, sum_gu, grad_down, d_projected = ffn_grads(
        reps, count, d_attn, w_out, queries, keys, values, cosine, sine, normed_mid, d_gu, part_down, probs, damp, d_rows, 9
    )
    input_grad, sum_in, sum_out, gain_tiles = closing(
        reps, count, d_projected, w_in, attended, normed_in, d_attn.reshape(seq_len, width), tokens, d_middle,
        gain_rows, gain_terms, piece, 12,
    )
    norm_table, gradients, new_means, new_squares, fresh = lamb_step(
        reps,
        count,
        (sum_in, sum_out, sum_gu, gain_tiles),
        grad_down,
        (norm_gains.T, mean_gains.T, square_gains.T),
        (
            (inproj, mean_inproj, square_inproj),
            (outproj, mean_outproj, square_outproj),
            (ffn_gate, mean_gate, square_gate),
            (ffn_up, mean_up, square_up),
            (ffn_down, mean_down, square_down),
        ),
        14,
    )
    return (
        layer_out,
        input_grad,
        *gradients,
        *new_means,
        *new_squares,
        *fresh,
        norm_table,
    )


def fits(mesh, shapes):
    reps, count = mesh.shape["rep"], mesh.shape["shard"]
    total = reps * count
    tokens, piece_starts, outproj, ffn_gate = shapes
    o_rows = outproj[0] // total
    return (
        reps == 4
        and count == HEADS
        and piece_starts[0] == reps
        and tokens[0] % (total * UNITS * 16) == 0
        and HEAD_DIM % o_rows == 0
        and o_rows % (16 * reps) == 0
        and HEAD_DIM // o_rows == total // HEADS
        and ffn_gate[1] % (total * 96) == 0
    )


def solution(mesh):
    split = P(("rep", "shard"), None)

    def step(*args):
        shapes = args[0].shape, args[2].shape, args[4].shape, args[5].shape
        body = split_device if fits(mesh, shapes) else per_device
        return jax.shard_map(
            body,
            mesh=mesh,
            in_specs=(split, split, P()) + (split,) * 18,
            out_specs=(split,) * 26 + (P(),),
            check_vma=False,
        )(*args)

    return step
```

```python
import functools

import jax
import jax.numpy as jnp
from jax import lax
from jax.experimental import pallas as pl
from jax.experimental.pallas import tpu as pltpu
import numpy as np
from jax.sharding import PartitionSpec as P

HEADS = 8
KV_HEADS = 4
HEAD_DIM = 256
PIC = 256


def rms_norm(values_in, gain_col):
    return (
        values_in
        * lax.rsqrt(jnp.mean(values_in * values_in, axis=-1, keepdims=True) + 1e-06)
        * (1.0 + gain_col)
    )


def geglu(gate_lin, up_lin):
    return jax.nn.gelu(gate_lin, approximate=True) * up_lin


def rotate(flat, position, head_count, sign):
    row_count = flat.shape[0]
    width = flat.shape[1] // head_count
    half = width // 2
    vectors = flat.reshape(row_count, head_count, width)
    freq = 10000.0 ** (-(jnp.arange(half, dtype=jnp.float32) * 2.0 / width))
    angle = position.astype(jnp.float32)[:, None] * freq[None, :]
    cosine = jnp.cos(angle)[:, None, :]
    sine = sign * jnp.sin(angle)[:, None, :]
    first = vectors[..., :half]
    second = vectors[..., half:]
    turned = jnp.concatenate(
        [first * cosine - second * sine, second * cosine + first * sine], axis=-1
    )
    return turned.reshape(row_count, head_count * width)


def owned_rows(activation, gradient, rep_index, width):
    piece = lax.dynamic_slice_in_dim(activation, rep_index * width, width, 1)
    return lax.dot_general(
        piece, gradient, (((0,), (0,)), ((), ())), preferred_element_type=jnp.float32
    )


def back_dot(gradient, weight):
    return lax.dot_general(
        gradient, weight, (((1,), (1,)), ((), ())), preferred_element_type=jnp.float32
    )


def describe(rows, piece_starts, seq_offset, seq_len):
    local_seq = rows // seq_len
    position = rows % seq_len
    global_seq = local_seq + seq_offset
    seq_total = piece_starts.shape[0]
    piece_count = piece_starts.shape[1]
    select = (global_seq[:, None] == jnp.arange(seq_total, dtype=jnp.int32)[None, :]).astype(
        jnp.int32
    )
    starts = jnp.sum(select[:, :, None] * piece_starts[None, :, :], axis=1)
    inside = ((position[:, None] >= starts) & (position[:, None] < starts + PIC)).astype(jnp.int32)
    labels = (
        global_seq[:, None] * piece_count + jnp.arange(piece_count, dtype=jnp.int32)[None, :] + 1
    )
    return (local_seq, position, jnp.sum(inside * labels, axis=1))


def visibility(piece_starts, query_rows, key_rows, seq_offset, seq_len):
    seq_q, pos_q, tag_q = describe(query_rows, piece_starts, seq_offset, seq_len)
    seq_k, pos_k, tag_k = describe(key_rows, piece_starts, seq_offset, seq_len)
    causal = pos_k[None, :] <= pos_q[:, None]
    same_piece = (tag_q[:, None] == tag_k[None, :]) & (tag_q[:, None] > 0)
    return (seq_q[:, None] == seq_k[None, :]) & (causal | same_piece)


def lamb_local(master, gradient, first, second):
    newmean = 0.5 * first + 0.5 * gradient
    newsquare = 0.5 * second + 0.5 * gradient * gradient
    step_dir = newmean / (jnp.sqrt(newsquare) + 1e-06) + 0.01 * master
    return (newmean, newsquare, step_dir)


def per_device(
    tokens,
    cotangent,
    piece_starts,
    inproj,
    outproj,
    ffn_gate,
    ffn_up,
    ffn_down,
    norm_gains,
    mean_inproj,
    mean_outproj,
    mean_gate,
    mean_up,
    mean_down,
    mean_gains,
    square_inproj,
    square_outproj,
    square_gate,
    square_up,
    square_down,
    square_gains,
):
    bf16 = jnp.bfloat16
    f32 = jnp.float32
    rep_count = lax.axis_size("rep")
    shard_count = lax.axis_size("shard")
    rep_index = lax.axis_index("rep")
    w_in, w_out, w_gate, w_up, w_down, gain_copy = (
        lax.all_gather(inproj.astype(bf16), ("rep", "shard"), axis=0, tiled=True),
        lax.all_gather(outproj.astype(bf16), ("rep", "shard"), axis=0, tiled=True),
        lax.all_gather(ffn_gate.astype(bf16), ("rep", "shard"), axis=0, tiled=True),
        lax.all_gather(ffn_up.astype(bf16), ("rep", "shard"), axis=0, tiled=True),
        lax.all_gather(ffn_down.astype(bf16), ("rep", "shard"), axis=0, tiled=True),
        lax.all_gather(norm_gains.astype(bf16), ("rep", "shard"), axis=0, tiled=True),
    )
    gains_used = gain_copy.astype(f32)
    residual = tokens.astype(f32)
    row_count = residual.shape[0]
    seq_len = row_count * shard_count
    q_width = HEADS * HEAD_DIM
    k_width = KV_HEADS * HEAD_DIM
    group_size = HEADS // KV_HEADS
    query_scale = HEAD_DIM ** (-0.5)
    local_rows = lax.axis_index("shard") * row_count + jnp.arange(row_count, dtype=jnp.int32)
    position = local_rows % seq_len
    normed_in = rms_norm(residual, gains_used[:, 0]).astype(bf16)
    projected = jnp.dot(normed_in, w_in, preferred_element_type=f32)
    queries = (rotate(projected[:, :q_width], position, HEADS, 1.0) * query_scale).astype(bf16)
    keys = rotate(projected[:, q_width : q_width + k_width], position, KV_HEADS, 1.0).astype(bf16)
    values = projected[:, q_width + k_width :].astype(bf16)
    all_keys, all_values = (
        lax.all_gather(keys, "shard", axis=0, tiled=True),
        lax.all_gather(values, "shard", axis=0, tiled=True),
    )
    key_rows = all_keys.shape[0]
    visible = visibility(
        piece_starts,
        local_rows,
        jnp.arange(key_rows, dtype=jnp.int32),
        rep_index * (key_rows // seq_len),
        seq_len,
    )
    query_heads = queries.reshape(row_count, KV_HEADS, group_size, HEAD_DIM)
    key_heads = all_keys.reshape(key_rows, KV_HEADS, HEAD_DIM)
    value_heads = all_values.reshape(key_rows, KV_HEADS, HEAD_DIM)

    def capped_scores():
        raw_scores = jnp.einsum(
            "tgrd,kgd->grtk", query_heads, key_heads, preferred_element_type=f32
        )
        bent_scores = jnp.tanh(raw_scores / 50.0)
        return (bent_scores, jnp.where(visible, 50.0 * bent_scores, -1e30))

    bent_scores, masked = capped_scores()
    top_score = jnp.max(masked, axis=-1, keepdims=True)
    log_total = top_score + jnp.log(jnp.sum(jnp.exp(masked - top_score), axis=-1, keepdims=True))
    probs_low = jnp.exp(masked - log_total).astype(bf16)
    attended = (
        jnp.einsum("grtk,kgd->tgrd", probs_low, value_heads, preferred_element_type=f32)
        .reshape(row_count, q_width)
        .astype(bf16)
    )
    attn_proj = jnp.dot(attended, w_out, preferred_element_type=f32)
    middle = residual + rms_norm(attn_proj, gains_used[:, 1])
    normed_mid = rms_norm(middle, gains_used[:, 2]).astype(bf16)
    gate_lin = jnp.dot(normed_mid, w_gate, preferred_element_type=f32)
    up_lin = jnp.dot(normed_mid, w_up, preferred_element_type=f32)
    hidden = geglu(gate_lin, up_lin).astype(bf16)
    ffn_proj = jnp.dot(hidden, w_down, preferred_element_type=f32)
    layer_out = (middle + rms_norm(ffn_proj, gains_used[:, 3])).astype(bf16)
    d_out = cotangent.astype(f32)
    _, post_back = jax.vjp(rms_norm, ffn_proj, gains_used[:, 3])
    d_ffn, d_gain3 = post_back(d_out)
    d_ffn_low = d_ffn.astype(bf16)
    hidden_all, d_ffn_all = (
        lax.all_gather(hidden, "rep", axis=0, tiled=True),
        lax.all_gather(d_ffn_low, "rep", axis=0, tiled=True),
    )
    part_down = owned_rows(hidden_all, d_ffn_all, rep_index, hidden.shape[1] // rep_count)
    d_hidden = back_dot(d_ffn_low, w_down)
    _, glu_back = jax.vjp(geglu, gate_lin, up_lin)
    d_gate, d_up = glu_back(d_hidden)
    d_gate_low = d_gate.astype(bf16)
    d_up_low = d_up.astype(bf16)
    gate_up_grad = jnp.concatenate([d_gate_low, d_up_low], axis=1)
    mid_all, gate_up_all = (
        lax.all_gather(normed_mid, "rep", axis=0, tiled=True),
        lax.all_gather(gate_up_grad, "rep", axis=0, tiled=True),
    )
    part_gate_up = owned_rows(mid_all, gate_up_all, rep_index, normed_mid.shape[1] // rep_count)
    d_mid_in = back_dot(d_gate_low, w_gate) + back_dot(d_up_low, w_up)
    _, pre_back = jax.vjp(rms_norm, middle, gains_used[:, 2])
    d_mid_part, d_gain2 = pre_back(d_mid_in)
    d_middle = d_out + d_mid_part
    _, attn_back = jax.vjp(rms_norm, attn_proj, gains_used[:, 1])
    d_attn, d_gain1 = attn_back(d_middle)
    d_attn_low = d_attn.astype(bf16)
    d_attended = back_dot(d_attn_low, w_out).astype(bf16)
    d_heads = d_attended.reshape(row_count, KV_HEADS, group_size, HEAD_DIM)
    bent_again, masked_again = capped_scores()
    attn_probs = jnp.exp(masked_again - log_total)
    probs_again = attn_probs.astype(bf16)
    d_probs = jnp.einsum("tgrd,kgd->grtk", d_heads, value_heads, preferred_element_type=f32)
    d_scores = (
        attn_probs
        * (d_probs - jnp.sum(attn_probs * d_probs, axis=-1, keepdims=True))
        * (1.0 - bent_again * bent_again)
    ).astype(bf16)
    d_queries = jnp.einsum(
        "grtk,kgd->tgrd", d_scores, key_heads, preferred_element_type=f32
    ).reshape(row_count, q_width)
    d_key = jnp.einsum("grtk,tgrd->kgd", d_scores, query_heads, preferred_element_type=f32).reshape(
        row_count * lax.axis_size("shard"), k_width
    )
    d_value = jnp.einsum(
        "grtk,tgrd->kgd", probs_again, d_heads, preferred_element_type=f32
    ).reshape(row_count * lax.axis_size("shard"), k_width)
    d_key_value = lax.psum_scatter(
        jnp.concatenate([d_key, d_value], axis=1), "shard", scatter_dimension=0, tiled=True
    )
    d_projected = jnp.concatenate(
        [
            rotate(d_queries, position, HEADS, -1.0) * query_scale,
            rotate(d_key_value[:, :k_width], position, KV_HEADS, -1.0),
            d_key_value[:, k_width:],
        ],
        axis=1,
    ).astype(bf16)
    d_normed_in = back_dot(d_projected, w_in)
    _, first_back = jax.vjp(rms_norm, residual, gains_used[:, 0])
    d_input_part, d_gain0 = first_back(d_normed_in)
    input_grad = d_middle + d_input_part
    gain_grad = jnp.stack([d_gain0, d_gain1, d_gain2, d_gain3], axis=1)
    attended_all, d_attn_all, normed_all, d_proj_all = (
        lax.all_gather(attended, "rep", axis=0, tiled=True),
        lax.all_gather(d_attn_low, "rep", axis=0, tiled=True),
        lax.all_gather(normed_in, "rep", axis=0, tiled=True),
        lax.all_gather(d_projected, "rep", axis=0, tiled=True),
    )
    part_out = owned_rows(attended_all, d_attn_all, rep_index, attended.shape[1] // rep_count)
    part_in = owned_rows(normed_all, d_proj_all, rep_index, normed_in.shape[1] // rep_count)
    part_gain = lax.psum_scatter(gain_grad, "rep", scatter_dimension=0, tiled=True)
    owned = (
        lax.psum_scatter(part_in, "shard", scatter_dimension=0, tiled=True),
        lax.psum_scatter(part_gain, "shard", scatter_dimension=0, tiled=True),
        lax.psum_scatter(part_out, "shard", scatter_dimension=0, tiled=True),
        lax.psum_scatter(part_gate_up, "shard", scatter_dimension=0, tiled=True),
        lax.psum_scatter(part_down, "shard", scatter_dimension=0, tiled=True),
    )
    grad_inproj, grad_gains, grad_outproj, grad_gate_up, grad_down = owned
    split_at = grad_gate_up.shape[1] // 2
    grad_gate = grad_gate_up[:, :split_at]
    grad_up = grad_gate_up[:, split_at:]
    masters = (inproj, outproj, ffn_gate, ffn_up, ffn_down, norm_gains)
    gradients = (grad_inproj, grad_outproj, grad_gate, grad_up, grad_down, grad_gains)
    firsts = (mean_inproj, mean_outproj, mean_gate, mean_up, mean_down, mean_gains)
    seconds = (square_inproj, square_outproj, square_gate, square_up, square_down, square_gains)
    results = [
        lamb_local(masters[index], gradients[index], firsts[index], seconds[index])
        for index in range(6)
    ]
    weight_sums = jnp.stack([jnp.sum(master * master) for master in masters])
    step_sums = jnp.stack([jnp.sum(item[2] * item[2]) for item in results])
    totals = lax.psum(jnp.stack([weight_sums, step_sums]), ("rep", "shard"))
    counts = jnp.array([float(master.size * rep_count * shard_count) for master in masters], f32)
    norm_table = jnp.sqrt(totals / counts[None, :] + 1e-06)
    fresh = [
        masters[index] - 0.3 * norm_table[0, index] / norm_table[1, index] * results[index][2]
        for index in range(6)
    ]
    return (
        layer_out,
        input_grad,
        grad_inproj,
        grad_outproj,
        grad_gate,
        grad_up,
        grad_down,
        grad_gains,
        results[0][0],
        results[1][0],
        results[2][0],
        results[3][0],
        results[4][0],
        results[5][0],
        results[0][1],
        results[1][1],
        results[2][1],
        results[3][1],
        results[4][1],
        results[5][1],
        fresh[0],
        fresh[1],
        fresh[2],
        fresh[3],
        fresh[4],
        fresh[5],
        norm_table,
    )


MESH = pl.DeviceIdType.MESH
VM = pltpu.VMEM
HB = pl.ANY
UNITS = 4
VMEM_LIMIT = 60 << 20


def ring_places(count):
    inner = 2 if count == 8 else 4
    outer = count // inner

    def place(shard):
        major = shard // inner
        minor = shard % inner
        return minor * outer + major + (minor % 2) * (outer - 1 - 2 * major)

    def shard_at(spot):
        minor = spot // outer
        major = spot % outer
        return (major + (minor % 2) * (outer - 1 - 2 * major)) * inner + minor

    return place, shard_at


def meet(devices):
    barrier = pltpu.get_barrier_semaphore()
    for device in devices:
        pl.semaphore_signal(barrier, inc=1, device_id=device, device_id_type=MESH)
    pl.semaphore_wait(barrier, len(devices))


def remote(src, dst, send_sem, recv_sem, device):
    return pltpu.make_async_remote_copy(
        src_ref=src,
        dst_ref=dst,
        send_sem=send_sem,
        recv_sem=recv_sem,
        device_id=device,
        device_id_type=MESH,
    )


class Ring:
    def __init__(self, count):
        place, shard_at = ring_places(count)
        self.count = count
        self.half = count // 2
        self.rep = lax.axis_index("rep")
        self.me = lax.axis_index("shard")
        self.spot = place(self.me)
        self.shard_at = shard_at
        self.next = [(self.rep, self.at(1)), (self.rep, self.at(count - 1))]

    def at(self, ahead):
        return self.shard_at((self.spot + ahead) % self.count)

    def away(self, way, hops):
        return self.at(hops if way == 0 else self.count - hops)

    def units(self, way, hop):
        order = list(range(UNITS)) if way == 0 else list(range(UNITS))[::-1]
        return order if hop < self.half else order[: UNITS // 2]


def reduce_on_ring(ring, rows, take, first, landed, send, recv, finish, pause):
    f32 = jnp.float32
    hops = ring.half
    started = []

    def part(unit):
        return pl.ds(unit * (rows // UNITS), rows // UNITS)

    def step_copy(way, step, unit):
        return remote(
            landed.at[way, step - 1, part(unit)] if step else first.at[part(unit)],
            landed.at[way, step, part(unit)],
            send.at[way, step, unit],
            recv.at[way, step, unit],
            ring.next[way],
        )

    for step in range(hops):
        order = ring.units(0, hops - step), ring.units(1, hops - step)
        before = [ring.units(way, hops - step + 1) if step else [] for way in (0, 1)]
        for index in range(len(order[0])):
            for way in (0, 1):
                unit = order[way][index]
                block = take(ring.away(way, hops - step), part(unit)).astype(f32)
                if unit in before[way]:
                    step_copy(way, step - 1, unit).wait_recv()
                    block += landed[way, step - 1, part(unit), :].astype(f32)
                if step:
                    landed[way, step - 1, part(unit), :] = block.astype(landed.dtype)
                else:
                    first[part(unit), :] = block.astype(first.dtype)
                copy = step_copy(way, step, unit)
                copy.start()
                started.append(copy)
            if step or index == len(order[0]) - 1:
                pause()
    for unit in range(UNITS):
        total = take(ring.me, part(unit)).astype(f32)
        for way in (0, 1):
            step_copy(way, hops - 1, unit).wait_recv()
            total += landed[way, hops - 1, part(unit), :].astype(f32)
        finish(part(unit), total)
    return started


class Flow:
    def __init__(self, ring, rows, send, recv):
        self.ring, self.rows, self.send, self.recv = ring, rows, send, recv
        self.unit_rows = rows // UNITS
        self.started = []

    def span(self, slot, unit):
        return pl.ds(slot * self.rows + unit * self.unit_rows, self.unit_rows)

    def slot(self, way, hops):
        if hops == 0:
            return 0
        return self.ring.count - 1 if hops == self.ring.half else 2 * hops - 1 + way

    def go(self, copy):
        copy.start()
        self.started.append(copy)

    def finish(self):
        for copy in self.started:
            copy.wait_send()

    def gather_copy(self, buffer, way, hop, unit):
        return remote(
            buffer.at[self.span(self.slot(way, hop - 1), unit)],
            buffer.at[self.span(self.slot(way, hop), unit)],
            self.send.at[way, hop - 1, unit],
            self.recv.at[way, hop - 1, unit],
            self.ring.next[way],
        )

    def gather(self, buffer, group_work):
        ring = self.ring
        for index in range(UNITS):
            for way in (0, 1):
                self.go(self.gather_copy(buffer, way, 1, ring.units(way, 1)[index]))
        queue = list(group_work(0, 1))
        for hop in range(1, ring.half + 1):
            length = len(ring.units(0, hop))
            for index in range(length):
                for way in (0, 1):
                    unit = ring.units(way, hop)[index]
                    self.gather_copy(buffer, way, hop, unit).wait_recv()
                    if hop < ring.half and unit in ring.units(way, hop + 1):
                        self.go(self.gather_copy(buffer, way, hop + 1, unit))
                if queue:
                    queue.pop(0)()
            for piece in queue:
                piece()
            queue = list(group_work(2 * hop - 1, 2) if hop < ring.half else group_work(ring.count - 1, 1))
        for piece in queue:
            piece()
        self.finish()

    def reduce_copy(self, first, landed, way, step, unit):
        span = pl.ds(unit * self.unit_rows, self.unit_rows)
        src = first.at[span] if step == 0 else landed.at[way, step - 1, span]
        return remote(
            src,
            landed.at[way, step, span],
            self.send.at[way, step, unit],
            self.recv.at[way, step, unit],
            self.ring.next[way],
        )

    def reduce(self, first, landed, partial, group_work, finish, extra=()):
        extra = list(extra)
        ring = self.ring
        hops = ring.half
        f32 = jnp.float32
        for piece in group_work(ring.count - 1, 1, 0):
            piece()
        queue = list(group_work(2 * (hops - 1) - 1, 2, 1))
        for step in range(hops):
            order = ring.units(0, hops - step), ring.units(1, hops - step)
            before = [ring.units(way, hops - step + 1) if step else [] for way in (0, 1)]
            for index in range(len(order[0])):
                for way in (0, 1):
                    unit = order[way][index]
                    span = pl.ds(unit * self.unit_rows, self.unit_rows)
                    if step == 0:
                        first[span, :] = partial[0, pl.ds(unit * self.unit_rows, self.unit_rows), :].astype(first.dtype)
                    else:
                        side = 1 - way
                        block = partial[
                            step % 2, pl.ds(side * self.rows + unit * self.unit_rows, self.unit_rows), :
                        ]
                        if unit in before[way]:
                            self.reduce_copy(first, landed, way, step - 1, unit).wait_recv()
                            block = block + landed[way, step - 1, span, :].astype(f32)
                        landed[way, step - 1, span, :] = block.astype(landed.dtype)
                    self.go(self.reduce_copy(first, landed, way, step, unit))
                if queue:
                    queue.pop(0)()
                elif extra:
                    extra.pop(0)()
            for piece in queue:
                piece()
            ahead = hops - step - 2
            queue = []
            if step < hops - 1:
                queue = list(group_work(2 * ahead - 1, 2, step % 2) if ahead > 0 else group_work(0, 1, step % 2))
        for piece in extra:
            piece()
        for unit in range(UNITS):
            span = pl.ds(unit * self.unit_rows, self.unit_rows)
            total = partial[hops % 2, span, :]
            for way in (0, 1):
                self.reduce_copy(first, landed, way, hops - 1, unit).wait_recv()
                total = total + landed[way, hops - 1, span, :].astype(f32)
            finish(unit, total)
        self.finish()


def looped(piece, count):
    def all_of_it():
        def body(j, carry):
            piece(j)
            return carry

        lax.fori_loop(0, count, body, 0)

    return [all_of_it]


def gelu_pair(gate):
    inner = 0.7978845608028654 * (gate + 0.044715 * gate * gate * gate)
    bend = jnp.tanh(inner)
    value = 0.5 * gate * (1.0 + bend)
    slope = 0.5 * (1.0 + bend) + 0.5 * gate * (1.0 - bend * bend) * 0.7978845608028654 * (
        1.0 + 0.134145 * gate * gate
    )
    return value, slope


def ffn_kernel(
    count, attn_ref, tokens_ref, cot_ref, gains_ref, gate_hbm, up_hbm, dn_hbm,
    layer_ref, dmid_ref, dattn_ref, gg_ref, h3_hbm, dgu_hbm, part_hbm,
    gate_ref, up_ref, dn_ref, h3_ref, hid_ref, dffn_ref, dgu_ref,
    lin, partial, first, landed, middle, total_ref, s1, r1, s2, r2, s3, r3, s4, r4, loads, stores,
):
    f32, bf16 = jnp.float32, jnp.bfloat16
    ring = Ring(count)
    rows, width = attn_ref.shape
    part = hid_ref.shape[1]
    tile = part // 3
    wide = width // 3
    fetched = [
        pltpu.make_async_copy(src, dst, loads.at[index])
        for index, (src, dst) in enumerate(((gate_hbm, gate_ref), (up_hbm, up_ref), (dn_hbm, dn_ref)))
    ]
    for copy in fetched:
        copy.start()
    kept = []

    def keep_out(src, dst):
        copy = pltpu.make_async_copy(src, dst, stores.at[len(kept)])
        copy.start()
        kept.append(copy)

    meet(ring.next)

    def gain(index):
        return 1.0 + gains_ref[index : index + 1, :]

    def scale_of(value):
        return lax.rsqrt(jnp.mean(value * value, axis=-1, keepdims=True) + 1e-06)

    half = rows // 2
    halves = [pl.ds(0, half), pl.ds(half, half)]
    for span in halves:
        proj = attn_ref[span, :]
        mid = tokens_ref[span, :].astype(f32) + proj * scale_of(proj) * gain(1)
        middle[span, :] = mid
        h3_ref[span, :] = (mid * scale_of(mid) * gain(2)).astype(bf16)

    def lin_work(slot, blocks):
        at = pl.ds(slot * rows, blocks * rows)

        def piece(j):
            lo = pl.ds(pl.multiple_of(j * tile, 128), tile)
            hi = pl.ds(pl.multiple_of(part + j * tile, 128), tile)
            gate = jnp.dot(h3_ref[at, :], gate_ref[:, lo], preferred_element_type=f32)
            up = jnp.dot(h3_ref[at, :], up_ref[:, lo], preferred_element_type=f32)
            value, slope = gelu_pair(gate)
            hid_ref[at, lo] = (value * up).astype(bf16)
            lin[at, lo] = (up * slope).astype(bf16)
            lin[at, hi] = value.astype(bf16)

        return looped(piece, 3)

    def down_work(slot, blocks, side):
        at = pl.ds(slot * rows, blocks * rows)

        def piece(j):
            cols = pl.ds(pl.multiple_of(j * wide, 128), wide)
            partial[side, pl.ds(0, blocks * rows), cols] = jnp.dot(
                hid_ref[at, :], dn_ref[:, cols], preferred_element_type=f32
            )

        return looped(piece, 3)

    def nt(left, right):
        return lax.dot_general(left, right, (((1,), (1,)), ((), ())), preferred_element_type=f32)

    def back_work(slot, blocks):
        at = pl.ds(slot * rows, blocks * rows)

        def piece(j):
            lo = pl.ds(pl.multiple_of(j * tile, 128), tile)
            hi = pl.ds(pl.multiple_of(part + j * tile, 128), tile)
            d_hidden = nt(dffn_ref[at, :], dn_ref[lo, :])
            dgu_ref[at, lo] = (d_hidden * lin[at, lo].astype(f32)).astype(bf16)
            dgu_ref[at, hi] = (d_hidden * lin[at, hi].astype(f32)).astype(bf16)

        return looped(piece, 3)

    def input_work(slot, blocks, side):
        at = pl.ds(slot * rows, blocks * rows)

        def piece(j):
            cols = pl.ds(pl.multiple_of(j * wide, 128), wide)
            partial[side, pl.ds(0, blocks * rows), cols] = nt(dgu_ref[at, :part], gate_ref[cols, :]) + nt(
                dgu_ref[at, part:], up_ref[cols, :]
            )

        return looped(piece, 3)

    def keep(unit, total):
        total_ref[pl.ds(unit * (rows // UNITS), rows // UNITS), :] = total

    def lin_first(slot, blocks):
        work = lin_work(slot, blocks)
        return [lambda: (fetched[0].wait(), fetched[1].wait())] + work if slot == 0 else work

    Flow(ring, rows, s1, r1).gather(h3_ref, lin_first)
    keep_out(h3_ref, h3_hbm)
    fetched[2].wait()
    Flow(ring, rows, s2, r2).reduce(first, landed, partial, down_work, keep)

    def back_norm(value, index, grad):
        scale = scale_of(value)
        normed = value * scale
        weighted = grad * gain(index)
        inner = jnp.mean(weighted * normed, axis=-1, keepdims=True)
        return scale * (weighted - normed * inner), jnp.sum(grad * normed, axis=0, keepdims=True)

    gg = jnp.zeros((1, width), f32)
    for span in halves:
        proj = total_ref[span, :]
        scale = scale_of(proj)
        layer_ref[span, :] = (middle[span, :] + proj * scale * gain(3)).astype(bf16)
        d_ffn, term = back_norm(proj, 3, cot_ref[span, :].astype(f32))
        gg += term
        dffn_ref[span, :] = d_ffn.astype(bf16)
    gg_ref[3:4, :] = gg

    Flow(ring, rows, s3, r3).gather(dffn_ref, back_work)
    keep_out(dgu_ref, dgu_hbm)

    def make_down(j):
        span = pl.ds(j * tile, tile)

        def body(n, carry):
            cols = pl.ds(pl.multiple_of(n * wide, 128), wide)
            lin[span, cols] = tn(hid_ref[:, span], dffn_ref[:, cols]).astype(bf16)
            return carry

        lax.fori_loop(0, 3, body, 0)
        keep_out(lin.at[span, pl.ds(0, width)], part_hbm.at[span])

    Flow(ring, rows, s4, r4).reduce(
        first, landed, partial, input_work, keep, [functools.partial(make_down, j) for j in range(3)]
    )

    gg1 = jnp.zeros((1, width), f32)
    gg2 = jnp.zeros((1, width), f32)
    for span in halves:
        d_mid, term = back_norm(middle[span, :], 2, total_ref[span, :])
        gg2 += term
        d_mid = d_mid + cot_ref[span, :].astype(f32)
        dmid_ref[span, :] = d_mid
        d_attn, term = back_norm(attn_ref[span, :], 1, d_mid)
        gg1 += term
        dattn_ref[span, :] = d_attn.astype(bf16)
    gg_ref[1:2, :] = gg1
    gg_ref[2:3, :] = gg2
    gg_ref[0:1, :] = jnp.zeros((1, width), f32)
    gg_ref[4:8, :] = jnp.zeros((4, width), f32)
    for copy in kept:
        copy.wait()


def feed_forward(attn_proj, tokens, cotangent, gain_rows, w_gate, w_up, w_down, count, collective_id):
    f32, bf16 = jnp.float32, jnp.bfloat16
    rows, width = attn_proj.shape
    part = w_down.shape[0]
    every = rows * count
    dma = pltpu.SemaphoreType.DMA
    shape = jax.ShapeDtypeStruct
    return pl.pallas_call(
        functools.partial(ffn_kernel, count),
        out_shape=[
            shape((rows, width), bf16),
            shape((rows, width), f32),
            shape((rows, width), bf16),
            shape((8, width), f32),
            shape((every, width), bf16),
            shape((every, 2 * part), bf16),
            shape((part, width), bf16),
        ],
        in_specs=[pl.BlockSpec(memory_space=VM)] * 4 + [pl.BlockSpec(memory_space=HB)] * 3,
        out_specs=[pl.BlockSpec(memory_space=VM)] * 4 + [pl.BlockSpec(memory_space=HB)] * 3,
        scratch_shapes=[
            pltpu.VMEM(w_gate.shape, bf16),
            pltpu.VMEM(w_up.shape, bf16),
            pltpu.VMEM(w_down.shape, bf16),
            pltpu.VMEM((every, width), bf16),
            pltpu.VMEM((every, part), bf16),
            pltpu.VMEM((every, width), bf16),
            pltpu.VMEM((every, 2 * part), bf16),
            pltpu.VMEM((max(every, part), max(2 * part, width)), bf16),
            pltpu.VMEM((2, 2 * rows, width), f32),
            pltpu.VMEM((rows, width), bf16),
            pltpu.VMEM((2, count // 2, rows, width), bf16),
            pltpu.VMEM((rows, width), f32),
            pltpu.VMEM((rows, width), f32),
        ]
        + [dma((2, count // 2, UNITS))] * 8
        + [dma((3,)), dma((5,))],
        compiler_params=pltpu.CompilerParams(
            collective_id=collective_id, has_side_effects=True, vmem_limit_bytes=VMEM_LIMIT
        ),
        name="feed_forward",
    )(attn_proj, tokens, cotangent, gain_rows, w_gate, w_up, w_down)


def attention_kernel(
    reps, count, h1_ref, in_ref, got_ref, cos_ref, sin_ref, tagq_ref, tagk_ref, cut_ref,
    proj_ref, q_ref, k_ref, v_ref, att_ref, probs_ref, damp_ref, wo_ref, up_ref,
    part, first, landed, r_send, r_recv, w_sems, loc
):
    f32, bf16 = jnp.float32, jnp.bfloat16
    ring = Ring(count)
    rows = proj_ref.shape[0]
    seq_len = h1_ref.shape[0]
    tall = seq_len // 4
    half = HEAD_DIM // 2
    meet(near_devices(ring))
    weights = Fetch(ring, cut_ref, up_ref, w_sems)
    weights.begin()
    own = pltpu.make_async_copy(cut_ref.at[ring.me], up_ref.at[ring.rep, ring.me], loc)
    own.start()
    piece = got_ref.shape[2]
    for block in range(got_ref.shape[1]):
        for j in range(reps):
            start = (block * reps + j) * piece
            wo_ref[start : start + piece, :] = got_ref[j, block]

    def project(i, carry):
        at = pl.ds(pl.multiple_of(i * tall, 16), tall)
        flat = jnp.dot(h1_ref[at, :], in_ref[...], preferred_element_type=f32)
        cosine, sine = cos_ref[at, :], sin_ref[at, :]

        def turned(start):
            first, second = flat[:, start : start + half], flat[:, start + half : start + HEAD_DIM]
            return jnp.concatenate([first * cosine - second * sine, second * cosine + first * sine], axis=1)

        q_ref[at, :] = (turned(0) * HEAD_DIM ** (-0.5)).astype(bf16)
        k_ref[at, :] = turned(HEAD_DIM).astype(bf16)
        v_ref[at, :] = flat[:, 2 * HEAD_DIM :].astype(bf16)
        return carry

    lax.fori_loop(0, 4, project, 0)

    def attend(shard):
        at = pl.ds(pl.multiple_of(shard * rows, 16), rows)
        raw = lax.dot_general(q_ref[at, :], k_ref[...], (((1,), (1,)), ((), ())), preferred_element_type=f32)
        bent = jnp.tanh(raw * (1.0 / 50.0))
        query_at = shard * rows + lax.broadcasted_iota(jnp.int32, (rows, seq_len), 0)
        key_at = lax.broadcasted_iota(jnp.int32, (rows, seq_len), 1)
        tag = tagq_ref[at, :]
        visible = (key_at <= query_at) | ((tag == tagk_ref[...]) & (tag > 0))
        masked = jnp.where(visible, 50.0 * bent, -1e30)
        expo = jnp.exp(masked - jnp.max(masked, axis=-1, keepdims=True))
        probs = expo / jnp.sum(expo, axis=-1, keepdims=True)
        low = probs.astype(bf16)
        probs_ref[at, :] = low
        damp_ref[at, :] = (probs * (1.0 - bent * bent)).astype(bf16)
        attended = jnp.dot(low, v_ref[...], preferred_element_type=f32).astype(bf16)
        att_ref[at, :] = attended
        part[at, :] = jnp.dot(attended, wo_ref[...], preferred_element_type=f32)

    def attend_both(hop):
        def body(way, carry):
            attend(ring.at(hop + way * (count - 2 * hop)))
            return carry

        lax.fori_loop(0, 2 if hop else 1, body, 0)

    work = weights.steps()
    first_of_step = [0] + [1 + UNITS * step for step in range(ring.half - 1)]
    calls = []

    def pause():
        call = len(calls)
        calls.append(call)
        if call in first_of_step:
            attend_both(ring.half - 1 - first_of_step.index(call))
            return
        for _ in range(min(3, len(work))):
            work.pop(0)()

    def finish(span, total):
        proj_ref[span, :] = total

    def take(shard, span):
        return part[pl.ds(pl.multiple_of(shard * rows + span.start, 16), span.size), :]

    attend(ring.at(ring.half))
    started = reduce_on_ring(ring, rows, take, first, landed, r_send, r_recv, finish, pause)
    for piece in work:
        piece()
    weights.finish()
    own.wait()
    for copy in started:
        copy.wait_send()


def attention(reps, count, normed, w_in, w_out, cosine, sine, tag, cut_up, collective_id):
    dma = pltpu.SemaphoreType.DMA
    low, f32 = jnp.bfloat16, jnp.float32
    shape = jax.ShapeDtypeStruct
    seq_len, width = normed.shape
    rows = seq_len // count
    hops = count // 2
    head = shape((seq_len, HEAD_DIM), low)
    square = shape((seq_len, seq_len), low)
    return pl.pallas_call(
        functools.partial(attention_kernel, reps, count),
        out_shape=[
            shape((rows, width), f32), head, head, head, head, square, square, shape((HEAD_DIM, width), low),
            shape((reps,) + cut_up.shape, low),
        ],
        in_specs=[pl.BlockSpec(memory_space=VM)] * 7 + [pl.BlockSpec(memory_space=HB)],
        out_specs=[pl.BlockSpec(memory_space=VM)] * 8 + [pl.BlockSpec(memory_space=HB)],
        scratch_shapes=[
            pltpu.VMEM((seq_len, width), f32),
            pltpu.VMEM((rows, width), low),
            pltpu.VMEM((2, hops, rows, width), low),
            dma((2, hops, UNITS)),
            dma((2, hops, UNITS)),
            dma((8, count)),
            dma,
        ],
        compiler_params=pltpu.CompilerParams(
            collective_id=collective_id, has_side_effects=True, vmem_limit_bytes=VMEM_LIMIT
        ),
        name="attention",
    )(normed, w_in, w_out, cosine, sine, tag[:, None], tag[None, :], cut_up)


class Fetch:
    def __init__(self, ring, cut, out, sems):
        self.ring, self.cut, self.out = ring, cut, out
        self.rep, self.me, self.count = ring.rep, ring.me, ring.count
        self.across, self.beside = rep_partners(ring.rep)
        self.sems = sems
        self.started = []

    def go(self, copy):
        copy.start()
        self.started.append(copy)

    def spread(self, k):
        to = (self.me + k) % self.count
        return remote(
            self.cut.at[to], self.out.at[self.rep, self.me], self.sems.at[0, k], self.sems.at[1, k], (self.rep, to)
        )

    def arrived(self, k):
        frm = (self.me + self.count - k) % self.count
        return remote(
            self.cut.at[frm], self.out.at[self.rep, frm], self.sems.at[0, k], self.sems.at[1, k], (self.rep, frm)
        )

    def forward(self, k, hop):
        frm = (self.me + self.count - k) % self.count
        rep = self.across if hop == 2 else self.rep
        block = self.out.at[rep, frm] if k or hop == 2 else self.cut.at[self.me]
        to = self.across if hop == 0 else self.beside
        return remote(
            block,
            self.out.at[rep, frm],
            self.sems.at[2 + 2 * hop, k],
            self.sems.at[3 + 2 * hop, k],
            (to, self.me),
        )

    def pass_on(self, k):
        if k:
            self.arrived(k).wait_recv()
        self.go(self.forward(k, 0))
        self.go(self.forward(k, 1))

    def pass_beside(self, k):
        self.forward(k, 0).wait_recv()
        self.go(self.forward(k, 2))

    def begin(self):
        for k in range(1, self.count):
            self.go(self.spread(k))
        self.pass_on(0)

    def steps(self):
        work = [functools.partial(self.pass_on, k) for k in range(1, self.count)]
        return work + [functools.partial(self.pass_beside, k) for k in range(self.count)]

    def finish(self):
        for k in range(self.count):
            self.forward(k, 1).wait_recv()
            self.forward(k, 2).wait_recv()
        for copy in self.started:
            copy.wait_send()


def rep_partners(rep):
    return (rep + 2) % 4, rep + 1 - 2 * (rep % 2)


def everyone(rep, me, reps, count):
    here = rep * count + me
    total = reps * count
    return [
        (((here + k) % total) // count, ((here + k) % total) % count) for k in range(1, total)
    ]


def opening_kernel(
    reps, count, tok_ref, gain_ref, in_hbm, dn_hbm, ou_hbm, gate_hbm, up_hbm,
    h1_ref, gains_ref, w_in, w_gate, w_dn, w_ou, cut_up,
    in_f, dn_f, ou_f, gate_f, up_f, in_ref, dn_ref, ou_ref, gate_ref, tok_all, gain_all,
    t_send, t_recv, g_send, g_recv, i_sems, u_sems, o_send, o_recv, n_send, n_recv, loc, loads
):
    f32 = jnp.float32
    ring = Ring(count)
    rep, me = ring.rep, ring.me
    across, beside = rep_partners(rep)
    others = everyone(rep, me, reps, count)
    mine = rep * count + me
    d_rows = in_ref.shape[1]
    rows = tok_ref.shape[0]
    fetched = [
        pltpu.make_async_copy(src, dst, loads.at[index])
        for index, (src, dst) in enumerate(
            ((in_hbm, in_f), (dn_hbm, dn_f), (ou_hbm, ou_f), (gate_hbm, gate_f), (up_hbm, up_f))
        )
    ]
    for copy in fetched:
        copy.start()
    meet(others)
    started = []

    def go(copy):
        copy.start()
        started.append(copy)

    for k, device in enumerate(others):
        go(remote(gain_ref, gain_all.at[mine], g_send.at[k], g_recv.at[k], device))
    gain_all[mine] = gain_ref[...]
    ins = Fetch(ring, in_ref, w_in, i_sems)
    gates = Fetch(ring, gate_ref, w_gate, u_sems)
    gather = Gather(ring, tok_ref, tok_all, t_send, t_recv)
    fetched[0].wait()
    cut_heads(count, in_f, in_ref)
    ins.begin()
    fetched[1].wait()
    dn_ref[...] = dn_f[...].astype(dn_ref.dtype)
    dn_x = remote(dn_ref, w_dn.at[rep], n_send.at[0], n_recv.at[0], (across, me))
    dn_c = remote(dn_ref, w_dn.at[rep], n_send.at[1], n_recv.at[1], (beside, me))
    dn_d = remote(w_dn.at[across], w_dn.at[across], n_send.at[2], n_recv.at[2], (beside, me))
    go(dn_x)
    go(dn_c)
    fetched[2].wait()
    for j in range(reps):
        ou_ref[j] = ou_f[j * ou_ref.shape[1] : (j + 1) * ou_ref.shape[1], :].astype(ou_ref.dtype)

    per_head = count * reps // HEADS
    target = mine // per_head
    slot = mine % per_head

    def ou_copy(j):
        return remote(ou_ref.at[j], w_ou.at[j, slot], o_send.at[j], o_recv.at[slot], (j, target))

    def is_self(j):
        return (rep == j) & (me == target)

    for j in range(reps):
        @pl.when(jnp.logical_not(is_self(j)))
        def _():
            ou_copy(j).start()

        @pl.when(is_self(j))
        def _():
            pltpu.make_async_copy(ou_ref.at[j], w_ou.at[j, slot], o_recv.at[slot]).start()

    fetched[3].wait()
    cut_units(reps, count, gate_f, gate_ref)
    gates.begin()
    locals_ = []
    for index, (src, dst) in enumerate(
        ((in_ref.at[me], w_in.at[rep, me]), (gate_ref.at[me], w_gate.at[rep, me]), (dn_ref, w_dn.at[rep]))
    ):
        copy = pltpu.make_async_copy(src, dst, loc.at[index])
        copy.start()
        locals_.append(copy)

    for k in range(len(others)):
        frm = (mine + len(others) - k) % (reps * count)
        remote(gain_ref, gain_all.at[frm], g_send.at[k], g_recv.at[k], others[k]).wait_recv()
    gains_ref[...] = jnp.concatenate([gain_all[device, :, 0:d_rows] for device in range(reps * count)], axis=1)
    gain = 1.0 + gains_ref[0:1, :]

    def norm(value):
        value = value.astype(f32)
        return (value * lax.rsqrt(jnp.mean(value * value, axis=-1, keepdims=True) + 1e-06) * gain).astype(h1_ref.dtype)

    def norm_block(shard):
        for unit in range(UNITS):
            span = pl.ds(unit * (rows // UNITS), rows // UNITS)
            h1_ref[shard, span, :] = norm(tok_all[shard, span, :])

    for unit in range(UNITS):
        span = pl.ds(unit * (rows // UNITS), rows // UNITS)
        h1_ref[me, span, :] = norm(tok_ref[span, :])

    hops = gather.steps()

    def take_hop(hop):
        for _ in range(len(ring.units(0, hop))):
            hops.pop(0)()
        for way in (0, 1) if hop < ring.half else (0,):
            norm_block(ring.away(1 - way, hop))

    for k in range(1, count):
        ins.pass_on(k)
    fetched[4].wait()
    cut_units(reps, count, up_f, cut_up)
    gather.begin()
    for k in range(1, count):
        gates.pass_on(k)
    for i in range(per_head):
        remote(
            ou_ref.at[0], w_ou.at[rep, i], o_send.at[0], o_recv.at[i], (across, me)
        ).wait_recv()
    ou_x = remote(w_ou.at[rep], w_ou.at[rep], n_send.at[3], n_recv.at[3], (across, me))
    ou_c = remote(w_ou.at[rep], w_ou.at[rep], n_send.at[4], n_recv.at[4], (beside, me))
    ou_d = remote(w_ou.at[across], w_ou.at[across], n_send.at[5], n_recv.at[5], (beside, me))
    go(ou_x)
    go(ou_c)
    take_hop(1)
    dn_x.wait_recv()
    go(dn_d)
    take_hop(2)
    for k in range(count):
        ins.pass_beside(k)
    for hop in range(3, ring.half + 1):
        take_hop(hop)
    ou_x.wait_recv()
    go(ou_d)
    for k in range(count):
        gates.pass_beside(k)
    ins.finish()
    gates.finish()
    for copy in (dn_c, dn_d, ou_c, ou_d):
        copy.wait_recv()
    for copy in started:
        copy.wait_send()
    gather.finish()
    for j in range(reps):
        @pl.when(jnp.logical_not(is_self(j)))
        def _():
            ou_copy(j).wait_send()
    for copy in locals_:
        copy.wait()


def opening(reps, count, tokens, gain_tile, inproj, outproj, ffn_gate, ffn_up, ffn_down, collective_id):
    dma = pltpu.SemaphoreType.DMA
    per_head = count * reps // HEADS
    total = reps * count
    low, f32 = jnp.bfloat16, jnp.float32
    shape = jax.ShapeDtypeStruct
    hops = dma((2, count // 2, UNITS))
    width = tokens.shape[1]
    gathered = (count,) + tokens.shape
    d_rows = inproj.shape[0]
    heads = (count, d_rows, 3 * HEAD_DIM)
    units = (count, d_rows, ffn_gate.shape[1] // count)
    outs = (reps, outproj.shape[0] // reps, width)
    vm, hb = pl.BlockSpec(memory_space=VM), pl.BlockSpec(memory_space=HB)
    return pl.pallas_call(
        functools.partial(opening_kernel, reps, count),
        out_shape=[
            shape(gathered, low),
            shape((8, width), f32),
            shape((reps,) + heads, low),
            shape((reps,) + units, low),
            shape((reps,) + ffn_down.shape, low),
            shape((reps, per_head) + outs[1:], low),
            shape(units, low),
        ],
        in_specs=[vm] * 2 + [hb] * 5,
        out_specs=[vm] * 2 + [hb] * 4 + [vm],
        scratch_shapes=[
            pltpu.VMEM(inproj.shape, f32),
            pltpu.VMEM(ffn_down.shape, f32),
            pltpu.VMEM(outproj.shape, f32),
            pltpu.VMEM(ffn_gate.shape, f32),
            pltpu.VMEM(ffn_up.shape, f32),
            pltpu.VMEM(heads, low),
            pltpu.VMEM(ffn_down.shape, low),
            pltpu.VMEM(outs, low),
            pltpu.VMEM(units, low),
            pltpu.VMEM(gathered, low),
            pltpu.VMEM((total,) + gain_tile.shape, f32),
            hops,
            hops,
            dma((total - 1,)),
            dma((total - 1,)),
            dma((8, count)),
            dma((8, count)),
            dma((reps,)),
            dma((per_head,)),
            dma((6,)),
            dma((6,)),
            dma((3,)),
            dma((5,)),
        ],
        compiler_params=pltpu.CompilerParams(
            collective_id=collective_id, has_side_effects=True, vmem_limit_bytes=VMEM_LIMIT
        ),
        name="opening",
    )(tokens, gain_tile, inproj, ffn_down, outproj, ffn_gate, ffn_up)


def cut_units(reps, count, ref, cut):
    block = ref.shape[1] // (reps * count)
    for shard in range(count):
        pieces = [ref[:, (r * count + shard) * block : (r * count + shard + 1) * block] for r in range(reps)]
        cut[shard] = jnp.concatenate(pieces, axis=1).astype(cut.dtype)


def cut_heads(count, ref, cut):
    group = HEADS // KV_HEADS
    for shard in range(count):
        heads = shard, HEADS + shard // group, HEADS + KV_HEADS + shard // group
        for index, head in enumerate(heads):
            cut[shard, :, index * HEAD_DIM : (index + 1) * HEAD_DIM] = ref[
                :, head * HEAD_DIM : (head + 1) * HEAD_DIM
            ].astype(cut.dtype)


class RepSum:
    def __init__(self, part, from_core, from_across, sems, rep, me):
        self.part, self.from_core, self.from_across = part, from_core, from_across
        self.c_send, self.c_recv, self.x_send, self.x_recv = sems
        self.across, self.beside = rep_partners(rep)
        self.rep, self.me = rep, me
        self.core = rep % 2
        self.chip = rep // 2

    def core_copy(self, side, piece):
        chip = 1 - self.chip if side == 0 else self.chip
        return remote(
            self.part(chip * 2 + 1 - self.core, piece),
            self.from_core.at[side, piece],
            self.c_send.at[side, piece],
            self.c_recv.at[side, piece],
            (self.beside, self.me),
        )

    def cross_copy(self, piece):
        return remote(
            self.from_core.at[0, piece],
            self.from_across.at[piece],
            self.x_send.at[piece],
            self.x_recv.at[piece],
            (self.across, self.me),
        )

    def begin(self, pieces):
        for side in (0, 1):
            for piece in pieces:
                self.core_copy(side, piece).start()

    def cross(self, piece):
        f32 = jnp.float32
        self.core_copy(0, piece).wait_recv()
        mine = self.part((1 - self.chip) * 2 + self.core, piece)[...].astype(f32)
        self.from_core[0, piece] = (mine + self.from_core[0, piece].astype(f32)).astype(jnp.bfloat16)
        self.cross_copy(piece).start()

    def total(self, piece):
        f32 = jnp.float32
        self.core_copy(1, piece).wait_recv()
        mine = self.part(self.rep, piece)[...].astype(f32) + self.from_core[1, piece].astype(f32)
        self.cross_copy(piece).wait_recv()
        return mine + self.from_across[piece].astype(f32)

    def finish(self, pieces):
        for piece in pieces:
            self.core_copy(0, piece).wait_send()
            self.core_copy(1, piece).wait_send()
            self.cross_copy(piece).wait_send()


class Spread:
    def __init__(self, blocks, out, send, recv, rep, me, count):
        self.blocks, self.out, self.send, self.recv = blocks, out, send, recv
        self.rep, self.me, self.count = rep, me, count

    def copy(self, k):
        to = (self.me + k) % self.count
        return remote(
            self.blocks.at[to], self.out.at[self.me], self.send.at[k], self.recv.at[k], (self.rep, to)
        )

    def arrived(self, k):
        frm = (self.me + self.count - k) % self.count
        return remote(
            self.blocks.at[frm], self.out.at[frm], self.send.at[k], self.recv.at[k], (self.rep, frm)
        )

    def finish(self):
        for k in range(1, self.count):
            self.arrived(k).wait_recv()
        for k in range(1, self.count):
            self.copy(k).wait_send()


def near_devices(ring):
    across, beside = rep_partners(ring.rep)
    return [(ring.rep, (ring.me + k) % ring.count) for k in range(1, ring.count)] + [
        (across, ring.me),
        (beside, ring.me),
    ]


class Gather:
    def __init__(self, ring, block, out, send, recv):
        self.ring, self.block, self.out, self.send, self.recv = ring, block, out, send, recv
        self.rows = block.shape[0] // UNITS
        self.started = []

    def copy(self, way, hop, unit):
        ring = self.ring
        origin = ring.away(1 - way, hop - 1) if hop > 1 else ring.me
        span = pl.ds(unit * self.rows, self.rows)
        return remote(
            self.block.at[span] if hop == 1 else self.out.at[origin, span],
            self.out.at[origin, span],
            self.send.at[way, hop - 1, unit],
            self.recv.at[way, hop - 1, unit],
            ring.next[way],
        )

    def go(self, copy):
        copy.start()
        self.started.append(copy)

    def begin(self):
        for index in range(UNITS):
            for way in (0, 1):
                self.go(self.copy(way, 1, self.ring.units(way, 1)[index]))

    def steps(self):
        ring = self.ring

        def step(hop, index):
            for way in (0, 1):
                unit = ring.units(way, hop)[index]
                self.copy(way, hop, unit).wait_recv()
                if hop < ring.half and unit in ring.units(way, hop + 1):
                    self.go(self.copy(way, hop + 1, unit))

        return [
            functools.partial(step, hop, index)
            for hop in range(1, ring.half + 1)
            for index in range(len(ring.units(0, hop)))
        ]

    def finish(self):
        for copy in self.started:
            copy.wait_send()


def tn(left, right):
    return lax.dot_general(left, right, (((0,), (0,)), ((), ())), preferred_element_type=jnp.float32)


DN_PIECES = 3


def ffn_grads_kernel(
    reps, count, dattn_ref, wo_ref, q_ref, k_ref, v_ref, cos_ref, sin_ref, h3_hbm, dgu_hbm, part_hbm, probs_hbm, damp_hbm,
    all_ref, sum_ref, down_ref, dproj,
    h3_ref, dgu_ref, g_part, g_core, g_from, d_part, d_core, d_from, probs_ref, damp_ref, d_key, d_value,
    t_send, t_recv, gc_s, gc_r, gx_s, gx_r, dc_s, dc_r, dx_s, dx_r, s_send, s_recv, loc, loads, square
):
    f32, bf16 = jnp.float32, jnp.bfloat16
    ring = Ring(count)
    rep, me = ring.rep, ring.me
    d_rows, columns = sum_ref.shape[1:]
    part, width = d_part.shape
    block = part // reps
    seq_len = q_ref.shape[0]
    blocks = 4
    tall = seq_len // blocks
    half = HEAD_DIM // 2
    fetched = [
        pltpu.make_async_copy(src, dst, loads.at[index])
        for index, (src, dst) in enumerate(((part_hbm, d_part), (h3_hbm, h3_ref), (dgu_hbm, dgu_ref)))
    ]
    for copy in fetched:
        copy.start()

    def squares(i):
        span = pl.ds(i * tall, tall)
        return [
            pltpu.make_async_copy(probs_hbm.at[span], probs_ref, square.at[0]),
            pltpu.make_async_copy(damp_hbm.at[span], damp_ref, square.at[1]),
        ]

    for copy in squares(0):
        copy.start()
    meet(near_devices(ring))
    gather = Gather(ring, dattn_ref, all_ref, t_send, t_recv)
    gather.begin()
    own = pltpu.make_async_copy(dattn_ref, all_ref.at[me], loc)
    own.start()

    def d_at(owner, piece):
        rows = block // DN_PIECES
        return d_part.at[pl.ds(owner * block + piece * rows, rows)]

    down = RepSum(d_at, d_core, d_from, (dc_s, dc_r, dx_s, dx_r), rep, me)
    gate_up = RepSum(
        lambda owner, piece: g_part.at[owner, piece], g_core, g_from, (gc_s, gc_r, gx_s, gx_r), rep, me
    )
    spread = Spread(g_from, sum_ref, s_send, s_recv, rep, me, count)
    d_pieces = list(range(DN_PIECES))
    g_pieces = [(me + k) % count for k in range(1, count)] + [me]

    def make_gate_up(owner):
        rows = count * d_rows
        step = columns // 3

        def body(n, carry):
            cols = pl.ds(pl.multiple_of(n * step, 128), step)
            made = tn(h3_ref[:, owner * rows : (owner + 1) * rows], dgu_ref[:, cols])
            g_part[owner, :, :, cols] = made.reshape(count, d_rows, step).astype(bf16)
            return carry

        lax.fori_loop(0, 3, body, 0)

    def nt(left, right):
        return lax.dot_general(left, right, (((1,), (1,)), ((), ())), preferred_element_type=f32)

    def unturned(flat, at):
        cosine, sine = cos_ref[at, :], sin_ref[at, :]
        low, high = flat[:, :half], flat[:, half:]
        return jnp.concatenate([low * cosine + high * sine, high * cosine - low * sine], axis=1)

    d_key[...] = jnp.zeros_like(d_key)
    d_value[...] = jnp.zeros_like(d_value)

    def attend(i):
        at = pl.ds(i * tall, tall)
        per = count // blocks
        d_out = all_ref[i * per : (i + 1) * per].reshape(tall, width)
        d_att = nt(d_out, wo_ref[...]).astype(bf16)
        d_probs = nt(d_att, v_ref[...])
        for copy in squares(i):
            copy.wait()
        probs = probs_ref[...]
        inner = jnp.sum(probs.astype(f32) * d_probs, axis=-1, keepdims=True)
        d_scores = (damp_ref[...].astype(f32) * (d_probs - inner)).astype(bf16)
        d_query = jnp.dot(d_scores, k_ref[...], preferred_element_type=f32)
        dproj[at, :HEAD_DIM] = (unturned(d_query, at) * HEAD_DIM ** (-0.5)).astype(bf16)
        d_key[...] += tn(d_scores, q_ref[at, :])
        d_value[...] += tn(probs, d_att)
        if i < blocks - 1:
            for copy in squares(i + 1):
                copy.start()

    def project():
        for i in range(blocks):
            at = pl.ds(i * tall, tall)
            dproj[at, HEAD_DIM : 2 * HEAD_DIM] = unturned(d_key[at, :], at).astype(bf16)
            dproj[at, 2 * HEAD_DIM :] = d_value[at, :].astype(bf16)

    def finish_gate_up(k):
        piece = g_pieces[k]
        total = gate_up.total(piece).astype(bf16)
        if k < count - 1:
            g_from[piece] = total
            spread.copy(k + 1).start()
        else:
            sum_ref[me] = total

    def finish_down(piece):
        rows = block // DN_PIECES
        down_ref[pl.ds(piece * rows, rows), :] = down.total(piece)

    fetched[0].wait()
    down.begin(d_pieces)
    for copy in fetched[1:]:
        copy.wait()
    work = [functools.partial(make_gate_up, 0)]
    work += [functools.partial(down.cross, piece) for piece in d_pieces]
    work += [functools.partial(make_gate_up, owner) for owner in range(1, reps)]
    work += [lambda: gate_up.begin(g_pieces)]
    work += [functools.partial(gate_up.cross, piece) for piece in g_pieces]
    for step in gather.steps():
        step()
        if work:
            work.pop(0)()
    for piece in work:
        piece()
    own.wait()
    after = [functools.partial(finish_gate_up, k) for k in range(count)]
    per = max(1, count // blocks)
    for i in range(blocks):
        attend(i)
        for _ in range(min(per, len(after) - 2)):
            after.pop(0)()
    project()
    for piece in d_pieces:
        finish_down(piece)
    for piece in after:
        piece()
    spread.finish()
    down.finish(d_pieces)
    gate_up.finish(g_pieces)
    gather.finish()


def ffn_grads(
    reps, count, d_attn, w_out, queries, keys, values, cosine, sine, h3, d_gu, part_down, probs, damp, d_rows, collective_id
):
    dma = pltpu.SemaphoreType.DMA
    low, f32 = jnp.bfloat16, jnp.float32
    shape = jax.ShapeDtypeStruct
    width = d_attn.shape[1]
    columns = d_gu.shape[1]
    part = part_down.shape[0]
    seq_len = h3.shape[0]
    block = part // reps
    blocks = (count, d_rows, columns)
    lots = (DN_PIECES, block // DN_PIECES, width)
    hops = dma((2, count // 2, UNITS))
    vm, hb = pl.BlockSpec(memory_space=VM), pl.BlockSpec(memory_space=HB)
    return pl.pallas_call(
        functools.partial(ffn_grads_kernel, reps, count),
        out_shape=[
            shape((count,) + d_attn.shape, low),
            shape(blocks, low),
            shape((block, width), f32),
            shape((seq_len, 3 * HEAD_DIM), low),
        ],
        in_specs=[vm] * 7 + [hb] * 5,
        out_specs=[vm] * 4,
        scratch_shapes=[
            pltpu.VMEM(h3.shape, low),
            pltpu.VMEM(d_gu.shape, low),
            pltpu.VMEM((reps,) + blocks, low),
            pltpu.VMEM((2,) + blocks, low),
            pltpu.VMEM(blocks, low),
            pltpu.VMEM((part, width), low),
            pltpu.VMEM((2,) + lots, low),
            pltpu.VMEM(lots, low),
            pltpu.VMEM((seq_len // 4, seq_len), low),
            pltpu.VMEM((seq_len // 4, seq_len), low),
            pltpu.VMEM((seq_len, HEAD_DIM), f32),
            pltpu.VMEM((seq_len, HEAD_DIM), f32),
            hops,
            hops,
            dma((2, count)),
            dma((2, count)),
            dma((count,)),
            dma((count,)),
            dma((2, DN_PIECES)),
            dma((2, DN_PIECES)),
            dma((DN_PIECES,)),
            dma((DN_PIECES,)),
            dma((count,)),
            dma((count,)),
            dma,
            dma((3,)),
            dma((2,)),
        ],
        compiler_params=pltpu.CompilerParams(
            collective_id=collective_id, has_side_effects=True, vmem_limit_bytes=VMEM_LIMIT
        ),
        name="ffn_grads",
    )(d_attn, w_out, queries, keys, values, cosine, sine, h3, d_gu, part_down, probs, damp)


def closing_kernel(
    reps, count, dproj, in_ref, att_ref, h1_hbm, dattn_hbm, tokens_ref, dmid_ref, gains_ref, gg_ref,
    grad_ref, sum_ref, out_ref, gain_ref,
    h1_ref, dattn_ref, x_part, i_part, o_part, first, landed, total_ref, tiles, i_core, i_from, o_core, o_from,
    r_send, r_recv, ic_s, ic_r, ix_s, ix_r, oc_s, oc_r, ox_s, ox_r, s_send, s_recv, p_send, p_recv,
    g_send, g_recv, loads
):
    f32, bf16 = jnp.float32, jnp.bfloat16
    ring = Ring(count)
    rep, me = ring.rep, ring.me
    here = rep * count + me
    others = everyone(rep, me, reps, count)
    full = o_part.shape[1]
    d_rows = sum_ref.shape[1]
    seq_len, width = dattn_ref.shape
    rows = grad_ref.shape[0]
    fetched = [
        pltpu.make_async_copy(h1_hbm, h1_ref, loads.at[0]),
        pltpu.make_async_copy(dattn_hbm, dattn_ref, loads.at[1]),
    ]
    for copy in fetched:
        copy.start()
    meet(others)
    tall = seq_len // 4

    def project(i, carry):
        at = pl.ds(pl.multiple_of(i * tall, 16), tall)
        x_part[at, :] = lax.dot_general(
            dproj[at, :], in_ref[...], (((1,), (1,)), ((), ())), preferred_element_type=f32
        ).astype(bf16)
        return carry

    lax.fori_loop(0, 4, project, 0)

    def make_out():
        fetched[1].wait()
        per = width // 3

        def body(n, carry):
            cols = pl.ds(pl.multiple_of(n * per, 128), per)
            made = tn(att_ref[...], dattn_ref[:, cols]).reshape(full, reps, HEAD_DIM // full // reps, per)
            for owner in range(reps):
                o_part[owner, :, :, cols] = made[:, owner].astype(bf16)
            return carry

        lax.fori_loop(0, 3, body, 0)

    def make_in(owner):
        if owner == 0:
            fetched[0].wait()
        deep = count * d_rows
        made = tn(h1_ref[:, owner * deep : (owner + 1) * deep], dproj[...])
        i_part[owner] = made.reshape(count, d_rows, 3 * HEAD_DIM).astype(bf16)

    o_pieces = list(range(full))
    i_pieces = [(me + k) % count for k in range(1, count)] + [me]
    ins = RepSum(lambda owner, piece: i_part.at[owner, piece], i_core, i_from, (ic_s, ic_r, ix_s, ix_r), rep, me)
    outs = RepSum(lambda owner, piece: o_part.at[owner, piece], o_core, o_from, (oc_s, oc_r, ox_s, ox_r), rep, me)
    spread = Spread(i_from, sum_ref, s_send, s_recv, rep, me, count)

    def o_owner(piece):
        where = me * full + piece
        return where // count, where % count

    def o_copy(piece):
        return remote(o_from.at[piece], out_ref.at[rep], p_send.at[piece], p_recv.at[rep], o_owner(piece))

    def o_self(piece):
        return me * full + piece == here

    def o_finish(piece):
        total = outs.total(piece).astype(bf16)
        o_from[piece] = total

        @pl.when(jnp.logical_not(o_self(piece)))
        def _():
            o_copy(piece).start()

        @pl.when(o_self(piece))
        def _():
            pltpu.make_async_copy(o_from.at[piece], out_ref.at[rep], p_recv.at[rep]).start()

    def i_finish(k):
        piece = i_pieces[k]
        total = ins.total(piece).astype(bf16)
        if k < count - 1:
            i_from[piece] = total
            spread.copy(k + 1).start()
        else:
            sum_ref[me] = total

    work = [functools.partial(make_in, owner) for owner in range(reps)]
    work += [lambda: ins.begin(i_pieces), make_out, lambda: outs.begin(o_pieces)]
    work += [functools.partial(ins.cross, piece) for piece in i_pieces]
    work += [functools.partial(outs.cross, piece) for piece in o_pieces]
    work += [functools.partial(i_finish, k) for k in range(count)]
    work += [functools.partial(o_finish, piece) for piece in o_pieces]

    terms = []
    gain = 1.0 + gains_ref[0:1, :]

    def pause():
        for _ in range(min(2, len(work))):
            work.pop(0)()

    def take(shard, span):
        return x_part[pl.ds(pl.multiple_of(shard * rows + span.start, 16), span.size), :]

    def finish(span, total):
        value = tokens_ref[span, :].astype(f32)
        scale = lax.rsqrt(jnp.mean(value * value, axis=-1, keepdims=True) + 1e-06)
        normed = value * scale
        weighted = total * gain
        inner = jnp.mean(weighted * normed, axis=-1, keepdims=True)
        grad_ref[span, :] = dmid_ref[span, :] + scale * (weighted - normed * inner)
        terms.append(jnp.sum(total * normed, axis=0, keepdims=True))

    started = reduce_on_ring(ring, rows, take, first, landed, r_send, r_recv, finish, pause)
    total_ref[...] = gg_ref[...]
    total_ref[0:1, :] = functools.reduce(jnp.add, terms)
    every = total_ref[...]
    for owner in range(reps * count):
        tiles[owner, :, 0:d_rows] = every[:, owner * d_rows : (owner + 1) * d_rows]
        tiles[owner, :, d_rows:] = jnp.zeros((8, 128 - d_rows), f32)
    for k, device in enumerate(others):
        to = (here + k + 1) % (reps * count)
        remote(tiles.at[to], gain_ref.at[here], g_send.at[k], g_recv.at[k], device).start()
    gain_ref[here] = tiles[here]
    for piece in work:
        piece()
    for k in range(len(others)):
        frm = (here + len(others) - k) % (reps * count)
        remote(tiles.at[frm], gain_ref.at[frm], g_send.at[k], g_recv.at[k], others[k]).wait_recv()
    for j in range(reps):
        remote(
            o_from.at[0], out_ref.at[j], p_send.at[0], p_recv.at[j], (rep, (me + 1) % count)
        ).wait_recv()
    for piece in o_pieces:
        @pl.when(jnp.logical_not(o_self(piece)))
        def _():
            o_copy(piece).wait_send()
    spread.finish()
    ins.finish(i_pieces)
    outs.finish(o_pieces)
    for k, device in enumerate(others):
        to = (here + k + 1) % (reps * count)
        remote(tiles.at[to], gain_ref.at[here], g_send.at[k], g_recv.at[k], device).wait_send()
    for copy in started:
        copy.wait_send()


def closing(
    reps, count, d_projected, w_in, attended, normed, d_attn, tokens, d_middle, gain_rows, gain_terms, piece, collective_id
):
    dma = pltpu.SemaphoreType.DMA
    low, f32 = jnp.bfloat16, jnp.float32
    shape = jax.ShapeDtypeStruct
    rows, width = tokens.shape
    seq_len = normed.shape[0]
    total = reps * count
    half = count // 2
    d_rows = width // total
    full = HEAD_DIM // (reps * piece)
    i_block = (count, d_rows, 3 * HEAD_DIM)
    o_block = (full, piece, width)
    hops = dma((2, half, UNITS))
    vm, hb = pl.BlockSpec(memory_space=VM), pl.BlockSpec(memory_space=HB)
    return pl.pallas_call(
        functools.partial(closing_kernel, reps, count),
        out_shape=[
            shape((rows, width), f32),
            shape(i_block, low),
            shape((reps, piece, width), low),
            shape((total, 8, 128), f32),
        ],
        in_specs=[vm] * 3 + [hb] * 2 + [vm] * 4,
        out_specs=[vm] * 4,
        scratch_shapes=[
            pltpu.VMEM((seq_len, width), low),
            pltpu.VMEM((seq_len, width), low),
            pltpu.VMEM((seq_len, width), low),
            pltpu.VMEM((reps,) + i_block, low),
            pltpu.VMEM((reps,) + o_block, low),
            pltpu.VMEM((rows, width), low),
            pltpu.VMEM((2, half, rows, width), low),
            pltpu.VMEM((8, width), f32),
            pltpu.VMEM((total, 8, 128), f32),
            pltpu.VMEM((2,) + i_block, low),
            pltpu.VMEM(i_block, low),
            pltpu.VMEM((2,) + o_block, low),
            pltpu.VMEM(o_block, low),
            hops,
            hops,
            dma((2, count)),
            dma((2, count)),
            dma((count,)),
            dma((count,)),
            dma((2, full)),
            dma((2, full)),
            dma((full,)),
            dma((full,)),
            dma((count,)),
            dma((count,)),
            dma((full,)),
            dma((reps,)),
            dma((total - 1,)),
            dma((total - 1,)),
            dma((2,)),
        ],
        compiler_params=pltpu.CompilerParams(
            collective_id=collective_id, has_side_effects=True, vmem_limit_bytes=VMEM_LIMIT
        ),
        name="closing",
    )(d_projected, w_in, attended, normed, d_attn, tokens, d_middle, gain_rows, gain_terms)


def tiles_of(ref):
    rows, columns = ref.shape
    tall = 72 if rows % 72 == 0 else 64 if rows % 64 == 0 else 8
    wide = 384 if columns % 384 == 0 else 256
    return rows // tall, columns // wide, tall, wide


def tile_at(ref, n):
    _, across, tall, wide = tiles_of(ref)
    down, right = n // across, n % across
    return pl.ds(pl.multiple_of(down * tall, 8), tall), pl.ds(pl.multiple_of(right * wide, 128), wide)


LAMB_ORDER = (4, 2, 3, 0, 1)


def lamb_kernel(reps, count, sum_in, sum_out, sum_gu, gain_tiles, g_master, g_mean, g_square, *refs):
    f32 = jnp.float32
    names = 5
    hbm_in, refs = [refs[3 * i : 3 * i + 3] for i in range(names)], refs[3 * names :]
    grad_dn, refs = refs[0], refs[1:]
    (sums_out, gg_out, gm_out, gs_out, gp_out), refs = refs[:5], refs[5:]
    hbm_out, refs = [refs[4 * i : 4 * i + 4] for i in range(names)], refs[4 * names :]
    masters, means, squares, grads = (refs[names * i : names * (i + 1)] for i in range(4))
    in_sem, out_sem, dn_sem = refs[4 * names :]
    total = reps * count
    group = HEADS // KV_HEADS

    def fetch(i, j):
        return pltpu.make_async_copy(hbm_in[i][j], (masters, means, squares)[j][i], in_sem.at[i, j])

    fetch_dn = pltpu.make_async_copy(grad_dn, grads[4], dn_sem)
    fetch_dn.start()

    def fetch_all(order):
        for i in order:
            for j in range(3):
                fetch(i, j).start()

    fetch_all(LAMB_ORDER[:2])

    def store(i, j):
        return pltpu.make_async_copy((grads, means, squares, masters)[j][i], hbm_out[i][j], out_sem.at[i, j])

    def join(index, ref):
        block = ref.shape[1] // total
        part = block * reps
        for first in range(0, total, 4):
            pieces = []
            for b in range(first, first + 4):
                start = index * part + (b // count) * block
                pieces.append(sum_gu[b % count, :, start : start + block].astype(f32))
            ref[:, first * block : (first + 4) * block] = jnp.concatenate(pieces, axis=1)

    def make_grad(i):
        if i == 0:
            for head in range(HEADS):
                grads[0][:, head * HEAD_DIM : (head + 1) * HEAD_DIM] = sum_in[head, :, :HEAD_DIM].astype(f32)
            for kind in (1, 2):
                for head in range(KV_HEADS):
                    start = (HEADS + (kind - 1) * KV_HEADS + head) * HEAD_DIM
                    parts = [
                        sum_in[head * group + g, :, kind * HEAD_DIM : (kind + 1) * HEAD_DIM].astype(f32)
                        for g in range(group)
                    ]
                    grads[0][:, start : start + HEAD_DIM] = functools.reduce(jnp.add, parts)
        elif i == 1:
            rows = sum_out.shape[1]
            for j in range(reps):
                grads[1][j * rows : (j + 1) * rows, :] = sum_out[j].astype(f32)
        elif i in (2, 3):
            join(i - 2, grads[i])
        else:
            fetch_dn.wait()

    def lamb(master, grad, mean, square):
        new_mean = 0.5 * (mean + grad)
        new_square = 0.5 * (square + grad * grad)
        root = new_square * lax.rsqrt(new_square)
        return new_mean, new_square, new_mean / (root + 1e-06) + 0.01 * master

    def sweep(i):
        down, across, tall, wide = tiles_of(masters[i])

        def body(n, carry):
            at = tile_at(masters[i], n)
            master = masters[i][at]
            new_mean, new_square, step = lamb(master, grads[i][at], means[i][at], squares[i][at])
            means[i][at] = new_mean
            squares[i][at] = new_square
            masters[i][at] = step

            def fold(value):
                return jnp.sum((value * value).reshape(tall // 8, 8, wide), axis=0)

            return carry[0] + fold(master), carry[1] + fold(step)

        zero = jnp.zeros((8, wide), f32)
        return lax.fori_loop(0, down * across, body, (zero, zero))

    at_row = lax.broadcasted_iota(jnp.int32, (8, 128), 0)
    at_lane = lax.broadcasted_iota(jnp.int32, (8, 128), 1)

    def note(sums, i, pair):
        for row in (0, 1):
            sums = sums + jnp.where((at_row == row) & (at_lane == i), jnp.sum(pair[row]), 0.0)
        return sums

    sums = jnp.zeros((8, 128), f32)
    for place, i in enumerate(LAMB_ORDER):
        make_grad(i)
        for j in range(3):
            fetch(i, j).wait()
        fetch_all(LAMB_ORDER[place + 2 : place + 3])
        pair = sweep(i)
        for j in range(4):
            store(i, j).start()
        sums = note(sums, i, pair)
    gain_total = functools.reduce(jnp.add, [gain_tiles[device] for device in range(total)])
    kinds, d_rows = g_master.shape
    gain_grad = gain_total[:kinds, :d_rows]
    gain_master = g_master[...]
    new_mean, new_square, gain_step = lamb(gain_master, gain_grad, g_mean[...], g_square[...])
    gg_out[...] = gain_grad
    gm_out[...] = new_mean
    gs_out[...] = new_square
    gp_out[...] = gain_step
    sums_out[...] = note(sums, 5, (gain_master * gain_master, gain_step * gain_step))
    for i in LAMB_ORDER:
        for j in range(4):
            store(i, j).wait()


def table_kernel(reps, count, sizes, x_ref, out_ref, near, far, held, n_send, n_recv, f_send, f_recv):
    f32 = jnp.float32
    rep = lax.axis_index("rep")
    me = lax.axis_index("shard")
    meet(
        [(rep, (me + k) % count) for k in range(1, count)] + [((rep + k) % reps, me) for k in range(1, reps)]
    )
    copies = []
    for k in range(1, count):
        copies.append(remote(x_ref, near.at[me], n_send.at[k], n_recv.at[k], (rep, (me + k) % count)))
    for copy in copies:
        copy.start()
    near[me] = x_ref[...]
    for k in range(1, count):
        frm = (me + count - k) % count
        remote(x_ref, near.at[frm], n_send.at[k], n_recv.at[k], (rep, frm)).wait_recv()
    sums = functools.reduce(jnp.add, [near[shard] for shard in range(count)])
    held[...] = sums
    more = []
    for k in range(1, reps):
        more.append(remote(held, far.at[rep], f_send.at[k], f_recv.at[k], ((rep + k) % reps, me)))
    for copy in more:
        copy.start()
    far[rep] = sums
    for k in range(1, reps):
        frm = (rep + reps - k) % reps
        remote(held, far.at[frm], f_send.at[k], f_recv.at[k], (frm, me)).wait_recv()
    totals = functools.reduce(jnp.add, [far[other] for other in range(reps)])
    at_lane = lax.broadcasted_iota(jnp.int32, (8, 128), 1)
    counts = jnp.ones((8, 128), f32)
    for i, size in enumerate(sizes):
        counts = jnp.where(at_lane == i, float(size), counts)
    out_ref[...] = jnp.sqrt(totals / counts + 1e-06)
    for copy in copies + more:
        copy.wait_send()


def fresh_kernel(table_ref, g_master, g_step, *refs):
    names = 5
    hbm_in, refs = [refs[2 * i : 2 * i + 2] for i in range(names)], refs[2 * names :]
    (gp_out, table_out), refs = refs[:2], refs[2:]
    hbm_out, refs = refs[:names], refs[names:]
    masters, steps, refs = refs[:names], refs[names : 2 * names], refs[2 * names :]
    in_sem, out_sem = refs

    def fetch(i, j):
        return pltpu.make_async_copy(hbm_in[i][j], (masters, steps)[j][i], in_sem.at[i, j])

    def store(i):
        return pltpu.make_async_copy(masters[i], hbm_out[i], out_sem.at[i])

    def fetch_all(order):
        for i in order:
            for j in (0, 1):
                fetch(i, j).start()

    fetch_all(LAMB_ORDER[:2])
    table_out[...] = table_ref[0:2, 0 : names + 1]
    rate = 0.3 * table_ref[0:1, :] / table_ref[1:2, :]
    gp_out[...] = g_master[...] - rate[:, 5:6] * g_step[...]
    for place, i in enumerate(LAMB_ORDER):
        down, across, _, _ = tiles_of(masters[i])
        scale = rate[:, i : i + 1]
        for j in (0, 1):
            fetch(i, j).wait()
        fetch_all(LAMB_ORDER[place + 2 : place + 3])

        def body(n, carry):
            at = tile_at(masters[i], n)
            masters[i][at] = masters[i][at] - scale * steps[i][at]
            return carry

        lax.fori_loop(0, down * across, body, 0)
        store(i).start()
    for i in LAMB_ORDER:
        store(i).wait()


def lamb_step(reps, count, sums, grad_down, gains, states, collective_id):
    dma = pltpu.SemaphoreType.DMA
    f32 = jnp.float32
    shape = jax.ShapeDtypeStruct
    shapes = [state[0].shape for state in states]
    like_gains = shape(gains[0].shape, f32)
    tile = shape((8, 128), f32)
    vm, hb = pl.BlockSpec(memory_space=VM), pl.BlockSpec(memory_space=HB)
    local = pltpu.CompilerParams(vmem_limit_bytes=VMEM_LIMIT)
    outs = pl.pallas_call(
        functools.partial(lamb_kernel, reps, count),
        out_shape=[tile] + [like_gains] * 4 + [shape(item, f32) for item in shapes for _ in range(4)],
        in_specs=[vm] * 7 + [hb] * 16,
        out_specs=[vm] * 5 + [hb] * 20,
        scratch_shapes=[pltpu.VMEM(item, f32) for _ in range(4) for item in shapes] + [dma((5, 3)), dma((5, 4)), dma],
        compiler_params=local,
        name="lamb_moments",
    )(*sums, *gains, *[item for state in states for item in state], grad_down)
    sums, gain_parts, parts = outs[0], outs[1:5], [outs[5 + 4 * i : 9 + 4 * i] for i in range(5)]
    sizes = [item[0] * item[1] * reps * count for item in shapes + [like_gains.shape]]
    table = pl.pallas_call(
        functools.partial(table_kernel, reps, count, sizes),
        out_shape=tile,
        in_specs=[vm],
        out_specs=vm,
        scratch_shapes=[
            pltpu.VMEM((count, 8, 128), f32),
            pltpu.VMEM((reps, 8, 128), f32),
            pltpu.VMEM((8, 128), f32),
            dma((count,)),
            dma((count,)),
            dma((reps,)),
            dma((reps,)),
        ],
        compiler_params=pltpu.CompilerParams(collective_id=collective_id, has_side_effects=True),
        name="norm_table",
    )(sums)
    fresh = pl.pallas_call(
        fresh_kernel,
        out_shape=[like_gains, shape((2, 6), f32)] + [shape(item, f32) for item in shapes],
        in_specs=[vm] * 3 + [hb] * 10,
        out_specs=[vm] * 2 + [hb] * 5,
        scratch_shapes=[pltpu.VMEM(item, f32) for _ in range(2) for item in shapes] + [dma((5, 2)), dma((5,))],
        compiler_params=local,
        name="lamb_masters",
    )(table, gains[0], gain_parts[3], *[item for i in range(5) for item in (states[i][0], parts[i][3])])
    rest = [[parts[i][j] for i in range(5)] + [gain_parts[j].T] for j in range(3)]
    return fresh[1], rest[0], rest[1], rest[2], list(fresh[2:]) + [fresh[0].T]


def rope_tables(seq_len):
    exponent = -np.arange(HEAD_DIM // 2, dtype=np.float32) * np.float32(2.0) / np.float32(HEAD_DIM)
    freq = np.float32(10000.0) ** exponent
    angle = (np.arange(seq_len, dtype=np.float32)[:, None] * freq[None, :]).astype(np.float64)
    return jnp.asarray(np.cos(angle).astype(np.float32)), jnp.asarray(np.sin(angle).astype(np.float32))


def split_device(
    tokens, cotangent, piece_starts, inproj, outproj, ffn_gate, ffn_up, ffn_down, norm_gains,
    mean_inproj, mean_outproj, mean_gate, mean_up, mean_down, mean_gains,
    square_inproj, square_outproj, square_gate, square_up, square_down, square_gains,
):
    bf16, f32 = jnp.bfloat16, jnp.float32
    reps, count = lax.axis_size("rep"), lax.axis_size("shard")
    rep = lax.axis_index("rep")
    me = lax.axis_index("shard")
    total = reps * count
    rows, width = tokens.shape
    seq_len = rows * count
    group = HEADS // KV_HEADS
    q_width, k_width = HEADS * HEAD_DIM, KV_HEADS * HEAD_DIM
    d_rows = inproj.shape[0]
    ff = ffn_gate.shape[1]
    ff_block = ff // total
    ff_part = ff // count
    o_rows = outproj.shape[0]
    per_head = HEAD_DIM // o_rows
    piece = o_rows // reps

    gain_tile = jnp.pad(norm_gains.T.astype(bf16).astype(f32), ((0, 4), (0, 128 - d_rows)))
    normed_in, gain_rows, got_in, got_gate, got_down, got_out, cut_up = opening(
        reps, count, tokens, gain_tile, inproj, outproj, ffn_gate, ffn_up, ffn_down, 1
    )
    normed_in = normed_in.reshape(seq_len, width)
    w_in = got_in.reshape(width, -1)
    w_gate = got_gate.reshape(width, ff_part)
    w_down = got_down.reshape(ff_part, width)

    position = jnp.arange(seq_len, dtype=jnp.int32)
    cosine, sine = rope_tables(seq_len)
    starts = lax.dynamic_slice_in_dim(piece_starts, rep, 1, 0)[0]
    inside = (position[:, None] >= starts[None, :]) & (position[:, None] < starts[None, :] + PIC)
    tag = jnp.sum(inside.astype(jnp.int32) * (jnp.arange(starts.shape[0], dtype=jnp.int32)[None, :] + 1), axis=1)
    attn_proj, queries, keys, values, attended, probs, damp, w_out, got_up = attention(
        reps, count, normed_in, w_in, got_out, cosine, sine, tag, cut_up, 4
    )
    w_up = got_up.reshape(width, ff_part)

    layer_out, d_middle, d_attn, gain_terms, normed_mid, d_gu, part_down = feed_forward(
        attn_proj, tokens, cotangent, gain_rows, w_gate, w_up, w_down, count, 5
    )
    d_attn, sum_gu, grad_down, d_projected = ffn_grads(
        reps, count, d_attn, w_out, queries, keys, values, cosine, sine, normed_mid, d_gu, part_down, probs, damp, d_rows, 9
    )
    input_grad, sum_in, sum_out, gain_tiles = closing(
        reps, count, d_projected, w_in, attended, normed_in, d_attn.reshape(seq_len, width), tokens, d_middle,
        gain_rows, gain_terms, piece, 12,
    )
    norm_table, gradients, new_means, new_squares, fresh = lamb_step(
        reps,
        count,
        (sum_in, sum_out, sum_gu, gain_tiles),
        grad_down,
        (norm_gains.T, mean_gains.T, square_gains.T),
        (
            (inproj, mean_inproj, square_inproj),
            (outproj, mean_outproj, square_outproj),
            (ffn_gate, mean_gate, square_gate),
            (ffn_up, mean_up, square_up),
            (ffn_down, mean_down, square_down),
        ),
        14,
    )
    return (
        layer_out,
        input_grad,
        *gradients,
        *new_means,
        *new_squares,
        *fresh,
        norm_table,
    )


def fits(mesh, shapes):
    reps, count = mesh.shape["rep"], mesh.shape["shard"]
    total = reps * count
    tokens, piece_starts, outproj, ffn_gate = shapes
    o_rows = outproj[0] // total
    return (
        reps == 4
        and count == HEADS
        and piece_starts[0] == reps
        and tokens[0] % (total * UNITS * 16) == 0
        and HEAD_DIM % o_rows == 0
        and o_rows % (16 * reps) == 0
        and HEAD_DIM // o_rows == total // HEADS
        and ffn_gate[1] % (total * 96) == 0
    )


def solution(mesh):
    split = P(("rep", "shard"), None)

    def step(*args):
        shapes = args[0].shape, args[2].shape, args[4].shape, args[5].shape
        body = split_device if fits(mesh, shapes) else per_device
        return jax.shard_map(
            body,
            mesh=mesh,
            in_specs=(split, split, P()) + (split,) * 18,
            out_specs=(split,) * 26 + (P(),),
            check_vma=False,
        )(*args)

    return step
```

```python
import functools

import jax
import jax.numpy as jnp
from jax import lax
from jax.experimental import pallas as pl
from jax.experimental.pallas import tpu as pltpu
import numpy as np
from jax.sharding import PartitionSpec as P

HEADS = 8
KV_HEADS = 4
HEAD_DIM = 256
PIC = 256


def rms_norm(values_in, gain_col):
    return (
        values_in
        * lax.rsqrt(jnp.mean(values_in * values_in, axis=-1, keepdims=True) + 1e-06)
        * (1.0 + gain_col)
    )


def geglu(gate_lin, up_lin):
    return jax.nn.gelu(gate_lin, approximate=True) * up_lin


def rotate(flat, position, head_count, sign):
    row_count = flat.shape[0]
    width = flat.shape[1] // head_count
    half = width // 2
    vectors = flat.reshape(row_count, head_count, width)
    freq = 10000.0 ** (-(jnp.arange(half, dtype=jnp.float32) * 2.0 / width))
    angle = position.astype(jnp.float32)[:, None] * freq[None, :]
    cosine = jnp.cos(angle)[:, None, :]
    sine = sign * jnp.sin(angle)[:, None, :]
    first = vectors[..., :half]
    second = vectors[..., half:]
    turned = jnp.concatenate(
        [first * cosine - second * sine, second * cosine + first * sine], axis=-1
    )
    return turned.reshape(row_count, head_count * width)


def owned_rows(activation, gradient, rep_index, width):
    piece = lax.dynamic_slice_in_dim(activation, rep_index * width, width, 1)
    return lax.dot_general(
        piece, gradient, (((0,), (0,)), ((), ())), preferred_element_type=jnp.float32
    )


def back_dot(gradient, weight):
    return lax.dot_general(
        gradient, weight, (((1,), (1,)), ((), ())), preferred_element_type=jnp.float32
    )


def describe(rows, piece_starts, seq_offset, seq_len):
    local_seq = rows // seq_len
    position = rows % seq_len
    global_seq = local_seq + seq_offset
    seq_total = piece_starts.shape[0]
    piece_count = piece_starts.shape[1]
    select = (global_seq[:, None] == jnp.arange(seq_total, dtype=jnp.int32)[None, :]).astype(
        jnp.int32
    )
    starts = jnp.sum(select[:, :, None] * piece_starts[None, :, :], axis=1)
    inside = ((position[:, None] >= starts) & (position[:, None] < starts + PIC)).astype(jnp.int32)
    labels = (
        global_seq[:, None] * piece_count + jnp.arange(piece_count, dtype=jnp.int32)[None, :] + 1
    )
    return (local_seq, position, jnp.sum(inside * labels, axis=1))


def visibility(piece_starts, query_rows, key_rows, seq_offset, seq_len):
    seq_q, pos_q, tag_q = describe(query_rows, piece_starts, seq_offset, seq_len)
    seq_k, pos_k, tag_k = describe(key_rows, piece_starts, seq_offset, seq_len)
    causal = pos_k[None, :] <= pos_q[:, None]
    same_piece = (tag_q[:, None] == tag_k[None, :]) & (tag_q[:, None] > 0)
    return (seq_q[:, None] == seq_k[None, :]) & (causal | same_piece)


def lamb_local(master, gradient, first, second):
    newmean = 0.5 * first + 0.5 * gradient
    newsquare = 0.5 * second + 0.5 * gradient * gradient
    step_dir = newmean / (jnp.sqrt(newsquare) + 1e-06) + 0.01 * master
    return (newmean, newsquare, step_dir)


def per_device(
    tokens,
    cotangent,
    piece_starts,
    inproj,
    outproj,
    ffn_gate,
    ffn_up,
    ffn_down,
    norm_gains,
    mean_inproj,
    mean_outproj,
    mean_gate,
    mean_up,
    mean_down,
    mean_gains,
    square_inproj,
    square_outproj,
    square_gate,
    square_up,
    square_down,
    square_gains,
):
    bf16 = jnp.bfloat16
    f32 = jnp.float32
    rep_count = lax.axis_size("rep")
    shard_count = lax.axis_size("shard")
    rep_index = lax.axis_index("rep")
    w_in, w_out, w_gate, w_up, w_down, gain_copy = (
        lax.all_gather(inproj.astype(bf16), ("rep", "shard"), axis=0, tiled=True),
        lax.all_gather(outproj.astype(bf16), ("rep", "shard"), axis=0, tiled=True),
        lax.all_gather(ffn_gate.astype(bf16), ("rep", "shard"), axis=0, tiled=True),
        lax.all_gather(ffn_up.astype(bf16), ("rep", "shard"), axis=0, tiled=True),
        lax.all_gather(ffn_down.astype(bf16), ("rep", "shard"), axis=0, tiled=True),
        lax.all_gather(norm_gains.astype(bf16), ("rep", "shard"), axis=0, tiled=True),
    )
    gains_used = gain_copy.astype(f32)
    residual = tokens.astype(f32)
    row_count = residual.shape[0]
    seq_len = row_count * shard_count
    q_width = HEADS * HEAD_DIM
    k_width = KV_HEADS * HEAD_DIM
    group_size = HEADS // KV_HEADS
    query_scale = HEAD_DIM ** (-0.5)
    local_rows = lax.axis_index("shard") * row_count + jnp.arange(row_count, dtype=jnp.int32)
    position = local_rows % seq_len
    normed_in = rms_norm(residual, gains_used[:, 0]).astype(bf16)
    projected = jnp.dot(normed_in, w_in, preferred_element_type=f32)
    queries = (rotate(projected[:, :q_width], position, HEADS, 1.0) * query_scale).astype(bf16)
    keys = rotate(projected[:, q_width : q_width + k_width], position, KV_HEADS, 1.0).astype(bf16)
    values = projected[:, q_width + k_width :].astype(bf16)
    all_keys, all_values = (
        lax.all_gather(keys, "shard", axis=0, tiled=True),
        lax.all_gather(values, "shard", axis=0, tiled=True),
    )
    key_rows = all_keys.shape[0]
    visible = visibility(
        piece_starts,
        local_rows,
        jnp.arange(key_rows, dtype=jnp.int32),
        rep_index * (key_rows // seq_len),
        seq_len,
    )
    query_heads = queries.reshape(row_count, KV_HEADS, group_size, HEAD_DIM)
    key_heads = all_keys.reshape(key_rows, KV_HEADS, HEAD_DIM)
    value_heads = all_values.reshape(key_rows, KV_HEADS, HEAD_DIM)

    def capped_scores():
        raw_scores = jnp.einsum(
            "tgrd,kgd->grtk", query_heads, key_heads, preferred_element_type=f32
        )
        bent_scores = jnp.tanh(raw_scores / 50.0)
        return (bent_scores, jnp.where(visible, 50.0 * bent_scores, -1e30))

    bent_scores, masked = capped_scores()
    top_score = jnp.max(masked, axis=-1, keepdims=True)
    log_total = top_score + jnp.log(jnp.sum(jnp.exp(masked - top_score), axis=-1, keepdims=True))
    probs_low = jnp.exp(masked - log_total).astype(bf16)
    attended = (
        jnp.einsum("grtk,kgd->tgrd", probs_low, value_heads, preferred_element_type=f32)
        .reshape(row_count, q_width)
        .astype(bf16)
    )
    attn_proj = jnp.dot(attended, w_out, preferred_element_type=f32)
    middle = residual + rms_norm(attn_proj, gains_used[:, 1])
    normed_mid = rms_norm(middle, gains_used[:, 2]).astype(bf16)
    gate_lin = jnp.dot(normed_mid, w_gate, preferred_element_type=f32)
    up_lin = jnp.dot(normed_mid, w_up, preferred_element_type=f32)
    hidden = geglu(gate_lin, up_lin).astype(bf16)
    ffn_proj = jnp.dot(hidden, w_down, preferred_element_type=f32)
    layer_out = (middle + rms_norm(ffn_proj, gains_used[:, 3])).astype(bf16)
    d_out = cotangent.astype(f32)
    _, post_back = jax.vjp(rms_norm, ffn_proj, gains_used[:, 3])
    d_ffn, d_gain3 = post_back(d_out)
    d_ffn_low = d_ffn.astype(bf16)
    hidden_all, d_ffn_all = (
        lax.all_gather(hidden, "rep", axis=0, tiled=True),
        lax.all_gather(d_ffn_low, "rep", axis=0, tiled=True),
    )
    part_down = owned_rows(hidden_all, d_ffn_all, rep_index, hidden.shape[1] // rep_count)
    d_hidden = back_dot(d_ffn_low, w_down)
    _, glu_back = jax.vjp(geglu, gate_lin, up_lin)
    d_gate, d_up = glu_back(d_hidden)
    d_gate_low = d_gate.astype(bf16)
    d_up_low = d_up.astype(bf16)
    gate_up_grad = jnp.concatenate([d_gate_low, d_up_low], axis=1)
    mid_all, gate_up_all = (
        lax.all_gather(normed_mid, "rep", axis=0, tiled=True),
        lax.all_gather(gate_up_grad, "rep", axis=0, tiled=True),
    )
    part_gate_up = owned_rows(mid_all, gate_up_all, rep_index, normed_mid.shape[1] // rep_count)
    d_mid_in = back_dot(d_gate_low, w_gate) + back_dot(d_up_low, w_up)
    _, pre_back = jax.vjp(rms_norm, middle, gains_used[:, 2])
    d_mid_part, d_gain2 = pre_back(d_mid_in)
    d_middle = d_out + d_mid_part
    _, attn_back = jax.vjp(rms_norm, attn_proj, gains_used[:, 1])
    d_attn, d_gain1 = attn_back(d_middle)
    d_attn_low = d_attn.astype(bf16)
    d_attended = back_dot(d_attn_low, w_out).astype(bf16)
    d_heads = d_attended.reshape(row_count, KV_HEADS, group_size, HEAD_DIM)
    bent_again, masked_again = capped_scores()
    attn_probs = jnp.exp(masked_again - log_total)
    probs_again = attn_probs.astype(bf16)
    d_probs = jnp.einsum("tgrd,kgd->grtk", d_heads, value_heads, preferred_element_type=f32)
    d_scores = (
        attn_probs
        * (d_probs - jnp.sum(attn_probs * d_probs, axis=-1, keepdims=True))
        * (1.0 - bent_again * bent_again)
    ).astype(bf16)
    d_queries = jnp.einsum(
        "grtk,kgd->tgrd", d_scores, key_heads, preferred_element_type=f32
    ).reshape(row_count, q_width)
    d_key = jnp.einsum("grtk,tgrd->kgd", d_scores, query_heads, preferred_element_type=f32).reshape(
        row_count * lax.axis_size("shard"), k_width
    )
    d_value = jnp.einsum(
        "grtk,tgrd->kgd", probs_again, d_heads, preferred_element_type=f32
    ).reshape(row_count * lax.axis_size("shard"), k_width)
    d_key_value = lax.psum_scatter(
        jnp.concatenate([d_key, d_value], axis=1), "shard", scatter_dimension=0, tiled=True
    )
    d_projected = jnp.concatenate(
        [
            rotate(d_queries, position, HEADS, -1.0) * query_scale,
            rotate(d_key_value[:, :k_width], position, KV_HEADS, -1.0),
            d_key_value[:, k_width:],
        ],
        axis=1,
    ).astype(bf16)
    d_normed_in = back_dot(d_projected, w_in)
    _, first_back = jax.vjp(rms_norm, residual, gains_used[:, 0])
    d_input_part, d_gain0 = first_back(d_normed_in)
    input_grad = d_middle + d_input_part
    gain_grad = jnp.stack([d_gain0, d_gain1, d_gain2, d_gain3], axis=1)
    attended_all, d_attn_all, normed_all, d_proj_all = (
        lax.all_gather(attended, "rep", axis=0, tiled=True),
        lax.all_gather(d_attn_low, "rep", axis=0, tiled=True),
        lax.all_gather(normed_in, "rep", axis=0, tiled=True),
        lax.all_gather(d_projected, "rep", axis=0, tiled=True),
    )
    part_out = owned_rows(attended_all, d_attn_all, rep_index, attended.shape[1] // rep_count)
    part_in = owned_rows(normed_all, d_proj_all, rep_index, normed_in.shape[1] // rep_count)
    part_gain = lax.psum_scatter(gain_grad, "rep", scatter_dimension=0, tiled=True)
    owned = (
        lax.psum_scatter(part_in, "shard", scatter_dimension=0, tiled=True),
        lax.psum_scatter(part_gain, "shard", scatter_dimension=0, tiled=True),
        lax.psum_scatter(part_out, "shard", scatter_dimension=0, tiled=True),
        lax.psum_scatter(part_gate_up, "shard", scatter_dimension=0, tiled=True),
        lax.psum_scatter(part_down, "shard", scatter_dimension=0, tiled=True),
    )
    grad_inproj, grad_gains, grad_outproj, grad_gate_up, grad_down = owned
    split_at = grad_gate_up.shape[1] // 2
    grad_gate = grad_gate_up[:, :split_at]
    grad_up = grad_gate_up[:, split_at:]
    masters = (inproj, outproj, ffn_gate, ffn_up, ffn_down, norm_gains)
    gradients = (grad_inproj, grad_outproj, grad_gate, grad_up, grad_down, grad_gains)
    firsts = (mean_inproj, mean_outproj, mean_gate, mean_up, mean_down, mean_gains)
    seconds = (square_inproj, square_outproj, square_gate, square_up, square_down, square_gains)
    results = [
        lamb_local(masters[index], gradients[index], firsts[index], seconds[index])
        for index in range(6)
    ]
    weight_sums = jnp.stack([jnp.sum(master * master) for master in masters])
    step_sums = jnp.stack([jnp.sum(item[2] * item[2]) for item in results])
    totals = lax.psum(jnp.stack([weight_sums, step_sums]), ("rep", "shard"))
    counts = jnp.array([float(master.size * rep_count * shard_count) for master in masters], f32)
    norm_table = jnp.sqrt(totals / counts[None, :] + 1e-06)
    fresh = [
        masters[index] - 0.3 * norm_table[0, index] / norm_table[1, index] * results[index][2]
        for index in range(6)
    ]
    return (
        layer_out,
        input_grad,
        grad_inproj,
        grad_outproj,
        grad_gate,
        grad_up,
        grad_down,
        grad_gains,
        results[0][0],
        results[1][0],
        results[2][0],
        results[3][0],
        results[4][0],
        results[5][0],
        results[0][1],
        results[1][1],
        results[2][1],
        results[3][1],
        results[4][1],
        results[5][1],
        fresh[0],
        fresh[1],
        fresh[2],
        fresh[3],
        fresh[4],
        fresh[5],
        norm_table,
    )


MESH = pl.DeviceIdType.MESH
VM = pltpu.VMEM
HB = pl.ANY
UNITS = 4
VMEM_LIMIT = 60 << 20


def ring_places(count):
    inner = 2 if count == 8 else 4
    outer = count // inner

    def place(shard):
        major = shard // inner
        minor = shard % inner
        return minor * outer + major + (minor % 2) * (outer - 1 - 2 * major)

    def shard_at(spot):
        minor = spot // outer
        major = spot % outer
        return (major + (minor % 2) * (outer - 1 - 2 * major)) * inner + minor

    return place, shard_at


def meet(devices):
    barrier = pltpu.get_barrier_semaphore()
    for device in devices:
        pl.semaphore_signal(barrier, inc=1, device_id=device, device_id_type=MESH)
    pl.semaphore_wait(barrier, len(devices))


def remote(src, dst, send_sem, recv_sem, device):
    return pltpu.make_async_remote_copy(
        src_ref=src,
        dst_ref=dst,
        send_sem=send_sem,
        recv_sem=recv_sem,
        device_id=device,
        device_id_type=MESH,
    )


class Ring:
    def __init__(self, count):
        place, shard_at = ring_places(count)
        self.count = count
        self.half = count // 2
        self.rep = lax.axis_index("rep")
        self.me = lax.axis_index("shard")
        self.spot = place(self.me)
        self.shard_at = shard_at
        self.next = [(self.rep, self.at(1)), (self.rep, self.at(count - 1))]

    def at(self, ahead):
        return self.shard_at((self.spot + ahead) % self.count)

    def away(self, way, hops):
        return self.at(hops if way == 0 else self.count - hops)

    def units(self, way, hop):
        order = list(range(UNITS)) if way == 0 else list(range(UNITS))[::-1]
        return order if hop < self.half else order[: UNITS // 2]


def reduce_on_ring(ring, rows, take, first, landed, send, recv, finish, pause):
    f32 = jnp.float32
    hops = ring.half
    started = []

    def part(unit):
        return pl.ds(unit * (rows // UNITS), rows // UNITS)

    def step_copy(way, step, unit):
        return remote(
            landed.at[way, step - 1, part(unit)] if step else first.at[part(unit)],
            landed.at[way, step, part(unit)],
            send.at[way, step, unit],
            recv.at[way, step, unit],
            ring.next[way],
        )

    for step in range(hops):
        order = ring.units(0, hops - step), ring.units(1, hops - step)
        before = [ring.units(way, hops - step + 1) if step else [] for way in (0, 1)]
        for index in range(len(order[0])):
            for way in (0, 1):
                unit = order[way][index]
                block = take(ring.away(way, hops - step), part(unit)).astype(f32)
                if unit in before[way]:
                    step_copy(way, step - 1, unit).wait_recv()
                    block += landed[way, step - 1, part(unit), :].astype(f32)
                if step:
                    landed[way, step - 1, part(unit), :] = block.astype(landed.dtype)
                else:
                    first[part(unit), :] = block.astype(first.dtype)
                copy = step_copy(way, step, unit)
                copy.start()
                started.append(copy)
            if step or index == len(order[0]) - 1:
                pause()
    for unit in range(UNITS):
        total = take(ring.me, part(unit)).astype(f32)
        for way in (0, 1):
            step_copy(way, hops - 1, unit).wait_recv()
            total += landed[way, hops - 1, part(unit), :].astype(f32)
        finish(part(unit), total)
    return started


class Flow:
    def __init__(self, ring, rows, send, recv):
        self.ring, self.rows, self.send, self.recv = ring, rows, send, recv
        self.unit_rows = rows // UNITS
        self.started = []

    def span(self, slot, unit):
        return pl.ds(slot * self.rows + unit * self.unit_rows, self.unit_rows)

    def slot(self, way, hops):
        if hops == 0:
            return 0
        return self.ring.count - 1 if hops == self.ring.half else 2 * hops - 1 + way

    def go(self, copy):
        copy.start()
        self.started.append(copy)

    def finish(self):
        for copy in self.started:
            copy.wait_send()

    def gather_copy(self, buffer, way, hop, unit):
        return remote(
            buffer.at[self.span(self.slot(way, hop - 1), unit)],
            buffer.at[self.span(self.slot(way, hop), unit)],
            self.send.at[way, hop - 1, unit],
            self.recv.at[way, hop - 1, unit],
            self.ring.next[way],
        )

    def gather(self, buffer, group_work):
        ring = self.ring
        for index in range(UNITS):
            for way in (0, 1):
                self.go(self.gather_copy(buffer, way, 1, ring.units(way, 1)[index]))
        queue = list(group_work(0, 1))
        for hop in range(1, ring.half + 1):
            length = len(ring.units(0, hop))
            for index in range(length):
                for way in (0, 1):
                    unit = ring.units(way, hop)[index]
                    self.gather_copy(buffer, way, hop, unit).wait_recv()
                    if hop < ring.half and unit in ring.units(way, hop + 1):
                        self.go(self.gather_copy(buffer, way, hop + 1, unit))
                if queue:
                    queue.pop(0)()
            for piece in queue:
                piece()
            queue = list(group_work(2 * hop - 1, 2) if hop < ring.half else group_work(ring.count - 1, 1))
        for piece in queue:
            piece()
        self.finish()

    def reduce_copy(self, first, landed, way, step, unit):
        span = pl.ds(unit * self.unit_rows, self.unit_rows)
        src = first.at[span] if step == 0 else landed.at[way, step - 1, span]
        return remote(
            src,
            landed.at[way, step, span],
            self.send.at[way, step, unit],
            self.recv.at[way, step, unit],
            self.ring.next[way],
        )

    def reduce(self, first, landed, partial, group_work, finish, extra=()):
        extra = list(extra)
        ring = self.ring
        hops = ring.half
        f32 = jnp.float32
        for piece in group_work(ring.count - 1, 1, 0):
            piece()
        queue = list(group_work(2 * (hops - 1) - 1, 2, 1))
        for step in range(hops):
            order = ring.units(0, hops - step), ring.units(1, hops - step)
            before = [ring.units(way, hops - step + 1) if step else [] for way in (0, 1)]
            for index in range(len(order[0])):
                for way in (0, 1):
                    unit = order[way][index]
                    span = pl.ds(unit * self.unit_rows, self.unit_rows)
                    if step == 0:
                        first[span, :] = partial[0, pl.ds(unit * self.unit_rows, self.unit_rows), :].astype(first.dtype)
                    else:
                        side = 1 - way
                        block = partial[
                            step % 2, pl.ds(side * self.rows + unit * self.unit_rows, self.unit_rows), :
                        ]
                        if unit in before[way]:
                            self.reduce_copy(first, landed, way, step - 1, unit).wait_recv()
                            block = block + landed[way, step - 1, span, :].astype(f32)
                        landed[way, step - 1, span, :] = block.astype(landed.dtype)
                    self.go(self.reduce_copy(first, landed, way, step, unit))
                if queue:
                    queue.pop(0)()
                elif extra:
                    extra.pop(0)()
            for piece in queue:
                piece()
            ahead = hops - step - 2
            queue = []
            if step < hops - 1:
                queue = list(group_work(2 * ahead - 1, 2, step % 2) if ahead > 0 else group_work(0, 1, step % 2))
        for piece in extra:
            piece()
        for unit in range(UNITS):
            span = pl.ds(unit * self.unit_rows, self.unit_rows)
            total = partial[hops % 2, span, :]
            for way in (0, 1):
                self.reduce_copy(first, landed, way, hops - 1, unit).wait_recv()
                total = total + landed[way, hops - 1, span, :].astype(f32)
            finish(unit, total)
        self.finish()


def looped(piece, count):
    def all_of_it():
        def body(j, carry):
            piece(j)
            return carry

        lax.fori_loop(0, count, body, 0)

    return [all_of_it]


def gelu_pair(gate):
    inner = 0.7978845608028654 * (gate + 0.044715 * gate * gate * gate)
    bend = jnp.tanh(inner)
    value = 0.5 * gate * (1.0 + bend)
    slope = 0.5 * (1.0 + bend) + 0.5 * gate * (1.0 - bend * bend) * 0.7978845608028654 * (
        1.0 + 0.134145 * gate * gate
    )
    return value, slope


def ffn_kernel(
    count, attn_ref, tokens_ref, cot_ref, gains_ref, gate_hbm, up_hbm, dn_hbm,
    layer_ref, dmid_ref, dattn_ref, gg_ref, h3_hbm, dgu_hbm, part_hbm,
    gate_ref, up_ref, dn_ref, h3_ref, hid_ref, dffn_ref, dgu_ref,
    lin, partial, first, landed, middle, total_ref, s1, r1, s2, r2, s3, r3, s4, r4, loads, stores,
):
    f32, bf16 = jnp.float32, jnp.bfloat16
    ring = Ring(count)
    rows, width = attn_ref.shape
    part = hid_ref.shape[1]
    tile = part // 3
    wide = width // 3
    fetched = [
        pltpu.make_async_copy(src, dst, loads.at[index])
        for index, (src, dst) in enumerate(((gate_hbm, gate_ref), (up_hbm, up_ref), (dn_hbm, dn_ref)))
    ]
    for copy in fetched:
        copy.start()
    kept = []

    def keep_out(src, dst):
        copy = pltpu.make_async_copy(src, dst, stores.at[len(kept)])
        copy.start()
        kept.append(copy)

    meet(ring.next)

    def gain(index):
        return 1.0 + gains_ref[index : index + 1, :]

    def scale_of(value):
        return lax.rsqrt(jnp.mean(value * value, axis=-1, keepdims=True) + 1e-06)

    half = rows // 2
    halves = [pl.ds(0, half), pl.ds(half, half)]
    for span in halves:
        proj = attn_ref[span, :]
        mid = tokens_ref[span, :].astype(f32) + proj * scale_of(proj) * gain(1)
        middle[span, :] = mid
        h3_ref[span, :] = (mid * scale_of(mid) * gain(2)).astype(bf16)

    def lin_work(slot, blocks):
        at = pl.ds(slot * rows, blocks * rows)

        def piece(j):
            lo = pl.ds(pl.multiple_of(j * tile, 128), tile)
            hi = pl.ds(pl.multiple_of(part + j * tile, 128), tile)
            gate = jnp.dot(h3_ref[at, :], gate_ref[:, lo], preferred_element_type=f32)
            up = jnp.dot(h3_ref[at, :], up_ref[:, lo], preferred_element_type=f32)
            value, slope = gelu_pair(gate)
            hid_ref[at, lo] = (value * up).astype(bf16)
            lin[at, lo] = (up * slope).astype(bf16)
            lin[at, hi] = value.astype(bf16)

        return looped(piece, 3)

    def down_work(slot, blocks, side):
        at = pl.ds(slot * rows, blocks * rows)

        def piece(j):
            cols = pl.ds(pl.multiple_of(j * wide, 128), wide)
            partial[side, pl.ds(0, blocks * rows), cols] = jnp.dot(
                hid_ref[at, :], dn_ref[:, cols], preferred_element_type=f32
            )

        return looped(piece, 3)

    def nt(left, right):
        return lax.dot_general(left, right, (((1,), (1,)), ((), ())), preferred_element_type=f32)

    def back_work(slot, blocks):
        at = pl.ds(slot * rows, blocks * rows)

        def piece(j):
            lo = pl.ds(pl.multiple_of(j * tile, 128), tile)
            hi = pl.ds(pl.multiple_of(part + j * tile, 128), tile)
            d_hidden = nt(dffn_ref[at, :], dn_ref[lo, :])
            dgu_ref[at, lo] = (d_hidden * lin[at, lo].astype(f32)).astype(bf16)
            dgu_ref[at, hi] = (d_hidden * lin[at, hi].astype(f32)).astype(bf16)

        return looped(piece, 3)

    def input_work(slot, blocks, side):
        at = pl.ds(slot * rows, blocks * rows)

        def piece(j):
            cols = pl.ds(pl.multiple_of(j * wide, 128), wide)
            partial[side, pl.ds(0, blocks * rows), cols] = nt(dgu_ref[at, :part], gate_ref[cols, :]) + nt(
                dgu_ref[at, part:], up_ref[cols, :]
            )

        return looped(piece, 3)

    def keep(unit, total):
        total_ref[pl.ds(unit * (rows // UNITS), rows // UNITS), :] = total

    def lin_first(slot, blocks):
        work = lin_work(slot, blocks)
        return [lambda: (fetched[0].wait(), fetched[1].wait())] + work if slot == 0 else work

    Flow(ring, rows, s1, r1).gather(h3_ref, lin_first)
    keep_out(h3_ref, h3_hbm)
    fetched[2].wait()
    Flow(ring, rows, s2, r2).reduce(first, landed, partial, down_work, keep)

    def back_norm(value, index, grad):
        scale = scale_of(value)
        normed = value * scale
        weighted = grad * gain(index)
        inner = jnp.mean(weighted * normed, axis=-1, keepdims=True)
        return scale * (weighted - normed * inner), jnp.sum(grad * normed, axis=0, keepdims=True)

    gg = jnp.zeros((1, width), f32)
    for span in halves:
        proj = total_ref[span, :]
        scale = scale_of(proj)
        layer_ref[span, :] = (middle[span, :] + proj * scale * gain(3)).astype(bf16)
        d_ffn, term = back_norm(proj, 3, cot_ref[span, :].astype(f32))
        gg += term
        dffn_ref[span, :] = d_ffn.astype(bf16)
    gg_ref[3:4, :] = gg

    Flow(ring, rows, s3, r3).gather(dffn_ref, back_work)
    keep_out(dgu_ref, dgu_hbm)

    def make_down(j):
        span = pl.ds(j * tile, tile)

        def body(n, carry):
            cols = pl.ds(pl.multiple_of(n * wide, 128), wide)
            lin[span, cols] = tn(hid_ref[:, span], dffn_ref[:, cols]).astype(bf16)
            return carry

        lax.fori_loop(0, 3, body, 0)
        keep_out(lin.at[span, pl.ds(0, width)], part_hbm.at[span])

    Flow(ring, rows, s4, r4).reduce(
        first, landed, partial, input_work, keep, [functools.partial(make_down, j) for j in range(3)]
    )

    gg1 = jnp.zeros((1, width), f32)
    gg2 = jnp.zeros((1, width), f32)
    for span in halves:
        d_mid, term = back_norm(middle[span, :], 2, total_ref[span, :])
        gg2 += term
        d_mid = d_mid + cot_ref[span, :].astype(f32)
        dmid_ref[span, :] = d_mid
        d_attn, term = back_norm(attn_ref[span, :], 1, d_mid)
        gg1 += term
        dattn_ref[span, :] = d_attn.astype(bf16)
    gg_ref[1:2, :] = gg1
    gg_ref[2:3, :] = gg2
    gg_ref[0:1, :] = jnp.zeros((1, width), f32)
    gg_ref[4:8, :] = jnp.zeros((4, width), f32)
    for copy in kept:
        copy.wait()


def feed_forward(attn_proj, tokens, cotangent, gain_rows, w_gate, w_up, w_down, count, collective_id):
    f32, bf16 = jnp.float32, jnp.bfloat16
    rows, width = attn_proj.shape
    part = w_down.shape[0]
    every = rows * count
    dma = pltpu.SemaphoreType.DMA
    shape = jax.ShapeDtypeStruct
    return pl.pallas_call(
        functools.partial(ffn_kernel, count),
        out_shape=[
            shape((rows, width), bf16),
            shape((rows, width), f32),
            shape((rows, width), bf16),
            shape((8, width), f32),
            shape((every, width), bf16),
            shape((every, 2 * part), bf16),
            shape((part, width), bf16),
        ],
        in_specs=[pl.BlockSpec(memory_space=VM)] * 4 + [pl.BlockSpec(memory_space=HB)] * 3,
        out_specs=[pl.BlockSpec(memory_space=VM)] * 4 + [pl.BlockSpec(memory_space=HB)] * 3,
        scratch_shapes=[
            pltpu.VMEM(w_gate.shape, bf16),
            pltpu.VMEM(w_up.shape, bf16),
            pltpu.VMEM(w_down.shape, bf16),
            pltpu.VMEM((every, width), bf16),
            pltpu.VMEM((every, part), bf16),
            pltpu.VMEM((every, width), bf16),
            pltpu.VMEM((every, 2 * part), bf16),
            pltpu.VMEM((max(every, part), max(2 * part, width)), bf16),
            pltpu.VMEM((2, 2 * rows, width), f32),
            pltpu.VMEM((rows, width), bf16),
            pltpu.VMEM((2, count // 2, rows, width), bf16),
            pltpu.VMEM((rows, width), f32),
            pltpu.VMEM((rows, width), f32),
        ]
        + [dma((2, count // 2, UNITS))] * 8
        + [dma((3,)), dma((5,))],
        compiler_params=pltpu.CompilerParams(
            collective_id=collective_id, has_side_effects=True, vmem_limit_bytes=VMEM_LIMIT
        ),
        name="feed_forward",
    )(attn_proj, tokens, cotangent, gain_rows, w_gate, w_up, w_down)


def attention_kernel(
    reps, count, h1_ref, in_ref, got_ref, cos_ref, sin_ref, tagq_ref, tagk_ref, cut_ref,
    proj_ref, q_ref, k_ref, v_ref, att_ref, probs_ref, damp_ref, wo_ref, up_ref,
    part, first, landed, r_send, r_recv, w_sems, loc
):
    f32, bf16 = jnp.float32, jnp.bfloat16
    ring = Ring(count)
    rows = proj_ref.shape[0]
    seq_len = h1_ref.shape[0]
    tall = seq_len // 4
    half = HEAD_DIM // 2
    meet(near_devices(ring))
    weights = Fetch(ring, cut_ref, up_ref, w_sems)
    weights.begin()
    own = pltpu.make_async_copy(cut_ref.at[ring.me], up_ref.at[ring.rep, ring.me], loc)
    own.start()
    piece = got_ref.shape[2]
    for block in range(got_ref.shape[1]):
        for j in range(reps):
            start = (block * reps + j) * piece
            wo_ref[start : start + piece, :] = got_ref[j, block]

    def project(i, carry):
        at = pl.ds(pl.multiple_of(i * tall, 16), tall)
        flat = jnp.dot(h1_ref[at, :], in_ref[...], preferred_element_type=f32)
        cosine, sine = cos_ref[at, :], sin_ref[at, :]

        def turned(start):
            first, second = flat[:, start : start + half], flat[:, start + half : start + HEAD_DIM]
            return jnp.concatenate([first * cosine - second * sine, second * cosine + first * sine], axis=1)

        q_ref[at, :] = (turned(0) * HEAD_DIM ** (-0.5)).astype(bf16)
        k_ref[at, :] = turned(HEAD_DIM).astype(bf16)
        v_ref[at, :] = flat[:, 2 * HEAD_DIM :].astype(bf16)
        return carry

    lax.fori_loop(0, 4, project, 0)

    def attend(shard):
        at = pl.ds(pl.multiple_of(shard * rows, 16), rows)
        raw = lax.dot_general(q_ref[at, :], k_ref[...], (((1,), (1,)), ((), ())), preferred_element_type=f32)
        bent = jnp.tanh(raw * (1.0 / 50.0))
        query_at = shard * rows + lax.broadcasted_iota(jnp.int32, (rows, seq_len), 0)
        key_at = lax.broadcasted_iota(jnp.int32, (rows, seq_len), 1)
        tag = tagq_ref[at, :]
        visible = (key_at <= query_at) | ((tag == tagk_ref[...]) & (tag > 0))
        masked = jnp.where(visible, 50.0 * bent, -1e30)
        expo = jnp.exp(masked - jnp.max(masked, axis=-1, keepdims=True))
        probs = expo / jnp.sum(expo, axis=-1, keepdims=True)
        low = probs.astype(bf16)
        probs_ref[at, :] = low
        damp_ref[at, :] = (probs * (1.0 - bent * bent)).astype(bf16)
        attended = jnp.dot(low, v_ref[...], preferred_element_type=f32).astype(bf16)
        att_ref[at, :] = attended
        part[at, :] = jnp.dot(attended, wo_ref[...], preferred_element_type=f32)

    def attend_both(hop):
        def body(way, carry):
            attend(ring.at(hop + way * (count - 2 * hop)))
            return carry

        lax.fori_loop(0, 2 if hop else 1, body, 0)

    work = weights.steps()
    first_of_step = [0] + [1 + UNITS * step for step in range(ring.half - 1)]
    calls = []

    def pause():
        call = len(calls)
        calls.append(call)
        if call in first_of_step:
            attend_both(ring.half - 1 - first_of_step.index(call))
            return
        for _ in range(min(3, len(work))):
            work.pop(0)()

    def finish(span, total):
        proj_ref[span, :] = total

    def take(shard, span):
        return part[pl.ds(pl.multiple_of(shard * rows + span.start, 16), span.size), :]

    attend(ring.at(ring.half))
    started = reduce_on_ring(ring, rows, take, first, landed, r_send, r_recv, finish, pause)
    for piece in work:
        piece()
    weights.finish()
    own.wait()
    for copy in started:
        copy.wait_send()


def attention(reps, count, normed, w_in, w_out, cosine, sine, tag, cut_up, collective_id):
    dma = pltpu.SemaphoreType.DMA
    low, f32 = jnp.bfloat16, jnp.float32
    shape = jax.ShapeDtypeStruct
    seq_len, width = normed.shape
    rows = seq_len // count
    hops = count // 2
    head = shape((seq_len, HEAD_DIM), low)
    square = shape((seq_len, seq_len), low)
    return pl.pallas_call(
        functools.partial(attention_kernel, reps, count),
        out_shape=[
            shape((rows, width), f32), head, head, head, head, square, square, shape((HEAD_DIM, width), low),
            shape((reps,) + cut_up.shape, low),
        ],
        in_specs=[pl.BlockSpec(memory_space=VM)] * 7 + [pl.BlockSpec(memory_space=HB)],
        out_specs=[pl.BlockSpec(memory_space=VM)] * 8 + [pl.BlockSpec(memory_space=HB)],
        scratch_shapes=[
            pltpu.VMEM((seq_len, width), f32),
            pltpu.VMEM((rows, width), low),
            pltpu.VMEM((2, hops, rows, width), low),
            dma((2, hops, UNITS)),
            dma((2, hops, UNITS)),
            dma((8, count)),
            dma,
        ],
        compiler_params=pltpu.CompilerParams(
            collective_id=collective_id, has_side_effects=True, vmem_limit_bytes=VMEM_LIMIT
        ),
        name="attention",
    )(normed, w_in, w_out, cosine, sine, tag[:, None], tag[None, :], cut_up)


class Fetch:
    def __init__(self, ring, cut, out, sems):
        self.ring, self.cut, self.out = ring, cut, out
        self.rep, self.me, self.count = ring.rep, ring.me, ring.count
        self.across, self.beside = rep_partners(ring.rep)
        self.sems = sems
        self.started = []

    def go(self, copy):
        copy.start()
        self.started.append(copy)

    def spread(self, k):
        to = (self.me + k) % self.count
        return remote(
            self.cut.at[to], self.out.at[self.rep, self.me], self.sems.at[0, k], self.sems.at[1, k], (self.rep, to)
        )

    def arrived(self, k):
        frm = (self.me + self.count - k) % self.count
        return remote(
            self.cut.at[frm], self.out.at[self.rep, frm], self.sems.at[0, k], self.sems.at[1, k], (self.rep, frm)
        )

    def forward(self, k, hop):
        frm = (self.me + self.count - k) % self.count
        rep = self.across if hop == 2 else self.rep
        block = self.out.at[rep, frm] if k or hop == 2 else self.cut.at[self.me]
        to = self.across if hop == 0 else self.beside
        return remote(
            block,
            self.out.at[rep, frm],
            self.sems.at[2 + 2 * hop, k],
            self.sems.at[3 + 2 * hop, k],
            (to, self.me),
        )

    def pass_on(self, k):
        if k:
            self.arrived(k).wait_recv()
        self.go(self.forward(k, 0))
        self.go(self.forward(k, 1))

    def pass_beside(self, k):
        self.forward(k, 0).wait_recv()
        self.go(self.forward(k, 2))

    def begin(self):
        for k in range(1, self.count):
            self.go(self.spread(k))
        self.pass_on(0)

    def steps(self):
        work = [functools.partial(self.pass_on, k) for k in range(1, self.count)]
        return work + [functools.partial(self.pass_beside, k) for k in range(self.count)]

    def finish(self):
        for k in range(self.count):
            self.forward(k, 1).wait_recv()
            self.forward(k, 2).wait_recv()
        for copy in self.started:
            copy.wait_send()


def rep_partners(rep):
    return (rep + 2) % 4, rep + 1 - 2 * (rep % 2)


def everyone(rep, me, reps, count):
    here = rep * count + me
    total = reps * count
    return [
        (((here + k) % total) // count, ((here + k) % total) % count) for k in range(1, total)
    ]


def opening_kernel(
    reps, count, tok_ref, gain_ref, in_hbm, dn_hbm, ou_hbm, gate_hbm, up_hbm,
    h1_ref, gains_ref, w_in, w_gate, w_dn, w_ou, cut_up,
    in_f, dn_f, ou_f, gate_f, up_f, in_ref, dn_ref, ou_ref, gate_ref, tok_all, gain_all,
    t_send, t_recv, g_send, g_recv, i_sems, u_sems, o_send, o_recv, n_send, n_recv, loc, loads
):
    f32 = jnp.float32
    ring = Ring(count)
    rep, me = ring.rep, ring.me
    across, beside = rep_partners(rep)
    others = everyone(rep, me, reps, count)
    mine = rep * count + me
    d_rows = in_ref.shape[1]
    rows = tok_ref.shape[0]
    fetched = [
        pltpu.make_async_copy(src, dst, loads.at[index])
        for index, (src, dst) in enumerate(
            ((in_hbm, in_f), (dn_hbm, dn_f), (ou_hbm, ou_f), (gate_hbm, gate_f), (up_hbm, up_f))
        )
    ]
    for copy in fetched:
        copy.start()
    meet(others)
    started = []

    def go(copy):
        copy.start()
        started.append(copy)

    for k, device in enumerate(others):
        go(remote(gain_ref, gain_all.at[mine], g_send.at[k], g_recv.at[k], device))
    gain_all[mine] = gain_ref[...]
    ins = Fetch(ring, in_ref, w_in, i_sems)
    gates = Fetch(ring, gate_ref, w_gate, u_sems)
    gather = Gather(ring, tok_ref, tok_all, t_send, t_recv)
    fetched[0].wait()
    cut_heads(count, in_f, in_ref)
    ins.begin()
    fetched[1].wait()
    dn_ref[...] = dn_f[...].astype(dn_ref.dtype)
    dn_x = remote(dn_ref, w_dn.at[rep], n_send.at[0], n_recv.at[0], (across, me))
    dn_c = remote(dn_ref, w_dn.at[rep], n_send.at[1], n_recv.at[1], (beside, me))
    dn_d = remote(w_dn.at[across], w_dn.at[across], n_send.at[2], n_recv.at[2], (beside, me))
    go(dn_x)
    go(dn_c)
    fetched[2].wait()
    for j in range(reps):
        ou_ref[j] = ou_f[j * ou_ref.shape[1] : (j + 1) * ou_ref.shape[1], :].astype(ou_ref.dtype)

    per_head = count * reps // HEADS
    target = mine // per_head
    slot = mine % per_head

    def ou_copy(j):
        return remote(ou_ref.at[j], w_ou.at[j, slot], o_send.at[j], o_recv.at[slot], (j, target))

    def is_self(j):
        return (rep == j) & (me == target)

    for j in range(reps):
        @pl.when(jnp.logical_not(is_self(j)))
        def _():
            ou_copy(j).start()

        @pl.when(is_self(j))
        def _():
            pltpu.make_async_copy(ou_ref.at[j], w_ou.at[j, slot], o_recv.at[slot]).start()

    fetched[3].wait()
    cut_units(reps, count, gate_f, gate_ref)
    gates.begin()
    locals_ = []
    for index, (src, dst) in enumerate(
        ((in_ref.at[me], w_in.at[rep, me]), (gate_ref.at[me], w_gate.at[rep, me]), (dn_ref, w_dn.at[rep]))
    ):
        copy = pltpu.make_async_copy(src, dst, loc.at[index])
        copy.start()
        locals_.append(copy)

    for k in range(len(others)):
        frm = (mine + len(others) - k) % (reps * count)
        remote(gain_ref, gain_all.at[frm], g_send.at[k], g_recv.at[k], others[k]).wait_recv()
    gains_ref[...] = jnp.concatenate([gain_all[device, :, 0:d_rows] for device in range(reps * count)], axis=1)
    gain = 1.0 + gains_ref[0:1, :]

    def norm(value):
        value = value.astype(f32)
        return (value * lax.rsqrt(jnp.mean(value * value, axis=-1, keepdims=True) + 1e-06) * gain).astype(h1_ref.dtype)

    def norm_block(shard):
        for unit in range(UNITS):
            span = pl.ds(unit * (rows // UNITS), rows // UNITS)
            h1_ref[shard, span, :] = norm(tok_all[shard, span, :])

    for unit in range(UNITS):
        span = pl.ds(unit * (rows // UNITS), rows // UNITS)
        h1_ref[me, span, :] = norm(tok_ref[span, :])

    hops = gather.steps()

    def take_hop(hop):
        for _ in range(len(ring.units(0, hop))):
            hops.pop(0)()
        for way in (0, 1) if hop < ring.half else (0,):
            norm_block(ring.away(1 - way, hop))

    for k in range(1, count):
        ins.pass_on(k)
    fetched[4].wait()
    cut_units(reps, count, up_f, cut_up)
    gather.begin()
    for k in range(1, count):
        gates.pass_on(k)
    for i in range(per_head):
        remote(
            ou_ref.at[0], w_ou.at[rep, i], o_send.at[0], o_recv.at[i], (across, me)
        ).wait_recv()
    ou_x = remote(w_ou.at[rep], w_ou.at[rep], n_send.at[3], n_recv.at[3], (across, me))
    ou_c = remote(w_ou.at[rep], w_ou.at[rep], n_send.at[4], n_recv.at[4], (beside, me))
    ou_d = remote(w_ou.at[across], w_ou.at[across], n_send.at[5], n_recv.at[5], (beside, me))
    go(ou_x)
    go(ou_c)
    take_hop(1)
    dn_x.wait_recv()
    go(dn_d)
    take_hop(2)
    for k in range(count):
        ins.pass_beside(k)
    for hop in range(3, ring.half + 1):
        take_hop(hop)
    ou_x.wait_recv()
    go(ou_d)
    for k in range(count):
        gates.pass_beside(k)
    ins.finish()
    gates.finish()
    for copy in (dn_c, dn_d, ou_c, ou_d):
        copy.wait_recv()
    for copy in started:
        copy.wait_send()
    gather.finish()
    for j in range(reps):
        @pl.when(jnp.logical_not(is_self(j)))
        def _():
            ou_copy(j).wait_send()
    for copy in locals_:
        copy.wait()


def opening(reps, count, tokens, gain_tile, inproj, outproj, ffn_gate, ffn_up, ffn_down, collective_id):
    dma = pltpu.SemaphoreType.DMA
    per_head = count * reps // HEADS
    total = reps * count
    low, f32 = jnp.bfloat16, jnp.float32
    shape = jax.ShapeDtypeStruct
    hops = dma((2, count // 2, UNITS))
    width = tokens.shape[1]
    gathered = (count,) + tokens.shape
    d_rows = inproj.shape[0]
    heads = (count, d_rows, 3 * HEAD_DIM)
    units = (count, d_rows, ffn_gate.shape[1] // count)
    outs = (reps, outproj.shape[0] // reps, width)
    vm, hb = pl.BlockSpec(memory_space=VM), pl.BlockSpec(memory_space=HB)
    return pl.pallas_call(
        functools.partial(opening_kernel, reps, count),
        out_shape=[
            shape(gathered, low),
            shape((8, width), f32),
            shape((reps,) + heads, low),
            shape((reps,) + units, low),
            shape((reps,) + ffn_down.shape, low),
            shape((reps, per_head) + outs[1:], low),
            shape(units, low),
        ],
        in_specs=[vm] * 2 + [hb] * 5,
        out_specs=[vm] * 2 + [hb] * 4 + [vm],
        scratch_shapes=[
            pltpu.VMEM(inproj.shape, f32),
            pltpu.VMEM(ffn_down.shape, f32),
            pltpu.VMEM(outproj.shape, f32),
            pltpu.VMEM(ffn_gate.shape, f32),
            pltpu.VMEM(ffn_up.shape, f32),
            pltpu.VMEM(heads, low),
            pltpu.VMEM(ffn_down.shape, low),
            pltpu.VMEM(outs, low),
            pltpu.VMEM(units, low),
            pltpu.VMEM(gathered, low),
            pltpu.VMEM((total,) + gain_tile.shape, f32),
            hops,
            hops,
            dma((total - 1,)),
            dma((total - 1,)),
            dma((8, count)),
            dma((8, count)),
            dma((reps,)),
            dma((per_head,)),
            dma((6,)),
            dma((6,)),
            dma((3,)),
            dma((5,)),
        ],
        compiler_params=pltpu.CompilerParams(
            collective_id=collective_id, has_side_effects=True, vmem_limit_bytes=VMEM_LIMIT
        ),
        name="opening",
    )(tokens, gain_tile, inproj, ffn_down, outproj, ffn_gate, ffn_up)


def cut_units(reps, count, ref, cut):
    block = ref.shape[1] // (reps * count)
    for shard in range(count):
        pieces = [ref[:, (r * count + shard) * block : (r * count + shard + 1) * block] for r in range(reps)]
        cut[shard] = jnp.concatenate(pieces, axis=1).astype(cut.dtype)


def cut_heads(count, ref, cut):
    group = HEADS // KV_HEADS
    for shard in range(count):
        heads = shard, HEADS + shard // group, HEADS + KV_HEADS + shard // group
        for index, head in enumerate(heads):
            cut[shard, :, index * HEAD_DIM : (index + 1) * HEAD_DIM] = ref[
                :, head * HEAD_DIM : (head + 1) * HEAD_DIM
            ].astype(cut.dtype)


class RepSum:
    def __init__(self, part, from_core, from_across, sems, rep, me):
        self.part, self.from_core, self.from_across = part, from_core, from_across
        self.c_send, self.c_recv, self.x_send, self.x_recv = sems
        self.across, self.beside = rep_partners(rep)
        self.rep, self.me = rep, me
        self.core = rep % 2
        self.chip = rep // 2

    def core_copy(self, side, piece):
        chip = 1 - self.chip if side == 0 else self.chip
        return remote(
            self.part(chip * 2 + 1 - self.core, piece),
            self.from_core.at[side, piece],
            self.c_send.at[side, piece],
            self.c_recv.at[side, piece],
            (self.beside, self.me),
        )

    def cross_copy(self, piece):
        return remote(
            self.from_core.at[0, piece],
            self.from_across.at[piece],
            self.x_send.at[piece],
            self.x_recv.at[piece],
            (self.across, self.me),
        )

    def begin(self, pieces):
        for side in (0, 1):
            for piece in pieces:
                self.core_copy(side, piece).start()

    def cross(self, piece):
        f32 = jnp.float32
        self.core_copy(0, piece).wait_recv()
        mine = self.part((1 - self.chip) * 2 + self.core, piece)[...].astype(f32)
        self.from_core[0, piece] = (mine + self.from_core[0, piece].astype(f32)).astype(jnp.bfloat16)
        self.cross_copy(piece).start()

    def total(self, piece):
        f32 = jnp.float32
        self.core_copy(1, piece).wait_recv()
        mine = self.part(self.rep, piece)[...].astype(f32) + self.from_core[1, piece].astype(f32)
        self.cross_copy(piece).wait_recv()
        return mine + self.from_across[piece].astype(f32)

    def finish(self, pieces):
        for piece in pieces:
            self.core_copy(0, piece).wait_send()
            self.core_copy(1, piece).wait_send()
            self.cross_copy(piece).wait_send()


class Spread:
    def __init__(self, blocks, out, send, recv, rep, me, count):
        self.blocks, self.out, self.send, self.recv = blocks, out, send, recv
        self.rep, self.me, self.count = rep, me, count

    def copy(self, k):
        to = (self.me + k) % self.count
        return remote(
            self.blocks.at[to], self.out.at[self.me], self.send.at[k], self.recv.at[k], (self.rep, to)
        )

    def arrived(self, k):
        frm = (self.me + self.count - k) % self.count
        return remote(
            self.blocks.at[frm], self.out.at[frm], self.send.at[k], self.recv.at[k], (self.rep, frm)
        )

    def finish(self):
        for k in range(1, self.count):
            self.arrived(k).wait_recv()
        for k in range(1, self.count):
            self.copy(k).wait_send()


def near_devices(ring):
    across, beside = rep_partners(ring.rep)
    return [(ring.rep, (ring.me + k) % ring.count) for k in range(1, ring.count)] + [
        (across, ring.me),
        (beside, ring.me),
    ]


class Gather:
    def __init__(self, ring, block, out, send, recv):
        self.ring, self.block, self.out, self.send, self.recv = ring, block, out, send, recv
        self.rows = block.shape[0] // UNITS
        self.started = []

    def copy(self, way, hop, unit):
        ring = self.ring
        origin = ring.away(1 - way, hop - 1) if hop > 1 else ring.me
        span = pl.ds(unit * self.rows, self.rows)
        return remote(
            self.block.at[span] if hop == 1 else self.out.at[origin, span],
            self.out.at[origin, span],
            self.send.at[way, hop - 1, unit],
            self.recv.at[way, hop - 1, unit],
            ring.next[way],
        )

    def go(self, copy):
        copy.start()
        self.started.append(copy)

    def begin(self):
        for index in range(UNITS):
            for way in (0, 1):
                self.go(self.copy(way, 1, self.ring.units(way, 1)[index]))

    def steps(self):
        ring = self.ring

        def step(hop, index):
            for way in (0, 1):
                unit = ring.units(way, hop)[index]
                self.copy(way, hop, unit).wait_recv()
                if hop < ring.half and unit in ring.units(way, hop + 1):
                    self.go(self.copy(way, hop + 1, unit))

        return [
            functools.partial(step, hop, index)
            for hop in range(1, ring.half + 1)
            for index in range(len(ring.units(0, hop)))
        ]

    def finish(self):
        for copy in self.started:
            copy.wait_send()


def tn(left, right):
    return lax.dot_general(left, right, (((0,), (0,)), ((), ())), preferred_element_type=jnp.float32)


DN_PIECES = 3


def ffn_grads_kernel(
    reps, count, dattn_ref, wo_ref, q_ref, k_ref, v_ref, cos_ref, sin_ref, h3_hbm, dgu_hbm, part_hbm, probs_hbm, damp_hbm,
    all_ref, sum_ref, down_ref, dproj,
    h3_ref, dgu_ref, g_part, g_core, g_from, d_part, d_core, d_from, probs_ref, damp_ref, d_key, d_value,
    t_send, t_recv, gc_s, gc_r, gx_s, gx_r, dc_s, dc_r, dx_s, dx_r, s_send, s_recv, loc, loads, square
):
    f32, bf16 = jnp.float32, jnp.bfloat16
    ring = Ring(count)
    rep, me = ring.rep, ring.me
    d_rows, columns = sum_ref.shape[1:]
    part, width = d_part.shape
    block = part // reps
    seq_len = q_ref.shape[0]
    blocks = 4
    tall = seq_len // blocks
    half = HEAD_DIM // 2
    fetched = [
        pltpu.make_async_copy(src, dst, loads.at[index])
        for index, (src, dst) in enumerate(((part_hbm, d_part), (h3_hbm, h3_ref), (dgu_hbm, dgu_ref)))
    ]
    for copy in fetched:
        copy.start()

    def squares(i):
        span = pl.ds(i * tall, tall)
        return [
            pltpu.make_async_copy(probs_hbm.at[span], probs_ref, square.at[0]),
            pltpu.make_async_copy(damp_hbm.at[span], damp_ref, square.at[1]),
        ]

    for copy in squares(0):
        copy.start()
    meet(near_devices(ring))
    gather = Gather(ring, dattn_ref, all_ref, t_send, t_recv)
    gather.begin()
    own = pltpu.make_async_copy(dattn_ref, all_ref.at[me], loc)
    own.start()

    def d_at(owner, piece):
        rows = block // DN_PIECES
        return d_part.at[pl.ds(owner * block + piece * rows, rows)]

    down = RepSum(d_at, d_core, d_from, (dc_s, dc_r, dx_s, dx_r), rep, me)
    gate_up = RepSum(
        lambda owner, piece: g_part.at[owner, piece], g_core, g_from, (gc_s, gc_r, gx_s, gx_r), rep, me
    )
    spread = Spread(g_from, sum_ref, s_send, s_recv, rep, me, count)
    d_pieces = list(range(DN_PIECES))
    g_pieces = [(me + k) % count for k in range(1, count)] + [me]

    def make_gate_up(owner):
        rows = count * d_rows
        step = columns // 3

        def body(n, carry):
            cols = pl.ds(pl.multiple_of(n * step, 128), step)
            made = tn(h3_ref[:, owner * rows : (owner + 1) * rows], dgu_ref[:, cols])
            g_part[owner, :, :, cols] = made.reshape(count, d_rows, step).astype(bf16)
            return carry

        lax.fori_loop(0, 3, body, 0)

    def nt(left, right):
        return lax.dot_general(left, right, (((1,), (1,)), ((), ())), preferred_element_type=f32)

    def unturned(flat, at):
        cosine, sine = cos_ref[at, :], sin_ref[at, :]
        low, high = flat[:, :half], flat[:, half:]
        return jnp.concatenate([low * cosine + high * sine, high * cosine - low * sine], axis=1)

    d_key[...] = jnp.zeros_like(d_key)
    d_value[...] = jnp.zeros_like(d_value)

    def attend(i):
        at = pl.ds(i * tall, tall)
        per = count // blocks
        d_out = all_ref[i * per : (i + 1) * per].reshape(tall, width)
        d_att = nt(d_out, wo_ref[...]).astype(bf16)
        d_probs = nt(d_att, v_ref[...])
        for copy in squares(i):
            copy.wait()
        probs = probs_ref[...]
        inner = jnp.sum(probs.astype(f32) * d_probs, axis=-1, keepdims=True)
        d_scores = (damp_ref[...].astype(f32) * (d_probs - inner)).astype(bf16)
        d_query = jnp.dot(d_scores, k_ref[...], preferred_element_type=f32)
        dproj[at, :HEAD_DIM] = (unturned(d_query, at) * HEAD_DIM ** (-0.5)).astype(bf16)
        d_key[...] += tn(d_scores, q_ref[at, :])
        d_value[...] += tn(probs, d_att)
        if i < blocks - 1:
            for copy in squares(i + 1):
                copy.start()

    def project():
        for i in range(blocks):
            at = pl.ds(i * tall, tall)
            dproj[at, HEAD_DIM : 2 * HEAD_DIM] = unturned(d_key[at, :], at).astype(bf16)
            dproj[at, 2 * HEAD_DIM :] = d_value[at, :].astype(bf16)

    def finish_gate_up(k):
        piece = g_pieces[k]
        total = gate_up.total(piece).astype(bf16)
        if k < count - 1:
            g_from[piece] = total
            spread.copy(k + 1).start()
        else:
            sum_ref[me] = total

    def finish_down(piece):
        rows = block // DN_PIECES
        down_ref[pl.ds(piece * rows, rows), :] = down.total(piece)

    fetched[0].wait()
    down.begin(d_pieces)
    for copy in fetched[1:]:
        copy.wait()
    work = [lambda: [down.cross(piece) for piece in d_pieces]]
    work += [functools.partial(make_gate_up, owner) for owner in range(reps)]
    work += [lambda: gate_up.begin(g_pieces)]

    def cross_two(k):
        for piece in g_pieces[k : k + 2]:
            gate_up.cross(piece)

    work += [functools.partial(cross_two, k) for k in range(0, count, 2)]
    for step in gather.steps():
        step()
        if work:
            work.pop(0)()
    for piece in work:
        piece()
    own.wait()
    after = [functools.partial(finish_gate_up, k) for k in range(count)]
    per = max(1, count // blocks)
    for i in range(blocks):
        attend(i)
        for _ in range(min(per, len(after) - 2)):
            after.pop(0)()
    project()
    for piece in d_pieces:
        finish_down(piece)
    for piece in after:
        piece()
    spread.finish()
    down.finish(d_pieces)
    gate_up.finish(g_pieces)
    gather.finish()


def ffn_grads(
    reps, count, d_attn, w_out, queries, keys, values, cosine, sine, h3, d_gu, part_down, probs, damp, d_rows, collective_id
):
    dma = pltpu.SemaphoreType.DMA
    low, f32 = jnp.bfloat16, jnp.float32
    shape = jax.ShapeDtypeStruct
    width = d_attn.shape[1]
    columns = d_gu.shape[1]
    part = part_down.shape[0]
    seq_len = h3.shape[0]
    block = part // reps
    blocks = (count, d_rows, columns)
    lots = (DN_PIECES, block // DN_PIECES, width)
    hops = dma((2, count // 2, UNITS))
    vm, hb = pl.BlockSpec(memory_space=VM), pl.BlockSpec(memory_space=HB)
    return pl.pallas_call(
        functools.partial(ffn_grads_kernel, reps, count),
        out_shape=[
            shape((count,) + d_attn.shape, low),
            shape(blocks, low),
            shape((block, width), f32),
            shape((seq_len, 3 * HEAD_DIM), low),
        ],
        in_specs=[vm] * 7 + [hb] * 5,
        out_specs=[vm] * 4,
        scratch_shapes=[
            pltpu.VMEM(h3.shape, low),
            pltpu.VMEM(d_gu.shape, low),
            pltpu.VMEM((reps,) + blocks, low),
            pltpu.VMEM((2,) + blocks, low),
            pltpu.VMEM(blocks, low),
            pltpu.VMEM((part, width), low),
            pltpu.VMEM((2,) + lots, low),
            pltpu.VMEM(lots, low),
            pltpu.VMEM((seq_len // 4, seq_len), low),
            pltpu.VMEM((seq_len // 4, seq_len), low),
            pltpu.VMEM((seq_len, HEAD_DIM), f32),
            pltpu.VMEM((seq_len, HEAD_DIM), f32),
            hops,
            hops,
            dma((2, count)),
            dma((2, count)),
            dma((count,)),
            dma((count,)),
            dma((2, DN_PIECES)),
            dma((2, DN_PIECES)),
            dma((DN_PIECES,)),
            dma((DN_PIECES,)),
            dma((count,)),
            dma((count,)),
            dma,
            dma((3,)),
            dma((2,)),
        ],
        compiler_params=pltpu.CompilerParams(
            collective_id=collective_id, has_side_effects=True, vmem_limit_bytes=VMEM_LIMIT
        ),
        name="ffn_grads",
    )(d_attn, w_out, queries, keys, values, cosine, sine, h3, d_gu, part_down, probs, damp)


def closing_kernel(
    reps, count, dproj, in_ref, att_ref, h1_hbm, dattn_hbm, tokens_ref, dmid_ref, gains_ref, gg_ref,
    grad_ref, sum_ref, out_ref, gain_ref,
    h1_ref, dattn_ref, x_part, i_part, o_part, first, landed, total_ref, tiles, i_core, i_from, o_core, o_from,
    r_send, r_recv, ic_s, ic_r, ix_s, ix_r, oc_s, oc_r, ox_s, ox_r, s_send, s_recv, p_send, p_recv,
    g_send, g_recv, loads
):
    f32, bf16 = jnp.float32, jnp.bfloat16
    ring = Ring(count)
    rep, me = ring.rep, ring.me
    here = rep * count + me
    others = everyone(rep, me, reps, count)
    full = o_part.shape[1]
    d_rows = sum_ref.shape[1]
    seq_len, width = dattn_ref.shape
    rows = grad_ref.shape[0]
    fetched = [
        pltpu.make_async_copy(h1_hbm, h1_ref, loads.at[0]),
        pltpu.make_async_copy(dattn_hbm, dattn_ref, loads.at[1]),
    ]
    for copy in fetched:
        copy.start()
    meet(others)
    tall = seq_len // 4

    def project(i, carry):
        at = pl.ds(pl.multiple_of(i * tall, 16), tall)
        x_part[at, :] = lax.dot_general(
            dproj[at, :], in_ref[...], (((1,), (1,)), ((), ())), preferred_element_type=f32
        ).astype(bf16)
        return carry

    lax.fori_loop(0, 4, project, 0)

    def make_out():
        fetched[1].wait()
        per = width // 3

        def body(n, carry):
            cols = pl.ds(pl.multiple_of(n * per, 128), per)
            made = tn(att_ref[...], dattn_ref[:, cols]).reshape(full, reps, HEAD_DIM // full // reps, per)
            for owner in range(reps):
                o_part[owner, :, :, cols] = made[:, owner].astype(bf16)
            return carry

        lax.fori_loop(0, 3, body, 0)

    def make_in(owner):
        if owner == 0:
            fetched[0].wait()
        deep = count * d_rows
        made = tn(h1_ref[:, owner * deep : (owner + 1) * deep], dproj[...])
        i_part[owner] = made.reshape(count, d_rows, 3 * HEAD_DIM).astype(bf16)

    o_pieces = list(range(full))
    i_pieces = [(me + k) % count for k in range(1, count)] + [me]
    ins = RepSum(lambda owner, piece: i_part.at[owner, piece], i_core, i_from, (ic_s, ic_r, ix_s, ix_r), rep, me)
    outs = RepSum(lambda owner, piece: o_part.at[owner, piece], o_core, o_from, (oc_s, oc_r, ox_s, ox_r), rep, me)
    spread = Spread(i_from, sum_ref, s_send, s_recv, rep, me, count)

    def o_owner(piece):
        where = me * full + piece
        return where // count, where % count

    def o_copy(piece):
        return remote(o_from.at[piece], out_ref.at[rep], p_send.at[piece], p_recv.at[rep], o_owner(piece))

    def o_self(piece):
        return me * full + piece == here

    def o_finish(piece):
        total = outs.total(piece).astype(bf16)
        o_from[piece] = total

        @pl.when(jnp.logical_not(o_self(piece)))
        def _():
            o_copy(piece).start()

        @pl.when(o_self(piece))
        def _():
            pltpu.make_async_copy(o_from.at[piece], out_ref.at[rep], p_recv.at[rep]).start()

    def i_finish(k):
        piece = i_pieces[k]
        total = ins.total(piece).astype(bf16)
        if k < count - 1:
            i_from[piece] = total
            spread.copy(k + 1).start()
        else:
            sum_ref[me] = total

    work = [functools.partial(make_in, owner) for owner in range(reps)]
    work += [lambda: ins.begin(i_pieces), make_out, lambda: outs.begin(o_pieces)]
    work += [functools.partial(ins.cross, piece) for piece in i_pieces]
    work += [functools.partial(outs.cross, piece) for piece in o_pieces]
    work += [functools.partial(i_finish, k) for k in range(count)]
    work += [functools.partial(o_finish, piece) for piece in o_pieces]

    terms = []
    gain = 1.0 + gains_ref[0:1, :]

    def pause():
        for _ in range(min(2, len(work))):
            work.pop(0)()

    def take(shard, span):
        return x_part[pl.ds(pl.multiple_of(shard * rows + span.start, 16), span.size), :]

    def finish(span, total):
        value = tokens_ref[span, :].astype(f32)
        scale = lax.rsqrt(jnp.mean(value * value, axis=-1, keepdims=True) + 1e-06)
        normed = value * scale
        weighted = total * gain
        inner = jnp.mean(weighted * normed, axis=-1, keepdims=True)
        grad_ref[span, :] = dmid_ref[span, :] + scale * (weighted - normed * inner)
        terms.append(jnp.sum(total * normed, axis=0, keepdims=True))

    started = reduce_on_ring(ring, rows, take, first, landed, r_send, r_recv, finish, pause)
    total_ref[...] = gg_ref[...]
    total_ref[0:1, :] = functools.reduce(jnp.add, terms)
    every = total_ref[...]
    for owner in range(reps * count):
        tiles[owner, :, 0:d_rows] = every[:, owner * d_rows : (owner + 1) * d_rows]
        tiles[owner, :, d_rows:] = jnp.zeros((8, 128 - d_rows), f32)
    for k, device in enumerate(others):
        to = (here + k + 1) % (reps * count)
        remote(tiles.at[to], gain_ref.at[here], g_send.at[k], g_recv.at[k], device).start()
    gain_ref[here] = tiles[here]
    for piece in work:
        piece()
    for k in range(len(others)):
        frm = (here + len(others) - k) % (reps * count)
        remote(tiles.at[frm], gain_ref.at[frm], g_send.at[k], g_recv.at[k], others[k]).wait_recv()
    for j in range(reps):
        remote(
            o_from.at[0], out_ref.at[j], p_send.at[0], p_recv.at[j], (rep, (me + 1) % count)
        ).wait_recv()
    for piece in o_pieces:
        @pl.when(jnp.logical_not(o_self(piece)))
        def _():
            o_copy(piece).wait_send()
    spread.finish()
    ins.finish(i_pieces)
    outs.finish(o_pieces)
    for k, device in enumerate(others):
        to = (here + k + 1) % (reps * count)
        remote(tiles.at[to], gain_ref.at[here], g_send.at[k], g_recv.at[k], device).wait_send()
    for copy in started:
        copy.wait_send()


def closing(
    reps, count, d_projected, w_in, attended, normed, d_attn, tokens, d_middle, gain_rows, gain_terms, piece, collective_id
):
    dma = pltpu.SemaphoreType.DMA
    low, f32 = jnp.bfloat16, jnp.float32
    shape = jax.ShapeDtypeStruct
    rows, width = tokens.shape
    seq_len = normed.shape[0]
    total = reps * count
    half = count // 2
    d_rows = width // total
    full = HEAD_DIM // (reps * piece)
    i_block = (count, d_rows, 3 * HEAD_DIM)
    o_block = (full, piece, width)
    hops = dma((2, half, UNITS))
    vm, hb = pl.BlockSpec(memory_space=VM), pl.BlockSpec(memory_space=HB)
    return pl.pallas_call(
        functools.partial(closing_kernel, reps, count),
        out_shape=[
            shape((rows, width), f32),
            shape(i_block, low),
            shape((reps, piece, width), low),
            shape((total, 8, 128), f32),
        ],
        in_specs=[vm] * 3 + [hb] * 2 + [vm] * 4,
        out_specs=[vm] * 4,
        scratch_shapes=[
            pltpu.VMEM((seq_len, width), low),
            pltpu.VMEM((seq_len, width), low),
            pltpu.VMEM((seq_len, width), low),
            pltpu.VMEM((reps,) + i_block, low),
            pltpu.VMEM((reps,) + o_block, low),
            pltpu.VMEM((rows, width), low),
            pltpu.VMEM((2, half, rows, width), low),
            pltpu.VMEM((8, width), f32),
            pltpu.VMEM((total, 8, 128), f32),
            pltpu.VMEM((2,) + i_block, low),
            pltpu.VMEM(i_block, low),
            pltpu.VMEM((2,) + o_block, low),
            pltpu.VMEM(o_block, low),
            hops,
            hops,
            dma((2, count)),
            dma((2, count)),
            dma((count,)),
            dma((count,)),
            dma((2, full)),
            dma((2, full)),
            dma((full,)),
            dma((full,)),
            dma((count,)),
            dma((count,)),
            dma((full,)),
            dma((reps,)),
            dma((total - 1,)),
            dma((total - 1,)),
            dma((2,)),
        ],
        compiler_params=pltpu.CompilerParams(
            collective_id=collective_id, has_side_effects=True, vmem_limit_bytes=VMEM_LIMIT
        ),
        name="closing",
    )(d_projected, w_in, attended, normed, d_attn, tokens, d_middle, gain_rows, gain_terms)


def tiles_of(ref):
    rows, columns = ref.shape
    tall = 72 if rows % 72 == 0 else 64 if rows % 64 == 0 else 8
    wide = 384 if columns % 384 == 0 else 256
    return rows // tall, columns // wide, tall, wide


def tile_at(ref, n):
    _, across, tall, wide = tiles_of(ref)
    down, right = n // across, n % across
    return pl.ds(pl.multiple_of(down * tall, 8), tall), pl.ds(pl.multiple_of(right * wide, 128), wide)


LAMB_ORDER = (1, 4, 2, 3, 0)


def lamb_kernel(reps, count, sum_in, sum_out, sum_gu, gain_tiles, g_master, g_mean, g_square, *refs):
    f32 = jnp.float32
    names = 5
    hbm_in, refs = [refs[3 * i : 3 * i + 3] for i in range(names)], refs[3 * names :]
    grad_dn, refs = refs[0], refs[1:]
    (sums_out, gg_out, gm_out, gs_out, gp_out), refs = refs[:5], refs[5:]
    hbm_out, refs = [refs[4 * i : 4 * i + 4] for i in range(names)], refs[4 * names :]
    masters, means, squares, grads = (refs[names * i : names * (i + 1)] for i in range(4))
    in_sem, out_sem, dn_sem = refs[4 * names :]
    total = reps * count
    group = HEADS // KV_HEADS

    def fetch(i, j):
        return pltpu.make_async_copy(hbm_in[i][j], (masters, means, squares)[j][i], in_sem.at[i, j])

    fetch_dn = pltpu.make_async_copy(grad_dn, grads[4], dn_sem)
    fetch_dn.start()

    def fetch_all(order):
        for i in order:
            for j in range(3):
                fetch(i, j).start()

    fetch_all(LAMB_ORDER[:2])

    def store(i, j):
        return pltpu.make_async_copy((grads, means, squares, masters)[j][i], hbm_out[i][j], out_sem.at[i, j])

    def join(index, ref):
        block = ref.shape[1] // total
        part = block * reps
        for first in range(0, total, 4):
            pieces = []
            for b in range(first, first + 4):
                start = index * part + (b // count) * block
                pieces.append(sum_gu[b % count, :, start : start + block].astype(f32))
            ref[:, first * block : (first + 4) * block] = jnp.concatenate(pieces, axis=1)

    def make_grad(i):
        if i == 0:
            for head in range(HEADS):
                grads[0][:, head * HEAD_DIM : (head + 1) * HEAD_DIM] = sum_in[head, :, :HEAD_DIM].astype(f32)
            for kind in (1, 2):
                for head in range(KV_HEADS):
                    start = (HEADS + (kind - 1) * KV_HEADS + head) * HEAD_DIM
                    parts = [
                        sum_in[head * group + g, :, kind * HEAD_DIM : (kind + 1) * HEAD_DIM].astype(f32)
                        for g in range(group)
                    ]
                    grads[0][:, start : start + HEAD_DIM] = functools.reduce(jnp.add, parts)
        elif i == 1:
            rows = sum_out.shape[1]
            for j in range(reps):
                grads[1][j * rows : (j + 1) * rows, :] = sum_out[j].astype(f32)
        elif i in (2, 3):
            join(i - 2, grads[i])
        else:
            fetch_dn.wait()

    def lamb(master, grad, mean, square):
        new_mean = 0.5 * (mean + grad)
        new_square = 0.5 * (square + grad * grad)
        root = new_square * lax.rsqrt(new_square)
        return new_mean, new_square, new_mean / (root + 1e-06) + 0.01 * master

    def sweep(i):
        down, across, tall, wide = tiles_of(masters[i])

        def body(n, carry):
            at = tile_at(masters[i], n)
            master = masters[i][at]
            new_mean, new_square, step = lamb(master, grads[i][at], means[i][at], squares[i][at])
            means[i][at] = new_mean
            squares[i][at] = new_square
            masters[i][at] = step

            def fold(value):
                return jnp.sum((value * value).reshape(tall // 8, 8, wide), axis=0)

            return carry[0] + fold(master), carry[1] + fold(step)

        zero = jnp.zeros((8, wide), f32)
        return lax.fori_loop(0, down * across, body, (zero, zero))

    at_row = lax.broadcasted_iota(jnp.int32, (8, 128), 0)
    at_lane = lax.broadcasted_iota(jnp.int32, (8, 128), 1)

    def note(sums, i, pair):
        for row in (0, 1):
            sums = sums + jnp.where((at_row == row) & (at_lane == i), jnp.sum(pair[row]), 0.0)
        return sums

    sums = jnp.zeros((8, 128), f32)
    for place, i in enumerate(LAMB_ORDER):
        make_grad(i)
        for j in range(3):
            fetch(i, j).wait()
        fetch_all(LAMB_ORDER[place + 2 : place + 3])
        pair = sweep(i)
        for j in range(4):
            store(i, j).start()
        sums = note(sums, i, pair)
    gain_total = functools.reduce(jnp.add, [gain_tiles[device] for device in range(total)])
    kinds, d_rows = g_master.shape
    gain_grad = gain_total[:kinds, :d_rows]
    gain_master = g_master[...]
    new_mean, new_square, gain_step = lamb(gain_master, gain_grad, g_mean[...], g_square[...])
    gg_out[...] = gain_grad
    gm_out[...] = new_mean
    gs_out[...] = new_square
    gp_out[...] = gain_step
    sums_out[...] = note(sums, 5, (gain_master * gain_master, gain_step * gain_step))
    for i in LAMB_ORDER:
        for j in range(4):
            store(i, j).wait()


def table_kernel(reps, count, sizes, x_ref, out_ref, near, far, held, n_send, n_recv, f_send, f_recv):
    f32 = jnp.float32
    rep = lax.axis_index("rep")
    me = lax.axis_index("shard")
    meet(
        [(rep, (me + k) % count) for k in range(1, count)] + [((rep + k) % reps, me) for k in range(1, reps)]
    )
    copies = []
    for k in range(1, count):
        copies.append(remote(x_ref, near.at[me], n_send.at[k], n_recv.at[k], (rep, (me + k) % count)))
    for copy in copies:
        copy.start()
    near[me] = x_ref[...]
    for k in range(1, count):
        frm = (me + count - k) % count
        remote(x_ref, near.at[frm], n_send.at[k], n_recv.at[k], (rep, frm)).wait_recv()
    sums = functools.reduce(jnp.add, [near[shard] for shard in range(count)])
    held[...] = sums
    more = []
    for k in range(1, reps):
        more.append(remote(held, far.at[rep], f_send.at[k], f_recv.at[k], ((rep + k) % reps, me)))
    for copy in more:
        copy.start()
    far[rep] = sums
    for k in range(1, reps):
        frm = (rep + reps - k) % reps
        remote(held, far.at[frm], f_send.at[k], f_recv.at[k], (frm, me)).wait_recv()
    totals = functools.reduce(jnp.add, [far[other] for other in range(reps)])
    at_lane = lax.broadcasted_iota(jnp.int32, (8, 128), 1)
    counts = jnp.ones((8, 128), f32)
    for i, size in enumerate(sizes):
        counts = jnp.where(at_lane == i, float(size), counts)
    out_ref[...] = jnp.sqrt(totals / counts + 1e-06)
    for copy in copies + more:
        copy.wait_send()


def fresh_kernel(table_ref, g_master, g_step, *refs):
    names = 5
    hbm_in, refs = [refs[2 * i : 2 * i + 2] for i in range(names)], refs[2 * names :]
    (gp_out, table_out), refs = refs[:2], refs[2:]
    hbm_out, refs = refs[:names], refs[names:]
    masters, steps, refs = refs[:names], refs[names : 2 * names], refs[2 * names :]
    in_sem, out_sem = refs

    def fetch(i, j):
        return pltpu.make_async_copy(hbm_in[i][j], (masters, steps)[j][i], in_sem.at[i, j])

    def store(i):
        return pltpu.make_async_copy(masters[i], hbm_out[i], out_sem.at[i])

    def fetch_all(order):
        for i in order:
            for j in (0, 1):
                fetch(i, j).start()

    fetch_all(LAMB_ORDER[:2])
    table_out[...] = table_ref[0:2, 0 : names + 1]
    rate = 0.3 * table_ref[0:1, :] / table_ref[1:2, :]
    gp_out[...] = g_master[...] - rate[:, 5:6] * g_step[...]
    for place, i in enumerate(LAMB_ORDER):
        down, across, _, _ = tiles_of(masters[i])
        scale = rate[:, i : i + 1]
        for j in (0, 1):
            fetch(i, j).wait()
        fetch_all(LAMB_ORDER[place + 2 : place + 3])

        def body(n, carry):
            at = tile_at(masters[i], n)
            masters[i][at] = masters[i][at] - scale * steps[i][at]
            return carry

        lax.fori_loop(0, down * across, body, 0)
        store(i).start()
    for i in LAMB_ORDER:
        store(i).wait()


def lamb_step(reps, count, sums, grad_down, gains, states, collective_id):
    dma = pltpu.SemaphoreType.DMA
    f32 = jnp.float32
    shape = jax.ShapeDtypeStruct
    shapes = [state[0].shape for state in states]
    like_gains = shape(gains[0].shape, f32)
    tile = shape((8, 128), f32)
    vm, hb = pl.BlockSpec(memory_space=VM), pl.BlockSpec(memory_space=HB)
    local = pltpu.CompilerParams(vmem_limit_bytes=VMEM_LIMIT)
    outs = pl.pallas_call(
        functools.partial(lamb_kernel, reps, count),
        out_shape=[tile] + [like_gains] * 4 + [shape(item, f32) for item in shapes for _ in range(4)],
        in_specs=[vm] * 7 + [hb] * 16,
        out_specs=[vm] * 5 + [hb] * 20,
        scratch_shapes=[pltpu.VMEM(item, f32) for _ in range(4) for item in shapes] + [dma((5, 3)), dma((5, 4)), dma],
        compiler_params=local,
        name="lamb_moments",
    )(*sums, *gains, *[item for state in states for item in state], grad_down)
    sums, gain_parts, parts = outs[0], outs[1:5], [outs[5 + 4 * i : 9 + 4 * i] for i in range(5)]
    sizes = [item[0] * item[1] * reps * count for item in shapes + [like_gains.shape]]
    table = pl.pallas_call(
        functools.partial(table_kernel, reps, count, sizes),
        out_shape=tile,
        in_specs=[vm],
        out_specs=vm,
        scratch_shapes=[
            pltpu.VMEM((count, 8, 128), f32),
            pltpu.VMEM((reps, 8, 128), f32),
            pltpu.VMEM((8, 128), f32),
            dma((count,)),
            dma((count,)),
            dma((reps,)),
            dma((reps,)),
        ],
        compiler_params=pltpu.CompilerParams(collective_id=collective_id, has_side_effects=True),
        name="norm_table",
    )(sums)
    fresh = pl.pallas_call(
        fresh_kernel,
        out_shape=[like_gains, shape((2, 6), f32)] + [shape(item, f32) for item in shapes],
        in_specs=[vm] * 3 + [hb] * 10,
        out_specs=[vm] * 2 + [hb] * 5,
        scratch_shapes=[pltpu.VMEM(item, f32) for _ in range(2) for item in shapes] + [dma((5, 2)), dma((5,))],
        compiler_params=local,
        name="lamb_masters",
    )(table, gains[0], gain_parts[3], *[item for i in range(5) for item in (states[i][0], parts[i][3])])
    rest = [[parts[i][j] for i in range(5)] + [gain_parts[j].T] for j in range(3)]
    return fresh[1], rest[0], rest[1], rest[2], list(fresh[2:]) + [fresh[0].T]


def rope_tables(seq_len):
    exponent = -np.arange(HEAD_DIM // 2, dtype=np.float32) * np.float32(2.0) / np.float32(HEAD_DIM)
    freq = np.float32(10000.0) ** exponent
    angle = (np.arange(seq_len, dtype=np.float32)[:, None] * freq[None, :]).astype(np.float64)
    return jnp.asarray(np.cos(angle).astype(np.float32)), jnp.asarray(np.sin(angle).astype(np.float32))


def split_device(
    tokens, cotangent, piece_starts, inproj, outproj, ffn_gate, ffn_up, ffn_down, norm_gains,
    mean_inproj, mean_outproj, mean_gate, mean_up, mean_down, mean_gains,
    square_inproj, square_outproj, square_gate, square_up, square_down, square_gains,
):
    bf16, f32 = jnp.bfloat16, jnp.float32
    reps, count = lax.axis_size("rep"), lax.axis_size("shard")
    rep = lax.axis_index("rep")
    me = lax.axis_index("shard")
    total = reps * count
    rows, width = tokens.shape
    seq_len = rows * count
    group = HEADS // KV_HEADS
    q_width, k_width = HEADS * HEAD_DIM, KV_HEADS * HEAD_DIM
    d_rows = inproj.shape[0]
    ff = ffn_gate.shape[1]
    ff_block = ff // total
    ff_part = ff // count
    o_rows = outproj.shape[0]
    per_head = HEAD_DIM // o_rows
    piece = o_rows // reps

    gain_tile = jnp.pad(norm_gains.T.astype(bf16).astype(f32), ((0, 4), (0, 128 - d_rows)))
    normed_in, gain_rows, got_in, got_gate, got_down, got_out, cut_up = opening(
        reps, count, tokens, gain_tile, inproj, outproj, ffn_gate, ffn_up, ffn_down, 1
    )
    normed_in = normed_in.reshape(seq_len, width)
    w_in = got_in.reshape(width, -1)
    w_gate = got_gate.reshape(width, ff_part)
    w_down = got_down.reshape(ff_part, width)

    position = jnp.arange(seq_len, dtype=jnp.int32)
    cosine, sine = rope_tables(seq_len)
    starts = lax.dynamic_slice_in_dim(piece_starts, rep, 1, 0)[0]
    inside = (position[:, None] >= starts[None, :]) & (position[:, None] < starts[None, :] + PIC)
    tag = jnp.sum(inside.astype(jnp.int32) * (jnp.arange(starts.shape[0], dtype=jnp.int32)[None, :] + 1), axis=1)
    attn_proj, queries, keys, values, attended, probs, damp, w_out, got_up = attention(
        reps, count, normed_in, w_in, got_out, cosine, sine, tag, cut_up, 4
    )
    w_up = got_up.reshape(width, ff_part)

    layer_out, d_middle, d_attn, gain_terms, normed_mid, d_gu, part_down = feed_forward(
        attn_proj, tokens, cotangent, gain_rows, w_gate, w_up, w_down, count, 5
    )
    d_attn, sum_gu, grad_down, d_projected = ffn_grads(
        reps, count, d_attn, w_out, queries, keys, values, cosine, sine, normed_mid, d_gu, part_down, probs, damp, d_rows, 9
    )
    input_grad, sum_in, sum_out, gain_tiles = closing(
        reps, count, d_projected, w_in, attended, normed_in, d_attn.reshape(seq_len, width), tokens, d_middle,
        gain_rows, gain_terms, piece, 12,
    )
    norm_table, gradients, new_means, new_squares, fresh = lamb_step(
        reps,
        count,
        (sum_in, sum_out, sum_gu, gain_tiles),
        grad_down,
        (norm_gains.T, mean_gains.T, square_gains.T),
        (
            (inproj, mean_inproj, square_inproj),
            (outproj, mean_outproj, square_outproj),
            (ffn_gate, mean_gate, square_gate),
            (ffn_up, mean_up, square_up),
            (ffn_down, mean_down, square_down),
        ),
        14,
    )
    return (
        layer_out,
        input_grad,
        *gradients,
        *new_means,
        *new_squares,
        *fresh,
        norm_table,
    )


def fits(mesh, shapes):
    reps, count = mesh.shape["rep"], mesh.shape["shard"]
    total = reps * count
    tokens, piece_starts, outproj, ffn_gate = shapes
    o_rows = outproj[0] // total
    return (
        reps == 4
        and count == HEADS
        and piece_starts[0] == reps
        and tokens[0] % (total * UNITS * 16) == 0
        and HEAD_DIM % o_rows == 0
        and o_rows % (16 * reps) == 0
        and HEAD_DIM // o_rows == total // HEADS
        and ffn_gate[1] % (total * 96) == 0
    )


def solution(mesh):
    split = P(("rep", "shard"), None)

    def step(*args):
        shapes = args[0].shape, args[2].shape, args[4].shape, args[5].shape
        body = split_device if fits(mesh, shapes) else per_device
        return jax.shard_map(
            body,
            mesh=mesh,
            in_specs=(split, split, P()) + (split,) * 18,
            out_specs=(split,) * 26 + (P(),),
            check_vma=False,
        )(*args)

    return step
```

```python
import functools

import jax
import jax.numpy as jnp
from jax import lax
from jax.experimental import pallas as pl
from jax.experimental.pallas import tpu as pltpu
import numpy as np
from jax.sharding import PartitionSpec as P

HEADS = 8
KV_HEADS = 4
HEAD_DIM = 256
PIC = 256


def rms_norm(values_in, gain_col):
    return (
        values_in
        * lax.rsqrt(jnp.mean(values_in * values_in, axis=-1, keepdims=True) + 1e-06)
        * (1.0 + gain_col)
    )


def geglu(gate_lin, up_lin):
    return jax.nn.gelu(gate_lin, approximate=True) * up_lin


def rotate(flat, position, head_count, sign):
    row_count = flat.shape[0]
    width = flat.shape[1] // head_count
    half = width // 2
    vectors = flat.reshape(row_count, head_count, width)
    freq = 10000.0 ** (-(jnp.arange(half, dtype=jnp.float32) * 2.0 / width))
    angle = position.astype(jnp.float32)[:, None] * freq[None, :]
    cosine = jnp.cos(angle)[:, None, :]
    sine = sign * jnp.sin(angle)[:, None, :]
    first = vectors[..., :half]
    second = vectors[..., half:]
    turned = jnp.concatenate(
        [first * cosine - second * sine, second * cosine + first * sine], axis=-1
    )
    return turned.reshape(row_count, head_count * width)


def owned_rows(activation, gradient, rep_index, width):
    piece = lax.dynamic_slice_in_dim(activation, rep_index * width, width, 1)
    return lax.dot_general(
        piece, gradient, (((0,), (0,)), ((), ())), preferred_element_type=jnp.float32
    )


def back_dot(gradient, weight):
    return lax.dot_general(
        gradient, weight, (((1,), (1,)), ((), ())), preferred_element_type=jnp.float32
    )


def describe(rows, piece_starts, seq_offset, seq_len):
    local_seq = rows // seq_len
    position = rows % seq_len
    global_seq = local_seq + seq_offset
    seq_total = piece_starts.shape[0]
    piece_count = piece_starts.shape[1]
    select = (global_seq[:, None] == jnp.arange(seq_total, dtype=jnp.int32)[None, :]).astype(
        jnp.int32
    )
    starts = jnp.sum(select[:, :, None] * piece_starts[None, :, :], axis=1)
    inside = ((position[:, None] >= starts) & (position[:, None] < starts + PIC)).astype(jnp.int32)
    labels = (
        global_seq[:, None] * piece_count + jnp.arange(piece_count, dtype=jnp.int32)[None, :] + 1
    )
    return (local_seq, position, jnp.sum(inside * labels, axis=1))


def visibility(piece_starts, query_rows, key_rows, seq_offset, seq_len):
    seq_q, pos_q, tag_q = describe(query_rows, piece_starts, seq_offset, seq_len)
    seq_k, pos_k, tag_k = describe(key_rows, piece_starts, seq_offset, seq_len)
    causal = pos_k[None, :] <= pos_q[:, None]
    same_piece = (tag_q[:, None] == tag_k[None, :]) & (tag_q[:, None] > 0)
    return (seq_q[:, None] == seq_k[None, :]) & (causal | same_piece)


def lamb_local(master, gradient, first, second):
    newmean = 0.5 * first + 0.5 * gradient
    newsquare = 0.5 * second + 0.5 * gradient * gradient
    step_dir = newmean / (jnp.sqrt(newsquare) + 1e-06) + 0.01 * master
    return (newmean, newsquare, step_dir)


def per_device(
    tokens,
    cotangent,
    piece_starts,
    inproj,
    outproj,
    ffn_gate,
    ffn_up,
    ffn_down,
    norm_gains,
    mean_inproj,
    mean_outproj,
    mean_gate,
    mean_up,
    mean_down,
    mean_gains,
    square_inproj,
    square_outproj,
    square_gate,
    square_up,
    square_down,
    square_gains,
):
    bf16 = jnp.bfloat16
    f32 = jnp.float32
    rep_count = lax.axis_size("rep")
    shard_count = lax.axis_size("shard")
    rep_index = lax.axis_index("rep")
    w_in, w_out, w_gate, w_up, w_down, gain_copy = (
        lax.all_gather(inproj.astype(bf16), ("rep", "shard"), axis=0, tiled=True),
        lax.all_gather(outproj.astype(bf16), ("rep", "shard"), axis=0, tiled=True),
        lax.all_gather(ffn_gate.astype(bf16), ("rep", "shard"), axis=0, tiled=True),
        lax.all_gather(ffn_up.astype(bf16), ("rep", "shard"), axis=0, tiled=True),
        lax.all_gather(ffn_down.astype(bf16), ("rep", "shard"), axis=0, tiled=True),
        lax.all_gather(norm_gains.astype(bf16), ("rep", "shard"), axis=0, tiled=True),
    )
    gains_used = gain_copy.astype(f32)
    residual = tokens.astype(f32)
    row_count = residual.shape[0]
    seq_len = row_count * shard_count
    q_width = HEADS * HEAD_DIM
    k_width = KV_HEADS * HEAD_DIM
    group_size = HEADS // KV_HEADS
    query_scale = HEAD_DIM ** (-0.5)
    local_rows = lax.axis_index("shard") * row_count + jnp.arange(row_count, dtype=jnp.int32)
    position = local_rows % seq_len
    normed_in = rms_norm(residual, gains_used[:, 0]).astype(bf16)
    projected = jnp.dot(normed_in, w_in, preferred_element_type=f32)
    queries = (rotate(projected[:, :q_width], position, HEADS, 1.0) * query_scale).astype(bf16)
    keys = rotate(projected[:, q_width : q_width + k_width], position, KV_HEADS, 1.0).astype(bf16)
    values = projected[:, q_width + k_width :].astype(bf16)
    all_keys, all_values = (
        lax.all_gather(keys, "shard", axis=0, tiled=True),
        lax.all_gather(values, "shard", axis=0, tiled=True),
    )
    key_rows = all_keys.shape[0]
    visible = visibility(
        piece_starts,
        local_rows,
        jnp.arange(key_rows, dtype=jnp.int32),
        rep_index * (key_rows // seq_len),
        seq_len,
    )
    query_heads = queries.reshape(row_count, KV_HEADS, group_size, HEAD_DIM)
    key_heads = all_keys.reshape(key_rows, KV_HEADS, HEAD_DIM)
    value_heads = all_values.reshape(key_rows, KV_HEADS, HEAD_DIM)

    def capped_scores():
        raw_scores = jnp.einsum(
            "tgrd,kgd->grtk", query_heads, key_heads, preferred_element_type=f32
        )
        bent_scores = jnp.tanh(raw_scores / 50.0)
        return (bent_scores, jnp.where(visible, 50.0 * bent_scores, -1e30))

    bent_scores, masked = capped_scores()
    top_score = jnp.max(masked, axis=-1, keepdims=True)
    log_total = top_score + jnp.log(jnp.sum(jnp.exp(masked - top_score), axis=-1, keepdims=True))
    probs_low = jnp.exp(masked - log_total).astype(bf16)
    attended = (
        jnp.einsum("grtk,kgd->tgrd", probs_low, value_heads, preferred_element_type=f32)
        .reshape(row_count, q_width)
        .astype(bf16)
    )
    attn_proj = jnp.dot(attended, w_out, preferred_element_type=f32)
    middle = residual + rms_norm(attn_proj, gains_used[:, 1])
    normed_mid = rms_norm(middle, gains_used[:, 2]).astype(bf16)
    gate_lin = jnp.dot(normed_mid, w_gate, preferred_element_type=f32)
    up_lin = jnp.dot(normed_mid, w_up, preferred_element_type=f32)
    hidden = geglu(gate_lin, up_lin).astype(bf16)
    ffn_proj = jnp.dot(hidden, w_down, preferred_element_type=f32)
    layer_out = (middle + rms_norm(ffn_proj, gains_used[:, 3])).astype(bf16)
    d_out = cotangent.astype(f32)
    _, post_back = jax.vjp(rms_norm, ffn_proj, gains_used[:, 3])
    d_ffn, d_gain3 = post_back(d_out)
    d_ffn_low = d_ffn.astype(bf16)
    hidden_all, d_ffn_all = (
        lax.all_gather(hidden, "rep", axis=0, tiled=True),
        lax.all_gather(d_ffn_low, "rep", axis=0, tiled=True),
    )
    part_down = owned_rows(hidden_all, d_ffn_all, rep_index, hidden.shape[1] // rep_count)
    d_hidden = back_dot(d_ffn_low, w_down)
    _, glu_back = jax.vjp(geglu, gate_lin, up_lin)
    d_gate, d_up = glu_back(d_hidden)
    d_gate_low = d_gate.astype(bf16)
    d_up_low = d_up.astype(bf16)
    gate_up_grad = jnp.concatenate([d_gate_low, d_up_low], axis=1)
    mid_all, gate_up_all = (
        lax.all_gather(normed_mid, "rep", axis=0, tiled=True),
        lax.all_gather(gate_up_grad, "rep", axis=0, tiled=True),
    )
    part_gate_up = owned_rows(mid_all, gate_up_all, rep_index, normed_mid.shape[1] // rep_count)
    d_mid_in = back_dot(d_gate_low, w_gate) + back_dot(d_up_low, w_up)
    _, pre_back = jax.vjp(rms_norm, middle, gains_used[:, 2])
    d_mid_part, d_gain2 = pre_back(d_mid_in)
    d_middle = d_out + d_mid_part
    _, attn_back = jax.vjp(rms_norm, attn_proj, gains_used[:, 1])
    d_attn, d_gain1 = attn_back(d_middle)
    d_attn_low = d_attn.astype(bf16)
    d_attended = back_dot(d_attn_low, w_out).astype(bf16)
    d_heads = d_attended.reshape(row_count, KV_HEADS, group_size, HEAD_DIM)
    bent_again, masked_again = capped_scores()
    attn_probs = jnp.exp(masked_again - log_total)
    probs_again = attn_probs.astype(bf16)
    d_probs = jnp.einsum("tgrd,kgd->grtk", d_heads, value_heads, preferred_element_type=f32)
    d_scores = (
        attn_probs
        * (d_probs - jnp.sum(attn_probs * d_probs, axis=-1, keepdims=True))
        * (1.0 - bent_again * bent_again)
    ).astype(bf16)
    d_queries = jnp.einsum(
        "grtk,kgd->tgrd", d_scores, key_heads, preferred_element_type=f32
    ).reshape(row_count, q_width)
    d_key = jnp.einsum("grtk,tgrd->kgd", d_scores, query_heads, preferred_element_type=f32).reshape(
        row_count * lax.axis_size("shard"), k_width
    )
    d_value = jnp.einsum(
        "grtk,tgrd->kgd", probs_again, d_heads, preferred_element_type=f32
    ).reshape(row_count * lax.axis_size("shard"), k_width)
    d_key_value = lax.psum_scatter(
        jnp.concatenate([d_key, d_value], axis=1), "shard", scatter_dimension=0, tiled=True
    )
    d_projected = jnp.concatenate(
        [
            rotate(d_queries, position, HEADS, -1.0) * query_scale,
            rotate(d_key_value[:, :k_width], position, KV_HEADS, -1.0),
            d_key_value[:, k_width:],
        ],
        axis=1,
    ).astype(bf16)
    d_normed_in = back_dot(d_projected, w_in)
    _, first_back = jax.vjp(rms_norm, residual, gains_used[:, 0])
    d_input_part, d_gain0 = first_back(d_normed_in)
    input_grad = d_middle + d_input_part
    gain_grad = jnp.stack([d_gain0, d_gain1, d_gain2, d_gain3], axis=1)
    attended_all, d_attn_all, normed_all, d_proj_all = (
        lax.all_gather(attended, "rep", axis=0, tiled=True),
        lax.all_gather(d_attn_low, "rep", axis=0, tiled=True),
        lax.all_gather(normed_in, "rep", axis=0, tiled=True),
        lax.all_gather(d_projected, "rep", axis=0, tiled=True),
    )
    part_out = owned_rows(attended_all, d_attn_all, rep_index, attended.shape[1] // rep_count)
    part_in = owned_rows(normed_all, d_proj_all, rep_index, normed_in.shape[1] // rep_count)
    part_gain = lax.psum_scatter(gain_grad, "rep", scatter_dimension=0, tiled=True)
    owned = (
        lax.psum_scatter(part_in, "shard", scatter_dimension=0, tiled=True),
        lax.psum_scatter(part_gain, "shard", scatter_dimension=0, tiled=True),
        lax.psum_scatter(part_out, "shard", scatter_dimension=0, tiled=True),
        lax.psum_scatter(part_gate_up, "shard", scatter_dimension=0, tiled=True),
        lax.psum_scatter(part_down, "shard", scatter_dimension=0, tiled=True),
    )
    grad_inproj, grad_gains, grad_outproj, grad_gate_up, grad_down = owned
    split_at = grad_gate_up.shape[1] // 2
    grad_gate = grad_gate_up[:, :split_at]
    grad_up = grad_gate_up[:, split_at:]
    masters = (inproj, outproj, ffn_gate, ffn_up, ffn_down, norm_gains)
    gradients = (grad_inproj, grad_outproj, grad_gate, grad_up, grad_down, grad_gains)
    firsts = (mean_inproj, mean_outproj, mean_gate, mean_up, mean_down, mean_gains)
    seconds = (square_inproj, square_outproj, square_gate, square_up, square_down, square_gains)
    results = [
        lamb_local(masters[index], gradients[index], firsts[index], seconds[index])
        for index in range(6)
    ]
    weight_sums = jnp.stack([jnp.sum(master * master) for master in masters])
    step_sums = jnp.stack([jnp.sum(item[2] * item[2]) for item in results])
    totals = lax.psum(jnp.stack([weight_sums, step_sums]), ("rep", "shard"))
    counts = jnp.array([float(master.size * rep_count * shard_count) for master in masters], f32)
    norm_table = jnp.sqrt(totals / counts[None, :] + 1e-06)
    fresh = [
        masters[index] - 0.3 * norm_table[0, index] / norm_table[1, index] * results[index][2]
        for index in range(6)
    ]
    return (
        layer_out,
        input_grad,
        grad_inproj,
        grad_outproj,
        grad_gate,
        grad_up,
        grad_down,
        grad_gains,
        results[0][0],
        results[1][0],
        results[2][0],
        results[3][0],
        results[4][0],
        results[5][0],
        results[0][1],
        results[1][1],
        results[2][1],
        results[3][1],
        results[4][1],
        results[5][1],
        fresh[0],
        fresh[1],
        fresh[2],
        fresh[3],
        fresh[4],
        fresh[5],
        norm_table,
    )


MESH = pl.DeviceIdType.MESH
VM = pltpu.VMEM
HB = pl.ANY
UNITS = 4
VMEM_LIMIT = 60 << 20


def ring_places(count):
    inner = 2 if count == 8 else 4
    outer = count // inner

    def place(shard):
        major = shard // inner
        minor = shard % inner
        return minor * outer + major + (minor % 2) * (outer - 1 - 2 * major)

    def shard_at(spot):
        minor = spot // outer
        major = spot % outer
        return (major + (minor % 2) * (outer - 1 - 2 * major)) * inner + minor

    return place, shard_at


def meet(devices):
    barrier = pltpu.get_barrier_semaphore()
    for device in devices:
        pl.semaphore_signal(barrier, inc=1, device_id=device, device_id_type=MESH)
    pl.semaphore_wait(barrier, len(devices))


def remote(src, dst, send_sem, recv_sem, device):
    return pltpu.make_async_remote_copy(
        src_ref=src,
        dst_ref=dst,
        send_sem=send_sem,
        recv_sem=recv_sem,
        device_id=device,
        device_id_type=MESH,
    )


class Ring:
    def __init__(self, count):
        place, shard_at = ring_places(count)
        self.count = count
        self.half = count // 2
        self.rep = lax.axis_index("rep")
        self.me = lax.axis_index("shard")
        self.spot = place(self.me)
        self.shard_at = shard_at
        self.next = [(self.rep, self.at(1)), (self.rep, self.at(count - 1))]

    def at(self, ahead):
        return self.shard_at((self.spot + ahead) % self.count)

    def away(self, way, hops):
        return self.at(hops if way == 0 else self.count - hops)

    def units(self, way, hop):
        order = list(range(UNITS)) if way == 0 else list(range(UNITS))[::-1]
        return order if hop < self.half else order[: UNITS // 2]


def reduce_on_ring(ring, rows, take, first, landed, send, recv, finish, pause):
    f32 = jnp.float32
    hops = ring.half
    started = []

    def part(unit):
        return pl.ds(unit * (rows // UNITS), rows // UNITS)

    def step_copy(way, step, unit):
        return remote(
            landed.at[way, step - 1, part(unit)] if step else first.at[part(unit)],
            landed.at[way, step, part(unit)],
            send.at[way, step, unit],
            recv.at[way, step, unit],
            ring.next[way],
        )

    for step in range(hops):
        order = ring.units(0, hops - step), ring.units(1, hops - step)
        before = [ring.units(way, hops - step + 1) if step else [] for way in (0, 1)]
        for index in range(len(order[0])):
            for way in (0, 1):
                unit = order[way][index]
                block = take(ring.away(way, hops - step), part(unit)).astype(f32)
                if unit in before[way]:
                    step_copy(way, step - 1, unit).wait_recv()
                    block += landed[way, step - 1, part(unit), :].astype(f32)
                if step:
                    landed[way, step - 1, part(unit), :] = block.astype(landed.dtype)
                else:
                    first[part(unit), :] = block.astype(first.dtype)
                copy = step_copy(way, step, unit)
                copy.start()
                started.append(copy)
            if step or index == len(order[0]) - 1:
                pause()
    for unit in range(UNITS):
        total = take(ring.me, part(unit)).astype(f32)
        for way in (0, 1):
            step_copy(way, hops - 1, unit).wait_recv()
            total += landed[way, hops - 1, part(unit), :].astype(f32)
        finish(part(unit), total)
    return started


class Flow:
    def __init__(self, ring, rows, send, recv):
        self.ring, self.rows, self.send, self.recv = ring, rows, send, recv
        self.unit_rows = rows // UNITS
        self.started = []

    def span(self, slot, unit):
        return pl.ds(slot * self.rows + unit * self.unit_rows, self.unit_rows)

    def slot(self, way, hops):
        if hops == 0:
            return 0
        return self.ring.count - 1 if hops == self.ring.half else 2 * hops - 1 + way

    def go(self, copy):
        copy.start()
        self.started.append(copy)

    def finish(self):
        for copy in self.started:
            copy.wait_send()

    def gather_copy(self, buffer, way, hop, unit):
        return remote(
            buffer.at[self.span(self.slot(way, hop - 1), unit)],
            buffer.at[self.span(self.slot(way, hop), unit)],
            self.send.at[way, hop - 1, unit],
            self.recv.at[way, hop - 1, unit],
            self.ring.next[way],
        )

    def gather(self, buffer, group_work):
        ring = self.ring
        for index in range(UNITS):
            for way in (0, 1):
                self.go(self.gather_copy(buffer, way, 1, ring.units(way, 1)[index]))
        queue = list(group_work(0, 1))
        for hop in range(1, ring.half + 1):
            length = len(ring.units(0, hop))
            for index in range(length):
                for way in (0, 1):
                    unit = ring.units(way, hop)[index]
                    self.gather_copy(buffer, way, hop, unit).wait_recv()
                    if hop < ring.half and unit in ring.units(way, hop + 1):
                        self.go(self.gather_copy(buffer, way, hop + 1, unit))
                if queue:
                    queue.pop(0)()
            for piece in queue:
                piece()
            queue = list(group_work(2 * hop - 1, 2) if hop < ring.half else group_work(ring.count - 1, 1))
        for piece in queue:
            piece()
        self.finish()

    def reduce_copy(self, first, landed, way, step, unit):
        span = pl.ds(unit * self.unit_rows, self.unit_rows)
        src = first.at[span] if step == 0 else landed.at[way, step - 1, span]
        return remote(
            src,
            landed.at[way, step, span],
            self.send.at[way, step, unit],
            self.recv.at[way, step, unit],
            self.ring.next[way],
        )

    def reduce(self, first, landed, partial, group_work, finish, extra=()):
        extra = list(extra)
        ring = self.ring
        hops = ring.half
        f32 = jnp.float32
        for piece in group_work(ring.count - 1, 1, 0):
            piece()
        queue = list(group_work(2 * (hops - 1) - 1, 2, 1))
        for step in range(hops):
            order = ring.units(0, hops - step), ring.units(1, hops - step)
            before = [ring.units(way, hops - step + 1) if step else [] for way in (0, 1)]
            for index in range(len(order[0])):
                for way in (0, 1):
                    unit = order[way][index]
                    span = pl.ds(unit * self.unit_rows, self.unit_rows)
                    if step == 0:
                        first[span, :] = partial[0, pl.ds(unit * self.unit_rows, self.unit_rows), :].astype(first.dtype)
                    else:
                        side = 1 - way
                        block = partial[
                            step % 2, pl.ds(side * self.rows + unit * self.unit_rows, self.unit_rows), :
                        ]
                        if unit in before[way]:
                            self.reduce_copy(first, landed, way, step - 1, unit).wait_recv()
                            block = block + landed[way, step - 1, span, :].astype(f32)
                        landed[way, step - 1, span, :] = block.astype(landed.dtype)
                    self.go(self.reduce_copy(first, landed, way, step, unit))
                if queue:
                    queue.pop(0)()
                elif extra:
                    extra.pop(0)()
            for piece in queue:
                piece()
            ahead = hops - step - 2
            queue = []
            if step < hops - 1:
                queue = list(group_work(2 * ahead - 1, 2, step % 2) if ahead > 0 else group_work(0, 1, step % 2))
        for piece in extra:
            piece()
        for unit in range(UNITS):
            span = pl.ds(unit * self.unit_rows, self.unit_rows)
            total = partial[hops % 2, span, :]
            for way in (0, 1):
                self.reduce_copy(first, landed, way, hops - 1, unit).wait_recv()
                total = total + landed[way, hops - 1, span, :].astype(f32)
            finish(unit, total)
        self.finish()


def looped(piece, count):
    def all_of_it():
        def body(j, carry):
            piece(j)
            return carry

        lax.fori_loop(0, count, body, 0)

    return [all_of_it]


def gelu_pair(gate):
    inner = 0.7978845608028654 * (gate + 0.044715 * gate * gate * gate)
    bend = jnp.tanh(inner)
    value = 0.5 * gate * (1.0 + bend)
    slope = 0.5 * (1.0 + bend) + 0.5 * gate * (1.0 - bend * bend) * 0.7978845608028654 * (
        1.0 + 0.134145 * gate * gate
    )
    return value, slope


def ffn_kernel(
    count, attn_ref, tokens_ref, cot_ref, gains_ref, gate_hbm, up_hbm, dn_hbm,
    layer_ref, dmid_ref, dattn_ref, gg_ref, h3_hbm, dgu_hbm, part_hbm,
    gate_ref, up_ref, dn_ref, h3_ref, hid_ref, dffn_ref, dgu_ref,
    lin, partial, first, landed, middle, total_ref, s1, r1, s2, r2, s3, r3, s4, r4, loads, stores,
):
    f32, bf16 = jnp.float32, jnp.bfloat16
    ring = Ring(count)
    rows, width = attn_ref.shape
    part = hid_ref.shape[1]
    tile = part // 3
    wide = width // 3
    fetched = [
        pltpu.make_async_copy(src, dst, loads.at[index])
        for index, (src, dst) in enumerate(((gate_hbm, gate_ref), (up_hbm, up_ref), (dn_hbm, dn_ref)))
    ]
    for copy in fetched:
        copy.start()
    kept = []

    def keep_out(src, dst):
        copy = pltpu.make_async_copy(src, dst, stores.at[len(kept)])
        copy.start()
        kept.append(copy)

    meet(ring.next)

    def gain(index):
        return 1.0 + gains_ref[index : index + 1, :]

    def scale_of(value):
        return lax.rsqrt(jnp.mean(value * value, axis=-1, keepdims=True) + 1e-06)

    half = rows // 2
    halves = [pl.ds(0, half), pl.ds(half, half)]
    for span in halves:
        proj = attn_ref[span, :]
        mid = tokens_ref[span, :].astype(f32) + proj * scale_of(proj) * gain(1)
        middle[span, :] = mid
        h3_ref[span, :] = (mid * scale_of(mid) * gain(2)).astype(bf16)

    def lin_work(slot, blocks):
        at = pl.ds(slot * rows, blocks * rows)

        def piece(j):
            lo = pl.ds(pl.multiple_of(j * tile, 128), tile)
            hi = pl.ds(pl.multiple_of(part + j * tile, 128), tile)
            gate = jnp.dot(h3_ref[at, :], gate_ref[:, lo], preferred_element_type=f32)
            up = jnp.dot(h3_ref[at, :], up_ref[:, lo], preferred_element_type=f32)
            value, slope = gelu_pair(gate)
            hid_ref[at, lo] = (value * up).astype(bf16)
            lin[at, lo] = (up * slope).astype(bf16)
            lin[at, hi] = value.astype(bf16)

        return looped(piece, 3)

    def down_work(slot, blocks, side):
        at = pl.ds(slot * rows, blocks * rows)

        def piece(j):
            cols = pl.ds(pl.multiple_of(j * wide, 128), wide)
            partial[side, pl.ds(0, blocks * rows), cols] = jnp.dot(
                hid_ref[at, :], dn_ref[:, cols], preferred_element_type=f32
            )

        return looped(piece, 3)

    def nt(left, right):
        return lax.dot_general(left, right, (((1,), (1,)), ((), ())), preferred_element_type=f32)

    def back_work(slot, blocks):
        at = pl.ds(slot * rows, blocks * rows)

        def piece(j):
            lo = pl.ds(pl.multiple_of(j * tile, 128), tile)
            hi = pl.ds(pl.multiple_of(part + j * tile, 128), tile)
            d_hidden = nt(dffn_ref[at, :], dn_ref[lo, :])
            dgu_ref[at, lo] = (d_hidden * lin[at, lo].astype(f32)).astype(bf16)
            dgu_ref[at, hi] = (d_hidden * lin[at, hi].astype(f32)).astype(bf16)

        return looped(piece, 3)

    def input_work(slot, blocks, side):
        at = pl.ds(slot * rows, blocks * rows)

        def piece(j):
            cols = pl.ds(pl.multiple_of(j * wide, 128), wide)
            partial[side, pl.ds(0, blocks * rows), cols] = nt(dgu_ref[at, :part], gate_ref[cols, :]) + nt(
                dgu_ref[at, part:], up_ref[cols, :]
            )

        return looped(piece, 3)

    def keep(unit, total):
        total_ref[pl.ds(unit * (rows // UNITS), rows // UNITS), :] = total

    def lin_first(slot, blocks):
        work = lin_work(slot, blocks)
        return [lambda: (fetched[0].wait(), fetched[1].wait())] + work if slot == 0 else work

    Flow(ring, rows, s1, r1).gather(h3_ref, lin_first)
    keep_out(h3_ref, h3_hbm)
    fetched[2].wait()
    Flow(ring, rows, s2, r2).reduce(first, landed, partial, down_work, keep)

    def back_norm(value, index, grad):
        scale = scale_of(value)
        normed = value * scale
        weighted = grad * gain(index)
        inner = jnp.mean(weighted * normed, axis=-1, keepdims=True)
        return scale * (weighted - normed * inner), jnp.sum(grad * normed, axis=0, keepdims=True)

    gg = jnp.zeros((1, width), f32)
    for span in halves:
        proj = total_ref[span, :]
        scale = scale_of(proj)
        layer_ref[span, :] = (middle[span, :] + proj * scale * gain(3)).astype(bf16)
        d_ffn, term = back_norm(proj, 3, cot_ref[span, :].astype(f32))
        gg += term
        dffn_ref[span, :] = d_ffn.astype(bf16)
    gg_ref[3:4, :] = gg

    Flow(ring, rows, s3, r3).gather(dffn_ref, back_work)
    keep_out(dgu_ref, dgu_hbm)

    def make_down(j):
        span = pl.ds(j * tile, tile)

        def body(n, carry):
            cols = pl.ds(pl.multiple_of(n * wide, 128), wide)
            lin[span, cols] = tn(hid_ref[:, span], dffn_ref[:, cols]).astype(bf16)
            return carry

        lax.fori_loop(0, 3, body, 0)
        keep_out(lin.at[span, pl.ds(0, width)], part_hbm.at[span])

    Flow(ring, rows, s4, r4).reduce(
        first, landed, partial, input_work, keep, [functools.partial(make_down, j) for j in range(3)]
    )

    gg1 = jnp.zeros((1, width), f32)
    gg2 = jnp.zeros((1, width), f32)
    for span in halves:
        d_mid, term = back_norm(middle[span, :], 2, total_ref[span, :])
        gg2 += term
        d_mid = d_mid + cot_ref[span, :].astype(f32)
        dmid_ref[span, :] = d_mid
        d_attn, term = back_norm(attn_ref[span, :], 1, d_mid)
        gg1 += term
        dattn_ref[span, :] = d_attn.astype(bf16)
    gg_ref[1:2, :] = gg1
    gg_ref[2:3, :] = gg2
    gg_ref[0:1, :] = jnp.zeros((1, width), f32)
    gg_ref[4:8, :] = jnp.zeros((4, width), f32)
    for copy in kept:
        copy.wait()


def feed_forward(attn_proj, tokens, cotangent, gain_rows, w_gate, w_up, w_down, count, collective_id):
    f32, bf16 = jnp.float32, jnp.bfloat16
    rows, width = attn_proj.shape
    part = w_down.shape[0]
    every = rows * count
    dma = pltpu.SemaphoreType.DMA
    shape = jax.ShapeDtypeStruct
    return pl.pallas_call(
        functools.partial(ffn_kernel, count),
        out_shape=[
            shape((rows, width), bf16),
            shape((rows, width), f32),
            shape((rows, width), bf16),
            shape((8, width), f32),
            shape((every, width), bf16),
            shape((every, 2 * part), bf16),
            shape((part, width), bf16),
        ],
        in_specs=[pl.BlockSpec(memory_space=VM)] * 4 + [pl.BlockSpec(memory_space=HB)] * 3,
        out_specs=[pl.BlockSpec(memory_space=VM)] * 4 + [pl.BlockSpec(memory_space=HB)] * 3,
        scratch_shapes=[
            pltpu.VMEM(w_gate.shape, bf16),
            pltpu.VMEM(w_up.shape, bf16),
            pltpu.VMEM(w_down.shape, bf16),
            pltpu.VMEM((every, width), bf16),
            pltpu.VMEM((every, part), bf16),
            pltpu.VMEM((every, width), bf16),
            pltpu.VMEM((every, 2 * part), bf16),
            pltpu.VMEM((max(every, part), max(2 * part, width)), bf16),
            pltpu.VMEM((2, 2 * rows, width), f32),
            pltpu.VMEM((rows, width), bf16),
            pltpu.VMEM((2, count // 2, rows, width), bf16),
            pltpu.VMEM((rows, width), f32),
            pltpu.VMEM((rows, width), f32),
        ]
        + [dma((2, count // 2, UNITS))] * 8
        + [dma((3,)), dma((5,))],
        compiler_params=pltpu.CompilerParams(
            collective_id=collective_id, has_side_effects=True, vmem_limit_bytes=VMEM_LIMIT
        ),
        name="feed_forward",
    )(attn_proj, tokens, cotangent, gain_rows, w_gate, w_up, w_down)


def attention_kernel(
    reps, count, h1_ref, in_ref, got_ref, cos_ref, sin_ref, tagq_ref, tagk_ref, cut_ref,
    proj_ref, q_ref, k_ref, v_ref, att_ref, probs_ref, damp_ref, wo_ref, up_ref,
    part, first, landed, r_send, r_recv, w_sems, loc
):
    f32, bf16 = jnp.float32, jnp.bfloat16
    ring = Ring(count)
    rows = proj_ref.shape[0]
    seq_len = h1_ref.shape[0]
    tall = seq_len // 4
    half = HEAD_DIM // 2
    meet(near_devices(ring))
    weights = Fetch(ring, cut_ref, up_ref, w_sems)
    weights.begin()
    own = pltpu.make_async_copy(cut_ref.at[ring.me], up_ref.at[ring.rep, ring.me], loc)
    own.start()
    piece = got_ref.shape[2]
    for block in range(got_ref.shape[1]):
        for j in range(reps):
            start = (block * reps + j) * piece
            wo_ref[start : start + piece, :] = got_ref[j, block]

    def project(i, carry):
        at = pl.ds(pl.multiple_of(i * tall, 16), tall)
        flat = jnp.dot(h1_ref[at, :], in_ref[...], preferred_element_type=f32)
        cosine, sine = cos_ref[at, :], sin_ref[at, :]

        def turned(start):
            first, second = flat[:, start : start + half], flat[:, start + half : start + HEAD_DIM]
            return jnp.concatenate([first * cosine - second * sine, second * cosine + first * sine], axis=1)

        q_ref[at, :] = (turned(0) * HEAD_DIM ** (-0.5)).astype(bf16)
        k_ref[at, :] = turned(HEAD_DIM).astype(bf16)
        v_ref[at, :] = flat[:, 2 * HEAD_DIM :].astype(bf16)
        return carry

    lax.fori_loop(0, 4, project, 0)

    def attend(shard):
        at = pl.ds(pl.multiple_of(shard * rows, 16), rows)
        raw = lax.dot_general(q_ref[at, :], k_ref[...], (((1,), (1,)), ((), ())), preferred_element_type=f32)
        bent = jnp.tanh(raw * (1.0 / 50.0))
        query_at = shard * rows + lax.broadcasted_iota(jnp.int32, (rows, seq_len), 0)
        key_at = lax.broadcasted_iota(jnp.int32, (rows, seq_len), 1)
        tag = tagq_ref[at, :]
        visible = (key_at <= query_at) | ((tag == tagk_ref[...]) & (tag > 0))
        masked = jnp.where(visible, 50.0 * bent, -1e30)
        expo = jnp.exp(masked - jnp.max(masked, axis=-1, keepdims=True))
        probs = expo / jnp.sum(expo, axis=-1, keepdims=True)
        low = probs.astype(bf16)
        probs_ref[at, :] = low
        damp_ref[at, :] = (probs * (1.0 - bent * bent)).astype(bf16)
        attended = jnp.dot(low, v_ref[...], preferred_element_type=f32).astype(bf16)
        att_ref[at, :] = attended
        part[at, :] = jnp.dot(attended, wo_ref[...], preferred_element_type=f32)

    def attend_both(hop):
        def body(way, carry):
            attend(ring.at(hop + way * (count - 2 * hop)))
            return carry

        lax.fori_loop(0, 2 if hop else 1, body, 0)

    work = weights.steps()
    first_of_step = [0] + [1 + UNITS * step for step in range(ring.half - 1)]
    calls = []

    def pause():
        call = len(calls)
        calls.append(call)
        if call in first_of_step:
            attend_both(ring.half - 1 - first_of_step.index(call))
            return
        for _ in range(min(3, len(work))):
            work.pop(0)()

    def finish(span, total):
        proj_ref[span, :] = total

    def take(shard, span):
        return part[pl.ds(pl.multiple_of(shard * rows + span.start, 16), span.size), :]

    attend(ring.at(ring.half))
    started = reduce_on_ring(ring, rows, take, first, landed, r_send, r_recv, finish, pause)
    for piece in work:
        piece()
    weights.finish()
    own.wait()
    for copy in started:
        copy.wait_send()


def attention(reps, count, normed, w_in, w_out, cosine, sine, tag, cut_up, collective_id):
    dma = pltpu.SemaphoreType.DMA
    low, f32 = jnp.bfloat16, jnp.float32
    shape = jax.ShapeDtypeStruct
    seq_len, width = normed.shape
    rows = seq_len // count
    hops = count // 2
    head = shape((seq_len, HEAD_DIM), low)
    square = shape((seq_len, seq_len), low)
    return pl.pallas_call(
        functools.partial(attention_kernel, reps, count),
        out_shape=[
            shape((rows, width), f32), head, head, head, head, square, square, shape((HEAD_DIM, width), low),
            shape((reps,) + cut_up.shape, low),
        ],
        in_specs=[pl.BlockSpec(memory_space=VM)] * 7 + [pl.BlockSpec(memory_space=HB)],
        out_specs=[pl.BlockSpec(memory_space=VM)] * 8 + [pl.BlockSpec(memory_space=HB)],
        scratch_shapes=[
            pltpu.VMEM((seq_len, width), f32),
            pltpu.VMEM((rows, width), low),
            pltpu.VMEM((2, hops, rows, width), low),
            dma((2, hops, UNITS)),
            dma((2, hops, UNITS)),
            dma((8, count)),
            dma,
        ],
        compiler_params=pltpu.CompilerParams(
            collective_id=collective_id, has_side_effects=True, vmem_limit_bytes=VMEM_LIMIT
        ),
        name="attention",
    )(normed, w_in, w_out, cosine, sine, tag[:, None], tag[None, :], cut_up)


class Fetch:
    def __init__(self, ring, cut, out, sems):
        self.ring, self.cut, self.out = ring, cut, out
        self.rep, self.me, self.count = ring.rep, ring.me, ring.count
        self.across, self.beside = rep_partners(ring.rep)
        self.sems = sems
        self.started = []

    def go(self, copy):
        copy.start()
        self.started.append(copy)

    def spread(self, k):
        to = (self.me + k) % self.count
        return remote(
            self.cut.at[to], self.out.at[self.rep, self.me], self.sems.at[0, k], self.sems.at[1, k], (self.rep, to)
        )

    def arrived(self, k):
        frm = (self.me + self.count - k) % self.count
        return remote(
            self.cut.at[frm], self.out.at[self.rep, frm], self.sems.at[0, k], self.sems.at[1, k], (self.rep, frm)
        )

    def forward(self, k, hop):
        frm = (self.me + self.count - k) % self.count
        rep = self.across if hop == 2 else self.rep
        block = self.out.at[rep, frm] if k or hop == 2 else self.cut.at[self.me]
        to = self.across if hop == 0 else self.beside
        return remote(
            block,
            self.out.at[rep, frm],
            self.sems.at[2 + 2 * hop, k],
            self.sems.at[3 + 2 * hop, k],
            (to, self.me),
        )

    def pass_on(self, k):
        if k:
            self.arrived(k).wait_recv()
        self.go(self.forward(k, 0))
        self.go(self.forward(k, 1))

    def pass_beside(self, k):
        self.forward(k, 0).wait_recv()
        self.go(self.forward(k, 2))

    def begin(self):
        for k in range(1, self.count):
            self.go(self.spread(k))
        self.pass_on(0)

    def steps(self):
        work = [functools.partial(self.pass_on, k) for k in range(1, self.count)]
        return work + [functools.partial(self.pass_beside, k) for k in range(self.count)]

    def finish(self):
        for k in range(self.count):
            self.forward(k, 1).wait_recv()
            self.forward(k, 2).wait_recv()
        for copy in self.started:
            copy.wait_send()


def rep_partners(rep):
    return (rep + 2) % 4, rep + 1 - 2 * (rep % 2)


def everyone(rep, me, reps, count):
    here = rep * count + me
    total = reps * count
    return [
        (((here + k) % total) // count, ((here + k) % total) % count) for k in range(1, total)
    ]


def opening_kernel(
    reps, count, tok_ref, gain_ref, in_hbm, dn_hbm, ou_hbm, gate_hbm, up_hbm,
    h1_ref, gains_ref, w_in, w_gate, w_dn, w_ou, cut_up,
    in_f, dn_f, ou_f, gate_f, up_f, in_ref, dn_ref, ou_ref, gate_ref, tok_all, gain_all,
    t_send, t_recv, g_send, g_recv, i_sems, u_sems, o_send, o_recv, n_send, n_recv, loc, loads
):
    f32 = jnp.float32
    ring = Ring(count)
    rep, me = ring.rep, ring.me
    across, beside = rep_partners(rep)
    others = everyone(rep, me, reps, count)
    mine = rep * count + me
    d_rows = in_ref.shape[1]
    rows = tok_ref.shape[0]
    fetched = [
        pltpu.make_async_copy(src, dst, loads.at[index])
        for index, (src, dst) in enumerate(
            ((in_hbm, in_f), (dn_hbm, dn_f), (ou_hbm, ou_f), (gate_hbm, gate_f), (up_hbm, up_f))
        )
    ]
    for copy in fetched:
        copy.start()
    meet(others)
    started = []

    def go(copy):
        copy.start()
        started.append(copy)

    for k, device in enumerate(others):
        go(remote(gain_ref, gain_all.at[mine], g_send.at[k], g_recv.at[k], device))
    gain_all[mine] = gain_ref[...]
    ins = Fetch(ring, in_ref, w_in, i_sems)
    gates = Fetch(ring, gate_ref, w_gate, u_sems)
    gather = Gather(ring, tok_ref, tok_all, t_send, t_recv)
    fetched[0].wait()
    cut_heads(count, in_f, in_ref)
    ins.begin()
    fetched[1].wait()
    dn_ref[...] = dn_f[...].astype(dn_ref.dtype)
    dn_x = remote(dn_ref, w_dn.at[rep], n_send.at[0], n_recv.at[0], (across, me))
    dn_c = remote(dn_ref, w_dn.at[rep], n_send.at[1], n_recv.at[1], (beside, me))
    dn_d = remote(w_dn.at[across], w_dn.at[across], n_send.at[2], n_recv.at[2], (beside, me))
    go(dn_x)
    go(dn_c)
    fetched[2].wait()
    for j in range(reps):
        ou_ref[j] = ou_f[j * ou_ref.shape[1] : (j + 1) * ou_ref.shape[1], :].astype(ou_ref.dtype)

    per_head = count * reps // HEADS
    target = mine // per_head
    slot = mine % per_head

    def ou_copy(j):
        return remote(ou_ref.at[j], w_ou.at[j, slot], o_send.at[j], o_recv.at[slot], (j, target))

    def is_self(j):
        return (rep == j) & (me == target)

    for j in range(reps):
        @pl.when(jnp.logical_not(is_self(j)))
        def _():
            ou_copy(j).start()

        @pl.when(is_self(j))
        def _():
            pltpu.make_async_copy(ou_ref.at[j], w_ou.at[j, slot], o_recv.at[slot]).start()

    fetched[3].wait()
    cut_units(reps, count, gate_f, gate_ref)
    gates.begin()
    locals_ = []
    for index, (src, dst) in enumerate(
        ((in_ref.at[me], w_in.at[rep, me]), (gate_ref.at[me], w_gate.at[rep, me]), (dn_ref, w_dn.at[rep]))
    ):
        copy = pltpu.make_async_copy(src, dst, loc.at[index])
        copy.start()
        locals_.append(copy)

    for k in range(len(others)):
        frm = (mine + len(others) - k) % (reps * count)
        remote(gain_ref, gain_all.at[frm], g_send.at[k], g_recv.at[k], others[k]).wait_recv()
    gains_ref[...] = jnp.concatenate([gain_all[device, :, 0:d_rows] for device in range(reps * count)], axis=1)
    gain = 1.0 + gains_ref[0:1, :]

    def norm(value):
        value = value.astype(f32)
        return (value * lax.rsqrt(jnp.mean(value * value, axis=-1, keepdims=True) + 1e-06) * gain).astype(h1_ref.dtype)

    def norm_block(shard):
        for unit in range(UNITS):
            span = pl.ds(unit * (rows // UNITS), rows // UNITS)
            h1_ref[shard, span, :] = norm(tok_all[shard, span, :])

    for unit in range(UNITS):
        span = pl.ds(unit * (rows // UNITS), rows // UNITS)
        h1_ref[me, span, :] = norm(tok_ref[span, :])

    hops = gather.steps()

    def take_hop(hop):
        for _ in range(len(ring.units(0, hop))):
            hops.pop(0)()
        for way in (0, 1) if hop < ring.half else (0,):
            norm_block(ring.away(1 - way, hop))

    for k in range(1, count):
        ins.pass_on(k)
    fetched[4].wait()
    cut_units(reps, count, up_f, cut_up)
    gather.begin()
    for k in range(1, count):
        gates.pass_on(k)
    for i in range(per_head):
        remote(
            ou_ref.at[0], w_ou.at[rep, i], o_send.at[0], o_recv.at[i], (across, me)
        ).wait_recv()
    ou_x = remote(w_ou.at[rep], w_ou.at[rep], n_send.at[3], n_recv.at[3], (across, me))
    ou_c = remote(w_ou.at[rep], w_ou.at[rep], n_send.at[4], n_recv.at[4], (beside, me))
    ou_d = remote(w_ou.at[across], w_ou.at[across], n_send.at[5], n_recv.at[5], (beside, me))
    go(ou_x)
    go(ou_c)
    take_hop(1)
    dn_x.wait_recv()
    go(dn_d)
    take_hop(2)
    for k in range(count):
        ins.pass_beside(k)
    for hop in range(3, ring.half + 1):
        take_hop(hop)
    ou_x.wait_recv()
    go(ou_d)
    for k in range(count):
        gates.pass_beside(k)
    ins.finish()
    gates.finish()
    for copy in (dn_c, dn_d, ou_c, ou_d):
        copy.wait_recv()
    for copy in started:
        copy.wait_send()
    gather.finish()
    for j in range(reps):
        @pl.when(jnp.logical_not(is_self(j)))
        def _():
            ou_copy(j).wait_send()
    for copy in locals_:
        copy.wait()


def opening(reps, count, tokens, gain_tile, inproj, outproj, ffn_gate, ffn_up, ffn_down, collective_id):
    dma = pltpu.SemaphoreType.DMA
    per_head = count * reps // HEADS
    total = reps * count
    low, f32 = jnp.bfloat16, jnp.float32
    shape = jax.ShapeDtypeStruct
    hops = dma((2, count // 2, UNITS))
    width = tokens.shape[1]
    gathered = (count,) + tokens.shape
    d_rows = inproj.shape[0]
    heads = (count, d_rows, 3 * HEAD_DIM)
    units = (count, d_rows, ffn_gate.shape[1] // count)
    outs = (reps, outproj.shape[0] // reps, width)
    vm, hb = pl.BlockSpec(memory_space=VM), pl.BlockSpec(memory_space=HB)
    return pl.pallas_call(
        functools.partial(opening_kernel, reps, count),
        out_shape=[
            shape(gathered, low),
            shape((8, width), f32),
            shape((reps,) + heads, low),
            shape((reps,) + units, low),
            shape((reps,) + ffn_down.shape, low),
            shape((reps, per_head) + outs[1:], low),
            shape(units, low),
        ],
        in_specs=[vm] * 2 + [hb] * 5,
        out_specs=[vm] * 2 + [hb] * 4 + [vm],
        scratch_shapes=[
            pltpu.VMEM(inproj.shape, f32),
            pltpu.VMEM(ffn_down.shape, f32),
            pltpu.VMEM(outproj.shape, f32),
            pltpu.VMEM(ffn_gate.shape, f32),
            pltpu.VMEM(ffn_up.shape, f32),
            pltpu.VMEM(heads, low),
            pltpu.VMEM(ffn_down.shape, low),
            pltpu.VMEM(outs, low),
            pltpu.VMEM(units, low),
            pltpu.VMEM(gathered, low),
            pltpu.VMEM((total,) + gain_tile.shape, f32),
            hops,
            hops,
            dma((total - 1,)),
            dma((total - 1,)),
            dma((8, count)),
            dma((8, count)),
            dma((reps,)),
            dma((per_head,)),
            dma((6,)),
            dma((6,)),
            dma((3,)),
            dma((5,)),
        ],
        compiler_params=pltpu.CompilerParams(
            collective_id=collective_id, has_side_effects=True, vmem_limit_bytes=VMEM_LIMIT
        ),
        name="opening",
    )(tokens, gain_tile, inproj, ffn_down, outproj, ffn_gate, ffn_up)


def cut_units(reps, count, ref, cut):
    block = ref.shape[1] // (reps * count)
    for shard in range(count):
        pieces = [ref[:, (r * count + shard) * block : (r * count + shard + 1) * block] for r in range(reps)]
        cut[shard] = jnp.concatenate(pieces, axis=1).astype(cut.dtype)


def cut_heads(count, ref, cut):
    group = HEADS // KV_HEADS
    for shard in range(count):
        heads = shard, HEADS + shard // group, HEADS + KV_HEADS + shard // group
        for index, head in enumerate(heads):
            cut[shard, :, index * HEAD_DIM : (index + 1) * HEAD_DIM] = ref[
                :, head * HEAD_DIM : (head + 1) * HEAD_DIM
            ].astype(cut.dtype)


class RepSum:
    def __init__(self, part, from_core, from_across, sems, rep, me):
        self.part, self.from_core, self.from_across = part, from_core, from_across
        self.c_send, self.c_recv, self.x_send, self.x_recv = sems
        self.across, self.beside = rep_partners(rep)
        self.rep, self.me = rep, me
        self.core = rep % 2
        self.chip = rep // 2

    def core_copy(self, side, piece):
        chip = 1 - self.chip if side == 0 else self.chip
        return remote(
            self.part(chip * 2 + 1 - self.core, piece),
            self.from_core.at[side, piece],
            self.c_send.at[side, piece],
            self.c_recv.at[side, piece],
            (self.beside, self.me),
        )

    def cross_copy(self, piece):
        return remote(
            self.from_core.at[0, piece],
            self.from_across.at[piece],
            self.x_send.at[piece],
            self.x_recv.at[piece],
            (self.across, self.me),
        )

    def begin(self, pieces):
        for side in (0, 1):
            for piece in pieces:
                self.core_copy(side, piece).start()

    def cross(self, piece):
        f32 = jnp.float32
        self.core_copy(0, piece).wait_recv()
        mine = self.part((1 - self.chip) * 2 + self.core, piece)[...].astype(f32)
        self.from_core[0, piece] = (mine + self.from_core[0, piece].astype(f32)).astype(jnp.bfloat16)
        self.cross_copy(piece).start()

    def total(self, piece):
        f32 = jnp.float32
        self.core_copy(1, piece).wait_recv()
        mine = self.part(self.rep, piece)[...].astype(f32) + self.from_core[1, piece].astype(f32)
        self.cross_copy(piece).wait_recv()
        return mine + self.from_across[piece].astype(f32)

    def finish(self, pieces):
        for piece in pieces:
            self.core_copy(0, piece).wait_send()
            self.core_copy(1, piece).wait_send()
            self.cross_copy(piece).wait_send()


class Spread:
    def __init__(self, blocks, out, send, recv, rep, me, count):
        self.blocks, self.out, self.send, self.recv = blocks, out, send, recv
        self.rep, self.me, self.count = rep, me, count

    def copy(self, k):
        to = (self.me + k) % self.count
        return remote(
            self.blocks.at[to], self.out.at[self.me], self.send.at[k], self.recv.at[k], (self.rep, to)
        )

    def arrived(self, k):
        frm = (self.me + self.count - k) % self.count
        return remote(
            self.blocks.at[frm], self.out.at[frm], self.send.at[k], self.recv.at[k], (self.rep, frm)
        )

    def finish(self):
        for k in range(1, self.count):
            self.arrived(k).wait_recv()
        for k in range(1, self.count):
            self.copy(k).wait_send()


def near_devices(ring):
    across, beside = rep_partners(ring.rep)
    return [(ring.rep, (ring.me + k) % ring.count) for k in range(1, ring.count)] + [
        (across, ring.me),
        (beside, ring.me),
    ]


class Gather:
    def __init__(self, ring, block, out, send, recv):
        self.ring, self.block, self.out, self.send, self.recv = ring, block, out, send, recv
        self.rows = block.shape[0] // UNITS
        self.started = []

    def copy(self, way, hop, unit):
        ring = self.ring
        origin = ring.away(1 - way, hop - 1) if hop > 1 else ring.me
        span = pl.ds(unit * self.rows, self.rows)
        return remote(
            self.block.at[span] if hop == 1 else self.out.at[origin, span],
            self.out.at[origin, span],
            self.send.at[way, hop - 1, unit],
            self.recv.at[way, hop - 1, unit],
            ring.next[way],
        )

    def go(self, copy):
        copy.start()
        self.started.append(copy)

    def begin(self):
        for index in range(UNITS):
            for way in (0, 1):
                self.go(self.copy(way, 1, self.ring.units(way, 1)[index]))

    def steps(self):
        ring = self.ring

        def step(hop, index):
            for way in (0, 1):
                unit = ring.units(way, hop)[index]
                self.copy(way, hop, unit).wait_recv()
                if hop < ring.half and unit in ring.units(way, hop + 1):
                    self.go(self.copy(way, hop + 1, unit))

        return [
            functools.partial(step, hop, index)
            for hop in range(1, ring.half + 1)
            for index in range(len(ring.units(0, hop)))
        ]

    def finish(self):
        for copy in self.started:
            copy.wait_send()


def tn(left, right):
    return lax.dot_general(left, right, (((0,), (0,)), ((), ())), preferred_element_type=jnp.float32)


DN_PIECES = 3


def ffn_grads_kernel(
    reps, count, dattn_ref, wo_ref, q_ref, k_ref, v_ref, cos_ref, sin_ref, h3_hbm, dgu_hbm, part_hbm, probs_hbm, damp_hbm,
    all_ref, sum_ref, down_ref, dproj,
    h3_ref, dgu_ref, g_part, g_core, g_from, d_part, d_core, d_from, probs_ref, damp_ref, d_key, d_value,
    t_send, t_recv, gc_s, gc_r, gx_s, gx_r, dc_s, dc_r, dx_s, dx_r, s_send, s_recv, loc, loads, square
):
    f32, bf16 = jnp.float32, jnp.bfloat16
    ring = Ring(count)
    rep, me = ring.rep, ring.me
    d_rows, columns = sum_ref.shape[1:]
    part, width = d_part.shape
    block = part // reps
    seq_len = q_ref.shape[0]
    blocks = 4
    tall = seq_len // blocks
    half = HEAD_DIM // 2
    fetched = [
        pltpu.make_async_copy(src, dst, loads.at[index])
        for index, (src, dst) in enumerate(((part_hbm, d_part), (h3_hbm, h3_ref), (dgu_hbm, dgu_ref)))
    ]
    for copy in fetched:
        copy.start()

    def squares(i):
        span = pl.ds(i * tall, tall)
        return [
            pltpu.make_async_copy(probs_hbm.at[span], probs_ref, square.at[0]),
            pltpu.make_async_copy(damp_hbm.at[span], damp_ref, square.at[1]),
        ]

    for copy in squares(0):
        copy.start()
    meet(near_devices(ring))
    gather = Gather(ring, dattn_ref, all_ref, t_send, t_recv)
    gather.begin()
    own = pltpu.make_async_copy(dattn_ref, all_ref.at[me], loc)
    own.start()

    def d_at(owner, piece):
        rows = block // DN_PIECES
        return d_part.at[pl.ds(owner * block + piece * rows, rows)]

    down = RepSum(d_at, d_core, d_from, (dc_s, dc_r, dx_s, dx_r), rep, me)
    gate_up = RepSum(
        lambda owner, piece: g_part.at[owner, piece], g_core, g_from, (gc_s, gc_r, gx_s, gx_r), rep, me
    )
    spread = Spread(g_from, sum_ref, s_send, s_recv, rep, me, count)
    d_pieces = list(range(DN_PIECES))
    g_pieces = [(me + k) % count for k in range(1, count)] + [me]

    def make_gate_up(owner):
        rows = count * d_rows
        step = columns // 3

        def body(n, carry):
            cols = pl.ds(pl.multiple_of(n * step, 128), step)
            made = tn(h3_ref[:, owner * rows : (owner + 1) * rows], dgu_ref[:, cols])
            g_part[owner, :, :, cols] = made.reshape(count, d_rows, step).astype(bf16)
            return carry

        lax.fori_loop(0, 3, body, 0)

    def nt(left, right):
        return lax.dot_general(left, right, (((1,), (1,)), ((), ())), preferred_element_type=f32)

    def unturned(flat, at):
        cosine, sine = cos_ref[at, :], sin_ref[at, :]
        low, high = flat[:, :half], flat[:, half:]
        return jnp.concatenate([low * cosine + high * sine, high * cosine - low * sine], axis=1)

    d_key[...] = jnp.zeros_like(d_key)
    d_value[...] = jnp.zeros_like(d_value)

    def attend(i):
        at = pl.ds(i * tall, tall)
        per = count // blocks
        d_out = all_ref[i * per : (i + 1) * per].reshape(tall, width)
        d_att = nt(d_out, wo_ref[...]).astype(bf16)
        d_probs = nt(d_att, v_ref[...])
        for copy in squares(i):
            copy.wait()
        probs = probs_ref[...]
        inner = jnp.sum(probs.astype(f32) * d_probs, axis=-1, keepdims=True)
        d_scores = (damp_ref[...].astype(f32) * (d_probs - inner)).astype(bf16)
        d_query = jnp.dot(d_scores, k_ref[...], preferred_element_type=f32)
        dproj[at, :HEAD_DIM] = (unturned(d_query, at) * HEAD_DIM ** (-0.5)).astype(bf16)
        d_key[...] += tn(d_scores, q_ref[at, :])
        d_value[...] += tn(probs, d_att)
        if i < blocks - 1:
            for copy in squares(i + 1):
                copy.start()

    def project():
        for i in range(blocks):
            at = pl.ds(i * tall, tall)
            dproj[at, HEAD_DIM : 2 * HEAD_DIM] = unturned(d_key[at, :], at).astype(bf16)
            dproj[at, 2 * HEAD_DIM :] = d_value[at, :].astype(bf16)

    def finish_gate_up(k):
        piece = g_pieces[k]
        total = gate_up.total(piece).astype(bf16)
        if k < count - 1:
            g_from[piece] = total
            spread.copy(k + 1).start()
        else:
            sum_ref[me] = total

    def finish_down(piece):
        rows = block // DN_PIECES
        down_ref[pl.ds(piece * rows, rows), :] = down.total(piece)

    fetched[0].wait()
    down.begin(d_pieces)
    work = [lambda: [down.cross(piece) for piece in d_pieces]]
    work += [lambda: [copy.wait() for copy in fetched[1:]]]
    work += [functools.partial(make_gate_up, owner) for owner in range(reps)]
    work += [lambda: gate_up.begin(g_pieces)]

    def cross_two(k):
        for piece in g_pieces[k : k + 2]:
            gate_up.cross(piece)

    work += [functools.partial(cross_two, k) for k in range(0, count, 2)]
    for step in gather.steps():
        step()
        if work:
            work.pop(0)()
    for piece in work:
        piece()
    own.wait()
    after = [functools.partial(finish_gate_up, k) for k in range(count)]
    per = max(1, count // blocks)
    for i in range(blocks):
        attend(i)
        for _ in range(min(per, len(after) - 2)):
            after.pop(0)()
    project()
    for piece in d_pieces:
        finish_down(piece)
    for piece in after:
        piece()
    spread.finish()
    down.finish(d_pieces)
    gate_up.finish(g_pieces)
    gather.finish()


def ffn_grads(
    reps, count, d_attn, w_out, queries, keys, values, cosine, sine, h3, d_gu, part_down, probs, damp, d_rows, collective_id
):
    dma = pltpu.SemaphoreType.DMA
    low, f32 = jnp.bfloat16, jnp.float32
    shape = jax.ShapeDtypeStruct
    width = d_attn.shape[1]
    columns = d_gu.shape[1]
    part = part_down.shape[0]
    seq_len = h3.shape[0]
    block = part // reps
    blocks = (count, d_rows, columns)
    lots = (DN_PIECES, block // DN_PIECES, width)
    hops = dma((2, count // 2, UNITS))
    vm, hb = pl.BlockSpec(memory_space=VM), pl.BlockSpec(memory_space=HB)
    return pl.pallas_call(
        functools.partial(ffn_grads_kernel, reps, count),
        out_shape=[
            shape((count,) + d_attn.shape, low),
            shape(blocks, low),
            shape((block, width), f32),
            shape((seq_len, 3 * HEAD_DIM), low),
        ],
        in_specs=[vm] * 7 + [hb] * 5,
        out_specs=[vm] * 4,
        scratch_shapes=[
            pltpu.VMEM(h3.shape, low),
            pltpu.VMEM(d_gu.shape, low),
            pltpu.VMEM((reps,) + blocks, low),
            pltpu.VMEM((2,) + blocks, low),
            pltpu.VMEM(blocks, low),
            pltpu.VMEM((part, width), low),
            pltpu.VMEM((2,) + lots, low),
            pltpu.VMEM(lots, low),
            pltpu.VMEM((seq_len // 4, seq_len), low),
            pltpu.VMEM((seq_len // 4, seq_len), low),
            pltpu.VMEM((seq_len, HEAD_DIM), f32),
            pltpu.VMEM((seq_len, HEAD_DIM), f32),
            hops,
            hops,
            dma((2, count)),
            dma((2, count)),
            dma((count,)),
            dma((count,)),
            dma((2, DN_PIECES)),
            dma((2, DN_PIECES)),
            dma((DN_PIECES,)),
            dma((DN_PIECES,)),
            dma((count,)),
            dma((count,)),
            dma,
            dma((3,)),
            dma((2,)),
        ],
        compiler_params=pltpu.CompilerParams(
            collective_id=collective_id, has_side_effects=True, vmem_limit_bytes=VMEM_LIMIT
        ),
        name="ffn_grads",
    )(d_attn, w_out, queries, keys, values, cosine, sine, h3, d_gu, part_down, probs, damp)


def closing_kernel(
    reps, count, dproj, in_ref, att_ref, h1_hbm, dattn_hbm, tokens_ref, dmid_ref, gains_ref, gg_ref,
    grad_ref, sum_ref, out_ref, gain_ref,
    h1_ref, dattn_ref, x_part, i_part, o_part, first, landed, total_ref, tiles, i_core, i_from, o_core, o_from,
    r_send, r_recv, ic_s, ic_r, ix_s, ix_r, oc_s, oc_r, ox_s, ox_r, s_send, s_recv, p_send, p_recv,
    g_send, g_recv, loads
):
    f32, bf16 = jnp.float32, jnp.bfloat16
    ring = Ring(count)
    rep, me = ring.rep, ring.me
    here = rep * count + me
    others = everyone(rep, me, reps, count)
    full = o_part.shape[1]
    d_rows = sum_ref.shape[1]
    seq_len, width = dattn_ref.shape
    rows = grad_ref.shape[0]
    fetched = [
        pltpu.make_async_copy(h1_hbm, h1_ref, loads.at[0]),
        pltpu.make_async_copy(dattn_hbm, dattn_ref, loads.at[1]),
    ]
    for copy in fetched:
        copy.start()
    meet(others)
    tall = seq_len // 4

    def project(i, carry):
        at = pl.ds(pl.multiple_of(i * tall, 16), tall)
        x_part[at, :] = lax.dot_general(
            dproj[at, :], in_ref[...], (((1,), (1,)), ((), ())), preferred_element_type=f32
        ).astype(bf16)
        return carry

    lax.fori_loop(0, 4, project, 0)

    def make_out():
        fetched[1].wait()
        per = width // 3

        def body(n, carry):
            cols = pl.ds(pl.multiple_of(n * per, 128), per)
            made = tn(att_ref[...], dattn_ref[:, cols]).reshape(full, reps, HEAD_DIM // full // reps, per)
            for owner in range(reps):
                o_part[owner, :, :, cols] = made[:, owner].astype(bf16)
            return carry

        lax.fori_loop(0, 3, body, 0)

    def make_in(owner):
        if owner == 0:
            fetched[0].wait()
        deep = count * d_rows
        made = tn(h1_ref[:, owner * deep : (owner + 1) * deep], dproj[...])
        i_part[owner] = made.reshape(count, d_rows, 3 * HEAD_DIM).astype(bf16)

    o_pieces = list(range(full))
    i_pieces = [(me + k) % count for k in range(1, count)] + [me]
    ins = RepSum(lambda owner, piece: i_part.at[owner, piece], i_core, i_from, (ic_s, ic_r, ix_s, ix_r), rep, me)
    outs = RepSum(lambda owner, piece: o_part.at[owner, piece], o_core, o_from, (oc_s, oc_r, ox_s, ox_r), rep, me)
    spread = Spread(i_from, sum_ref, s_send, s_recv, rep, me, count)

    def o_owner(piece):
        where = me * full + piece
        return where // count, where % count

    def o_copy(piece):
        return remote(o_from.at[piece], out_ref.at[rep], p_send.at[piece], p_recv.at[rep], o_owner(piece))

    def o_self(piece):
        return me * full + piece == here

    def o_finish(piece):
        total = outs.total(piece).astype(bf16)
        o_from[piece] = total

        @pl.when(jnp.logical_not(o_self(piece)))
        def _():
            o_copy(piece).start()

        @pl.when(o_self(piece))
        def _():
            pltpu.make_async_copy(o_from.at[piece], out_ref.at[rep], p_recv.at[rep]).start()

    def i_finish(k):
        piece = i_pieces[k]
        total = ins.total(piece).astype(bf16)
        if k < count - 1:
            i_from[piece] = total
            spread.copy(k + 1).start()
        else:
            sum_ref[me] = total

    work = [functools.partial(make_in, owner) for owner in range(reps)]
    work += [lambda: ins.begin(i_pieces), make_out, lambda: outs.begin(o_pieces)]
    work += [functools.partial(ins.cross, piece) for piece in i_pieces]
    work += [functools.partial(outs.cross, piece) for piece in o_pieces]
    work += [functools.partial(i_finish, k) for k in range(count)]
    work += [functools.partial(o_finish, piece) for piece in o_pieces]

    terms = []
    gain = 1.0 + gains_ref[0:1, :]

    def pause():
        for _ in range(min(2, len(work))):
            work.pop(0)()

    def take(shard, span):
        return x_part[pl.ds(pl.multiple_of(shard * rows + span.start, 16), span.size), :]

    def finish(span, total):
        value = tokens_ref[span, :].astype(f32)
        scale = lax.rsqrt(jnp.mean(value * value, axis=-1, keepdims=True) + 1e-06)
        normed = value * scale
        weighted = total * gain
        inner = jnp.mean(weighted * normed, axis=-1, keepdims=True)
        grad_ref[span, :] = dmid_ref[span, :] + scale * (weighted - normed * inner)
        terms.append(jnp.sum(total * normed, axis=0, keepdims=True))

    started = reduce_on_ring(ring, rows, take, first, landed, r_send, r_recv, finish, pause)
    total_ref[...] = gg_ref[...]
    total_ref[0:1, :] = functools.reduce(jnp.add, terms)
    every = total_ref[...]
    for owner in range(reps * count):
        tiles[owner, :, 0:d_rows] = every[:, owner * d_rows : (owner + 1) * d_rows]
        tiles[owner, :, d_rows:] = jnp.zeros((8, 128 - d_rows), f32)
    for k, device in enumerate(others):
        to = (here + k + 1) % (reps * count)
        remote(tiles.at[to], gain_ref.at[here], g_send.at[k], g_recv.at[k], device).start()
    gain_ref[here] = tiles[here]
    for piece in work:
        piece()
    for k in range(len(others)):
        frm = (here + len(others) - k) % (reps * count)
        remote(tiles.at[frm], gain_ref.at[frm], g_send.at[k], g_recv.at[k], others[k]).wait_recv()
    for j in range(reps):
        remote(
            o_from.at[0], out_ref.at[j], p_send.at[0], p_recv.at[j], (rep, (me + 1) % count)
        ).wait_recv()
    for piece in o_pieces:
        @pl.when(jnp.logical_not(o_self(piece)))
        def _():
            o_copy(piece).wait_send()
    spread.finish()
    ins.finish(i_pieces)
    outs.finish(o_pieces)
    for k, device in enumerate(others):
        to = (here + k + 1) % (reps * count)
        remote(tiles.at[to], gain_ref.at[here], g_send.at[k], g_recv.at[k], device).wait_send()
    for copy in started:
        copy.wait_send()


def closing(
    reps, count, d_projected, w_in, attended, normed, d_attn, tokens, d_middle, gain_rows, gain_terms, piece, collective_id
):
    dma = pltpu.SemaphoreType.DMA
    low, f32 = jnp.bfloat16, jnp.float32
    shape = jax.ShapeDtypeStruct
    rows, width = tokens.shape
    seq_len = normed.shape[0]
    total = reps * count
    half = count // 2
    d_rows = width // total
    full = HEAD_DIM // (reps * piece)
    i_block = (count, d_rows, 3 * HEAD_DIM)
    o_block = (full, piece, width)
    hops = dma((2, half, UNITS))
    vm, hb = pl.BlockSpec(memory_space=VM), pl.BlockSpec(memory_space=HB)
    return pl.pallas_call(
        functools.partial(closing_kernel, reps, count),
        out_shape=[
            shape((rows, width), f32),
            shape(i_block, low),
            shape((reps, piece, width), low),
            shape((total, 8, 128), f32),
        ],
        in_specs=[vm] * 3 + [hb] * 2 + [vm] * 4,
        out_specs=[vm] * 4,
        scratch_shapes=[
            pltpu.VMEM((seq_len, width), low),
            pltpu.VMEM((seq_len, width), low),
            pltpu.VMEM((seq_len, width), low),
            pltpu.VMEM((reps,) + i_block, low),
            pltpu.VMEM((reps,) + o_block, low),
            pltpu.VMEM((rows, width), low),
            pltpu.VMEM((2, half, rows, width), low),
            pltpu.VMEM((8, width), f32),
            pltpu.VMEM((total, 8, 128), f32),
            pltpu.VMEM((2,) + i_block, low),
            pltpu.VMEM(i_block, low),
            pltpu.VMEM((2,) + o_block, low),
            pltpu.VMEM(o_block, low),
            hops,
            hops,
            dma((2, count)),
            dma((2, count)),
            dma((count,)),
            dma((count,)),
            dma((2, full)),
            dma((2, full)),
            dma((full,)),
            dma((full,)),
            dma((count,)),
            dma((count,)),
            dma((full,)),
            dma((reps,)),
            dma((total - 1,)),
            dma((total - 1,)),
            dma((2,)),
        ],
        compiler_params=pltpu.CompilerParams(
            collective_id=collective_id, has_side_effects=True, vmem_limit_bytes=VMEM_LIMIT
        ),
        name="closing",
    )(d_projected, w_in, attended, normed, d_attn, tokens, d_middle, gain_rows, gain_terms)


def tiles_of(ref):
    rows, columns = ref.shape
    tall = 72 if rows % 72 == 0 else 64 if rows % 64 == 0 else 8
    wide = 384 if columns % 384 == 0 else 256
    return rows // tall, columns // wide, tall, wide


def tile_at(ref, n):
    _, across, tall, wide = tiles_of(ref)
    down, right = n // across, n % across
    return pl.ds(pl.multiple_of(down * tall, 8), tall), pl.ds(pl.multiple_of(right * wide, 128), wide)


LAMB_ORDER = (1, 4, 2, 3, 0)


def lamb_kernel(reps, count, sum_in, sum_out, sum_gu, gain_tiles, g_master, g_mean, g_square, *refs):
    f32 = jnp.float32
    names = 5
    hbm_in, refs = [refs[3 * i : 3 * i + 3] for i in range(names)], refs[3 * names :]
    grad_dn, refs = refs[0], refs[1:]
    (sums_out, gg_out, gm_out, gs_out, gp_out), refs = refs[:5], refs[5:]
    hbm_out, refs = [refs[4 * i : 4 * i + 4] for i in range(names)], refs[4 * names :]
    masters, means, squares, grads = (refs[names * i : names * (i + 1)] for i in range(4))
    in_sem, out_sem, dn_sem = refs[4 * names :]
    total = reps * count
    group = HEADS // KV_HEADS

    def fetch(i, j):
        return pltpu.make_async_copy(hbm_in[i][j], (masters, means, squares)[j][i], in_sem.at[i, j])

    fetch_dn = pltpu.make_async_copy(grad_dn, grads[4], dn_sem)
    fetch_dn.start()

    def fetch_all(order):
        for i in order:
            for j in range(3):
                fetch(i, j).start()

    fetch_all(LAMB_ORDER[:2])

    def store(i, j):
        return pltpu.make_async_copy((grads, means, squares, masters)[j][i], hbm_out[i][j], out_sem.at[i, j])

    def join(index, ref):
        block = ref.shape[1] // total
        part = block * reps
        for first in range(0, total, 4):
            pieces = []
            for b in range(first, first + 4):
                start = index * part + (b // count) * block
                pieces.append(sum_gu[b % count, :, start : start + block].astype(f32))
            ref[:, first * block : (first + 4) * block] = jnp.concatenate(pieces, axis=1)

    def make_grad(i):
        if i == 0:
            for head in range(HEADS):
                grads[0][:, head * HEAD_DIM : (head + 1) * HEAD_DIM] = sum_in[head, :, :HEAD_DIM].astype(f32)
            for kind in (1, 2):
                for head in range(KV_HEADS):
                    start = (HEADS + (kind - 1) * KV_HEADS + head) * HEAD_DIM
                    parts = [
                        sum_in[head * group + g, :, kind * HEAD_DIM : (kind + 1) * HEAD_DIM].astype(f32)
                        for g in range(group)
                    ]
                    grads[0][:, start : start + HEAD_DIM] = functools.reduce(jnp.add, parts)
        elif i == 1:
            rows = sum_out.shape[1]
            for j in range(reps):
                grads[1][j * rows : (j + 1) * rows, :] = sum_out[j].astype(f32)
        elif i in (2, 3):
            join(i - 2, grads[i])
        else:
            fetch_dn.wait()

    def lamb(master, grad, mean, square):
        new_mean = 0.5 * (mean + grad)
        new_square = 0.5 * (square + grad * grad)
        root = new_square * lax.rsqrt(new_square)
        return new_mean, new_square, new_mean / (root + 1e-06) + 0.01 * master

    def sweep(i):
        down, across, tall, wide = tiles_of(masters[i])

        def body(n, carry):
            at = tile_at(masters[i], n)
            master = masters[i][at]
            new_mean, new_square, step = lamb(master, grads[i][at], means[i][at], squares[i][at])
            means[i][at] = new_mean
            squares[i][at] = new_square
            masters[i][at] = step

            def fold(value):
                return jnp.sum((value * value).reshape(tall // 8, 8, wide), axis=0)

            return carry[0] + fold(master), carry[1] + fold(step)

        zero = jnp.zeros((8, wide), f32)
        return lax.fori_loop(0, down * across, body, (zero, zero))

    at_row = lax.broadcasted_iota(jnp.int32, (8, 128), 0)
    at_lane = lax.broadcasted_iota(jnp.int32, (8, 128), 1)

    def note(sums, i, pair):
        for row in (0, 1):
            sums = sums + jnp.where((at_row == row) & (at_lane == i), jnp.sum(pair[row]), 0.0)
        return sums

    sums = jnp.zeros((8, 128), f32)
    for place, i in enumerate(LAMB_ORDER):
        make_grad(i)
        for j in range(3):
            fetch(i, j).wait()
        fetch_all(LAMB_ORDER[place + 2 : place + 3])
        pair = sweep(i)
        for j in range(4):
            store(i, j).start()
        sums = note(sums, i, pair)
    gain_total = functools.reduce(jnp.add, [gain_tiles[device] for device in range(total)])
    kinds, d_rows = g_master.shape
    gain_grad = gain_total[:kinds, :d_rows]
    gain_master = g_master[...]
    new_mean, new_square, gain_step = lamb(gain_master, gain_grad, g_mean[...], g_square[...])
    gg_out[...] = gain_grad
    gm_out[...] = new_mean
    gs_out[...] = new_square
    gp_out[...] = gain_step
    sums_out[...] = note(sums, 5, (gain_master * gain_master, gain_step * gain_step))
    for i in LAMB_ORDER:
        for j in range(4):
            store(i, j).wait()


def table_kernel(reps, count, sizes, x_ref, out_ref, near, far, held, n_send, n_recv, f_send, f_recv):
    f32 = jnp.float32
    rep = lax.axis_index("rep")
    me = lax.axis_index("shard")
    meet(
        [(rep, (me + k) % count) for k in range(1, count)] + [((rep + k) % reps, me) for k in range(1, reps)]
    )
    copies = []
    for k in range(1, count):
        copies.append(remote(x_ref, near.at[me], n_send.at[k], n_recv.at[k], (rep, (me + k) % count)))
    for copy in copies:
        copy.start()
    near[me] = x_ref[...]
    for k in range(1, count):
        frm = (me + count - k) % count
        remote(x_ref, near.at[frm], n_send.at[k], n_recv.at[k], (rep, frm)).wait_recv()
    sums = functools.reduce(jnp.add, [near[shard] for shard in range(count)])
    held[...] = sums
    more = []
    for k in range(1, reps):
        more.append(remote(held, far.at[rep], f_send.at[k], f_recv.at[k], ((rep + k) % reps, me)))
    for copy in more:
        copy.start()
    far[rep] = sums
    for k in range(1, reps):
        frm = (rep + reps - k) % reps
        remote(held, far.at[frm], f_send.at[k], f_recv.at[k], (frm, me)).wait_recv()
    totals = functools.reduce(jnp.add, [far[other] for other in range(reps)])
    at_lane = lax.broadcasted_iota(jnp.int32, (8, 128), 1)
    counts = jnp.ones((8, 128), f32)
    for i, size in enumerate(sizes):
        counts = jnp.where(at_lane == i, float(size), counts)
    out_ref[...] = jnp.sqrt(totals / counts + 1e-06)
    for copy in copies + more:
        copy.wait_send()


def fresh_kernel(table_ref, g_master, g_step, *refs):
    names = 5
    hbm_in, refs = [refs[2 * i : 2 * i + 2] for i in range(names)], refs[2 * names :]
    (gp_out, table_out), refs = refs[:2], refs[2:]
    hbm_out, refs = refs[:names], refs[names:]
    masters, steps, refs = refs[:names], refs[names : 2 * names], refs[2 * names :]
    in_sem, out_sem = refs

    def fetch(i, j):
        return pltpu.make_async_copy(hbm_in[i][j], (masters, steps)[j][i], in_sem.at[i, j])

    def store(i):
        return pltpu.make_async_copy(masters[i], hbm_out[i], out_sem.at[i])

    def fetch_all(order):
        for i in order:
            for j in (0, 1):
                fetch(i, j).start()

    fetch_all(LAMB_ORDER[:2])
    table_out[...] = table_ref[0:2, 0 : names + 1]
    rate = 0.3 * table_ref[0:1, :] / table_ref[1:2, :]
    gp_out[...] = g_master[...] - rate[:, 5:6] * g_step[...]
    for place, i in enumerate(LAMB_ORDER):
        down, across, _, _ = tiles_of(masters[i])
        scale = rate[:, i : i + 1]
        for j in (0, 1):
            fetch(i, j).wait()
        fetch_all(LAMB_ORDER[place + 2 : place + 3])

        def body(n, carry):
            at = tile_at(masters[i], n)
            masters[i][at] = masters[i][at] - scale * steps[i][at]
            return carry

        lax.fori_loop(0, down * across, body, 0)
        store(i).start()
    for i in LAMB_ORDER:
        store(i).wait()


def lamb_step(reps, count, sums, grad_down, gains, states, collective_id):
    dma = pltpu.SemaphoreType.DMA
    f32 = jnp.float32
    shape = jax.ShapeDtypeStruct
    shapes = [state[0].shape for state in states]
    like_gains = shape(gains[0].shape, f32)
    tile = shape((8, 128), f32)
    vm, hb = pl.BlockSpec(memory_space=VM), pl.BlockSpec(memory_space=HB)
    local = pltpu.CompilerParams(vmem_limit_bytes=VMEM_LIMIT)
    outs = pl.pallas_call(
        functools.partial(lamb_kernel, reps, count),
        out_shape=[tile] + [like_gains] * 4 + [shape(item, f32) for item in shapes for _ in range(4)],
        in_specs=[vm] * 7 + [hb] * 16,
        out_specs=[vm] * 5 + [hb] * 20,
        scratch_shapes=[pltpu.VMEM(item, f32) for _ in range(4) for item in shapes] + [dma((5, 3)), dma((5, 4)), dma],
        compiler_params=local,
        name="lamb_moments",
    )(*sums, *gains, *[item for state in states for item in state], grad_down)
    sums, gain_parts, parts = outs[0], outs[1:5], [outs[5 + 4 * i : 9 + 4 * i] for i in range(5)]
    sizes = [item[0] * item[1] * reps * count for item in shapes + [like_gains.shape]]
    table = pl.pallas_call(
        functools.partial(table_kernel, reps, count, sizes),
        out_shape=tile,
        in_specs=[vm],
        out_specs=vm,
        scratch_shapes=[
            pltpu.VMEM((count, 8, 128), f32),
            pltpu.VMEM((reps, 8, 128), f32),
            pltpu.VMEM((8, 128), f32),
            dma((count,)),
            dma((count,)),
            dma((reps,)),
            dma((reps,)),
        ],
        compiler_params=pltpu.CompilerParams(collective_id=collective_id, has_side_effects=True),
        name="norm_table",
    )(sums)
    fresh = pl.pallas_call(
        fresh_kernel,
        out_shape=[like_gains, shape((2, 6), f32)] + [shape(item, f32) for item in shapes],
        in_specs=[vm] * 3 + [hb] * 10,
        out_specs=[vm] * 2 + [hb] * 5,
        scratch_shapes=[pltpu.VMEM(item, f32) for _ in range(2) for item in shapes] + [dma((5, 2)), dma((5,))],
        compiler_params=local,
        name="lamb_masters",
    )(table, gains[0], gain_parts[3], *[item for i in range(5) for item in (states[i][0], parts[i][3])])
    rest = [[parts[i][j] for i in range(5)] + [gain_parts[j].T] for j in range(3)]
    return fresh[1], rest[0], rest[1], rest[2], list(fresh[2:]) + [fresh[0].T]


def rope_tables(seq_len):
    exponent = -np.arange(HEAD_DIM // 2, dtype=np.float32) * np.float32(2.0) / np.float32(HEAD_DIM)
    freq = np.float32(10000.0) ** exponent
    angle = (np.arange(seq_len, dtype=np.float32)[:, None] * freq[None, :]).astype(np.float64)
    return jnp.asarray(np.cos(angle).astype(np.float32)), jnp.asarray(np.sin(angle).astype(np.float32))


def split_device(
    tokens, cotangent, piece_starts, inproj, outproj, ffn_gate, ffn_up, ffn_down, norm_gains,
    mean_inproj, mean_outproj, mean_gate, mean_up, mean_down, mean_gains,
    square_inproj, square_outproj, square_gate, square_up, square_down, square_gains,
):
    bf16, f32 = jnp.bfloat16, jnp.float32
    reps, count = lax.axis_size("rep"), lax.axis_size("shard")
    rep = lax.axis_index("rep")
    me = lax.axis_index("shard")
    total = reps * count
    rows, width = tokens.shape
    seq_len = rows * count
    group = HEADS // KV_HEADS
    q_width, k_width = HEADS * HEAD_DIM, KV_HEADS * HEAD_DIM
    d_rows = inproj.shape[0]
    ff = ffn_gate.shape[1]
    ff_block = ff // total
    ff_part = ff // count
    o_rows = outproj.shape[0]
    per_head = HEAD_DIM // o_rows
    piece = o_rows // reps

    gain_tile = jnp.pad(norm_gains.T.astype(bf16).astype(f32), ((0, 4), (0, 128 - d_rows)))
    normed_in, gain_rows, got_in, got_gate, got_down, got_out, cut_up = opening(
        reps, count, tokens, gain_tile, inproj, outproj, ffn_gate, ffn_up, ffn_down, 1
    )
    normed_in = normed_in.reshape(seq_len, width)
    w_in = got_in.reshape(width, -1)
    w_gate = got_gate.reshape(width, ff_part)
    w_down = got_down.reshape(ff_part, width)

    position = jnp.arange(seq_len, dtype=jnp.int32)
    cosine, sine = rope_tables(seq_len)
    starts = lax.dynamic_slice_in_dim(piece_starts, rep, 1, 0)[0]
    inside = (position[:, None] >= starts[None, :]) & (position[:, None] < starts[None, :] + PIC)
    tag = jnp.sum(inside.astype(jnp.int32) * (jnp.arange(starts.shape[0], dtype=jnp.int32)[None, :] + 1), axis=1)
    attn_proj, queries, keys, values, attended, probs, damp, w_out, got_up = attention(
        reps, count, normed_in, w_in, got_out, cosine, sine, tag, cut_up, 4
    )
    w_up = got_up.reshape(width, ff_part)

    layer_out, d_middle, d_attn, gain_terms, normed_mid, d_gu, part_down = feed_forward(
        attn_proj, tokens, cotangent, gain_rows, w_gate, w_up, w_down, count, 5
    )
    d_attn, sum_gu, grad_down, d_projected = ffn_grads(
        reps, count, d_attn, w_out, queries, keys, values, cosine, sine, normed_mid, d_gu, part_down, probs, damp, d_rows, 9
    )
    input_grad, sum_in, sum_out, gain_tiles = closing(
        reps, count, d_projected, w_in, attended, normed_in, d_attn.reshape(seq_len, width), tokens, d_middle,
        gain_rows, gain_terms, piece, 12,
    )
    norm_table, gradients, new_means, new_squares, fresh = lamb_step(
        reps,
        count,
        (sum_in, sum_out, sum_gu, gain_tiles),
        grad_down,
        (norm_gains.T, mean_gains.T, square_gains.T),
        (
            (inproj, mean_inproj, square_inproj),
            (outproj, mean_outproj, square_outproj),
            (ffn_gate, mean_gate, square_gate),
            (ffn_up, mean_up, square_up),
            (ffn_down, mean_down, square_down),
        ),
        14,
    )
    return (
        layer_out,
        input_grad,
        *gradients,
        *new_means,
        *new_squares,
        *fresh,
        norm_table,
    )


def fits(mesh, shapes):
    reps, count = mesh.shape["rep"], mesh.shape["shard"]
    total = reps * count
    tokens, piece_starts, outproj, ffn_gate = shapes
    o_rows = outproj[0] // total
    return (
        reps == 4
        and count == HEADS
        and piece_starts[0] == reps
        and tokens[0] % (total * UNITS * 16) == 0
        and HEAD_DIM % o_rows == 0
        and o_rows % (16 * reps) == 0
        and HEAD_DIM // o_rows == total // HEADS
        and ffn_gate[1] % (total * 96) == 0
    )


def solution(mesh):
    split = P(("rep", "shard"), None)

    def step(*args):
        shapes = args[0].shape, args[2].shape, args[4].shape, args[5].shape
        body = split_device if fits(mesh, shapes) else per_device
        return jax.shard_map(
            body,
            mesh=mesh,
            in_specs=(split, split, P()) + (split,) * 18,
            out_specs=(split,) * 26 + (P(),),
            check_vma=False,
        )(*args)

    return step
```
